32 devices in a mesh: grp: 2 (over y), gx: 16 (over z, x, core).
Axes of the slice: x: 2, y: 2, z: 4, core: 2. Of those that a mesh axis runs over, the one named last changes fastest.
Arguments:
- features: bfloat16 [128, 32, 64, 128], P('grp', 'gx'), parts along dimension 0, may hold values from -6 to 6
- cotangent: bfloat16 [128, 32, 64, 128], P('grp', 'gx'), parts along dimension 0, may hold values from -6 to 6
- spectral_weight: bfloat16 [16384, 64, 128], P('gx'), may hold values from -0.5 to 0.5
- channel_weight: bfloat16 [64, 64], replicated, may hold values from -0.75 to 0.75
- channel_bias: float32 [64], replicated, may hold values from -3 to 3
Outputs:
- activated: bfloat16 [128, 32, 64, 128], P('grp', 'gx'), parts along dimension 0
- feature_grad: bfloat16 [128, 32, 64, 128], P('grp', 'gx'), parts along dimension 0
- spectral_grad: bfloat16 [32768, 64, 128], P(('grp', 'gx')), parts along dimension 0
The draws below stay inside these ranges and needn't reach their ends.
There are 2 independent parts, one for each index of `grp`. The reference program is written for one: setup_inputs(seed, part) draws one part's arguments, and reference() takes and returns one part's arrays. A program takes and returns all parts, laid end to end along the dimension named above; an argument that names none is the same for every part. Nothing has to cross between parts.
All inputs are finite; a program needn't handle non-finite values.
Results may differ from the reference program's by a relative error of at most 0.018.
Values may be sent and summed in bfloat16 or wider, within the bound.
No kernel may reach another device: no remote copies, remote signals or barrier semaphores. Data moves between devices by JAX's collectives and lax.ppermute only.
A program may use at most 192 MiB of HBM per device.

```python
import math
import jax
import jax.numpy as jnp

C = 64
MX = 32
MY = 32
MZ = 16
NZ = 128
NY = 64
NX = 32
MODES = 16384


def level_of(stream_key, extent, shards, low, largest):
    def one(axis_at, shards_of):
        heights = jax.random.uniform(jax.random.fold_in(jax.random.fold_in(stream_key, 6), axis_at), (shards_of,), jnp.float32, low / len(shards), largest / len(shards))
        return jnp.repeat(jnp.exp(heights), extent[axis_at] // shards_of).reshape((-1,) + (1,) * (len(extent) - axis_at - 1))

    factor_of = one(*shards[0])
    for cut in shards[1:]:
        factor_of = factor_of * one(*cut)
    return factor_of


def noise(own_key, dims, scale, most, split=(), held_as=jnp.bfloat16):
    result = scale * jax.random.normal(own_key, dims, jnp.float32)
    if split:
        result = result * level_of(own_key, dims, split, -0.22, 0.18)
    return jnp.clip(result, -most, most).astype(held_as)


def setup_inputs(seed: int = 0, part: int = 0) -> dict:
    streams_of = jax.random.split(jax.random.key(seed), 6)
    own_keys = jax.random.split(jax.random.fold_in(streams_of[5], part), 6)
    return {
        "features": noise(own_keys[0], (C, NX, NY, NZ), 1.0, 6.0, ((1, 16),)),
        "cotangent": noise(own_keys[1], (C, NX, NY, NZ), 1.0, 6.0, ((1, 16),)),
        "spectral_weight": noise(streams_of[2], (MODES, C, 2 * C), (2 * C) ** -0.5, 0.5, ((0, 16),)),
        "channel_weight": noise(streams_of[3], (C, C), C ** -0.5, 0.75),
        "channel_bias": noise(streams_of[4], (C,), 0.5, 3.0, (), jnp.float32),
    }


SQRT_TWO_PI = math.sqrt(2.0 / math.pi)
CUBIC_COEF = 0.044715

def freq_index(retained, length):
    ladder = jnp.arange(retained, dtype=jnp.int32)
    return jnp.where(ladder < retained // 2, ladder, length - retained + ladder).astype(jnp.int32)

def cos_sin(wavenum, length):
    points = jnp.arange(length, dtype=jnp.int32)
    angles = (wavenum[:, None] * points[None, :] % length).astype(jnp.float32) * (2.0 * math.pi / length)
    return (jnp.cos(angles), jnp.sin(angles))

def analysis_pair(wavenum, length):
    cosine, sine_wave = cos_sin(wavenum, length)
    cosine, sine_wave = (cosine.T, sine_wave.T)
    return jnp.stack([jnp.stack([cosine, -sine_wave], 1), jnp.stack([sine_wave, cosine], 1)], 1).astype(jnp.bfloat16)

def synthesis_pair(wavenum, length):
    cosine, sine_wave = cos_sin(wavenum, length)
    return jnp.stack([jnp.stack([cosine, sine_wave], 1), jnp.stack([-sine_wave, cosine], 1)], 1).astype(jnp.bfloat16)

def depth_table(retained, length):
    cosine, sine_wave = cos_sin(jnp.arange(retained, dtype=jnp.int32), length)
    return jnp.concatenate([cosine, -sine_wave], 0).astype(jnp.bfloat16)

def gelu_parts(inputs):
    cubed_in = inputs * inputs * inputs
    tangent = jnp.tanh(SQRT_TWO_PI * (inputs + CUBIC_COEF * cubed_in))
    output = 0.5 * inputs * (1.0 + tangent)
    derivative = 0.5 * (1.0 + tangent) + 0.5 * inputs * (1.0 - tangent * tangent) * SQRT_TWO_PI * (1.0 + 3.0 * CUBIC_COEF * inputs * inputs)
    return (output, derivative)

def mode_product(coeffs, weights, channels):
    stacked = coeffs.reshape(coeffs.shape[0], 2, channels).astype(jnp.float32)
    halves = jnp.einsum('mac,mcj->amj', stacked, weights.astype(jnp.float32))
    real_out = halves[0, :, :channels] - halves[1, :, channels:]
    imag_out = halves[0, :, channels:] + halves[1, :, :channels]
    return jnp.concatenate([real_out, imag_out], 1).astype(jnp.bfloat16)

def mode_grads(coeffs, weights, grad_modes, channels, weight_scale, input_scale):
    number = coeffs.shape[0]
    stacked = coeffs.reshape(number, 2, channels).astype(jnp.float32)
    grad_pairs = grad_modes.reshape(number, 2, channels).astype(jnp.float32)
    real_w = jnp.einsum('mac,mao->mco', stacked, grad_pairs)
    imag_w = jnp.einsum('mc,mo->mco', stacked[:, 0], grad_pairs[:, 1]) - jnp.einsum('mc,mo->mco', stacked[:, 1], grad_pairs[:, 0])
    weight_grad = (jnp.concatenate([real_w, imag_w], 2) * weight_scale).astype(jnp.bfloat16)
    straight = jnp.concatenate([grad_pairs[:, 0], grad_pairs[:, 1]], 1)
    rotated = jnp.concatenate([grad_pairs[:, 1], -grad_pairs[:, 0]], 1)
    wide_weights = weights.astype(jnp.float32)
    real_x = jnp.einsum('mcj,mj->mc', wide_weights, straight)
    imag_x = jnp.einsum('mcj,mj->mc', wide_weights, rotated)
    input_grad = (jnp.concatenate([real_x, imag_x], 1) * input_scale).astype(jnp.bfloat16)
    return (weight_grad, input_grad)

def reference(features, cotangent, spectral_weight, channel_weight, channel_bias):
    wave_pairs = MY * MZ
    forward_scale = 1.0 / math.sqrt(NX * NY * NZ)
    inverse_scale = 1.0 / math.sqrt(MODES)
    weight_scale = math.sqrt(MODES / (NX * NY * NZ))
    depth_basis = depth_table(MZ, NZ)
    across_y = analysis_pair(freq_index(MY, NY), NY).astype(jnp.float32)
    across_x = analysis_pair(freq_index(MX, NX), NX).astype(jnp.float32)
    back_y = synthesis_pair(freq_index(MY, NY), NY).astype(jnp.float32)
    back_x = synthesis_pair(freq_index(MX, NX), NX).astype(jnp.float32)
    depth_part = jnp.dot(features, depth_basis.T, preferred_element_type=jnp.float32).astype(jnp.bfloat16)
    depth_five = depth_part.reshape(C, NX, NY, 2, MZ).astype(jnp.float32)
    plane_part = jnp.einsum('cxyaz,yabk->cxbkz', depth_five, across_y).astype(jnp.bfloat16).reshape(C, NX, 2, wave_pairs)
    mode_sums = jnp.einsum('cxaq,xabk->qkbc', plane_part.astype(jnp.float32), across_x).reshape(MODES, 2 * C)
    coeffs = (mode_sums * forward_scale).astype(jnp.bfloat16)
    mode_block = math.gcd(MODES, 1024)
    spectral_list = []
    for offset in range(0, MODES, mode_block):
        spectral_list.append(mode_product(coeffs[offset:offset + mode_block], spectral_weight[offset:offset + mode_block], C))
    spectral = jnp.concatenate(spectral_list, 0)
    planes_back = jnp.einsum('qkao,kabx->oxbq', spectral.reshape(wave_pairs, MX, 2, C).astype(jnp.float32), back_x).astype(jnp.bfloat16)
    slab_size = math.gcd(NX, 16)
    act_list = []
    upstream_list = []
    rows_list = []
    for offset in range(0, NX, slab_size):
        rows_back = planes_back[:, offset:offset + slab_size].reshape(C, slab_size, 2, MY, MZ).astype(jnp.float32)
        lines_back = jnp.einsum('oxakz,kaby->oxybz', rows_back, back_y).astype(jnp.bfloat16).reshape(C, slab_size, NY, 2 * MZ)
        spectral_term = jnp.dot(lines_back, depth_basis, preferred_element_type=jnp.float32) * inverse_scale
        local_in = features[:, offset:offset + slab_size]
        pointwise = jnp.dot(channel_weight, local_in.reshape(C, -1), preferred_element_type=jnp.float32).reshape(C, slab_size, NY, NZ)
        hidden = spectral_term + pointwise + channel_bias.astype(jnp.float32)[:, None, None, None]
        activated, derivative = gelu_parts(hidden)
        act_list.append(activated.astype(jnp.bfloat16))
        upstream = (cotangent[:, offset:offset + slab_size].astype(jnp.float32) * derivative).astype(jnp.bfloat16)
        upstream_list.append(upstream)
        lines_grad = (jnp.dot(upstream, depth_basis.T, preferred_element_type=jnp.float32) * inverse_scale).astype(jnp.bfloat16)
        lines_five = lines_grad.reshape(C, slab_size, NY, 2, MZ).astype(jnp.float32)
        rows_grad = jnp.einsum('oxybz,kaby->oxakz', lines_five, back_y).astype(jnp.bfloat16).reshape(C, slab_size, 2, wave_pairs)
        rows_list.append(rows_grad)
    activated_all = jnp.concatenate(act_list, 1)
    rows_all = jnp.concatenate(rows_list, 1)
    grad_sums = jnp.einsum('oxbq,kabx->qkao', rows_all.astype(jnp.float32), back_x).reshape(MODES, 2 * C)
    grad_modes = grad_sums.astype(jnp.bfloat16)
    weight_list = []
    coeff_list = []
    for offset in range(0, MODES, mode_block):
        weight_grad, input_grad = mode_grads(coeffs[offset:offset + mode_block], spectral_weight[offset:offset + mode_block], grad_modes[offset:offset + mode_block], C, weight_scale, forward_scale)
        weight_list.append(weight_grad)
        coeff_list.append(input_grad)
    spectral_grad = jnp.concatenate(weight_list, 0)
    coeff_grad = jnp.concatenate(coeff_list, 0)
    plane_grad = jnp.einsum('qkbc,xabk->cxaq', coeff_grad.reshape(wave_pairs, MX, 2, C).astype(jnp.float32), across_x).astype(jnp.bfloat16)
    grad_list = []
    for index_slab, offset in enumerate(range(0, NX, slab_size)):
        block_grad = plane_grad[:, offset:offset + slab_size].reshape(C, slab_size, 2, MY, MZ).astype(jnp.float32)
        depth_grad = jnp.einsum('cxbkz,yabk->cxyaz', block_grad, across_y).astype(jnp.bfloat16).reshape(C, slab_size, NY, 2 * MZ)
        upstream = upstream_list[index_slab]
        channel_back = jnp.dot(channel_weight.T, upstream.reshape(C, -1), preferred_element_type=jnp.float32).reshape(C, slab_size, NY, NZ)
        total_grad = jnp.dot(depth_grad, depth_basis, preferred_element_type=jnp.float32) + channel_back
        grad_list.append(total_grad.astype(jnp.bfloat16))
    feature_grad = jnp.concatenate(grad_list, 1)
    return (activated_all, feature_grad, spectral_grad)
```

```python
import math

import jax
import jax.numpy as jnp
from jax import lax
from jax.sharding import PartitionSpec as P

MX = 32
MY = 32
MZ = 16


SQRT_TWO_PI = math.sqrt(2.0 / math.pi)
CUBIC_COEF = 0.044715


def freq_index(retained, length):
    ladder = jnp.arange(retained, dtype=jnp.int32)
    return jnp.where(ladder < retained // 2, ladder, length - retained + ladder)


def cos_sin(wavenum, length):
    points = jnp.arange(length, dtype=jnp.int32)
    angles = (wavenum[:, None] * points[None, :] % length).astype(jnp.float32) * (
        2.0 * math.pi / length
    )
    return (jnp.cos(angles), jnp.sin(angles))


def analysis_pair(wavenum, length):
    cosine, sine_wave = cos_sin(wavenum, length)
    cosine, sine_wave = (cosine.T, sine_wave.T)
    return jnp.stack(
        [jnp.stack([cosine, -sine_wave], 1), jnp.stack([sine_wave, cosine], 1)], 1
    ).astype(jnp.bfloat16)


def synthesis_pair(wavenum, length):
    cosine, sine_wave = cos_sin(wavenum, length)
    return jnp.stack(
        [jnp.stack([cosine, sine_wave], 1), jnp.stack([-sine_wave, cosine], 1)], 1
    ).astype(jnp.bfloat16)


def depth_table(retained, length):
    cosine, sine_wave = cos_sin(jnp.arange(retained, dtype=jnp.int32), length)
    return jnp.concatenate([cosine, -sine_wave], 0).astype(jnp.bfloat16)


def gelu_parts(inputs):
    cubed_in = inputs * inputs * inputs
    tangent = jnp.tanh(SQRT_TWO_PI * (inputs + CUBIC_COEF * cubed_in))
    output = 0.5 * inputs * (1.0 + tangent)
    derivative = 0.5 * (1.0 + tangent) + 0.5 * inputs * (1.0 - tangent * tangent) * SQRT_TWO_PI * (
        1.0 + 3.0 * CUBIC_COEF * inputs * inputs
    )
    return (output, derivative)


def mode_product(coeffs, weights, channels):
    stacked = coeffs.reshape(coeffs.shape[0], 2, channels)
    halves = jnp.einsum("mac,mcj->amj", stacked, weights, preferred_element_type=jnp.float32)
    real_out = halves[0, :, :channels] - halves[1, :, channels:]
    imag_out = halves[0, :, channels:] + halves[1, :, :channels]
    return jnp.concatenate([real_out, imag_out], 1).astype(jnp.bfloat16)


def mode_grads(coeffs, weights, grad_modes, channels, weight_scale, input_scale):
    number = coeffs.shape[0]
    stacked = coeffs.reshape(number, 2, channels)
    grad_pairs = grad_modes.reshape(number, 2, channels)
    real_w = jnp.einsum("mac,mao->mco", stacked, grad_pairs, preferred_element_type=jnp.float32)
    imag_w = jnp.einsum(
        "mc,mo->mco", stacked[:, 0], grad_pairs[:, 1], preferred_element_type=jnp.float32
    ) - jnp.einsum(
        "mc,mo->mco", stacked[:, 1], grad_pairs[:, 0], preferred_element_type=jnp.float32
    )
    weight_grad = (jnp.concatenate([real_w, imag_w], 2) * weight_scale).astype(jnp.bfloat16)
    straight = jnp.concatenate([grad_pairs[:, 0], grad_pairs[:, 1]], 1)
    rotated = jnp.concatenate([grad_pairs[:, 1], -grad_pairs[:, 0]], 1)
    real_x = jnp.einsum("mcj,mj->mc", weights, straight, preferred_element_type=jnp.float32)
    imag_x = jnp.einsum("mcj,mj->mc", weights, rotated, preferred_element_type=jnp.float32)
    input_grad = (jnp.concatenate([real_x, imag_x], 1) * input_scale).astype(jnp.bfloat16)
    return (weight_grad, input_grad)


def body(features, cotangent, spectral_weight, channel_weight, channel_bias):
    channels, planes, lines, depth_len = features.shape
    devices = lax.axis_size("gx")
    all_planes = planes * devices
    owned_modes = spectral_weight.shape[0]
    wave_pairs = MY * MZ
    forward_scale = 1.0 / math.sqrt(all_planes * lines * depth_len)
    inverse_scale = 1.0 / math.sqrt(MX * wave_pairs)
    weight_scale = math.sqrt(MX * wave_pairs / (all_planes * lines * depth_len))
    depth_basis = depth_table(MZ, depth_len)
    across_y = analysis_pair(freq_index(MY, lines), lines)
    back_y = synthesis_pair(freq_index(MY, lines), lines)
    across_full = analysis_pair(freq_index(MX, all_planes), all_planes)
    back_full = synthesis_pair(freq_index(MX, all_planes), all_planes)
    depth_part = jnp.dot(features, depth_basis.T, preferred_element_type=jnp.float32).astype(
        jnp.bfloat16
    )
    plane_part = (
        jnp.einsum(
            "cxyaz,yabk->cxbkz",
            depth_part.reshape(channels, planes, lines, 2, MZ),
            across_y,
            preferred_element_type=jnp.float32,
        )
        .astype(jnp.bfloat16)
        .reshape(channels, planes, 2, wave_pairs)
    )
    all_rows = lax.all_to_all(plane_part, "gx", split_axis=3, concat_axis=1, tiled=True)
    mode_sums = jnp.einsum(
        "cxaq,xabk->qkbc", all_rows, across_full, preferred_element_type=jnp.float32
    ).reshape(owned_modes, 2 * channels)
    coeffs = (mode_sums * forward_scale).astype(jnp.bfloat16)
    spectral = mode_product(coeffs, spectral_weight, channels)
    planes_all = jnp.einsum(
        "qkao,kabx->oxbq",
        spectral.reshape(owned_modes // MX, MX, 2, channels),
        back_full,
        preferred_element_type=jnp.float32,
    ).astype(jnp.bfloat16)
    planes_back = lax.all_to_all(planes_all, "gx", split_axis=1, concat_axis=3, tiled=True)
    lines_back = (
        jnp.einsum(
            "oxakz,kaby->oxybz",
            planes_back.reshape(channels, planes, 2, MY, MZ),
            back_y,
            preferred_element_type=jnp.float32,
        )
        .astype(jnp.bfloat16)
        .reshape(channels, planes, lines, 2 * MZ)
    )
    spectral_term = (
        jnp.dot(lines_back, depth_basis, preferred_element_type=jnp.float32) * inverse_scale
    )
    pointwise = jnp.einsum(
        "oc,cxyz->oxyz", channel_weight, features, preferred_element_type=jnp.float32
    )
    hidden = spectral_term + pointwise + channel_bias[:, None, None, None]
    activated, derivative = gelu_parts(hidden)
    upstream = (cotangent.astype(jnp.float32) * derivative).astype(jnp.bfloat16)
    lines_grad = (
        jnp.dot(upstream, depth_basis.T, preferred_element_type=jnp.float32) * inverse_scale
    ).astype(jnp.bfloat16)
    rows_grad = (
        jnp.einsum(
            "oxybz,kaby->oxakz",
            lines_grad.reshape(channels, planes, lines, 2, MZ),
            back_y,
            preferred_element_type=jnp.float32,
        )
        .astype(jnp.bfloat16)
        .reshape(channels, planes, 2, wave_pairs)
    )
    all_grads = lax.all_to_all(rows_grad, "gx", split_axis=3, concat_axis=1, tiled=True)
    grad_sums = jnp.einsum(
        "oxbq,kabx->qkao", all_grads, back_full, preferred_element_type=jnp.float32
    ).reshape(owned_modes, 2 * channels)
    grad_modes = grad_sums.astype(jnp.bfloat16)
    spectral_grad, coeff_grad = mode_grads(
        coeffs, spectral_weight, grad_modes, channels, weight_scale, forward_scale
    )
    plane_all = jnp.einsum(
        "qkbc,xabk->cxaq",
        coeff_grad.reshape(owned_modes // MX, MX, 2, channels),
        across_full,
        preferred_element_type=jnp.float32,
    ).astype(jnp.bfloat16)
    plane_grad = lax.all_to_all(plane_all, "gx", split_axis=1, concat_axis=3, tiled=True)
    depth_grad = (
        jnp.einsum(
            "cxbkz,yabk->cxyaz",
            plane_grad.reshape(channels, planes, 2, MY, MZ),
            across_y,
            preferred_element_type=jnp.float32,
        )
        .astype(jnp.bfloat16)
        .reshape(channels, planes, lines, 2 * MZ)
    )
    channel_back = jnp.einsum(
        "oc,oxyz->cxyz", channel_weight, upstream, preferred_element_type=jnp.float32
    )
    feature_grad = (
        jnp.dot(depth_grad, depth_basis, preferred_element_type=jnp.float32) + channel_back
    ).astype(jnp.bfloat16)
    return (activated.astype(jnp.bfloat16), feature_grad, spectral_grad)


def solution(mesh):
    in_specs = (
        P("grp", "gx", None, None),
        P("grp", "gx", None, None),
        P("gx", None, None),
        P(),
        P(),
    )
    out_specs = (
        P("grp", "gx", None, None),
        P("grp", "gx", None, None),
        P(("grp", "gx"), None, None),
    )
    return jax.shard_map(body, mesh=mesh, in_specs=in_specs, out_specs=out_specs, check_vma=False)
```

```python
import functools
import math

import jax
import jax.numpy as jnp
import ml_dtypes
import numpy as np
from jax import lax
from jax.experimental import pallas as pl
from jax.experimental.pallas import tpu as pltpu
from jax.sharding import PartitionSpec as P

MX = 32
MY = 32
MZ = 16


SQRT_TWO_PI = math.sqrt(2.0 / math.pi)
CUBIC_COEF = 0.044715


def freq_index(retained, length):
    ladder = jnp.arange(retained, dtype=jnp.int32)
    return jnp.where(ladder < retained // 2, ladder, length - retained + ladder)


def cos_sin(wavenum, length):
    points = jnp.arange(length, dtype=jnp.int32)
    angles = (wavenum[:, None] * points[None, :] % length).astype(jnp.float32) * (
        2.0 * math.pi / length
    )
    return (jnp.cos(angles), jnp.sin(angles))


def analysis_pair(wavenum, length):
    cosine, sine_wave = cos_sin(wavenum, length)
    cosine, sine_wave = (cosine.T, sine_wave.T)
    return jnp.stack(
        [jnp.stack([cosine, -sine_wave], 1), jnp.stack([sine_wave, cosine], 1)], 1
    ).astype(jnp.bfloat16)


def synthesis_pair(wavenum, length):
    cosine, sine_wave = cos_sin(wavenum, length)
    return jnp.stack(
        [jnp.stack([cosine, sine_wave], 1), jnp.stack([-sine_wave, cosine], 1)], 1
    ).astype(jnp.bfloat16)


def depth_table(retained, length):
    cosine, sine_wave = cos_sin(jnp.arange(retained, dtype=jnp.int32), length)
    return jnp.concatenate([cosine, -sine_wave], 0).astype(jnp.bfloat16)


def gelu_parts(inputs):
    cubed_in = inputs * inputs * inputs
    tangent = jnp.tanh(SQRT_TWO_PI * (inputs + CUBIC_COEF * cubed_in))
    output = 0.5 * inputs * (1.0 + tangent)
    derivative = 0.5 * (1.0 + tangent) + 0.5 * inputs * (1.0 - tangent * tangent) * SQRT_TWO_PI * (
        1.0 + 3.0 * CUBIC_COEF * inputs * inputs
    )
    return (output, derivative)


def mode_product(coeffs, weights, channels):
    stacked = coeffs.reshape(coeffs.shape[0], 2, channels)
    halves = jnp.einsum("mac,mcj->amj", stacked, weights, preferred_element_type=jnp.float32)
    real_out = halves[0, :, :channels] - halves[1, :, channels:]
    imag_out = halves[0, :, channels:] + halves[1, :, :channels]
    return jnp.concatenate([real_out, imag_out], 1).astype(jnp.bfloat16)


def mode_grads(coeffs, weights, grad_modes, channels, weight_scale, input_scale):
    number = coeffs.shape[0]
    stacked = coeffs.reshape(number, 2, channels)
    grad_pairs = grad_modes.reshape(number, 2, channels)
    real_w = jnp.einsum("mac,mao->mco", stacked, grad_pairs, preferred_element_type=jnp.float32)
    imag_w = jnp.einsum(
        "mc,mo->mco", stacked[:, 0], grad_pairs[:, 1], preferred_element_type=jnp.float32
    ) - jnp.einsum(
        "mc,mo->mco", stacked[:, 1], grad_pairs[:, 0], preferred_element_type=jnp.float32
    )
    weight_grad = (jnp.concatenate([real_w, imag_w], 2) * weight_scale).astype(jnp.bfloat16)
    straight = jnp.concatenate([grad_pairs[:, 0], grad_pairs[:, 1]], 1)
    rotated = jnp.concatenate([grad_pairs[:, 1], -grad_pairs[:, 0]], 1)
    real_x = jnp.einsum("mcj,mj->mc", weights, straight, preferred_element_type=jnp.float32)
    imag_x = jnp.einsum("mcj,mj->mc", weights, rotated, preferred_element_type=jnp.float32)
    input_grad = (jnp.concatenate([real_x, imag_x], 1) * input_scale).astype(jnp.bfloat16)
    return (weight_grad, input_grad)


def general_body(features, cotangent, spectral_weight, channel_weight, channel_bias):
    channels, planes, lines, depth_len = features.shape
    devices = lax.axis_size("gx")
    all_planes = planes * devices
    owned_modes = spectral_weight.shape[0]
    wave_pairs = MY * MZ
    forward_scale = 1.0 / math.sqrt(all_planes * lines * depth_len)
    inverse_scale = 1.0 / math.sqrt(MX * wave_pairs)
    weight_scale = math.sqrt(MX * wave_pairs / (all_planes * lines * depth_len))
    depth_basis = depth_table(MZ, depth_len)
    across_y = analysis_pair(freq_index(MY, lines), lines)
    back_y = synthesis_pair(freq_index(MY, lines), lines)
    across_full = analysis_pair(freq_index(MX, all_planes), all_planes)
    back_full = synthesis_pair(freq_index(MX, all_planes), all_planes)
    depth_part = jnp.dot(features, depth_basis.T, preferred_element_type=jnp.float32).astype(
        jnp.bfloat16
    )
    plane_part = (
        jnp.einsum(
            "cxyaz,yabk->cxbkz",
            depth_part.reshape(channels, planes, lines, 2, MZ),
            across_y,
            preferred_element_type=jnp.float32,
        )
        .astype(jnp.bfloat16)
        .reshape(channels, planes, 2, wave_pairs)
    )
    all_rows = lax.all_to_all(plane_part, "gx", split_axis=3, concat_axis=1, tiled=True)
    mode_sums = jnp.einsum(
        "cxaq,xabk->qkbc", all_rows, across_full, preferred_element_type=jnp.float32
    ).reshape(owned_modes, 2 * channels)
    coeffs = (mode_sums * forward_scale).astype(jnp.bfloat16)
    spectral = mode_product(coeffs, spectral_weight, channels)
    planes_all = jnp.einsum(
        "qkao,kabx->oxbq",
        spectral.reshape(owned_modes // MX, MX, 2, channels),
        back_full,
        preferred_element_type=jnp.float32,
    ).astype(jnp.bfloat16)
    planes_back = lax.all_to_all(planes_all, "gx", split_axis=1, concat_axis=3, tiled=True)
    lines_back = (
        jnp.einsum(
            "oxakz,kaby->oxybz",
            planes_back.reshape(channels, planes, 2, MY, MZ),
            back_y,
            preferred_element_type=jnp.float32,
        )
        .astype(jnp.bfloat16)
        .reshape(channels, planes, lines, 2 * MZ)
    )
    spectral_term = (
        jnp.dot(lines_back, depth_basis, preferred_element_type=jnp.float32) * inverse_scale
    )
    pointwise = jnp.einsum(
        "oc,cxyz->oxyz", channel_weight, features, preferred_element_type=jnp.float32
    )
    hidden = spectral_term + pointwise + channel_bias[:, None, None, None]
    activated, derivative = gelu_parts(hidden)
    upstream = (cotangent.astype(jnp.float32) * derivative).astype(jnp.bfloat16)
    lines_grad = (
        jnp.dot(upstream, depth_basis.T, preferred_element_type=jnp.float32) * inverse_scale
    ).astype(jnp.bfloat16)
    rows_grad = (
        jnp.einsum(
            "oxybz,kaby->oxakz",
            lines_grad.reshape(channels, planes, lines, 2, MZ),
            back_y,
            preferred_element_type=jnp.float32,
        )
        .astype(jnp.bfloat16)
        .reshape(channels, planes, 2, wave_pairs)
    )
    all_grads = lax.all_to_all(rows_grad, "gx", split_axis=3, concat_axis=1, tiled=True)
    grad_sums = jnp.einsum(
        "oxbq,kabx->qkao", all_grads, back_full, preferred_element_type=jnp.float32
    ).reshape(owned_modes, 2 * channels)
    grad_modes = grad_sums.astype(jnp.bfloat16)
    spectral_grad, coeff_grad = mode_grads(
        coeffs, spectral_weight, grad_modes, channels, weight_scale, forward_scale
    )
    plane_all = jnp.einsum(
        "qkbc,xabk->cxaq",
        coeff_grad.reshape(owned_modes // MX, MX, 2, channels),
        across_full,
        preferred_element_type=jnp.float32,
    ).astype(jnp.bfloat16)
    plane_grad = lax.all_to_all(plane_all, "gx", split_axis=1, concat_axis=3, tiled=True)
    depth_grad = (
        jnp.einsum(
            "cxbkz,yabk->cxyaz",
            plane_grad.reshape(channels, planes, 2, MY, MZ),
            across_y,
            preferred_element_type=jnp.float32,
        )
        .astype(jnp.bfloat16)
        .reshape(channels, planes, lines, 2 * MZ)
    )
    channel_back = jnp.einsum(
        "oc,oxyz->cxyz", channel_weight, upstream, preferred_element_type=jnp.float32
    )
    feature_grad = (
        jnp.dot(depth_grad, depth_basis, preferred_element_type=jnp.float32) + channel_back
    ).astype(jnp.bfloat16)
    return (activated.astype(jnp.bfloat16), feature_grad, spectral_grad)


PLANES = 2
GROUP = 8
NT = (((1,), (1,)), ((), ()))
F32 = jnp.float32
BF16 = jnp.bfloat16


def np_freq(retained, length):
    ladder = np.arange(retained)
    return np.where(ladder < retained // 2, ladder, length - retained + ladder)


def np_angles(wavenum, length):
    points = np.arange(length)
    return (wavenum[:, None] * points[None, :] % length) * (2.0 * math.pi / length)


def as_bf16(table):
    return np.asarray(table, np.float32).astype(ml_dtypes.bfloat16)


def rotation(angle, sign):
    cosine, sine_wave = np.cos(angle), sign * np.sin(angle)
    return np.stack([np.stack([cosine, -sine_wave]), np.stack([sine_wave, cosine])])


@functools.lru_cache(maxsize=None)
def tables(devices, lines, depth_len):
    planes_all = devices * PLANES
    angle = np_angles(np.arange(MZ), depth_len)
    depth = np.stack([np.cos(angle), -np.sin(angle)])
    eye = np.eye(GROUP)
    depth_block = np.einsum("akz,ij->akijz", depth, eye).reshape(2 * MZ * GROUP, GROUP * depth_len)
    plane_eye = np.eye(PLANES)
    angle = np_angles(np_freq(MY, lines), lines).reshape(devices, MY // devices, lines)
    across = np.einsum("badly,xw->ldbxawy", rotation(angle, -1.0), plane_eye)
    across = across.reshape(MY * 2 * PLANES, 2 * PLANES * lines)
    back = np.einsum("pbdly,xw->pxyldbw", rotation(angle, 1.0), plane_eye)
    back = back.reshape(2 * PLANES * lines, MY * 2 * PLANES)
    angle = np_angles(np_freq(MX, planes_all), planes_all).reshape(MX // 4, 4, devices, PLANES)
    forward = rotation(angle, -1.0)
    rows = np.einsum("batksx->tbksax", forward).reshape(MX // 4, 2, 4, devices * 2 * PLANES)
    plain = rows.reshape(2 * MX, -1)
    both = np.stack([rows, rows[:, ::-1]], 1).reshape(4 * MX, -1)
    turned = np.concatenate([rows[:, 1:], -rows[:, :1]], 1).reshape(2 * MX, -1)
    straight_rotated = np.concatenate([plain, turned], 0)
    inverse = np.einsum("batksx->sbxtak", rotation(angle, 1.0)).reshape(-1, 2 * MX)
    return {
        "depth": as_bf16(depth_block),
        "across_y": as_bf16(across),
        "back_y": as_bf16(back),
        "plain_x": as_bf16(plain),
        "both_x": as_bf16(both),
        "straight_x": as_bf16(straight_rotated),
        "back_x": as_bf16(inverse),
    }


def dot_nn(left, right):
    return jnp.dot(left, right, preferred_element_type=F32)


def dot_nt(left, right):
    return lax.dot_general(left, right, NT, preferred_element_type=F32)


def lanes(shape):
    return lax.broadcasted_iota(jnp.int32, shape, len(shape) - 1)


def sublanes(shape):
    return lax.broadcasted_iota(jnp.int32, shape, len(shape) - 2)


def swap_halves(block):
    return pltpu.roll(block, 64, 1)


def depth_analysis(slabs, depth, scale, group, lines_ref):
    wide = jnp.concatenate(slabs, axis=1)
    parts = dot_nt(depth, wide)
    if scale is not None:
        parts = parts * scale
    width = wide.shape[0]
    start = pl.multiple_of(group * GROUP, GROUP)
    for a in range(2):
        lines_ref[:, pl.ds(start, GROUP), a * width : (a + 1) * width] = parts[
            a * MZ * GROUP : (a + 1) * MZ * GROUP
        ].reshape(MZ, GROUP, width)


def rows_analysis(lines_ref, across_ref, rows_ref, out_ref):
    channels, width = lines_ref.shape[1], lines_ref.shape[2]
    across = across_ref[...]
    half = across.shape[0] // 2
    for kzh in range(MZ // 2):
        pair = lines_ref[2 * kzh : 2 * kzh + 2].reshape(2 * channels, width).astype(BF16)
        rows = dot_nt(across, pair)
        for kyl in range(2):
            rows_ref[pl.ds(kyl * 8 + kzh, half, stride=16), :] = rows[
                kyl * half : (kyl + 1) * half
            ]
    out_ref[...] = rows_ref[...].astype(BF16)


def rows_gather(block_ref, rows_ref, spec_ref):
    rows_ref[...] = block_ref[...].astype(F32)
    count = rows_ref.shape[0] // 16
    eye = (sublanes((128, 128)) == lanes((128, 128))).astype(BF16)
    for kzh in range(MZ // 2):
        both = jnp.concatenate(
            [rows_ref[pl.ds(kyl * 8 + kzh, count, stride=16), :] for kyl in range(2)], axis=0
        ).astype(BF16)
        turned = dot_nt(eye, both)
        for h in range(2):
            spec_ref[:, (2 * kzh + h) * GROUP : (2 * kzh + h + 1) * GROUP, :] = turned[
                h * 64 : (h + 1) * 64
            ].reshape(8, GROUP, turned.shape[1])


def synthesis(group, spec_ref, back, depth, scale):
    lines = dot_nt(back, spec_ref[group].astype(BF16))
    if scale is not None:
        lines = lines * scale
    lines = lines.astype(BF16)
    half = lines.shape[0] // 2
    return dot_nn(jnp.concatenate([lines[:half], lines[half:]], axis=1), depth)


def flat(slab):
    return slab.reshape(slab.shape[0] * slab.shape[1], slab.shape[2])


def analysis_kernel(per_step, field_ref, depth_ref, across_ref, out_ref, lines_ref, rows_ref):
    step = pl.program_id(0)
    depth = depth_ref[...]
    for g in range(per_step):
        slabs = [flat(field_ref[g * GROUP + ci]) for ci in range(GROUP)]
        depth_analysis(slabs, depth, None, step * per_step + g, lines_ref)

    @pl.when(step == pl.num_programs(0) - 1)
    def _():
        rows_analysis(lines_ref, across_ref, rows_ref, out_ref)


def middle_kernel(
    per_step,
    inverse_scale,
    block_ref,
    point_ref,
    cot_ref,
    bias_ref,
    depth_ref,
    across_ref,
    back_ref,
    act_ref,
    up_ref,
    out_ref,
    lines_ref,
    rows_ref,
    spec_ref,
):
    step = pl.program_id(0)

    @pl.when(step == 0)
    def _():
        rows_gather(block_ref, rows_ref, spec_ref)

    depth = depth_ref[...]
    back = back_ref[...]
    for g in range(per_step):
        group = step * per_step + g
        spectral = synthesis(group, spec_ref, back, depth, inverse_scale)
        slabs = []
        for oi in range(GROUP):
            index = g * GROUP + oi
            hidden = (
                spectral[:, oi * 128 : (oi + 1) * 128]
                + flat(point_ref[index])
                + bias_ref[group * GROUP + oi]
            )
            square = hidden * hidden
            gate = 0.5 + 0.5 * jnp.tanh(
                hidden * (SQRT_TWO_PI + (SQRT_TWO_PI * CUBIC_COEF) * square)
            )
            slope = hidden * (2.0 * SQRT_TWO_PI + (6.0 * SQRT_TWO_PI * CUBIC_COEF) * square)
            derivative = gate + (gate - gate * gate) * slope
            upstream = (flat(cot_ref[index]).astype(F32) * derivative).astype(BF16)
            act_ref[index] = (hidden * gate).astype(BF16).reshape(act_ref.shape[1:])
            up_ref[index] = upstream.reshape(up_ref.shape[1:])
            slabs.append(upstream)
        depth_analysis(slabs, depth, inverse_scale, group, lines_ref)

    @pl.when(step == pl.num_programs(0) - 1)
    def _():
        rows_analysis(lines_ref, across_ref, rows_ref, out_ref)


def final_kernel(
    per_step, block_ref, point_ref, depth_ref, back_ref, out_ref, rows_ref, spec_ref
):
    step = pl.program_id(0)

    @pl.when(step == 0)
    def _():
        rows_gather(block_ref, rows_ref, spec_ref)

    depth = depth_ref[...]
    back = back_ref[...]
    for g in range(per_step):
        spectral = synthesis(step * per_step + g, spec_ref, back, depth, None)
        for ci in range(GROUP):
            index = g * GROUP + ci
            total = spectral[:, ci * 128 : (ci + 1) * 128] + flat(point_ref[index])
            out_ref[index] = total.astype(BF16).reshape(out_ref.shape[1:])


def point_kernel(transposed, weight_ref, field_ref, out_ref, wide_ref):
    size = wide_ref.shape[0]
    plane, chunk = pl.program_id(0), pl.program_id(1)

    @pl.when((plane == 0) & (chunk == 0))
    def _():
        tall = (sublanes((size, 64)) // 16 == lanes((size, 64))).astype(BF16)
        if transposed:
            left = lax.dot_general(
                tall, weight_ref[...], (((1,), (1,)), ((), ())), preferred_element_type=F32
            )
        else:
            left = dot_nn(tall, weight_ref[...])
        spread = dot_nt(left.astype(BF16), tall)
        same = sublanes((size, size)) % 16 == lanes((size, size)) % 16
        wide_ref[...] = jnp.where(same, spread, 0.0).astype(BF16)

    field = field_ref[:, 0]
    right = jnp.concatenate(
        [field[:, yc * 16 : (yc + 1) * 16].reshape(size, 128) for yc in range(4)], axis=1
    )
    rows = out_ref.shape[0] * 16
    start = pl.multiple_of(chunk * rows, rows)
    result = dot_nn(wide_ref[pl.ds(start, rows), :], right)
    for yc in range(4):
        out_ref[:, 0, yc * 16 : (yc + 1) * 16, :] = result[:, yc * 128 : (yc + 1) * 128].reshape(
            rows // 16, 16, 128
        )


def mode_kernel(
    per_step,
    scale,
    block_ref,
    weight_ref,
    both_ref,
    plain_ref,
    back_ref,
    coeff_ref,
    out_ref,
    rows_ref,
    res_ref,
):
    step = pl.program_id(0)
    count = rows_ref.shape[0] // 16

    @pl.when(step == 0)
    def _():
        rows_ref[...] = block_ref[...].astype(F32)

    low = lanes((128, 128)) < 64
    kxl = sublanes((128, 128)) % 4
    half = lanes((128, 128)) // 64
    first = (kxl == half).astype(BF16)
    second = (kxl == 2 + half).astype(BF16)
    low8 = lanes((8, 128)) < 64
    sign = jnp.where(sublanes((8, 128)) < 4, -1.0, 1.0)
    for jj in range(per_step):
        j = step * per_step + jj
        section = rows_ref[pl.ds(j, count, stride=16), :].astype(BF16)
        coeff_ref[jj] = (dot_nn(plain_ref[...], section) * scale).astype(BF16)
        coeffs = dot_nn(both_ref[...], section) * scale
        swapped = swap_halves(coeffs)
        left = []
        for h in range(2):
            twice = jnp.where(low if h == 0 else ~low, coeffs, swapped).astype(BF16)
            left.append((twice * first, twice * second))
        mixed = []
        for t in range(MX // 4):
            halves = []
            for h in range(2):
                one = jnp.concatenate([part[t * 16 : (t + 1) * 16] for part in left[h]], axis=1)
                start = ((jj * 2 + h) * MX + 4 * t) * 64
                halves.append(dot_nn(one, weight_ref[start : start + 256, :]))
            low_h, high_h = halves
            keep = jnp.where(low8, low_h[:8], sign * high_h[8:])
            move = jnp.where(low8, high_h[:8], sign * low_h[8:])
            mixed.append(keep + swap_halves(move))
        spectral = jnp.concatenate(mixed, axis=0).astype(BF16)
        res_ref[pl.ds(j, count, stride=16), :] = dot_nn(back_ref[...], spectral)

    @pl.when(step == pl.num_programs(0) - 1)
    def _():
        out_ref[...] = res_ref[...].astype(BF16)


def mode_grad_kernel(
    per_step,
    scale,
    block_ref,
    weight_ref,
    straight_ref,
    back_ref,
    pair_ref,
    out_ref,
    rows_ref,
    res_ref,
):
    step = pl.program_id(0)
    count = rows_ref.shape[0] // 16

    @pl.when(step == 0)
    def _():
        rows_ref[...] = block_ref[...].astype(F32)

    low = lanes((64, 128)) < 64
    low8 = lanes((8, 128)) < 64
    row = sublanes((8, 128)) % 4
    upper = row < 2
    valid = lanes((8, 128)) // 64 == row % 2
    for jj in range(per_step):
        j = step * per_step + jj
        section = rows_ref[pl.ds(j, count, stride=16), :]
        swapped = swap_halves(section)
        pairs = []
        for h in range(2):
            twice = jnp.where(low if h == 0 else ~low, section, swapped).astype(BF16)
            turned = dot_nn(straight_ref[...], twice)
            pair = jnp.where(low, turned[:64], turned[64:]).astype(BF16)
            pair_ref[jj * 2 + h] = pair
            pairs.append(pair)
        mixed = []
        for u in range(MX // 8):
            both = []
            for h in range(2):
                start = ((jj * 2 + h) * MX + 8 * u) * 64
                both.append(
                    dot_nt(pairs[h][u * 16 : (u + 1) * 16], weight_ref[start : start + 512, :])
                )
            for t in range(2):
                found = []
                for h in range(2):
                    rows = both[h][t * 8 : (t + 1) * 8, t * 256 : (t + 1) * 256]
                    found.append(jnp.where(valid, jnp.where(upper, rows[:, :128], rows[:, 128:]), 0.0))
                keep = jnp.where(low8, found[0], found[1])
                move = jnp.where(low8, found[1], found[0])
                mixed.append(keep + swap_halves(move))
        grads = (jnp.concatenate(mixed, axis=0) * scale).astype(BF16)
        res_ref[pl.ds(j, count, stride=16), :] = dot_nn(back_ref[...], grads)

    @pl.when(step == pl.num_programs(0) - 1)
    def _():
        out_ref[...] = res_ref[...].astype(BF16)


def weight_grad_kernel(per_step, scale, coeff_ref, pair_ref, out_ref):
    eye = (sublanes((128, 128)) == lanes((128, 128))).astype(BF16)
    even = (sublanes((64, 128)) % 2 == 0).astype(BF16)
    odd = (sublanes((64, 128)) % 2 == 1).astype(BF16)
    lane = lanes((64, 64))
    for jj in range(per_step):
        turned = (dot_nt(eye, coeff_ref[jj]) * scale).astype(BF16)
        for h in range(2):
            left = turned[h * 64 : (h + 1) * 64]
            pair = pair_ref[jj * 2 + h]
            right = jnp.concatenate([pair * even, pair * odd], axis=1)
            for t in range(MX // 4):
                for p in range(2):
                    mask = ((lane // 8 == t) & (lane % 4 // 2 == p)).astype(BF16)
                    both = dot_nn(left * mask, right)
                    mode = (jj * 2 + h) * MX + 4 * t + 2 * p
                    out_ref[mode] = both[:, :128].astype(BF16)
                    out_ref[mode + 1] = both[:, 128:].astype(BF16)


def whole(array):
    rank = len(array.shape)
    return pl.BlockSpec(array.shape, lambda *_: (0,) * rank)


def params(mib):
    return pltpu.CompilerParams(vmem_limit_bytes=mib * 1024 * 1024)


def cost(flops, moved):
    return pl.CostEstimate(flops=int(flops), bytes_accessed=int(moved), transcendentals=0)


def fast_body(features, cotangent, spectral_weight, channel_weight, channel_bias):
    channels, planes, lines, depth_len = features.shape
    devices = lax.axis_size("gx")
    owned_modes = spectral_weight.shape[0]
    wave_pairs = MY * MZ
    volume = planes * devices * lines * depth_len
    forward_scale = 1.0 / math.sqrt(volume)
    inverse_scale = 1.0 / math.sqrt(MX * wave_pairs)
    weight_scale = math.sqrt(MX * wave_pairs / volume)
    table = {name: jnp.asarray(value) for name, value in tables(devices, lines, depth_len).items()}
    per_step = 2
    steps = channels // (GROUP * per_step)
    step_channels = GROUP * per_step
    block_rows = devices * 64
    block_shape = jax.ShapeDtypeStruct((block_rows, 128), BF16)
    block_spec = whole(block_shape)
    field_spec = pl.BlockSpec(
        (step_channels, planes, lines, depth_len), lambda i: (i, 0, 0, 0)
    )
    lines_scratch = pltpu.VMEM((MZ, channels, 2 * planes * lines), F32)
    rows_scratch = pltpu.VMEM((block_rows, 128), F32)
    spec_scratch = pltpu.VMEM((channels // GROUP, MZ * GROUP, 128), F32)
    weight_rows = spectral_weight.reshape(owned_modes * channels, 2 * channels)
    field_bytes = features.size * 2

    def exchange(block):
        return lax.all_to_all(
            block.reshape(devices, 64, 128), "gx", 0, 0, tiled=True
        ).reshape(block_rows, 128)

    def point(field, transposed):
        rows = 16
        return pl.pallas_call(
            functools.partial(point_kernel, transposed),
            out_shape=jax.ShapeDtypeStruct(field.shape, F32),
            grid=(planes, channels // rows),
            in_specs=[
                pl.BlockSpec((channels, channels), lambda x, o: (0, 0)),
                pl.BlockSpec((channels, 1, lines, depth_len), lambda x, o: (0, x, 0, 0)),
            ],
            out_specs=pl.BlockSpec((rows, 1, lines, depth_len), lambda x, o: (o, x, 0, 0)),
            scratch_shapes=[pltpu.VMEM((channels * 16, channels * 16), BF16)],
            compiler_params=params(24),
            cost_estimate=cost(2 * 1024**3, 3 * field_bytes),
            name="channel_map_back" if transposed else "channel_map",
        )(channel_weight, field)

    block = pl.pallas_call(
        functools.partial(analysis_kernel, per_step),
        out_shape=block_shape,
        grid=(steps,),
        in_specs=[field_spec, whole(table["depth"]), whole(table["across_y"])],
        out_specs=block_spec,
        scratch_shapes=[lines_scratch, rows_scratch],
        compiler_params=params(24),
        cost_estimate=cost(2 * 256 * 1024 * 1024, field_bytes),
        name="field_analysis",
    )(features, table["depth"], table["across_y"])
    block = exchange(block)
    pointwise = point(features, False)

    mode_steps = 8
    per_mode_step = 16 // mode_steps
    weight_spec = pl.BlockSpec(
        (weight_rows.shape[0] // mode_steps, 2 * channels), lambda i: (i, 0)
    )
    coeffs, block = pl.pallas_call(
        functools.partial(mode_kernel, per_mode_step, forward_scale),
        out_shape=[jax.ShapeDtypeStruct((16, 64, 128), BF16), block_shape],
        grid=(mode_steps,),
        in_specs=[
            block_spec,
            weight_spec,
            whole(table["both_x"]),
            whole(table["plain_x"]),
            whole(table["back_x"]),
        ],
        out_specs=[pl.BlockSpec((per_mode_step, 64, 128), lambda i: (i, 0, 0)), block_spec],
        scratch_shapes=[rows_scratch, rows_scratch],
        compiler_params=params(24),
        cost_estimate=cost(256 * 2 * 16 * 256 * 128, 17 * 2**20),
        name="mode_product",
    )(block, weight_rows, table["both_x"], table["plain_x"], table["back_x"])
    block = exchange(block)

    activated, upstream, block = pl.pallas_call(
        functools.partial(middle_kernel, per_step, inverse_scale),
        out_shape=[
            jax.ShapeDtypeStruct(features.shape, BF16),
            jax.ShapeDtypeStruct(features.shape, BF16),
            block_shape,
        ],
        grid=(steps,),
        in_specs=[
            block_spec,
            field_spec,
            field_spec,
            pl.BlockSpec(memory_space=pltpu.SMEM),
            whole(table["depth"]),
            whole(table["across_y"]),
            whole(table["back_y"]),
        ],
        out_specs=[field_spec, field_spec, block_spec],
        scratch_shapes=[lines_scratch, rows_scratch, spec_scratch],
        compiler_params=params(32),
        cost_estimate=cost(2**30, 5 * field_bytes),
        name="gelu_and_gradient",
    )(
        block,
        pointwise,
        cotangent,
        channel_bias,
        table["depth"],
        table["across_y"],
        table["back_y"],
    )
    block = exchange(block)
    channel_back = point(upstream, True)

    pairs, block = pl.pallas_call(
        functools.partial(mode_grad_kernel, per_mode_step, forward_scale),
        out_shape=[jax.ShapeDtypeStruct((32, 64, 128), BF16), block_shape],
        grid=(mode_steps,),
        in_specs=[block_spec, weight_spec, whole(table["straight_x"]), whole(table["back_x"])],
        out_specs=[pl.BlockSpec((2 * per_mode_step, 64, 128), lambda i: (i, 0, 0)), block_spec],
        scratch_shapes=[rows_scratch, rows_scratch],
        compiler_params=params(24),
        cost_estimate=cost(256 * 2 * 16 * 256 * 128, 17 * 2**20),
        name="mode_gradient",
    )(block, weight_rows, table["straight_x"], table["back_x"])
    block = exchange(block)

    spectral_grad = pl.pallas_call(
        functools.partial(weight_grad_kernel, per_mode_step, weight_scale),
        out_shape=jax.ShapeDtypeStruct(spectral_weight.shape, BF16),
        grid=(mode_steps,),
        in_specs=[
            pl.BlockSpec((per_mode_step, 64, 128), lambda i: (i, 0, 0)),
            pl.BlockSpec((2 * per_mode_step, 64, 128), lambda i: (i, 0, 0)),
        ],
        out_specs=pl.BlockSpec(
            (owned_modes // mode_steps, channels, 2 * channels), lambda i: (i, 0, 0)
        ),
        compiler_params=params(24),
        cost_estimate=cost(512 * 2 * 64 * 64 * 256, 17 * 2**20),
        name="weight_gradient",
    )(coeffs, pairs)

    feature_grad = pl.pallas_call(
        functools.partial(final_kernel, per_step),
        out_shape=jax.ShapeDtypeStruct(features.shape, BF16),
        grid=(steps,),
        in_specs=[block_spec, field_spec, whole(table["depth"]), whole(table["back_y"])],
        out_specs=field_spec,
        scratch_shapes=[rows_scratch, spec_scratch],
        compiler_params=params(24),
        cost_estimate=cost(2**29, 3 * field_bytes),
        name="field_gradient",
    )(block, channel_back, table["depth"], table["back_y"])
    return (activated, feature_grad, spectral_grad)


def body(features, cotangent, spectral_weight, channel_weight, channel_bias):
    channels, planes, lines, depth_len = features.shape
    devices = lax.axis_size("gx")
    fits = (
        (channels, planes, lines, depth_len) == (64, PLANES, 64, 128)
        and spectral_weight.shape[0] == 2 * MZ * MX
        and devices * 2 == MY
        and devices * 2 == MX
    )
    run = fast_body if fits else general_body
    return run(features, cotangent, spectral_weight, channel_weight, channel_bias)


def solution(mesh):
    in_specs = (
        P("grp", "gx", None, None),
        P("grp", "gx", None, None),
        P("gx", None, None),
        P(),
        P(),
    )
    out_specs = (
        P("grp", "gx", None, None),
        P("grp", "gx", None, None),
        P(("grp", "gx"), None, None),
    )
    return jax.shard_map(body, mesh=mesh, in_specs=in_specs, out_specs=out_specs, check_vma=False)
```

```python
import functools
import math

import jax
import jax.numpy as jnp
import ml_dtypes
import numpy as np
from jax import lax
from jax.experimental import pallas as pl
from jax.experimental.pallas import tpu as pltpu
from jax.sharding import PartitionSpec as P

MX = 32
MY = 32
MZ = 16


SQRT_TWO_PI = math.sqrt(2.0 / math.pi)
CUBIC_COEF = 0.044715


def freq_index(retained, length):
    ladder = jnp.arange(retained, dtype=jnp.int32)
    return jnp.where(ladder < retained // 2, ladder, length - retained + ladder)


def cos_sin(wavenum, length):
    points = jnp.arange(length, dtype=jnp.int32)
    angles = (wavenum[:, None] * points[None, :] % length).astype(jnp.float32) * (
        2.0 * math.pi / length
    )
    return (jnp.cos(angles), jnp.sin(angles))


def analysis_pair(wavenum, length):
    cosine, sine_wave = cos_sin(wavenum, length)
    cosine, sine_wave = (cosine.T, sine_wave.T)
    return jnp.stack(
        [jnp.stack([cosine, -sine_wave], 1), jnp.stack([sine_wave, cosine], 1)], 1
    ).astype(jnp.bfloat16)


def synthesis_pair(wavenum, length):
    cosine, sine_wave = cos_sin(wavenum, length)
    return jnp.stack(
        [jnp.stack([cosine, sine_wave], 1), jnp.stack([-sine_wave, cosine], 1)], 1
    ).astype(jnp.bfloat16)


def depth_table(retained, length):
    cosine, sine_wave = cos_sin(jnp.arange(retained, dtype=jnp.int32), length)
    return jnp.concatenate([cosine, -sine_wave], 0).astype(jnp.bfloat16)


def gelu_parts(inputs):
    cubed_in = inputs * inputs * inputs
    tangent = jnp.tanh(SQRT_TWO_PI * (inputs + CUBIC_COEF * cubed_in))
    output = 0.5 * inputs * (1.0 + tangent)
    derivative = 0.5 * (1.0 + tangent) + 0.5 * inputs * (1.0 - tangent * tangent) * SQRT_TWO_PI * (
        1.0 + 3.0 * CUBIC_COEF * inputs * inputs
    )
    return (output, derivative)


def mode_product(coeffs, weights, channels):
    stacked = coeffs.reshape(coeffs.shape[0], 2, channels)
    halves = jnp.einsum("mac,mcj->amj", stacked, weights, preferred_element_type=jnp.float32)
    real_out = halves[0, :, :channels] - halves[1, :, channels:]
    imag_out = halves[0, :, channels:] + halves[1, :, :channels]
    return jnp.concatenate([real_out, imag_out], 1).astype(jnp.bfloat16)


def mode_grads(coeffs, weights, grad_modes, channels, weight_scale, input_scale):
    number = coeffs.shape[0]
    stacked = coeffs.reshape(number, 2, channels)
    grad_pairs = grad_modes.reshape(number, 2, channels)
    real_w = jnp.einsum("mac,mao->mco", stacked, grad_pairs, preferred_element_type=jnp.float32)
    imag_w = jnp.einsum(
        "mc,mo->mco", stacked[:, 0], grad_pairs[:, 1], preferred_element_type=jnp.float32
    ) - jnp.einsum(
        "mc,mo->mco", stacked[:, 1], grad_pairs[:, 0], preferred_element_type=jnp.float32
    )
    weight_grad = (jnp.concatenate([real_w, imag_w], 2) * weight_scale).astype(jnp.bfloat16)
    straight = jnp.concatenate([grad_pairs[:, 0], grad_pairs[:, 1]], 1)
    rotated = jnp.concatenate([grad_pairs[:, 1], -grad_pairs[:, 0]], 1)
    real_x = jnp.einsum("mcj,mj->mc", weights, straight, preferred_element_type=jnp.float32)
    imag_x = jnp.einsum("mcj,mj->mc", weights, rotated, preferred_element_type=jnp.float32)
    input_grad = (jnp.concatenate([real_x, imag_x], 1) * input_scale).astype(jnp.bfloat16)
    return (weight_grad, input_grad)


def general_body(features, cotangent, spectral_weight, channel_weight, channel_bias):
    channels, planes, lines, depth_len = features.shape
    devices = lax.axis_size("gx")
    all_planes = planes * devices
    owned_modes = spectral_weight.shape[0]
    wave_pairs = MY * MZ
    forward_scale = 1.0 / math.sqrt(all_planes * lines * depth_len)
    inverse_scale = 1.0 / math.sqrt(MX * wave_pairs)
    weight_scale = math.sqrt(MX * wave_pairs / (all_planes * lines * depth_len))
    depth_basis = depth_table(MZ, depth_len)
    across_y = analysis_pair(freq_index(MY, lines), lines)
    back_y = synthesis_pair(freq_index(MY, lines), lines)
    across_full = analysis_pair(freq_index(MX, all_planes), all_planes)
    back_full = synthesis_pair(freq_index(MX, all_planes), all_planes)
    depth_part = jnp.dot(features, depth_basis.T, preferred_element_type=jnp.float32).astype(
        jnp.bfloat16
    )
    plane_part = (
        jnp.einsum(
            "cxyaz,yabk->cxbkz",
            depth_part.reshape(channels, planes, lines, 2, MZ),
            across_y,
            preferred_element_type=jnp.float32,
        )
        .astype(jnp.bfloat16)
        .reshape(channels, planes, 2, wave_pairs)
    )
    all_rows = lax.all_to_all(plane_part, "gx", split_axis=3, concat_axis=1, tiled=True)
    mode_sums = jnp.einsum(
        "cxaq,xabk->qkbc", all_rows, across_full, preferred_element_type=jnp.float32
    ).reshape(owned_modes, 2 * channels)
    coeffs = (mode_sums * forward_scale).astype(jnp.bfloat16)
    spectral = mode_product(coeffs, spectral_weight, channels)
    planes_all = jnp.einsum(
        "qkao,kabx->oxbq",
        spectral.reshape(owned_modes // MX, MX, 2, channels),
        back_full,
        preferred_element_type=jnp.float32,
    ).astype(jnp.bfloat16)
    planes_back = lax.all_to_all(planes_all, "gx", split_axis=1, concat_axis=3, tiled=True)
    lines_back = (
        jnp.einsum(
            "oxakz,kaby->oxybz",
            planes_back.reshape(channels, planes, 2, MY, MZ),
            back_y,
            preferred_element_type=jnp.float32,
        )
        .astype(jnp.bfloat16)
        .reshape(channels, planes, lines, 2 * MZ)
    )
    spectral_term = (
        jnp.dot(lines_back, depth_basis, preferred_element_type=jnp.float32) * inverse_scale
    )
    pointwise = jnp.einsum(
        "oc,cxyz->oxyz", channel_weight, features, preferred_element_type=jnp.float32
    )
    hidden = spectral_term + pointwise + channel_bias[:, None, None, None]
    activated, derivative = gelu_parts(hidden)
    upstream = (cotangent.astype(jnp.float32) * derivative).astype(jnp.bfloat16)
    lines_grad = (
        jnp.dot(upstream, depth_basis.T, preferred_element_type=jnp.float32) * inverse_scale
    ).astype(jnp.bfloat16)
    rows_grad = (
        jnp.einsum(
            "oxybz,kaby->oxakz",
            lines_grad.reshape(channels, planes, lines, 2, MZ),
            back_y,
            preferred_element_type=jnp.float32,
        )
        .astype(jnp.bfloat16)
        .reshape(channels, planes, 2, wave_pairs)
    )
    all_grads = lax.all_to_all(rows_grad, "gx", split_axis=3, concat_axis=1, tiled=True)
    grad_sums = jnp.einsum(
        "oxbq,kabx->qkao", all_grads, back_full, preferred_element_type=jnp.float32
    ).reshape(owned_modes, 2 * channels)
    grad_modes = grad_sums.astype(jnp.bfloat16)
    spectral_grad, coeff_grad = mode_grads(
        coeffs, spectral_weight, grad_modes, channels, weight_scale, forward_scale
    )
    plane_all = jnp.einsum(
        "qkbc,xabk->cxaq",
        coeff_grad.reshape(owned_modes // MX, MX, 2, channels),
        across_full,
        preferred_element_type=jnp.float32,
    ).astype(jnp.bfloat16)
    plane_grad = lax.all_to_all(plane_all, "gx", split_axis=1, concat_axis=3, tiled=True)
    depth_grad = (
        jnp.einsum(
            "cxbkz,yabk->cxyaz",
            plane_grad.reshape(channels, planes, 2, MY, MZ),
            across_y,
            preferred_element_type=jnp.float32,
        )
        .astype(jnp.bfloat16)
        .reshape(channels, planes, lines, 2 * MZ)
    )
    channel_back = jnp.einsum(
        "oc,oxyz->cxyz", channel_weight, upstream, preferred_element_type=jnp.float32
    )
    feature_grad = (
        jnp.dot(depth_grad, depth_basis, preferred_element_type=jnp.float32) + channel_back
    ).astype(jnp.bfloat16)
    return (activated.astype(jnp.bfloat16), feature_grad, spectral_grad)


PLANES = 2
GROUP = 8
VMEM_MIB = 58
NT = (((1,), (1,)), ((), ()))
F32 = jnp.float32
BF16 = jnp.bfloat16


def np_freq(retained, length):
    ladder = np.arange(retained)
    return np.where(ladder < retained // 2, ladder, length - retained + ladder)


def np_angles(wavenum, length):
    points = np.arange(length)
    return (wavenum[:, None] * points[None, :] % length) * (2.0 * math.pi / length)


def as_bf16(table):
    return np.asarray(table, np.float32).astype(ml_dtypes.bfloat16)


def rotation(angle, sign):
    cosine, sine_wave = np.cos(angle), sign * np.sin(angle)
    return np.stack([np.stack([cosine, -sine_wave]), np.stack([sine_wave, cosine])])


@functools.lru_cache(maxsize=None)
def tables(devices, lines, depth_len):
    planes_all = devices * PLANES
    angle = np_angles(np.arange(MZ), depth_len)
    depth = np.stack([np.cos(angle), -np.sin(angle)])
    eye = np.eye(GROUP)
    depth_block = np.einsum("akz,ij->akijz", depth, eye).reshape(2 * MZ * GROUP, GROUP * depth_len)
    plane_eye = np.eye(PLANES)
    angle = np_angles(np_freq(MY, lines), lines).reshape(devices, MY // devices, lines)
    across = np.einsum("badly,xw->ldbxawy", rotation(angle, -1.0), plane_eye)
    across = across.reshape(MY * 2 * PLANES, 2 * PLANES * lines)
    back = np.einsum("pbdly,xw->pxyldbw", rotation(angle, 1.0), plane_eye)
    back = back.reshape(2 * PLANES * lines, MY * 2 * PLANES)
    angle = np_angles(np_freq(MX, planes_all), planes_all).reshape(MX // 4, 4, devices, PLANES)
    forward = rotation(angle, -1.0)
    rows = np.einsum("batksx->tbksax", forward).reshape(MX // 4, 2, 4, devices * 2 * PLANES)
    plain = rows.reshape(2 * MX, -1)
    both = np.stack([rows, rows[:, ::-1]], 1).reshape(4 * MX, -1)
    turned = np.concatenate([rows[:, 1:], -rows[:, :1]], 1).reshape(2 * MX, -1)
    straight_rotated = np.concatenate([plain, turned], 0)
    inverse = np.einsum("batksx->sbxtak", rotation(angle, 1.0)).reshape(-1, 2 * MX)
    return {
        "depth": as_bf16(depth_block),
        "across_y": as_bf16(across),
        "back_y": as_bf16(back),
        "plain_x": as_bf16(plain),
        "both_x": as_bf16(both),
        "straight_x": as_bf16(straight_rotated),
        "back_x": as_bf16(inverse),
    }


def dot_nn(left, right):
    return jnp.dot(left, right, preferred_element_type=F32)


def dot_nt(left, right):
    return lax.dot_general(left, right, NT, preferred_element_type=F32)


def lanes(shape):
    return lax.broadcasted_iota(jnp.int32, shape, len(shape) - 1)


def sublanes(shape):
    return lax.broadcasted_iota(jnp.int32, shape, len(shape) - 2)


def swap_halves(block):
    return pltpu.roll(block, 64, 1)


def depth_analysis(slabs, depth, scale, group, lines_ref):
    wide = jnp.concatenate(slabs, axis=1)
    parts = dot_nt(depth, wide)
    if scale is not None:
        parts = parts * scale
    width = wide.shape[0]
    start = pl.multiple_of(group * GROUP, GROUP)
    for a in range(2):
        lines_ref[:, pl.ds(start, GROUP), a * width : (a + 1) * width] = parts[
            a * MZ * GROUP : (a + 1) * MZ * GROUP
        ].reshape(MZ, GROUP, width)


def rows_analysis(lines_ref, across_ref, rows_ref, out_ref):
    channels, width = lines_ref.shape[1], lines_ref.shape[2]
    across = across_ref[...]
    half = across.shape[0] // 2
    for kzh in range(MZ // 2):
        pair = lines_ref[2 * kzh : 2 * kzh + 2].reshape(2 * channels, width).astype(BF16)
        rows = dot_nt(across, pair)
        for kyl in range(2):
            rows_ref[pl.ds(kyl * 8 + kzh, half, stride=16), :] = rows[
                kyl * half : (kyl + 1) * half
            ]
    out_ref[...] = rows_ref[...].astype(BF16)


def rows_gather(block_ref, rows_ref, spec_ref):
    rows_ref[...] = block_ref[...].astype(F32)
    count = rows_ref.shape[0] // 16
    eye = (sublanes((128, 128)) == lanes((128, 128))).astype(BF16)
    for kzh in range(MZ // 2):
        both = jnp.concatenate(
            [rows_ref[pl.ds(kyl * 8 + kzh, count, stride=16), :] for kyl in range(2)], axis=0
        ).astype(BF16)
        turned = dot_nt(eye, both)
        for h in range(2):
            spec_ref[:, (2 * kzh + h) * GROUP : (2 * kzh + h + 1) * GROUP, :] = turned[
                h * 64 : (h + 1) * 64
            ].reshape(8, GROUP, turned.shape[1])


def synthesis(group, spec_ref, back, depth, scale):
    lines = dot_nt(back, spec_ref[group].astype(BF16))
    if scale is not None:
        lines = lines * scale
    lines = lines.astype(BF16)
    half = lines.shape[0] // 2
    return dot_nn(jnp.concatenate([lines[:half], lines[half:]], axis=1), depth)


def flat(slab):
    return slab.reshape(slab.shape[0] * slab.shape[1], slab.shape[2])


def analysis_kernel(per_step, field_ref, depth_ref, across_ref, out_ref, lines_ref, rows_ref):
    step = pl.program_id(0)
    depth = depth_ref[...]
    for g in range(per_step):
        slabs = [flat(field_ref[g * GROUP + ci]) for ci in range(GROUP)]
        depth_analysis(slabs, depth, None, step * per_step + g, lines_ref)

    @pl.when(step == pl.num_programs(0) - 1)
    def _():
        rows_analysis(lines_ref, across_ref, rows_ref, out_ref)


def middle_kernel(
    per_step,
    inverse_scale,
    block_ref,
    point_ref,
    cot_ref,
    bias_ref,
    depth_ref,
    across_ref,
    back_ref,
    act_ref,
    up_ref,
    out_ref,
    lines_ref,
    rows_ref,
    spec_ref,
):
    step = pl.program_id(0)

    @pl.when(step == 0)
    def _():
        rows_gather(block_ref, rows_ref, spec_ref)

    depth = depth_ref[...]
    back = back_ref[...]
    for g in range(per_step):
        group = step * per_step + g
        spectral = synthesis(group, spec_ref, back, depth, inverse_scale)
        slabs = []
        for oi in range(GROUP):
            index = g * GROUP + oi
            hidden = (
                spectral[:, oi * 128 : (oi + 1) * 128]
                + flat(point_ref[index])
                + bias_ref[group * GROUP + oi]
            )
            square = hidden * hidden
            gate = 0.5 + 0.5 * jnp.tanh(
                hidden * (SQRT_TWO_PI + (SQRT_TWO_PI * CUBIC_COEF) * square)
            )
            slope = hidden * (2.0 * SQRT_TWO_PI + (6.0 * SQRT_TWO_PI * CUBIC_COEF) * square)
            derivative = gate + (gate - gate * gate) * slope
            upstream = (flat(cot_ref[index]).astype(F32) * derivative).astype(BF16)
            act_ref[index] = (hidden * gate).astype(BF16).reshape(act_ref.shape[1:])
            up_ref[index] = upstream.reshape(up_ref.shape[1:])
            slabs.append(upstream)
        depth_analysis(slabs, depth, inverse_scale, group, lines_ref)

    @pl.when(step == pl.num_programs(0) - 1)
    def _():
        rows_analysis(lines_ref, across_ref, rows_ref, out_ref)


def final_kernel(
    per_step, block_ref, point_ref, depth_ref, back_ref, out_ref, rows_ref, spec_ref
):
    step = pl.program_id(0)

    @pl.when(step == 0)
    def _():
        rows_gather(block_ref, rows_ref, spec_ref)

    depth = depth_ref[...]
    back = back_ref[...]
    for g in range(per_step):
        spectral = synthesis(step * per_step + g, spec_ref, back, depth, None)
        for ci in range(GROUP):
            index = g * GROUP + ci
            total = spectral[:, ci * 128 : (ci + 1) * 128] + flat(point_ref[index])
            out_ref[index] = total.astype(BF16).reshape(out_ref.shape[1:])


def point_kernel(transposed, weight_ref, field_ref, out_ref, wide_ref):
    size = wide_ref.shape[0]
    plane, chunk = pl.program_id(0), pl.program_id(1)

    @pl.when((plane == 0) & (chunk == 0))
    def _():
        tall = (sublanes((size, 64)) // 16 == lanes((size, 64))).astype(BF16)
        if transposed:
            left = lax.dot_general(
                tall, weight_ref[...], (((1,), (1,)), ((), ())), preferred_element_type=F32
            )
        else:
            left = dot_nn(tall, weight_ref[...])
        spread = dot_nt(left.astype(BF16), tall)
        same = sublanes((size, size)) % 16 == lanes((size, size)) % 16
        wide_ref[...] = jnp.where(same, spread, 0.0).astype(BF16)

    field = field_ref[:, 0]
    right = jnp.concatenate(
        [field[:, yc * 16 : (yc + 1) * 16].reshape(size, 128) for yc in range(4)], axis=1
    )
    rows = out_ref.shape[0] * 16
    start = pl.multiple_of(chunk * rows, rows)
    result = dot_nn(wide_ref[pl.ds(start, rows), :], right)
    for yc in range(4):
        out_ref[:, 0, yc * 16 : (yc + 1) * 16, :] = result[:, yc * 128 : (yc + 1) * 128].reshape(
            rows // 16, 16, 128
        )


def mode_kernel(
    per_step,
    scale,
    block_ref,
    weight_ref,
    both_ref,
    plain_ref,
    back_ref,
    coeff_ref,
    out_ref,
    rows_ref,
    res_ref,
):
    step = pl.program_id(0)
    count = rows_ref.shape[0] // 16

    @pl.when(step == 0)
    def _():
        rows_ref[...] = block_ref[...].astype(F32)

    low = lanes((128, 128)) < 64
    kxl = sublanes((128, 128)) % 4
    half = lanes((128, 128)) // 64
    first = (kxl == half).astype(BF16)
    second = (kxl == 2 + half).astype(BF16)
    low8 = lanes((8, 128)) < 64
    sign = jnp.where(sublanes((8, 128)) < 4, -1.0, 1.0)
    for jj in range(per_step):
        j = step * per_step + jj
        section = rows_ref[pl.ds(j, count, stride=16), :].astype(BF16)
        coeff_ref[jj] = (dot_nn(plain_ref[...], section) * scale).astype(BF16)
        coeffs = dot_nn(both_ref[...], section) * scale
        swapped = swap_halves(coeffs)
        left = []
        for h in range(2):
            twice = jnp.where(low if h == 0 else ~low, coeffs, swapped).astype(BF16)
            left.append((twice * first, twice * second))
        mixed = []
        for u in range(MX // 8):
            halves = []
            for h in range(2):
                one = jnp.concatenate([part[u * 32 : (u + 1) * 32] for part in left[h]], axis=1)
                start = ((jj * 2 + h) * MX + 8 * u) * 64
                two = jnp.concatenate(
                    [weight_ref[start : start + 256, :], weight_ref[start + 256 : start + 512, :]],
                    axis=1,
                )
                halves.append(dot_nn(one, two))
            for t in range(2):
                low_h, high_h = [
                    half[t * 16 : (t + 1) * 16, t * 128 : (t + 1) * 128] for half in halves
                ]
                keep = jnp.where(low8, low_h[:8], sign * high_h[8:])
                move = jnp.where(low8, high_h[:8], sign * low_h[8:])
                mixed.append(keep + swap_halves(move))
        spectral = jnp.concatenate(mixed, axis=0).astype(BF16)
        res_ref[pl.ds(j, count, stride=16), :] = dot_nn(back_ref[...], spectral)

    @pl.when(step == pl.num_programs(0) - 1)
    def _():
        out_ref[...] = res_ref[...].astype(BF16)


def mode_grad_kernel(
    per_step,
    scale,
    block_ref,
    weight_ref,
    straight_ref,
    back_ref,
    pair_ref,
    out_ref,
    rows_ref,
    res_ref,
):
    step = pl.program_id(0)
    count = rows_ref.shape[0] // 16

    @pl.when(step == 0)
    def _():
        rows_ref[...] = block_ref[...].astype(F32)

    low = lanes((64, 128)) < 64
    low16 = lanes((16, 128)) < 64
    row = sublanes((16, 128)) % 4
    upper = row < 2
    valid = lanes((16, 128)) // 64 == row % 2
    even = (sublanes((16, 128)) < 8).astype(BF16)
    odd = (sublanes((16, 128)) >= 8).astype(BF16)
    for jj in range(per_step):
        j = step * per_step + jj
        section = rows_ref[pl.ds(j, count, stride=16), :]
        swapped = swap_halves(section)
        pairs = []
        for h in range(2):
            twice = jnp.where(low if h == 0 else ~low, section, swapped).astype(BF16)
            turned = dot_nn(straight_ref[...], twice)
            pair = jnp.where(low, turned[:64], turned[64:]).astype(BF16)
            pair_ref[jj * 2 + h] = pair
            pairs.append(pair)
        mixed = []
        for u in range(MX // 8):
            found = []
            for h in range(2):
                pair = pairs[h][u * 16 : (u + 1) * 16]
                start = ((jj * 2 + h) * MX + 8 * u) * 64
                two = jnp.concatenate(
                    [weight_ref[start : start + 256, :], weight_ref[start + 256 : start + 512, :]],
                    axis=1,
                )
                rows = dot_nt(jnp.concatenate([pair * even, pair * odd], axis=1), two)
                found.append(jnp.where(valid, jnp.where(upper, rows[:, :128], rows[:, 128:]), 0.0))
            keep = jnp.where(low16, found[0], found[1])
            move = jnp.where(low16, found[1], found[0])
            mixed.append(keep + swap_halves(move))
        grads = (jnp.concatenate(mixed, axis=0) * scale).astype(BF16)
        res_ref[pl.ds(j, count, stride=16), :] = dot_nn(back_ref[...], grads)

    @pl.when(step == pl.num_programs(0) - 1)
    def _():
        out_ref[...] = res_ref[...].astype(BF16)


def weight_grad_kernel(per_step, scale, coeff_ref, pair_ref, out_ref):
    eye = (sublanes((128, 128)) == lanes((128, 128))).astype(BF16)
    even = (sublanes((64, 128)) % 2 == 0).astype(BF16)
    odd = (sublanes((64, 128)) % 2 == 1).astype(BF16)
    lane = lanes((64, 64))
    for jj in range(per_step):
        turned = (dot_nt(eye, coeff_ref[jj]) * scale).astype(BF16)
        for h in range(2):
            left = turned[h * 64 : (h + 1) * 64]
            pair = pair_ref[jj * 2 + h]
            right = jnp.concatenate([pair * even, pair * odd], axis=1)
            for t in range(MX // 4):
                for p in range(2):
                    mask = ((lane // 8 == t) & (lane % 4 // 2 == p)).astype(BF16)
                    both = dot_nn(left * mask, right)
                    mode = (jj * 2 + h) * MX + 4 * t + 2 * p
                    out_ref[mode] = both[:, :128].astype(BF16)
                    out_ref[mode + 1] = both[:, 128:].astype(BF16)


def whole(array):
    rank = len(array.shape)
    return pl.BlockSpec(array.shape, lambda *_: (0,) * rank)


def params(mib):
    return pltpu.CompilerParams(vmem_limit_bytes=mib * 1024 * 1024)


def cost(flops, moved):
    return pl.CostEstimate(flops=int(flops), bytes_accessed=int(moved), transcendentals=0)


def fast_body(features, cotangent, spectral_weight, channel_weight, channel_bias):
    channels, planes, lines, depth_len = features.shape
    devices = lax.axis_size("gx")
    owned_modes = spectral_weight.shape[0]
    wave_pairs = MY * MZ
    volume = planes * devices * lines * depth_len
    forward_scale = 1.0 / math.sqrt(volume)
    inverse_scale = 1.0 / math.sqrt(MX * wave_pairs)
    weight_scale = math.sqrt(MX * wave_pairs / volume)
    table = {name: jnp.asarray(value) for name, value in tables(devices, lines, depth_len).items()}
    per_step = 2
    steps = channels // (GROUP * per_step)
    step_channels = GROUP * per_step
    block_rows = devices * 64
    block_shape = jax.ShapeDtypeStruct((block_rows, 128), BF16)
    block_spec = whole(block_shape)
    field_spec = pl.BlockSpec(
        (step_channels, planes, lines, depth_len), lambda i: (i, 0, 0, 0)
    )
    lines_scratch = pltpu.VMEM((MZ, channels, 2 * planes * lines), F32)
    rows_scratch = pltpu.VMEM((block_rows, 128), F32)
    spec_scratch = pltpu.VMEM((channels // GROUP, MZ * GROUP, 128), F32)
    weight_rows = spectral_weight.reshape(owned_modes * channels, 2 * channels)
    field_bytes = features.size * 2

    def exchange(block):
        return lax.all_to_all(
            block.reshape(devices, 64, 128), "gx", 0, 0, tiled=True
        ).reshape(block_rows, 128)

    def point(field, transposed):
        rows = 16
        return pl.pallas_call(
            functools.partial(point_kernel, transposed),
            out_shape=jax.ShapeDtypeStruct(field.shape, F32),
            grid=(planes, channels // rows),
            in_specs=[
                pl.BlockSpec((channels, channels), lambda x, o: (0, 0)),
                pl.BlockSpec((channels, 1, lines, depth_len), lambda x, o: (0, x, 0, 0)),
            ],
            out_specs=pl.BlockSpec((rows, 1, lines, depth_len), lambda x, o: (o, x, 0, 0)),
            scratch_shapes=[pltpu.VMEM((channels * 16, channels * 16), BF16)],
            compiler_params=params(VMEM_MIB),
            cost_estimate=cost(2 * 1024**3, 3 * field_bytes),
            name="channel_map_back" if transposed else "channel_map",
        )(channel_weight, field)

    block = pl.pallas_call(
        functools.partial(analysis_kernel, per_step),
        out_shape=block_shape,
        grid=(steps,),
        in_specs=[field_spec, whole(table["depth"]), whole(table["across_y"])],
        out_specs=block_spec,
        scratch_shapes=[lines_scratch, rows_scratch],
        compiler_params=params(VMEM_MIB),
        cost_estimate=cost(2 * 256 * 1024 * 1024, field_bytes),
        name="field_analysis",
    )(features, table["depth"], table["across_y"])
    block = exchange(block)
    pointwise = point(features, False)

    mode_steps = 8
    per_mode_step = 16 // mode_steps
    weight_spec = pl.BlockSpec(
        (weight_rows.shape[0] // mode_steps, 2 * channels), lambda i: (i, 0)
    )
    coeffs, block = pl.pallas_call(
        functools.partial(mode_kernel, per_mode_step, forward_scale),
        out_shape=[jax.ShapeDtypeStruct((16, 64, 128), BF16), block_shape],
        grid=(mode_steps,),
        in_specs=[
            block_spec,
            weight_spec,
            whole(table["both_x"]),
            whole(table["plain_x"]),
            whole(table["back_x"]),
        ],
        out_specs=[pl.BlockSpec((per_mode_step, 64, 128), lambda i: (i, 0, 0)), block_spec],
        scratch_shapes=[rows_scratch, rows_scratch],
        compiler_params=params(VMEM_MIB),
        cost_estimate=cost(256 * 2 * 16 * 256 * 128, 17 * 2**20),
        name="mode_product",
    )(block, weight_rows, table["both_x"], table["plain_x"], table["back_x"])
    block = exchange(block)

    activated, upstream, block = pl.pallas_call(
        functools.partial(middle_kernel, per_step, inverse_scale),
        out_shape=[
            jax.ShapeDtypeStruct(features.shape, BF16),
            jax.ShapeDtypeStruct(features.shape, BF16),
            block_shape,
        ],
        grid=(steps,),
        in_specs=[
            block_spec,
            field_spec,
            field_spec,
            pl.BlockSpec(memory_space=pltpu.SMEM),
            whole(table["depth"]),
            whole(table["across_y"]),
            whole(table["back_y"]),
        ],
        out_specs=[field_spec, field_spec, block_spec],
        scratch_shapes=[lines_scratch, rows_scratch, spec_scratch],
        compiler_params=params(VMEM_MIB),
        cost_estimate=cost(2**30, 5 * field_bytes),
        name="gelu_and_gradient",
    )(
        block,
        pointwise,
        cotangent,
        channel_bias,
        table["depth"],
        table["across_y"],
        table["back_y"],
    )
    block = exchange(block)
    block, channel_back = lax.optimization_barrier((block, point(upstream, True)))

    pairs, block = pl.pallas_call(
        functools.partial(mode_grad_kernel, per_mode_step, forward_scale),
        out_shape=[jax.ShapeDtypeStruct((32, 64, 128), BF16), block_shape],
        grid=(mode_steps,),
        in_specs=[block_spec, weight_spec, whole(table["straight_x"]), whole(table["back_x"])],
        out_specs=[pl.BlockSpec((2 * per_mode_step, 64, 128), lambda i: (i, 0, 0)), block_spec],
        scratch_shapes=[rows_scratch, rows_scratch],
        compiler_params=params(VMEM_MIB),
        cost_estimate=cost(256 * 2 * 16 * 256 * 128, 17 * 2**20),
        name="mode_gradient",
    )(block, weight_rows, table["straight_x"], table["back_x"])
    block = exchange(block)

    spectral_grad = pl.pallas_call(
        functools.partial(weight_grad_kernel, per_mode_step, weight_scale),
        out_shape=jax.ShapeDtypeStruct(spectral_weight.shape, BF16),
        grid=(mode_steps,),
        in_specs=[
            pl.BlockSpec((per_mode_step, 64, 128), lambda i: (i, 0, 0)),
            pl.BlockSpec((2 * per_mode_step, 64, 128), lambda i: (i, 0, 0)),
        ],
        out_specs=pl.BlockSpec(
            (owned_modes // mode_steps, channels, 2 * channels), lambda i: (i, 0, 0)
        ),
        compiler_params=params(VMEM_MIB),
        cost_estimate=cost(512 * 2 * 64 * 64 * 256, 17 * 2**20),
        name="weight_gradient",
    )(coeffs, pairs)

    feature_grad = pl.pallas_call(
        functools.partial(final_kernel, per_step),
        out_shape=jax.ShapeDtypeStruct(features.shape, BF16),
        grid=(steps,),
        in_specs=[block_spec, field_spec, whole(table["depth"]), whole(table["back_y"])],
        out_specs=field_spec,
        scratch_shapes=[rows_scratch, spec_scratch],
        compiler_params=params(VMEM_MIB),
        cost_estimate=cost(2**29, 3 * field_bytes),
        name="field_gradient",
    )(block, channel_back, table["depth"], table["back_y"])
    return (activated, feature_grad, spectral_grad)


def body(features, cotangent, spectral_weight, channel_weight, channel_bias):
    channels, planes, lines, depth_len = features.shape
    devices = lax.axis_size("gx")
    fits = (
        (channels, planes, lines, depth_len) == (64, PLANES, 64, 128)
        and spectral_weight.shape[0] == 2 * MZ * MX
        and devices * 2 == MY
        and devices * 2 == MX
    )
    run = fast_body if fits else general_body
    return run(features, cotangent, spectral_weight, channel_weight, channel_bias)


def solution(mesh):
    in_specs = (
        P("grp", "gx", None, None),
        P("grp", "gx", None, None),
        P("gx", None, None),
        P(),
        P(),
    )
    out_specs = (
        P("grp", "gx", None, None),
        P("grp", "gx", None, None),
        P(("grp", "gx"), None, None),
    )
    return jax.shard_map(body, mesh=mesh, in_specs=in_specs, out_specs=out_specs, check_vma=False)
```

```python
import functools
import math

import jax
import jax.numpy as jnp
import ml_dtypes
import numpy as np
from jax import lax
from jax.experimental import pallas as pl
from jax.experimental.pallas import tpu as pltpu
from jax.sharding import PartitionSpec as P

MX = 32
MY = 32
MZ = 16


SQRT_TWO_PI = math.sqrt(2.0 / math.pi)
CUBIC_COEF = 0.044715


def freq_index(retained, length):
    ladder = jnp.arange(retained, dtype=jnp.int32)
    return jnp.where(ladder < retained // 2, ladder, length - retained + ladder)


def cos_sin(wavenum, length):
    points = jnp.arange(length, dtype=jnp.int32)
    angles = (wavenum[:, None] * points[None, :] % length).astype(jnp.float32) * (
        2.0 * math.pi / length
    )
    return (jnp.cos(angles), jnp.sin(angles))


def analysis_pair(wavenum, length):
    cosine, sine_wave = cos_sin(wavenum, length)
    cosine, sine_wave = (cosine.T, sine_wave.T)
    return jnp.stack(
        [jnp.stack([cosine, -sine_wave], 1), jnp.stack([sine_wave, cosine], 1)], 1
    ).astype(jnp.bfloat16)


def synthesis_pair(wavenum, length):
    cosine, sine_wave = cos_sin(wavenum, length)
    return jnp.stack(
        [jnp.stack([cosine, sine_wave], 1), jnp.stack([-sine_wave, cosine], 1)], 1
    ).astype(jnp.bfloat16)


def depth_table(retained, length):
    cosine, sine_wave = cos_sin(jnp.arange(retained, dtype=jnp.int32), length)
    return jnp.concatenate([cosine, -sine_wave], 0).astype(jnp.bfloat16)


def gelu_parts(inputs):
    cubed_in = inputs * inputs * inputs
    tangent = jnp.tanh(SQRT_TWO_PI * (inputs + CUBIC_COEF * cubed_in))
    output = 0.5 * inputs * (1.0 + tangent)
    derivative = 0.5 * (1.0 + tangent) + 0.5 * inputs * (1.0 - tangent * tangent) * SQRT_TWO_PI * (
        1.0 + 3.0 * CUBIC_COEF * inputs * inputs
    )
    return (output, derivative)


def mode_product(coeffs, weights, channels):
    stacked = coeffs.reshape(coeffs.shape[0], 2, channels)
    halves = jnp.einsum("mac,mcj->amj", stacked, weights, preferred_element_type=jnp.float32)
    real_out = halves[0, :, :channels] - halves[1, :, channels:]
    imag_out = halves[0, :, channels:] + halves[1, :, :channels]
    return jnp.concatenate([real_out, imag_out], 1).astype(jnp.bfloat16)


def mode_grads(coeffs, weights, grad_modes, channels, weight_scale, input_scale):
    number = coeffs.shape[0]
    stacked = coeffs.reshape(number, 2, channels)
    grad_pairs = grad_modes.reshape(number, 2, channels)
    real_w = jnp.einsum("mac,mao->mco", stacked, grad_pairs, preferred_element_type=jnp.float32)
    imag_w = jnp.einsum(
        "mc,mo->mco", stacked[:, 0], grad_pairs[:, 1], preferred_element_type=jnp.float32
    ) - jnp.einsum(
        "mc,mo->mco", stacked[:, 1], grad_pairs[:, 0], preferred_element_type=jnp.float32
    )
    weight_grad = (jnp.concatenate([real_w, imag_w], 2) * weight_scale).astype(jnp.bfloat16)
    straight = jnp.concatenate([grad_pairs[:, 0], grad_pairs[:, 1]], 1)
    rotated = jnp.concatenate([grad_pairs[:, 1], -grad_pairs[:, 0]], 1)
    real_x = jnp.einsum("mcj,mj->mc", weights, straight, preferred_element_type=jnp.float32)
    imag_x = jnp.einsum("mcj,mj->mc", weights, rotated, preferred_element_type=jnp.float32)
    input_grad = (jnp.concatenate([real_x, imag_x], 1) * input_scale).astype(jnp.bfloat16)
    return (weight_grad, input_grad)


def general_body(features, cotangent, spectral_weight, channel_weight, channel_bias):
    channels, planes, lines, depth_len = features.shape
    devices = lax.axis_size("gx")
    all_planes = planes * devices
    owned_modes = spectral_weight.shape[0]
    wave_pairs = MY * MZ
    forward_scale = 1.0 / math.sqrt(all_planes * lines * depth_len)
    inverse_scale = 1.0 / math.sqrt(MX * wave_pairs)
    weight_scale = math.sqrt(MX * wave_pairs / (all_planes * lines * depth_len))
    depth_basis = depth_table(MZ, depth_len)
    across_y = analysis_pair(freq_index(MY, lines), lines)
    back_y = synthesis_pair(freq_index(MY, lines), lines)
    across_full = analysis_pair(freq_index(MX, all_planes), all_planes)
    back_full = synthesis_pair(freq_index(MX, all_planes), all_planes)
    depth_part = jnp.dot(features, depth_basis.T, preferred_element_type=jnp.float32).astype(
        jnp.bfloat16
    )
    plane_part = (
        jnp.einsum(
            "cxyaz,yabk->cxbkz",
            depth_part.reshape(channels, planes, lines, 2, MZ),
            across_y,
            preferred_element_type=jnp.float32,
        )
        .astype(jnp.bfloat16)
        .reshape(channels, planes, 2, wave_pairs)
    )
    all_rows = lax.all_to_all(plane_part, "gx", split_axis=3, concat_axis=1, tiled=True)
    mode_sums = jnp.einsum(
        "cxaq,xabk->qkbc", all_rows, across_full, preferred_element_type=jnp.float32
    ).reshape(owned_modes, 2 * channels)
    coeffs = (mode_sums * forward_scale).astype(jnp.bfloat16)
    spectral = mode_product(coeffs, spectral_weight, channels)
    planes_all = jnp.einsum(
        "qkao,kabx->oxbq",
        spectral.reshape(owned_modes // MX, MX, 2, channels),
        back_full,
        preferred_element_type=jnp.float32,
    ).astype(jnp.bfloat16)
    planes_back = lax.all_to_all(planes_all, "gx", split_axis=1, concat_axis=3, tiled=True)
    lines_back = (
        jnp.einsum(
            "oxakz,kaby->oxybz",
            planes_back.reshape(channels, planes, 2, MY, MZ),
            back_y,
            preferred_element_type=jnp.float32,
        )
        .astype(jnp.bfloat16)
        .reshape(channels, planes, lines, 2 * MZ)
    )
    spectral_term = (
        jnp.dot(lines_back, depth_basis, preferred_element_type=jnp.float32) * inverse_scale
    )
    pointwise = jnp.einsum(
        "oc,cxyz->oxyz", channel_weight, features, preferred_element_type=jnp.float32
    )
    hidden = spectral_term + pointwise + channel_bias[:, None, None, None]
    activated, derivative = gelu_parts(hidden)
    upstream = (cotangent.astype(jnp.float32) * derivative).astype(jnp.bfloat16)
    lines_grad = (
        jnp.dot(upstream, depth_basis.T, preferred_element_type=jnp.float32) * inverse_scale
    ).astype(jnp.bfloat16)
    rows_grad = (
        jnp.einsum(
            "oxybz,kaby->oxakz",
            lines_grad.reshape(channels, planes, lines, 2, MZ),
            back_y,
            preferred_element_type=jnp.float32,
        )
        .astype(jnp.bfloat16)
        .reshape(channels, planes, 2, wave_pairs)
    )
    all_grads = lax.all_to_all(rows_grad, "gx", split_axis=3, concat_axis=1, tiled=True)
    grad_sums = jnp.einsum(
        "oxbq,kabx->qkao", all_grads, back_full, preferred_element_type=jnp.float32
    ).reshape(owned_modes, 2 * channels)
    grad_modes = grad_sums.astype(jnp.bfloat16)
    spectral_grad, coeff_grad = mode_grads(
        coeffs, spectral_weight, grad_modes, channels, weight_scale, forward_scale
    )
    plane_all = jnp.einsum(
        "qkbc,xabk->cxaq",
        coeff_grad.reshape(owned_modes // MX, MX, 2, channels),
        across_full,
        preferred_element_type=jnp.float32,
    ).astype(jnp.bfloat16)
    plane_grad = lax.all_to_all(plane_all, "gx", split_axis=1, concat_axis=3, tiled=True)
    depth_grad = (
        jnp.einsum(
            "cxbkz,yabk->cxyaz",
            plane_grad.reshape(channels, planes, 2, MY, MZ),
            across_y,
            preferred_element_type=jnp.float32,
        )
        .astype(jnp.bfloat16)
        .reshape(channels, planes, lines, 2 * MZ)
    )
    channel_back = jnp.einsum(
        "oc,oxyz->cxyz", channel_weight, upstream, preferred_element_type=jnp.float32
    )
    feature_grad = (
        jnp.dot(depth_grad, depth_basis, preferred_element_type=jnp.float32) + channel_back
    ).astype(jnp.bfloat16)
    return (activated.astype(jnp.bfloat16), feature_grad, spectral_grad)


PLANES = 2
GROUP = 8
VMEM_MIB = 58
NT = (((1,), (1,)), ((), ()))
F32 = jnp.float32
BF16 = jnp.bfloat16


def np_freq(retained, length):
    ladder = np.arange(retained)
    return np.where(ladder < retained // 2, ladder, length - retained + ladder)


def np_angles(wavenum, length):
    points = np.arange(length)
    return (wavenum[:, None] * points[None, :] % length) * (2.0 * math.pi / length)


def as_bf16(table):
    return np.asarray(table, np.float32).astype(ml_dtypes.bfloat16)


def rotation(angle, sign):
    cosine, sine_wave = np.cos(angle), sign * np.sin(angle)
    return np.stack([np.stack([cosine, -sine_wave]), np.stack([sine_wave, cosine])])


@functools.lru_cache(maxsize=None)
def tables(devices, lines, depth_len):
    planes_all = devices * PLANES
    angle = np_angles(np.arange(MZ), depth_len)
    depth = np.stack([np.cos(angle), -np.sin(angle)])
    eye = np.eye(GROUP)
    depth_block = np.einsum("akz,ij->akijz", depth, eye).reshape(2 * MZ * GROUP, GROUP * depth_len)
    plane_eye = np.eye(PLANES)
    angle = np_angles(np_freq(MY, lines), lines).reshape(devices, MY // devices, lines)
    across = np.einsum("badly,xw->ldbxawy", rotation(angle, -1.0), plane_eye)
    across = across.reshape(MY * 2 * PLANES, 2 * PLANES * lines)
    back = np.einsum("pbdly,xw->pxyldbw", rotation(angle, 1.0), plane_eye)
    back = back.reshape(2 * PLANES * lines, MY * 2 * PLANES)
    angle = np_angles(np_freq(MX, planes_all), planes_all).reshape(MX // 4, 4, devices, PLANES)
    forward = rotation(angle, -1.0)
    rows = np.einsum("batksx->tbksax", forward).reshape(MX // 4, 2, 4, devices * 2 * PLANES)
    plain = rows.reshape(2 * MX, -1)
    both = np.stack([rows, rows[:, ::-1]], 1).reshape(4 * MX, -1)
    turned = np.concatenate([rows[:, 1:], -rows[:, :1]], 1).reshape(2 * MX, -1)
    straight_rotated = np.concatenate([plain, turned], 0)
    inverse = np.einsum("batksx->sbxtak", rotation(angle, 1.0)).reshape(-1, 2 * MX)
    return {
        "depth": as_bf16(depth_block),
        "across_y": as_bf16(across),
        "back_y": as_bf16(back),
        "plain_x": as_bf16(plain),
        "both_x": as_bf16(both),
        "straight_x": as_bf16(straight_rotated),
        "back_x": as_bf16(inverse),
    }


def dot_nn(left, right):
    return jnp.dot(left, right, preferred_element_type=F32)


def dot_nt(left, right):
    return lax.dot_general(left, right, NT, preferred_element_type=F32)


def lanes(shape):
    return lax.broadcasted_iota(jnp.int32, shape, len(shape) - 1)


def sublanes(shape):
    return lax.broadcasted_iota(jnp.int32, shape, len(shape) - 2)


def swap_halves(block):
    return pltpu.roll(block, 64, 1)


def depth_analysis(slabs, depth, scale, group, lines_ref):
    wide = jnp.concatenate(slabs, axis=1)
    parts = dot_nt(depth, wide)
    if scale is not None:
        parts = parts * scale
    width = wide.shape[0]
    start = pl.multiple_of(group * GROUP, GROUP)
    for a in range(2):
        lines_ref[:, pl.ds(start, GROUP), a * width : (a + 1) * width] = parts[
            a * MZ * GROUP : (a + 1) * MZ * GROUP
        ].reshape(MZ, GROUP, width)


def rows_analysis(lines_ref, across_ref, rows_ref, out_ref):
    channels, width = lines_ref.shape[1], lines_ref.shape[2]
    across = across_ref[...]
    half = across.shape[0] // 2
    for kzh in range(MZ // 2):
        pair = lines_ref[2 * kzh : 2 * kzh + 2].reshape(2 * channels, width).astype(BF16)
        rows = dot_nt(across, pair)
        for kyl in range(2):
            rows_ref[pl.ds(kyl * 8 + kzh, half, stride=16), :] = rows[
                kyl * half : (kyl + 1) * half
            ]
    out_ref[...] = rows_ref[...].astype(BF16)


def rows_gather(block_ref, rows_ref, spec_ref):
    rows_ref[...] = block_ref[...].astype(F32)
    count = rows_ref.shape[0] // 16
    eye = (sublanes((128, 128)) == lanes((128, 128))).astype(BF16)
    for kzh in range(MZ // 2):
        both = jnp.concatenate(
            [rows_ref[pl.ds(kyl * 8 + kzh, count, stride=16), :] for kyl in range(2)], axis=0
        ).astype(BF16)
        turned = dot_nt(eye, both)
        for h in range(2):
            spec_ref[:, (2 * kzh + h) * GROUP : (2 * kzh + h + 1) * GROUP, :] = turned[
                h * 64 : (h + 1) * 64
            ].reshape(8, GROUP, turned.shape[1])


def synthesis(group, spec_ref, back, depth, scale):
    lines = dot_nt(back, spec_ref[group].astype(BF16))
    if scale is not None:
        lines = lines * scale
    lines = lines.astype(BF16)
    half = lines.shape[0] // 2
    return dot_nn(jnp.concatenate([lines[:half], lines[half:]], axis=1), depth)


def flat(slab):
    return slab.reshape(slab.shape[0] * slab.shape[1], slab.shape[2])


def analysis_kernel(per_step, field_ref, depth_ref, across_ref, out_ref, lines_ref, rows_ref):
    step = pl.program_id(0)
    depth = depth_ref[...]
    for g in range(per_step):
        slabs = [flat(field_ref[g * GROUP + ci]) for ci in range(GROUP)]
        depth_analysis(slabs, depth, None, step * per_step + g, lines_ref)

    @pl.when(step == pl.num_programs(0) - 1)
    def _():
        rows_analysis(lines_ref, across_ref, rows_ref, out_ref)


def middle_kernel(
    per_step,
    inverse_scale,
    block_ref,
    point_ref,
    cot_ref,
    bias_ref,
    depth_ref,
    across_ref,
    back_ref,
    act_ref,
    up_ref,
    out_ref,
    lines_ref,
    rows_ref,
    spec_ref,
):
    step = pl.program_id(0)

    @pl.when(step == 0)
    def _():
        rows_gather(block_ref, rows_ref, spec_ref)

    depth = depth_ref[...]
    back = back_ref[...]
    for g in range(per_step):
        group = step * per_step + g
        spectral = synthesis(group, spec_ref, back, depth, inverse_scale)
        slabs = []
        for oi in range(GROUP):
            index = g * GROUP + oi
            hidden = (
                spectral[:, oi * 128 : (oi + 1) * 128]
                + flat(point_ref[index])
                + bias_ref[group * GROUP + oi]
            )
            square = hidden * hidden
            gate = 0.5 + 0.5 * jnp.tanh(
                hidden * (SQRT_TWO_PI + (SQRT_TWO_PI * CUBIC_COEF) * square)
            )
            slope = hidden * (2.0 * SQRT_TWO_PI + (6.0 * SQRT_TWO_PI * CUBIC_COEF) * square)
            derivative = gate + (gate - gate * gate) * slope
            upstream = (flat(cot_ref[index]).astype(F32) * derivative).astype(BF16)
            act_ref[index] = (hidden * gate).astype(BF16).reshape(act_ref.shape[1:])
            up_ref[index] = upstream.reshape(up_ref.shape[1:])
            slabs.append(upstream)
        depth_analysis(slabs, depth, inverse_scale, group, lines_ref)

    @pl.when(step == pl.num_programs(0) - 1)
    def _():
        rows_analysis(lines_ref, across_ref, rows_ref, out_ref)


def final_kernel(
    per_step, block_ref, point_ref, depth_ref, back_ref, out_ref, rows_ref, spec_ref
):
    step = pl.program_id(0)

    @pl.when(step == 0)
    def _():
        rows_gather(block_ref, rows_ref, spec_ref)

    depth = depth_ref[...]
    back = back_ref[...]
    for g in range(per_step):
        spectral = synthesis(step * per_step + g, spec_ref, back, depth, None)
        for ci in range(GROUP):
            index = g * GROUP + ci
            total = spectral[:, ci * 128 : (ci + 1) * 128] + flat(point_ref[index])
            out_ref[index] = total.astype(BF16).reshape(out_ref.shape[1:])


def point_kernel(transposed, weight_ref, field_ref, out_ref, wide_ref):
    size = wide_ref.shape[0]
    plane, chunk = pl.program_id(0), pl.program_id(1)

    @pl.when((plane == 0) & (chunk == 0))
    def _():
        tall = (sublanes((size, 64)) // 16 == lanes((size, 64))).astype(BF16)
        if transposed:
            left = lax.dot_general(
                tall, weight_ref[...], (((1,), (1,)), ((), ())), preferred_element_type=F32
            )
        else:
            left = dot_nn(tall, weight_ref[...])
        spread = dot_nt(left.astype(BF16), tall)
        same = sublanes((size, size)) % 16 == lanes((size, size)) % 16
        wide_ref[...] = jnp.where(same, spread, 0.0).astype(BF16)

    field = field_ref[:, 0]
    right = jnp.concatenate(
        [field[:, yc * 16 : (yc + 1) * 16].reshape(size, 128) for yc in range(4)], axis=1
    )
    rows = out_ref.shape[0] * 16
    start = pl.multiple_of(chunk * rows, rows)
    result = dot_nn(wide_ref[pl.ds(start, rows), :], right)
    for yc in range(4):
        out_ref[:, 0, yc * 16 : (yc + 1) * 16, :] = result[:, yc * 128 : (yc + 1) * 128].reshape(
            rows // 16, 16, 128
        )


def start_weights(weight_hbm, weight_ref, sems):
    copies = []
    for j in range(16):
        rows = weight_ref.shape[0] // 16
        part = pl.ds(j * rows, rows)
        copy = pltpu.make_async_copy(weight_hbm.at[part], weight_ref.at[part], sems.at[j])
        copy.start()
        copies.append(copy)
    return copies


def mode_pair(weight_ref, j, h, u):
    start = ((j * 2 + h) * MX + 8 * u) * 64
    return jnp.concatenate(
        [weight_ref[start : start + 256, :], weight_ref[start + 256 : start + 512, :]], axis=1
    )


def plane_sums(back_ref, mixed_ref, res_ref, out_ref):
    count = res_ref.shape[0] // 16
    for quarter in range(4):
        wide = jnp.concatenate([mixed_ref[quarter * 4 + k] for k in range(4)], axis=1)
        rows = dot_nn(back_ref[...], wide)
        for k in range(4):
            res_ref[pl.ds(quarter * 4 + k, count, stride=16), :] = rows[:, k * 128 : (k + 1) * 128]
    out_ref[...] = res_ref[...].astype(BF16)


def mode_kernel(
    scale,
    block_ref,
    weight_hbm,
    both_ref,
    plain_ref,
    back_ref,
    coeff_ref,
    out_ref,
    weight_ref,
    rows_ref,
    left_ref,
    mixed_ref,
    sems,
):
    copies = start_weights(weight_hbm, weight_ref, sems)
    count = rows_ref.shape[0] // 16
    rows_ref[...] = block_ref[...].astype(F32)
    low = lanes((128, 128)) < 64
    kxl = sublanes((128, 128)) % 4
    half = lanes((128, 128)) // 64
    first = (kxl == half).astype(BF16)
    second = (kxl == 2 + half).astype(BF16)
    low8 = lanes((8, 128)) < 64
    sign = jnp.where(sublanes((8, 128)) < 4, -1.0, 1.0)
    for quarter in range(4):
        wide = jnp.concatenate(
            [rows_ref[pl.ds(quarter * 4 + k, count, stride=16), :] for k in range(4)], axis=1
        ).astype(BF16)
        plain = (dot_nn(plain_ref[...], wide) * scale).astype(BF16)
        both = dot_nn(both_ref[...], wide) * scale
        for k in range(4):
            j = quarter * 4 + k
            coeff_ref[j] = plain[:, k * 128 : (k + 1) * 128]
            coeffs = both[:, k * 128 : (k + 1) * 128]
            swapped = swap_halves(coeffs)
            for h in range(2):
                twice = jnp.where(low if h == 0 else ~low, coeffs, swapped).astype(BF16)
                left_ref[j, h] = jnp.concatenate([twice * first, twice * second], axis=1)
    for j in range(16):
        copies[j].wait()
        mixed = []
        for u in range(MX // 8):
            halves = [
                dot_nn(left_ref[j, h, u * 32 : (u + 1) * 32, :], mode_pair(weight_ref, j, h, u))
                for h in range(2)
            ]
            for t in range(2):
                low_h, high_h = [
                    part[t * 16 : (t + 1) * 16, t * 128 : (t + 1) * 128] for part in halves
                ]
                keep = jnp.where(low8, low_h[:8], sign * high_h[8:])
                move = jnp.where(low8, high_h[:8], sign * low_h[8:])
                mixed.append(keep + swap_halves(move))
        mixed_ref[j] = jnp.concatenate(mixed, axis=0).astype(BF16)
    plane_sums(back_ref, mixed_ref, rows_ref, out_ref)


def mode_grad_kernel(
    scale,
    block_ref,
    weight_hbm,
    straight_ref,
    back_ref,
    pair_ref,
    out_ref,
    weight_ref,
    rows_ref,
    mixed_ref,
    sems,
):
    copies = start_weights(weight_hbm, weight_ref, sems)
    count = rows_ref.shape[0] // 16
    rows_ref[...] = block_ref[...].astype(F32)
    low = lanes((64, 128)) < 64
    low16 = lanes((16, 128)) < 64
    row = sublanes((16, 128)) % 4
    upper = row < 2
    valid = lanes((16, 128)) // 64 == row % 2
    even = (sublanes((16, 128)) < 8).astype(BF16)
    odd = (sublanes((16, 128)) >= 8).astype(BF16)
    for j in range(16):
        section = rows_ref[pl.ds(j, count, stride=16), :]
        swapped = swap_halves(section)
        twice = jnp.concatenate(
            [jnp.where(low, section, swapped), jnp.where(low, swapped, section)], axis=1
        ).astype(BF16)
        turned = dot_nn(straight_ref[...], twice)
        for h in range(2):
            part = turned[:, h * 128 : (h + 1) * 128]
            pair_ref[2 * j + h] = jnp.where(low, part[:64], part[64:]).astype(BF16)
    for j in range(16):
        copies[j].wait()
        mixed = []
        for u in range(MX // 8):
            found = []
            for h in range(2):
                pair = pair_ref[2 * j + h, u * 16 : (u + 1) * 16, :]
                rows = dot_nt(
                    jnp.concatenate([pair * even, pair * odd], axis=1),
                    mode_pair(weight_ref, j, h, u),
                )
                found.append(jnp.where(valid, jnp.where(upper, rows[:, :128], rows[:, 128:]), 0.0))
            keep = jnp.where(low16, found[0], found[1])
            move = jnp.where(low16, found[1], found[0])
            mixed.append(keep + swap_halves(move))
        mixed_ref[j] = (jnp.concatenate(mixed, axis=0) * scale).astype(BF16)
    plane_sums(back_ref, mixed_ref, rows_ref, out_ref)


def weight_grad_kernel(per_step, scale, coeff_ref, pair_ref, out_ref, mask_ref):
    @pl.when(pl.program_id(0) == 0)
    def _():
        lane = lanes((128, 64))
        part = sublanes((128, 64)) // 64
        for t in range(MX // 4):
            mask_ref[t] = ((lane // 8 == t) & (lane % 4 // 2 == part)).astype(BF16)

    eye = (sublanes((128, 128)) == lanes((128, 128))).astype(BF16)
    even = (sublanes((64, 128)) % 2 == 0).astype(BF16)
    odd = (sublanes((64, 128)) % 2 == 1).astype(BF16)
    for jj in range(per_step):
        turned = (dot_nt(eye, coeff_ref[jj]) * scale).astype(BF16)
        for h in range(2):
            left = turned[h * 64 : (h + 1) * 64]
            left = jnp.concatenate([left, left], axis=0)
            pair = pair_ref[jj * 2 + h]
            right = jnp.concatenate([pair * even, pair * odd], axis=1)
            for t in range(MX // 4):
                four = dot_nn(left * mask_ref[t], right).astype(BF16)
                mode = (jj * 2 + h) * MX + 4 * t
                for k in range(4):
                    out_ref[mode + k] = four[
                        k // 2 * 64 : (k // 2 + 1) * 64, k % 2 * 128 : (k % 2 + 1) * 128
                    ]


def whole(array):
    rank = len(array.shape)
    return pl.BlockSpec(array.shape, lambda *_: (0,) * rank)


def params(mib):
    return pltpu.CompilerParams(vmem_limit_bytes=mib * 1024 * 1024)


def cost(flops, moved):
    return pl.CostEstimate(flops=int(flops), bytes_accessed=int(moved), transcendentals=0)


def fast_body(features, cotangent, spectral_weight, channel_weight, channel_bias):
    channels, planes, lines, depth_len = features.shape
    devices = lax.axis_size("gx")
    owned_modes = spectral_weight.shape[0]
    wave_pairs = MY * MZ
    volume = planes * devices * lines * depth_len
    forward_scale = 1.0 / math.sqrt(volume)
    inverse_scale = 1.0 / math.sqrt(MX * wave_pairs)
    weight_scale = math.sqrt(MX * wave_pairs / volume)
    table = {name: jnp.asarray(value) for name, value in tables(devices, lines, depth_len).items()}
    per_step = 2
    steps = channels // (GROUP * per_step)
    step_channels = GROUP * per_step
    block_rows = devices * 64
    block_shape = jax.ShapeDtypeStruct((block_rows, 128), BF16)
    block_spec = whole(block_shape)
    field_spec = pl.BlockSpec(
        (step_channels, planes, lines, depth_len), lambda i: (i, 0, 0, 0)
    )
    lines_scratch = pltpu.VMEM((MZ, channels, 2 * planes * lines), F32)
    rows_scratch = pltpu.VMEM((block_rows, 128), F32)
    spec_scratch = pltpu.VMEM((channels // GROUP, MZ * GROUP, 128), F32)
    weight_rows = spectral_weight.reshape(owned_modes * channels, 2 * channels)
    field_bytes = features.size * 2

    def exchange(block):
        return lax.all_to_all(
            block.reshape(devices, 64, 128), "gx", 0, 0, tiled=True
        ).reshape(block_rows, 128)

    def point(field, transposed):
        rows = 16
        return pl.pallas_call(
            functools.partial(point_kernel, transposed),
            out_shape=jax.ShapeDtypeStruct(field.shape, F32),
            grid=(planes, channels // rows),
            in_specs=[
                pl.BlockSpec((channels, channels), lambda x, o: (0, 0)),
                pl.BlockSpec((channels, 1, lines, depth_len), lambda x, o: (0, x, 0, 0)),
            ],
            out_specs=pl.BlockSpec((rows, 1, lines, depth_len), lambda x, o: (o, x, 0, 0)),
            scratch_shapes=[pltpu.VMEM((channels * 16, channels * 16), BF16)],
            compiler_params=params(VMEM_MIB),
            cost_estimate=cost(2 * 1024**3, 3 * field_bytes),
            name="channel_map_back" if transposed else "channel_map",
        )(channel_weight, field)

    block = pl.pallas_call(
        functools.partial(analysis_kernel, per_step),
        out_shape=block_shape,
        grid=(steps,),
        in_specs=[field_spec, whole(table["depth"]), whole(table["across_y"])],
        out_specs=block_spec,
        scratch_shapes=[lines_scratch, rows_scratch],
        compiler_params=params(VMEM_MIB),
        cost_estimate=cost(2 * 256 * 1024 * 1024, field_bytes),
        name="field_analysis",
    )(features, table["depth"], table["across_y"])
    block = exchange(block)
    pointwise = point(features, False)

    vmem = pl.BlockSpec(memory_space=pltpu.VMEM)
    hbm = pl.BlockSpec(memory_space=pl.ANY)
    weight_scratch = pltpu.VMEM(weight_rows.shape, BF16)
    mixed_scratch = pltpu.VMEM((16, 64, 128), BF16)
    weight_sems = pltpu.SemaphoreType.DMA((16,))
    coeffs, block = pl.pallas_call(
        functools.partial(mode_kernel, forward_scale),
        out_shape=[jax.ShapeDtypeStruct((16, 64, 128), BF16), block_shape],
        in_specs=[vmem, hbm, vmem, vmem, vmem],
        out_specs=[vmem, vmem],
        scratch_shapes=[
            weight_scratch,
            rows_scratch,
            pltpu.VMEM((16, 2, 128, 256), BF16),
            mixed_scratch,
            weight_sems,
        ],
        compiler_params=params(VMEM_MIB),
        cost_estimate=cost(256 * 2 * 16 * 256 * 128, 17 * 2**20),
        name="mode_product",
    )(block, weight_rows, table["both_x"], table["plain_x"], table["back_x"])
    block = exchange(block)

    activated, upstream, block = pl.pallas_call(
        functools.partial(middle_kernel, per_step, inverse_scale),
        out_shape=[
            jax.ShapeDtypeStruct(features.shape, BF16),
            jax.ShapeDtypeStruct(features.shape, BF16),
            block_shape,
        ],
        grid=(steps,),
        in_specs=[
            block_spec,
            field_spec,
            field_spec,
            pl.BlockSpec(memory_space=pltpu.SMEM),
            whole(table["depth"]),
            whole(table["across_y"]),
            whole(table["back_y"]),
        ],
        out_specs=[field_spec, field_spec, block_spec],
        scratch_shapes=[lines_scratch, rows_scratch, spec_scratch],
        compiler_params=params(VMEM_MIB),
        cost_estimate=cost(2**30, 5 * field_bytes),
        name="gelu_and_gradient",
    )(
        block,
        pointwise,
        cotangent,
        channel_bias,
        table["depth"],
        table["across_y"],
        table["back_y"],
    )
    block = exchange(block)
    block, channel_back = lax.optimization_barrier((block, point(upstream, True)))

    pairs, block = pl.pallas_call(
        functools.partial(mode_grad_kernel, forward_scale),
        out_shape=[jax.ShapeDtypeStruct((32, 64, 128), BF16), block_shape],
        in_specs=[vmem, hbm, vmem, vmem],
        out_specs=[vmem, vmem],
        scratch_shapes=[weight_scratch, rows_scratch, mixed_scratch, weight_sems],
        compiler_params=params(VMEM_MIB),
        cost_estimate=cost(256 * 2 * 16 * 256 * 128, 17 * 2**20),
        name="mode_gradient",
    )(block, weight_rows, table["straight_x"], table["back_x"])
    block = exchange(block)

    mode_steps = 8
    per_mode_step = 16 // mode_steps
    spectral_grad = pl.pallas_call(
        functools.partial(weight_grad_kernel, per_mode_step, weight_scale),
        out_shape=jax.ShapeDtypeStruct(spectral_weight.shape, BF16),
        grid=(mode_steps,),
        in_specs=[
            pl.BlockSpec((per_mode_step, 64, 128), lambda i: (i, 0, 0)),
            pl.BlockSpec((2 * per_mode_step, 64, 128), lambda i: (i, 0, 0)),
        ],
        out_specs=pl.BlockSpec(
            (owned_modes // mode_steps, channels, 2 * channels), lambda i: (i, 0, 0)
        ),
        scratch_shapes=[pltpu.VMEM((MX // 4, 128, 64), BF16)],
        compiler_params=params(VMEM_MIB),
        cost_estimate=cost(512 * 2 * 64 * 64 * 256, 17 * 2**20),
        name="weight_gradient",
    )(coeffs, pairs)

    feature_grad = pl.pallas_call(
        functools.partial(final_kernel, per_step),
        out_shape=jax.ShapeDtypeStruct(features.shape, BF16),
        grid=(steps,),
        in_specs=[block_spec, field_spec, whole(table["depth"]), whole(table["back_y"])],
        out_specs=field_spec,
        scratch_shapes=[rows_scratch, spec_scratch],
        compiler_params=params(VMEM_MIB),
        cost_estimate=cost(2**29, 3 * field_bytes),
        name="field_gradient",
    )(block, channel_back, table["depth"], table["back_y"])
    return (activated, feature_grad, spectral_grad)


def body(features, cotangent, spectral_weight, channel_weight, channel_bias):
    channels, planes, lines, depth_len = features.shape
    devices = lax.axis_size("gx")
    fits = (
        (channels, planes, lines, depth_len) == (64, PLANES, 64, 128)
        and spectral_weight.shape[0] == 2 * MZ * MX
        and devices * 2 == MY
        and devices * 2 == MX
    )
    run = fast_body if fits else general_body
    return run(features, cotangent, spectral_weight, channel_weight, channel_bias)


def solution(mesh):
    in_specs = (
        P("grp", "gx", None, None),
        P("grp", "gx", None, None),
        P("gx", None, None),
        P(),
        P(),
    )
    out_specs = (
        P("grp", "gx", None, None),
        P("grp", "gx", None, None),
        P(("grp", "gx"), None, None),
    )
    return jax.shard_map(body, mesh=mesh, in_specs=in_specs, out_specs=out_specs, check_vma=False)
```

```python
import functools
import math

import jax
import jax.numpy as jnp
import ml_dtypes
import numpy as np
from jax import lax
from jax.experimental import pallas as pl
from jax.experimental.pallas import tpu as pltpu
from jax.sharding import PartitionSpec as P

MX = 32
MY = 32
MZ = 16


SQRT_TWO_PI = math.sqrt(2.0 / math.pi)
CUBIC_COEF = 0.044715


def freq_index(retained, length):
    ladder = jnp.arange(retained, dtype=jnp.int32)
    return jnp.where(ladder < retained // 2, ladder, length - retained + ladder)


def cos_sin(wavenum, length):
    points = jnp.arange(length, dtype=jnp.int32)
    angles = (wavenum[:, None] * points[None, :] % length).astype(jnp.float32) * (
        2.0 * math.pi / length
    )
    return (jnp.cos(angles), jnp.sin(angles))


def analysis_pair(wavenum, length):
    cosine, sine_wave = cos_sin(wavenum, length)
    cosine, sine_wave = (cosine.T, sine_wave.T)
    return jnp.stack(
        [jnp.stack([cosine, -sine_wave], 1), jnp.stack([sine_wave, cosine], 1)], 1
    ).astype(jnp.bfloat16)


def synthesis_pair(wavenum, length):
    cosine, sine_wave = cos_sin(wavenum, length)
    return jnp.stack(
        [jnp.stack([cosine, sine_wave], 1), jnp.stack([-sine_wave, cosine], 1)], 1
    ).astype(jnp.bfloat16)


def depth_table(retained, length):
    cosine, sine_wave = cos_sin(jnp.arange(retained, dtype=jnp.int32), length)
    return jnp.concatenate([cosine, -sine_wave], 0).astype(jnp.bfloat16)


def gelu_parts(inputs):
    cubed_in = inputs * inputs * inputs
    tangent = jnp.tanh(SQRT_TWO_PI * (inputs + CUBIC_COEF * cubed_in))
    output = 0.5 * inputs * (1.0 + tangent)
    derivative = 0.5 * (1.0 + tangent) + 0.5 * inputs * (1.0 - tangent * tangent) * SQRT_TWO_PI * (
        1.0 + 3.0 * CUBIC_COEF * inputs * inputs
    )
    return (output, derivative)


def mode_product(coeffs, weights, channels):
    stacked = coeffs.reshape(coeffs.shape[0], 2, channels)
    halves = jnp.einsum("mac,mcj->amj", stacked, weights, preferred_element_type=jnp.float32)
    real_out = halves[0, :, :channels] - halves[1, :, channels:]
    imag_out = halves[0, :, channels:] + halves[1, :, :channels]
    return jnp.concatenate([real_out, imag_out], 1).astype(jnp.bfloat16)


def mode_grads(coeffs, weights, grad_modes, channels, weight_scale, input_scale):
    number = coeffs.shape[0]
    stacked = coeffs.reshape(number, 2, channels)
    grad_pairs = grad_modes.reshape(number, 2, channels)
    real_w = jnp.einsum("mac,mao->mco", stacked, grad_pairs, preferred_element_type=jnp.float32)
    imag_w = jnp.einsum(
        "mc,mo->mco", stacked[:, 0], grad_pairs[:, 1], preferred_element_type=jnp.float32
    ) - jnp.einsum(
        "mc,mo->mco", stacked[:, 1], grad_pairs[:, 0], preferred_element_type=jnp.float32
    )
    weight_grad = (jnp.concatenate([real_w, imag_w], 2) * weight_scale).astype(jnp.bfloat16)
    straight = jnp.concatenate([grad_pairs[:, 0], grad_pairs[:, 1]], 1)
    rotated = jnp.concatenate([grad_pairs[:, 1], -grad_pairs[:, 0]], 1)
    real_x = jnp.einsum("mcj,mj->mc", weights, straight, preferred_element_type=jnp.float32)
    imag_x = jnp.einsum("mcj,mj->mc", weights, rotated, preferred_element_type=jnp.float32)
    input_grad = (jnp.concatenate([real_x, imag_x], 1) * input_scale).astype(jnp.bfloat16)
    return (weight_grad, input_grad)


def general_body(features, cotangent, spectral_weight, channel_weight, channel_bias):
    channels, planes, lines, depth_len = features.shape
    devices = lax.axis_size("gx")
    all_planes = planes * devices
    owned_modes = spectral_weight.shape[0]
    wave_pairs = MY * MZ
    forward_scale = 1.0 / math.sqrt(all_planes * lines * depth_len)
    inverse_scale = 1.0 / math.sqrt(MX * wave_pairs)
    weight_scale = math.sqrt(MX * wave_pairs / (all_planes * lines * depth_len))
    depth_basis = depth_table(MZ, depth_len)
    across_y = analysis_pair(freq_index(MY, lines), lines)
    back_y = synthesis_pair(freq_index(MY, lines), lines)
    across_full = analysis_pair(freq_index(MX, all_planes), all_planes)
    back_full = synthesis_pair(freq_index(MX, all_planes), all_planes)
    depth_part = jnp.dot(features, depth_basis.T, preferred_element_type=jnp.float32).astype(
        jnp.bfloat16
    )
    plane_part = (
        jnp.einsum(
            "cxyaz,yabk->cxbkz",
            depth_part.reshape(channels, planes, lines, 2, MZ),
            across_y,
            preferred_element_type=jnp.float32,
        )
        .astype(jnp.bfloat16)
        .reshape(channels, planes, 2, wave_pairs)
    )
    all_rows = lax.all_to_all(plane_part, "gx", split_axis=3, concat_axis=1, tiled=True)
    mode_sums = jnp.einsum(
        "cxaq,xabk->qkbc", all_rows, across_full, preferred_element_type=jnp.float32
    ).reshape(owned_modes, 2 * channels)
    coeffs = (mode_sums * forward_scale).astype(jnp.bfloat16)
    spectral = mode_product(coeffs, spectral_weight, channels)
    planes_all = jnp.einsum(
        "qkao,kabx->oxbq",
        spectral.reshape(owned_modes // MX, MX, 2, channels),
        back_full,
        preferred_element_type=jnp.float32,
    ).astype(jnp.bfloat16)
    planes_back = lax.all_to_all(planes_all, "gx", split_axis=1, concat_axis=3, tiled=True)
    lines_back = (
        jnp.einsum(
            "oxakz,kaby->oxybz",
            planes_back.reshape(channels, planes, 2, MY, MZ),
            back_y,
            preferred_element_type=jnp.float32,
        )
        .astype(jnp.bfloat16)
        .reshape(channels, planes, lines, 2 * MZ)
    )
    spectral_term = (
        jnp.dot(lines_back, depth_basis, preferred_element_type=jnp.float32) * inverse_scale
    )
    pointwise = jnp.einsum(
        "oc,cxyz->oxyz", channel_weight, features, preferred_element_type=jnp.float32
    )
    hidden = spectral_term + pointwise + channel_bias[:, None, None, None]
    activated, derivative = gelu_parts(hidden)
    upstream = (cotangent.astype(jnp.float32) * derivative).astype(jnp.bfloat16)
    lines_grad = (
        jnp.dot(upstream, depth_basis.T, preferred_element_type=jnp.float32) * inverse_scale
    ).astype(jnp.bfloat16)
    rows_grad = (
        jnp.einsum(
            "oxybz,kaby->oxakz",
            lines_grad.reshape(channels, planes, lines, 2, MZ),
            back_y,
            preferred_element_type=jnp.float32,
        )
        .astype(jnp.bfloat16)
        .reshape(channels, planes, 2, wave_pairs)
    )
    all_grads = lax.all_to_all(rows_grad, "gx", split_axis=3, concat_axis=1, tiled=True)
    grad_sums = jnp.einsum(
        "oxbq,kabx->qkao", all_grads, back_full, preferred_element_type=jnp.float32
    ).reshape(owned_modes, 2 * channels)
    grad_modes = grad_sums.astype(jnp.bfloat16)
    spectral_grad, coeff_grad = mode_grads(
        coeffs, spectral_weight, grad_modes, channels, weight_scale, forward_scale
    )
    plane_all = jnp.einsum(
        "qkbc,xabk->cxaq",
        coeff_grad.reshape(owned_modes // MX, MX, 2, channels),
        across_full,
        preferred_element_type=jnp.float32,
    ).astype(jnp.bfloat16)
    plane_grad = lax.all_to_all(plane_all, "gx", split_axis=1, concat_axis=3, tiled=True)
    depth_grad = (
        jnp.einsum(
            "cxbkz,yabk->cxyaz",
            plane_grad.reshape(channels, planes, 2, MY, MZ),
            across_y,
            preferred_element_type=jnp.float32,
        )
        .astype(jnp.bfloat16)
        .reshape(channels, planes, lines, 2 * MZ)
    )
    channel_back = jnp.einsum(
        "oc,oxyz->cxyz", channel_weight, upstream, preferred_element_type=jnp.float32
    )
    feature_grad = (
        jnp.dot(depth_grad, depth_basis, preferred_element_type=jnp.float32) + channel_back
    ).astype(jnp.bfloat16)
    return (activated.astype(jnp.bfloat16), feature_grad, spectral_grad)


PLANES = 2
GROUP = 8
VMEM_MIB = 58
NT = (((1,), (1,)), ((), ()))
F32 = jnp.float32
BF16 = jnp.bfloat16


def np_freq(retained, length):
    ladder = np.arange(retained)
    return np.where(ladder < retained // 2, ladder, length - retained + ladder)


def np_angles(wavenum, length):
    points = np.arange(length)
    return (wavenum[:, None] * points[None, :] % length) * (2.0 * math.pi / length)


def as_bf16(table):
    return np.asarray(table, np.float32).astype(ml_dtypes.bfloat16)


def rotation(angle, sign):
    cosine, sine_wave = np.cos(angle), sign * np.sin(angle)
    return np.stack([np.stack([cosine, -sine_wave]), np.stack([sine_wave, cosine])])


@functools.lru_cache(maxsize=None)
def tables(devices, lines, depth_len):
    planes_all = devices * PLANES
    angle = np_angles(np.arange(MZ), depth_len)
    depth = np.stack([np.cos(angle), -np.sin(angle)])
    eye = np.eye(GROUP)
    depth_block = np.einsum("akz,ij->akijz", depth, eye).reshape(2 * MZ * GROUP, GROUP * depth_len)
    plane_eye = np.eye(PLANES)
    angle = np_angles(np_freq(MY, lines), lines).reshape(devices, MY // devices, lines)
    across = np.einsum("badly,xw->ldbxawy", rotation(angle, -1.0), plane_eye)
    across = across.reshape(MY * 2 * PLANES, 2 * PLANES * lines)
    back = np.einsum("pbdly,xw->pxyldbw", rotation(angle, 1.0), plane_eye)
    back = back.reshape(2 * PLANES * lines, MY * 2 * PLANES)
    angle = np_angles(np_freq(MX, planes_all), planes_all).reshape(MX // 4, 4, devices, PLANES)
    forward = rotation(angle, -1.0)
    rows = np.einsum("batksx->tbksax", forward).reshape(MX // 4, 2, 4, devices * 2 * PLANES)
    plain = rows.reshape(2 * MX, -1)
    both = np.stack([rows, rows[:, ::-1]], 1).reshape(4 * MX, -1)
    turned = np.concatenate([rows[:, 1:], -rows[:, :1]], 1).reshape(2 * MX, -1)
    straight_rotated = np.concatenate([plain, turned], 0)
    inverse = np.einsum("batksx->sbxtak", rotation(angle, 1.0)).reshape(-1, 2 * MX)
    return {
        "depth": as_bf16(depth_block),
        "across_y": as_bf16(across),
        "back_y": as_bf16(back),
        "plain_x": as_bf16(plain),
        "both_x": as_bf16(both),
        "straight_x": as_bf16(straight_rotated),
        "back_x": as_bf16(inverse),
    }


def dot_nn(left, right):
    return jnp.dot(left, right, preferred_element_type=F32)


def dot_nt(left, right):
    return lax.dot_general(left, right, NT, preferred_element_type=F32)


def lanes(shape):
    return lax.broadcasted_iota(jnp.int32, shape, len(shape) - 1)


def sublanes(shape):
    return lax.broadcasted_iota(jnp.int32, shape, len(shape) - 2)


def swap_halves(block):
    return pltpu.roll(block, 64, 1)


def store_blocks(me_ref, rows_ref, out_refs):
    size = rows_ref.shape[0] // len(out_refs)
    for r, out_ref in enumerate(out_refs):
        start = pl.multiple_of((me_ref[0] ^ r) * size, size)
        out_ref[...] = rows_ref[pl.ds(start, size), :].astype(BF16)


def load_blocks(me_ref, block_refs, rows_ref):
    size = rows_ref.shape[0] // len(block_refs)
    for r, block_ref in enumerate(block_refs):
        start = pl.multiple_of((me_ref[0] ^ r) * size, size)
        rows_ref[pl.ds(start, size), :] = block_ref[...].astype(F32)


def depth_analysis(slabs, depth, scale, group, lines_ref):
    wide = jnp.concatenate(slabs, axis=1)
    parts = dot_nt(depth, wide)
    if scale is not None:
        parts = parts * scale
    width = wide.shape[0]
    start = pl.multiple_of(group * GROUP, GROUP)
    for a in range(2):
        lines_ref[:, pl.ds(start, GROUP), a * width : (a + 1) * width] = parts[
            a * MZ * GROUP : (a + 1) * MZ * GROUP
        ].reshape(MZ, GROUP, width)


def rows_analysis(me_ref, lines_ref, across_ref, rows_ref, out_refs):
    channels, width = lines_ref.shape[1], lines_ref.shape[2]
    across = across_ref[...]
    half = across.shape[0] // 2
    for kzh in range(MZ // 2):
        pair = lines_ref[2 * kzh : 2 * kzh + 2].reshape(2 * channels, width).astype(BF16)
        rows = dot_nt(across, pair)
        for kyl in range(2):
            rows_ref[pl.ds(kyl * 8 + kzh, half, stride=16), :] = rows[
                kyl * half : (kyl + 1) * half
            ]
    store_blocks(me_ref, rows_ref, out_refs)


def rows_gather(me_ref, block_refs, rows_ref, spec_ref):
    load_blocks(me_ref, block_refs, rows_ref)
    count = rows_ref.shape[0] // 16
    eye = (sublanes((128, 128)) == lanes((128, 128))).astype(BF16)
    for kzh in range(MZ // 2):
        both = jnp.concatenate(
            [rows_ref[pl.ds(kyl * 8 + kzh, count, stride=16), :] for kyl in range(2)], axis=0
        ).astype(BF16)
        turned = dot_nt(eye, both)
        for h in range(2):
            spec_ref[:, (2 * kzh + h) * GROUP : (2 * kzh + h + 1) * GROUP, :] = turned[
                h * 64 : (h + 1) * 64
            ].reshape(8, GROUP, turned.shape[1])


def synthesis(group, spec_ref, back, depth, scale):
    lines = dot_nt(back, spec_ref[group].astype(BF16))
    if scale is not None:
        lines = lines * scale
    lines = lines.astype(BF16)
    half = lines.shape[0] // 2
    return dot_nn(jnp.concatenate([lines[:half], lines[half:]], axis=1), depth)


def flat(slab):
    return slab.reshape(slab.shape[0] * slab.shape[1], slab.shape[2])


def analysis_kernel(per_step, me_ref, field_ref, depth_ref, across_ref, *refs):
    out_refs, (lines_ref, rows_ref) = refs[:-2], refs[-2:]
    step = pl.program_id(0)
    depth = depth_ref[...]
    for g in range(per_step):
        slabs = [flat(field_ref[g * GROUP + ci]) for ci in range(GROUP)]
        depth_analysis(slabs, depth, None, step * per_step + g, lines_ref)

    @pl.when(step == pl.num_programs(0) - 1)
    def _():
        rows_analysis(me_ref, lines_ref, across_ref, rows_ref, out_refs)


def middle_kernel(per_step, inverse_scale, count, *refs):
    me_ref, block_refs, refs = refs[0], refs[1 : 1 + count], refs[1 + count :]
    point_ref, cot_ref, bias_ref, depth_ref, across_ref, back_ref, act_ref, up_ref = refs[:8]
    out_refs, (lines_ref, rows_ref, spec_ref) = refs[8:-3], refs[-3:]
    step = pl.program_id(0)

    @pl.when(step == 0)
    def _():
        rows_gather(me_ref, block_refs, rows_ref, spec_ref)

    depth = depth_ref[...]
    back = back_ref[...]
    for g in range(per_step):
        group = step * per_step + g
        spectral = synthesis(group, spec_ref, back, depth, inverse_scale)
        slabs = []
        for oi in range(GROUP):
            index = g * GROUP + oi
            hidden = (
                spectral[:, oi * 128 : (oi + 1) * 128]
                + flat(point_ref[index])
                + bias_ref[group * GROUP + oi]
            )
            square = hidden * hidden
            gate = 0.5 + 0.5 * jnp.tanh(
                hidden * (SQRT_TWO_PI + (SQRT_TWO_PI * CUBIC_COEF) * square)
            )
            slope = hidden * (2.0 * SQRT_TWO_PI + (6.0 * SQRT_TWO_PI * CUBIC_COEF) * square)
            derivative = gate + (gate - gate * gate) * slope
            upstream = (flat(cot_ref[index]).astype(F32) * derivative).astype(BF16)
            act_ref[index] = (hidden * gate).astype(BF16).reshape(act_ref.shape[1:])
            up_ref[index] = upstream.reshape(up_ref.shape[1:])
            slabs.append(upstream)
        depth_analysis(slabs, depth, inverse_scale, group, lines_ref)

    @pl.when(step == pl.num_programs(0) - 1)
    def _():
        rows_analysis(me_ref, lines_ref, across_ref, rows_ref, out_refs)


def final_kernel(per_step, count, *refs):
    me_ref, block_refs, refs = refs[0], refs[1 : 1 + count], refs[1 + count :]
    point_ref, depth_ref, back_ref, out_ref, rows_ref, spec_ref = refs
    step = pl.program_id(0)

    @pl.when(step == 0)
    def _():
        rows_gather(me_ref, block_refs, rows_ref, spec_ref)

    depth = depth_ref[...]
    back = back_ref[...]
    for g in range(per_step):
        spectral = synthesis(step * per_step + g, spec_ref, back, depth, None)
        for ci in range(GROUP):
            index = g * GROUP + ci
            total = spectral[:, ci * 128 : (ci + 1) * 128] + flat(point_ref[index])
            out_ref[index] = total.astype(BF16).reshape(out_ref.shape[1:])


def point_kernel(transposed, weight_ref, field_ref, out_ref, wide_ref):
    size = wide_ref.shape[0]
    plane, chunk = pl.program_id(0), pl.program_id(1)

    @pl.when((plane == 0) & (chunk == 0))
    def _():
        tall = (sublanes((size, 64)) // 16 == lanes((size, 64))).astype(BF16)
        if transposed:
            left = lax.dot_general(
                tall, weight_ref[...], (((1,), (1,)), ((), ())), preferred_element_type=F32
            )
        else:
            left = dot_nn(tall, weight_ref[...])
        spread = dot_nt(left.astype(BF16), tall)
        same = sublanes((size, size)) % 16 == lanes((size, size)) % 16
        wide_ref[...] = jnp.where(same, spread, 0.0).astype(BF16)

    field = field_ref[:, 0]
    right = jnp.concatenate(
        [field[:, yc * 16 : (yc + 1) * 16].reshape(size, 128) for yc in range(4)], axis=1
    )
    rows = out_ref.shape[0] * 16
    start = pl.multiple_of(chunk * rows, rows)
    result = dot_nn(wide_ref[pl.ds(start, rows), :], right)
    for yc in range(4):
        out_ref[:, 0, yc * 16 : (yc + 1) * 16, :] = result[:, yc * 128 : (yc + 1) * 128].reshape(
            rows // 16, 16, 128
        )


def start_weights(weight_hbm, weight_ref, sems):
    copies = []
    for j in range(16):
        rows = weight_ref.shape[0] // 16
        part = pl.ds(j * rows, rows)
        copy = pltpu.make_async_copy(weight_hbm.at[part], weight_ref.at[part], sems.at[j])
        copy.start()
        copies.append(copy)
    return copies


def mode_pair(weight_ref, j, h, u):
    start = ((j * 2 + h) * MX + 8 * u) * 64
    return jnp.concatenate(
        [weight_ref[start : start + 256, :], weight_ref[start + 256 : start + 512, :]], axis=1
    )


def plane_sums(me_ref, back_ref, mixed_ref, res_ref, out_refs):
    count = res_ref.shape[0] // 16
    for quarter in range(4):
        wide = jnp.concatenate([mixed_ref[quarter * 4 + k] for k in range(4)], axis=1)
        rows = dot_nn(back_ref[...], wide)
        for k in range(4):
            res_ref[pl.ds(quarter * 4 + k, count, stride=16), :] = rows[:, k * 128 : (k + 1) * 128]
    store_blocks(me_ref, res_ref, out_refs)


def mode_kernel(scale, devices, *refs):
    me_ref, block_refs, refs = refs[0], refs[1 : 1 + devices], refs[1 + devices :]
    weight_hbm, both_ref, plain_ref, back_ref, coeff_ref = refs[:5]
    out_refs, (weight_ref, rows_ref, left_ref, mixed_ref, sems) = refs[5:-5], refs[-5:]
    copies = start_weights(weight_hbm, weight_ref, sems)
    count = rows_ref.shape[0] // 16
    load_blocks(me_ref, block_refs, rows_ref)
    low = lanes((128, 128)) < 64
    kxl = sublanes((128, 128)) % 4
    half = lanes((128, 128)) // 64
    first = (kxl == half).astype(BF16)
    second = (kxl == 2 + half).astype(BF16)
    low8 = lanes((8, 128)) < 64
    sign = jnp.where(sublanes((8, 128)) < 4, -1.0, 1.0)
    for quarter in range(4):
        wide = jnp.concatenate(
            [rows_ref[pl.ds(quarter * 4 + k, count, stride=16), :] for k in range(4)], axis=1
        ).astype(BF16)
        plain = (dot_nn(plain_ref[...], wide) * scale).astype(BF16)
        both = dot_nn(both_ref[...], wide) * scale
        for k in range(4):
            j = quarter * 4 + k
            coeff_ref[j] = plain[:, k * 128 : (k + 1) * 128]
            coeffs = both[:, k * 128 : (k + 1) * 128]
            swapped = swap_halves(coeffs)
            for h in range(2):
                twice = jnp.where(low if h == 0 else ~low, coeffs, swapped).astype(BF16)
                left_ref[j, h] = jnp.concatenate([twice * first, twice * second], axis=1)
    for j in range(16):
        if j % 4 == 0:
            for copy in copies[j : j + 4]:
                copy.wait()
        mixed = []
        for u in range(MX // 8):
            halves = [
                dot_nn(left_ref[j, h, u * 32 : (u + 1) * 32, :], mode_pair(weight_ref, j, h, u))
                for h in range(2)
            ]
            for t in range(2):
                low_h, high_h = [
                    part[t * 16 : (t + 1) * 16, t * 128 : (t + 1) * 128] for part in halves
                ]
                keep = jnp.where(low8, low_h[:8], sign * high_h[8:])
                move = jnp.where(low8, high_h[:8], sign * low_h[8:])
                mixed.append(keep + swap_halves(move))
        mixed_ref[j] = jnp.concatenate(mixed, axis=0).astype(BF16)
    plane_sums(me_ref, back_ref, mixed_ref, rows_ref, out_refs)


def mode_grad_kernel(scale, devices, *refs):
    me_ref, block_refs, refs = refs[0], refs[1 : 1 + devices], refs[1 + devices :]
    weight_hbm, straight_ref, back_ref, pair_ref = refs[:4]
    out_refs, (weight_ref, rows_ref, mixed_ref, sems) = refs[4:-4], refs[-4:]
    copies = start_weights(weight_hbm, weight_ref, sems)
    count = rows_ref.shape[0] // 16
    load_blocks(me_ref, block_refs, rows_ref)
    low = lanes((64, 128)) < 64
    low16 = lanes((16, 128)) < 64
    row = sublanes((16, 128)) % 4
    upper = row < 2
    valid = lanes((16, 128)) // 64 == row % 2
    even = (sublanes((16, 128)) < 8).astype(BF16)
    odd = (sublanes((16, 128)) >= 8).astype(BF16)
    for j in range(16):
        section = rows_ref[pl.ds(j, count, stride=16), :]
        swapped = swap_halves(section)
        twice = jnp.concatenate(
            [jnp.where(low, section, swapped), jnp.where(low, swapped, section)], axis=1
        ).astype(BF16)
        turned = dot_nn(straight_ref[...], twice)
        for h in range(2):
            part = turned[:, h * 128 : (h + 1) * 128]
            pair_ref[2 * j + h] = jnp.where(low, part[:64], part[64:]).astype(BF16)
    for j in range(16):
        if j % 4 == 0:
            for copy in copies[j : j + 4]:
                copy.wait()
        mixed = []
        for u in range(MX // 8):
            found = []
            for h in range(2):
                pair = pair_ref[2 * j + h, u * 16 : (u + 1) * 16, :]
                rows = dot_nt(
                    jnp.concatenate([pair * even, pair * odd], axis=1),
                    mode_pair(weight_ref, j, h, u),
                )
                found.append(jnp.where(valid, jnp.where(upper, rows[:, :128], rows[:, 128:]), 0.0))
            keep = jnp.where(low16, found[0], found[1])
            move = jnp.where(low16, found[1], found[0])
            mixed.append(keep + swap_halves(move))
        mixed_ref[j] = (jnp.concatenate(mixed, axis=0) * scale).astype(BF16)
    plane_sums(me_ref, back_ref, mixed_ref, rows_ref, out_refs)


def weight_grad_kernel(per_step, scale, coeff_ref, pair_ref, out_ref, mask_ref):
    @pl.when(pl.program_id(0) == 0)
    def _():
        lane = lanes((128, 64))
        part = sublanes((128, 64)) // 64
        for t in range(MX // 4):
            mask_ref[t] = ((lane // 8 == t) & (lane % 4 // 2 == part)).astype(BF16)

    eye = (sublanes((128, 128)) == lanes((128, 128))).astype(BF16)
    even = (sublanes((64, 128)) % 2 == 0).astype(BF16)
    odd = (sublanes((64, 128)) % 2 == 1).astype(BF16)
    for jj in range(per_step):
        turned = (dot_nt(eye, coeff_ref[jj]) * scale).astype(BF16)
        for h in range(2):
            left = turned[h * 64 : (h + 1) * 64]
            left = jnp.concatenate([left, left], axis=0)
            pair = pair_ref[jj * 2 + h]
            right = jnp.concatenate([pair * even, pair * odd], axis=1)
            for t in range(MX // 4):
                four = dot_nn(left * mask_ref[t], right).astype(BF16)
                mode = (jj * 2 + h) * MX + 4 * t
                for k in range(4):
                    out_ref[mode + k] = four[
                        k // 2 * 64 : (k // 2 + 1) * 64, k % 2 * 128 : (k % 2 + 1) * 128
                    ]


def whole(array):
    rank = len(array.shape)
    return pl.BlockSpec(array.shape, lambda *_: (0,) * rank)


def params(mib):
    return pltpu.CompilerParams(vmem_limit_bytes=mib * 1024 * 1024)


def cost(flops, moved):
    return pl.CostEstimate(flops=int(flops), bytes_accessed=int(moved), transcendentals=0)


def fast_body(features, cotangent, spectral_weight, channel_weight, channel_bias):
    channels, planes, lines, depth_len = features.shape
    devices = lax.axis_size("gx")
    owned_modes = spectral_weight.shape[0]
    wave_pairs = MY * MZ
    volume = planes * devices * lines * depth_len
    forward_scale = 1.0 / math.sqrt(volume)
    inverse_scale = 1.0 / math.sqrt(MX * wave_pairs)
    weight_scale = math.sqrt(MX * wave_pairs / volume)
    table = {name: jnp.asarray(value) for name, value in tables(devices, lines, depth_len).items()}
    per_step = 2
    steps = channels // (GROUP * per_step)
    step_channels = GROUP * per_step
    block_rows = devices * 64
    one_block = jax.ShapeDtypeStruct((64, 128), BF16)
    block_shape = [one_block] * devices
    block_spec = [whole(one_block)] * devices
    me = lax.axis_index("gx").astype(jnp.int32).reshape(1)
    smem = pl.BlockSpec(memory_space=pltpu.SMEM)
    field_spec = pl.BlockSpec(
        (step_channels, planes, lines, depth_len), lambda i: (i, 0, 0, 0)
    )
    lines_scratch = pltpu.VMEM((MZ, channels, 2 * planes * lines), F32)
    rows_scratch = pltpu.VMEM((block_rows, 128), F32)
    spec_scratch = pltpu.VMEM((channels // GROUP, MZ * GROUP, 128), F32)
    weight_rows = spectral_weight.reshape(owned_modes * channels, 2 * channels)
    field_bytes = features.size * 2

    def exchange(blocks):
        return list(blocks[:1]) + [
            lax.ppermute(blocks[r], "gx", [(i, i ^ r) for i in range(devices)])
            for r in range(1, devices)
        ]

    def point(field, transposed):
        rows = 16
        return pl.pallas_call(
            functools.partial(point_kernel, transposed),
            out_shape=jax.ShapeDtypeStruct(field.shape, F32),
            grid=(planes, channels // rows),
            in_specs=[
                pl.BlockSpec((channels, channels), lambda x, o: (0, 0)),
                pl.BlockSpec((channels, 1, lines, depth_len), lambda x, o: (0, x, 0, 0)),
            ],
            out_specs=pl.BlockSpec((rows, 1, lines, depth_len), lambda x, o: (o, x, 0, 0)),
            scratch_shapes=[pltpu.VMEM((channels * 16, channels * 16), BF16)],
            compiler_params=params(VMEM_MIB),
            cost_estimate=cost(2 * 1024**3, 3 * field_bytes),
            name="channel_map_back" if transposed else "channel_map",
        )(channel_weight, field)

    block = pl.pallas_call(
        functools.partial(analysis_kernel, per_step),
        out_shape=block_shape,
        grid=(steps,),
        in_specs=[smem, field_spec, whole(table["depth"]), whole(table["across_y"])],
        out_specs=block_spec,
        scratch_shapes=[lines_scratch, rows_scratch],
        compiler_params=params(VMEM_MIB),
        cost_estimate=cost(2 * 256 * 1024 * 1024, field_bytes),
        name="field_analysis",
    )(me, features, table["depth"], table["across_y"])
    block = exchange(block)
    pointwise = point(features, False)

    vmem = pl.BlockSpec(memory_space=pltpu.VMEM)
    hbm = pl.BlockSpec(memory_space=pl.ANY)
    weight_scratch = pltpu.VMEM(weight_rows.shape, BF16)
    mixed_scratch = pltpu.VMEM((16, 64, 128), BF16)
    weight_sems = pltpu.SemaphoreType.DMA((16,))
    coeffs, *block = pl.pallas_call(
        functools.partial(mode_kernel, forward_scale, devices),
        out_shape=[jax.ShapeDtypeStruct((16, 64, 128), BF16), *block_shape],
        in_specs=[smem] + [vmem] * devices + [hbm, vmem, vmem, vmem],
        out_specs=[vmem] * (1 + devices),
        scratch_shapes=[
            weight_scratch,
            rows_scratch,
            pltpu.VMEM((16, 2, 128, 256), BF16),
            mixed_scratch,
            weight_sems,
        ],
        compiler_params=params(VMEM_MIB),
        cost_estimate=cost(256 * 2 * 16 * 256 * 128, 17 * 2**20),
        name="mode_product",
    )(me, *block, weight_rows, table["both_x"], table["plain_x"], table["back_x"])
    block = exchange(block)

    activated, upstream, *block = pl.pallas_call(
        functools.partial(middle_kernel, per_step, inverse_scale, devices),
        out_shape=[
            jax.ShapeDtypeStruct(features.shape, BF16),
            jax.ShapeDtypeStruct(features.shape, BF16),
            *block_shape,
        ],
        grid=(steps,),
        in_specs=[
            smem,
            *block_spec,
            field_spec,
            field_spec,
            pl.BlockSpec(memory_space=pltpu.SMEM),
            whole(table["depth"]),
            whole(table["across_y"]),
            whole(table["back_y"]),
        ],
        out_specs=[field_spec, field_spec, *block_spec],
        scratch_shapes=[lines_scratch, rows_scratch, spec_scratch],
        compiler_params=params(VMEM_MIB),
        cost_estimate=cost(2**30, 5 * field_bytes),
        name="gelu_and_gradient",
    )(
        me,
        *block,
        pointwise,
        cotangent,
        channel_bias,
        table["depth"],
        table["across_y"],
        table["back_y"],
    )
    block = exchange(block)
    block, channel_back = lax.optimization_barrier((block, point(upstream, True)))

    pairs, *block = pl.pallas_call(
        functools.partial(mode_grad_kernel, forward_scale, devices),
        out_shape=[jax.ShapeDtypeStruct((32, 64, 128), BF16), *block_shape],
        in_specs=[smem] + [vmem] * devices + [hbm, vmem, vmem],
        out_specs=[vmem] * (1 + devices),
        scratch_shapes=[weight_scratch, rows_scratch, mixed_scratch, weight_sems],
        compiler_params=params(VMEM_MIB),
        cost_estimate=cost(256 * 2 * 16 * 256 * 128, 17 * 2**20),
        name="mode_gradient",
    )(me, *block, weight_rows, table["straight_x"], table["back_x"])
    block = exchange(block)

    mode_steps = 8
    per_mode_step = 16 // mode_steps
    spectral_grad = pl.pallas_call(
        functools.partial(weight_grad_kernel, per_mode_step, weight_scale),
        out_shape=jax.ShapeDtypeStruct(spectral_weight.shape, BF16),
        grid=(mode_steps,),
        in_specs=[
            pl.BlockSpec((per_mode_step, 64, 128), lambda i: (i, 0, 0)),
            pl.BlockSpec((2 * per_mode_step, 64, 128), lambda i: (i, 0, 0)),
        ],
        out_specs=pl.BlockSpec(
            (owned_modes // mode_steps, channels, 2 * channels), lambda i: (i, 0, 0)
        ),
        scratch_shapes=[pltpu.VMEM((MX // 4, 128, 64), BF16)],
        compiler_params=params(VMEM_MIB),
        cost_estimate=cost(512 * 2 * 64 * 64 * 256, 17 * 2**20),
        name="weight_gradient",
    )(coeffs, pairs)

    feature_grad = pl.pallas_call(
        functools.partial(final_kernel, per_step, devices),
        out_shape=jax.ShapeDtypeStruct(features.shape, BF16),
        grid=(steps,),
        in_specs=[
            smem,
            *block_spec,
            field_spec,
            whole(table["depth"]),
            whole(table["back_y"]),
        ],
        out_specs=field_spec,
        scratch_shapes=[rows_scratch, spec_scratch],
        compiler_params=params(VMEM_MIB),
        cost_estimate=cost(2**29, 3 * field_bytes),
        name="field_gradient",
    )(me, *block, channel_back, table["depth"], table["back_y"])
    return (activated, feature_grad, spectral_grad)


def body(features, cotangent, spectral_weight, channel_weight, channel_bias):
    channels, planes, lines, depth_len = features.shape
    devices = lax.axis_size("gx")
    fits = (
        (channels, planes, lines, depth_len) == (64, PLANES, 64, 128)
        and spectral_weight.shape[0] == 2 * MZ * MX
        and devices * 2 == MY
        and devices * 2 == MX
    )
    run = fast_body if fits else general_body
    return run(features, cotangent, spectral_weight, channel_weight, channel_bias)


def solution(mesh):
    in_specs = (
        P("grp", "gx", None, None),
        P("grp", "gx", None, None),
        P("gx", None, None),
        P(),
        P(),
    )
    out_specs = (
        P("grp", "gx", None, None),
        P("grp", "gx", None, None),
        P(("grp", "gx"), None, None),
    )
    return jax.shard_map(body, mesh=mesh, in_specs=in_specs, out_specs=out_specs, check_vma=False)
```

```python
import functools
import math

import jax
import jax.numpy as jnp
import ml_dtypes
import numpy as np
from jax import lax
from jax.experimental import pallas as pl
from jax.experimental.pallas import tpu as pltpu
from jax.sharding import PartitionSpec as P

MX = 32
MY = 32
MZ = 16


SQRT_TWO_PI = math.sqrt(2.0 / math.pi)
CUBIC_COEF = 0.044715


def freq_index(retained, length):
    ladder = jnp.arange(retained, dtype=jnp.int32)
    return jnp.where(ladder < retained // 2, ladder, length - retained + ladder)


def cos_sin(wavenum, length):
    points = jnp.arange(length, dtype=jnp.int32)
    angles = (wavenum[:, None] * points[None, :] % length).astype(jnp.float32) * (
        2.0 * math.pi / length
    )
    return (jnp.cos(angles), jnp.sin(angles))


def analysis_pair(wavenum, length):
    cosine, sine_wave = cos_sin(wavenum, length)
    cosine, sine_wave = (cosine.T, sine_wave.T)
    return jnp.stack(
        [jnp.stack([cosine, -sine_wave], 1), jnp.stack([sine_wave, cosine], 1)], 1
    ).astype(jnp.bfloat16)


def synthesis_pair(wavenum, length):
    cosine, sine_wave = cos_sin(wavenum, length)
    return jnp.stack(
        [jnp.stack([cosine, sine_wave], 1), jnp.stack([-sine_wave, cosine], 1)], 1
    ).astype(jnp.bfloat16)


def depth_table(retained, length):
    cosine, sine_wave = cos_sin(jnp.arange(retained, dtype=jnp.int32), length)
    return jnp.concatenate([cosine, -sine_wave], 0).astype(jnp.bfloat16)


def gelu_parts(inputs):
    cubed_in = inputs * inputs * inputs
    tangent = jnp.tanh(SQRT_TWO_PI * (inputs + CUBIC_COEF * cubed_in))
    output = 0.5 * inputs * (1.0 + tangent)
    derivative = 0.5 * (1.0 + tangent) + 0.5 * inputs * (1.0 - tangent * tangent) * SQRT_TWO_PI * (
        1.0 + 3.0 * CUBIC_COEF * inputs * inputs
    )
    return (output, derivative)


def mode_product(coeffs, weights, channels):
    stacked = coeffs.reshape(coeffs.shape[0], 2, channels)
    halves = jnp.einsum("mac,mcj->amj", stacked, weights, preferred_element_type=jnp.float32)
    real_out = halves[0, :, :channels] - halves[1, :, channels:]
    imag_out = halves[0, :, channels:] + halves[1, :, :channels]
    return jnp.concatenate([real_out, imag_out], 1).astype(jnp.bfloat16)


def mode_grads(coeffs, weights, grad_modes, channels, weight_scale, input_scale):
    number = coeffs.shape[0]
    stacked = coeffs.reshape(number, 2, channels)
    grad_pairs = grad_modes.reshape(number, 2, channels)
    real_w = jnp.einsum("mac,mao->mco", stacked, grad_pairs, preferred_element_type=jnp.float32)
    imag_w = jnp.einsum(
        "mc,mo->mco", stacked[:, 0], grad_pairs[:, 1], preferred_element_type=jnp.float32
    ) - jnp.einsum(
        "mc,mo->mco", stacked[:, 1], grad_pairs[:, 0], preferred_element_type=jnp.float32
    )
    weight_grad = (jnp.concatenate([real_w, imag_w], 2) * weight_scale).astype(jnp.bfloat16)
    straight = jnp.concatenate([grad_pairs[:, 0], grad_pairs[:, 1]], 1)
    rotated = jnp.concatenate([grad_pairs[:, 1], -grad_pairs[:, 0]], 1)
    real_x = jnp.einsum("mcj,mj->mc", weights, straight, preferred_element_type=jnp.float32)
    imag_x = jnp.einsum("mcj,mj->mc", weights, rotated, preferred_element_type=jnp.float32)
    input_grad = (jnp.concatenate([real_x, imag_x], 1) * input_scale).astype(jnp.bfloat16)
    return (weight_grad, input_grad)


def general_body(features, cotangent, spectral_weight, channel_weight, channel_bias):
    channels, planes, lines, depth_len = features.shape
    devices = lax.axis_size("gx")
    all_planes = planes * devices
    owned_modes = spectral_weight.shape[0]
    wave_pairs = MY * MZ
    forward_scale = 1.0 / math.sqrt(all_planes * lines * depth_len)
    inverse_scale = 1.0 / math.sqrt(MX * wave_pairs)
    weight_scale = math.sqrt(MX * wave_pairs / (all_planes * lines * depth_len))
    depth_basis = depth_table(MZ, depth_len)
    across_y = analysis_pair(freq_index(MY, lines), lines)
    back_y = synthesis_pair(freq_index(MY, lines), lines)
    across_full = analysis_pair(freq_index(MX, all_planes), all_planes)
    back_full = synthesis_pair(freq_index(MX, all_planes), all_planes)
    depth_part = jnp.dot(features, depth_basis.T, preferred_element_type=jnp.float32).astype(
        jnp.bfloat16
    )
    plane_part = (
        jnp.einsum(
            "cxyaz,yabk->cxbkz",
            depth_part.reshape(channels, planes, lines, 2, MZ),
            across_y,
            preferred_element_type=jnp.float32,
        )
        .astype(jnp.bfloat16)
        .reshape(channels, planes, 2, wave_pairs)
    )
    all_rows = lax.all_to_all(plane_part, "gx", split_axis=3, concat_axis=1, tiled=True)
    mode_sums = jnp.einsum(
        "cxaq,xabk->qkbc", all_rows, across_full, preferred_element_type=jnp.float32
    ).reshape(owned_modes, 2 * channels)
    coeffs = (mode_sums * forward_scale).astype(jnp.bfloat16)
    spectral = mode_product(coeffs, spectral_weight, channels)
    planes_all = jnp.einsum(
        "qkao,kabx->oxbq",
        spectral.reshape(owned_modes // MX, MX, 2, channels),
        back_full,
        preferred_element_type=jnp.float32,
    ).astype(jnp.bfloat16)
    planes_back = lax.all_to_all(planes_all, "gx", split_axis=1, concat_axis=3, tiled=True)
    lines_back = (
        jnp.einsum(
            "oxakz,kaby->oxybz",
            planes_back.reshape(channels, planes, 2, MY, MZ),
            back_y,
            preferred_element_type=jnp.float32,
        )
        .astype(jnp.bfloat16)
        .reshape(channels, planes, lines, 2 * MZ)
    )
    spectral_term = (
        jnp.dot(lines_back, depth_basis, preferred_element_type=jnp.float32) * inverse_scale
    )
    pointwise = jnp.einsum(
        "oc,cxyz->oxyz", channel_weight, features, preferred_element_type=jnp.float32
    )
    hidden = spectral_term + pointwise + channel_bias[:, None, None, None]
    activated, derivative = gelu_parts(hidden)
    upstream = (cotangent.astype(jnp.float32) * derivative).astype(jnp.bfloat16)
    lines_grad = (
        jnp.dot(upstream, depth_basis.T, preferred_element_type=jnp.float32) * inverse_scale
    ).astype(jnp.bfloat16)
    rows_grad = (
        jnp.einsum(
            "oxybz,kaby->oxakz",
            lines_grad.reshape(channels, planes, lines, 2, MZ),
            back_y,
            preferred_element_type=jnp.float32,
        )
        .astype(jnp.bfloat16)
        .reshape(channels, planes, 2, wave_pairs)
    )
    all_grads = lax.all_to_all(rows_grad, "gx", split_axis=3, concat_axis=1, tiled=True)
    grad_sums = jnp.einsum(
        "oxbq,kabx->qkao", all_grads, back_full, preferred_element_type=jnp.float32
    ).reshape(owned_modes, 2 * channels)
    grad_modes = grad_sums.astype(jnp.bfloat16)
    spectral_grad, coeff_grad = mode_grads(
        coeffs, spectral_weight, grad_modes, channels, weight_scale, forward_scale
    )
    plane_all = jnp.einsum(
        "qkbc,xabk->cxaq",
        coeff_grad.reshape(owned_modes // MX, MX, 2, channels),
        across_full,
        preferred_element_type=jnp.float32,
    ).astype(jnp.bfloat16)
    plane_grad = lax.all_to_all(plane_all, "gx", split_axis=1, concat_axis=3, tiled=True)
    depth_grad = (
        jnp.einsum(
            "cxbkz,yabk->cxyaz",
            plane_grad.reshape(channels, planes, 2, MY, MZ),
            across_y,
            preferred_element_type=jnp.float32,
        )
        .astype(jnp.bfloat16)
        .reshape(channels, planes, lines, 2 * MZ)
    )
    channel_back = jnp.einsum(
        "oc,oxyz->cxyz", channel_weight, upstream, preferred_element_type=jnp.float32
    )
    feature_grad = (
        jnp.dot(depth_grad, depth_basis, preferred_element_type=jnp.float32) + channel_back
    ).astype(jnp.bfloat16)
    return (activated.astype(jnp.bfloat16), feature_grad, spectral_grad)


PLANES = 2
GROUP = 8
STEP = 16
VMEM_MIB = 40
NT = (((1,), (1,)), ((), ()))
F32 = jnp.float32
BF16 = jnp.bfloat16


def np_freq(retained, length):
    ladder = np.arange(retained)
    return np.where(ladder < retained // 2, ladder, length - retained + ladder)


def np_angles(wavenum, length):
    points = np.arange(length)
    return (wavenum[:, None] * points[None, :] % length) * (2.0 * math.pi / length)


def as_bf16(table):
    return np.asarray(table, np.float32).astype(ml_dtypes.bfloat16)


def rotation(angle, sign):
    cosine, sine_wave = np.cos(angle), sign * np.sin(angle)
    return np.stack([np.stack([cosine, -sine_wave]), np.stack([sine_wave, cosine])])


@functools.lru_cache(maxsize=None)
def tables(devices, lines, depth_len):
    planes_all = devices * PLANES
    angle = np_angles(np.arange(MZ), depth_len)
    depth = np.stack([np.cos(angle), -np.sin(angle)])
    eye = np.eye(GROUP)
    depth_block = np.einsum("akz,ij->akijz", depth, eye).reshape(2 * MZ * GROUP, GROUP * depth_len)
    plane_eye = np.eye(PLANES)
    angle = np_angles(np_freq(MY, lines), lines).reshape(devices, MY // devices, lines)
    across = np.einsum("badly,xw->ldbxawy", rotation(angle, -1.0), plane_eye)
    across = across.reshape(MY * 2 * PLANES, 2 * PLANES * lines)
    back = np.einsum("pbdly,xw->pxyldbw", rotation(angle, 1.0), plane_eye)
    back = back.reshape(2 * PLANES * lines, MY * 2 * PLANES)
    angle = np_angles(np_freq(MX, planes_all), planes_all).reshape(MX // 4, 4, devices, PLANES)
    forward = rotation(angle, -1.0)
    rows = np.einsum("batksx->tbksax", forward).reshape(MX // 4, 2, 4, devices * 2 * PLANES)
    plain = rows.reshape(2 * MX, -1)
    both = np.stack([rows, rows[:, ::-1]], 1).reshape(4 * MX, -1)
    turned = np.concatenate([rows[:, 1:], -rows[:, :1]], 1).reshape(2 * MX, -1)
    straight_rotated = np.concatenate([plain, turned], 0)
    inverse = np.einsum("batksx->sbxtak", rotation(angle, 1.0)).reshape(-1, 2 * MX)
    return {
        "depth": as_bf16(depth_block),
        "across_y": as_bf16(across),
        "back_y": as_bf16(back),
        "plain_x": as_bf16(plain),
        "both_x": as_bf16(both),
        "straight_x": as_bf16(straight_rotated),
        "back_x": as_bf16(inverse),
    }


def dot_nn(left, right):
    return jnp.dot(left, right, preferred_element_type=F32)


def dot_nt(left, right):
    return lax.dot_general(left, right, NT, preferred_element_type=F32)


def lanes(shape):
    return lax.broadcasted_iota(jnp.int32, shape, len(shape) - 1)


def sublanes(shape):
    return lax.broadcasted_iota(jnp.int32, shape, len(shape) - 2)


def swap_halves(block):
    return pltpu.roll(block, 64, 1)


def part_copy(source, target, sems, index, size):
    part = pl.ds(pl.multiple_of(index * size, size), size)
    return pltpu.make_async_copy(source.at[part], target.at[part], sems.at[index])


def start_parts(source, target, sems, size):
    for index in range(source.shape[0] // size):
        part_copy(source, target, sems, index, size).start()


def start_tables(pairs, sems):
    copies = []
    for index, (source, target) in enumerate(pairs):
        copy = pltpu.make_async_copy(source, target, sems.at[index])
        copy.start()
        copies.append(copy)
    return copies


def depth_analysis(slabs, depth, scale, group, lines_ref):
    wide = jnp.concatenate(slabs, axis=1)
    parts = dot_nt(depth, wide)
    if scale is not None:
        parts = parts * scale
    width = wide.shape[0]
    start = pl.multiple_of(group * GROUP, GROUP)
    for a in range(2):
        lines_ref[:, pl.ds(start, GROUP), a * width : (a + 1) * width] = parts[
            a * MZ * GROUP : (a + 1) * MZ * GROUP
        ].reshape(MZ, GROUP, width)


def rows_analysis(lines_ref, across_ref, rows_ref, out_ref):
    channels, width = lines_ref.shape[1], lines_ref.shape[2]
    across = across_ref[...]
    half = across.shape[0] // 2
    for kzh in range(MZ // 2):
        pair = lines_ref[2 * kzh : 2 * kzh + 2].reshape(2 * channels, width).astype(BF16)
        rows = dot_nt(across, pair)
        for kyl in range(2):
            rows_ref[pl.ds(kyl * 8 + kzh, half, stride=16), :] = rows[
                kyl * half : (kyl + 1) * half
            ]
    out_ref[...] = rows_ref[...].astype(BF16)


def rows_gather(block_ref, rows_ref, spec_ref):
    rows_ref[...] = block_ref[...].astype(F32)
    count = rows_ref.shape[0] // 16
    eye = (sublanes((128, 128)) == lanes((128, 128))).astype(BF16)
    for kzh in range(MZ // 2):
        both = jnp.concatenate(
            [rows_ref[pl.ds(kyl * 8 + kzh, count, stride=16), :] for kyl in range(2)], axis=0
        ).astype(BF16)
        turned = dot_nt(eye, both)
        for h in range(2):
            spec_ref[:, (2 * kzh + h) * GROUP : (2 * kzh + h + 1) * GROUP, :] = turned[
                h * 64 : (h + 1) * 64
            ].reshape(8, GROUP, turned.shape[1])


def synthesis(groups, spec_ref, back, depth, scale):
    wide = []
    for group in groups:
        lines = dot_nt(back, spec_ref[group].astype(BF16))
        if scale is not None:
            lines = lines * scale
        lines = lines.astype(BF16)
        half = lines.shape[0] // 2
        wide.append(jnp.concatenate([lines[:half], lines[half:]], axis=1))
    return dot_nn(jnp.concatenate(wide, axis=0), depth)


def flat(slab):
    return slab.reshape(slab.shape[0] * slab.shape[1], slab.shape[2])


def analysis_kernel(
    field_hbm,
    depth_hbm,
    across_hbm,
    out_ref,
    field_ref,
    depth_ref,
    across_ref,
    lines_ref,
    rows_ref,
    field_sems,
    table_sems,
):
    first, second = start_tables([(depth_hbm, depth_ref), (across_hbm, across_ref)], table_sems)
    start_parts(field_hbm, field_ref, field_sems, STEP)
    first.wait()

    @pl.loop(0, field_ref.shape[0] // STEP)
    def _(step):
        part_copy(field_hbm, field_ref, field_sems, step, STEP).wait()
        for g in range(STEP // GROUP):
            group = step * (STEP // GROUP) + g
            slabs = [flat(field_ref[group * GROUP + ci]) for ci in range(GROUP)]
            depth_analysis(slabs, depth_ref[...], None, group, lines_ref)

    second.wait()
    rows_analysis(lines_ref, across_ref, rows_ref, out_ref)


def middle_kernel(
    inverse_scale,
    block_ref,
    bias_ref,
    point_hbm,
    cot_hbm,
    depth_hbm,
    across_hbm,
    back_hbm,
    act_hbm,
    up_hbm,
    out_ref,
    point_ref,
    cot_ref,
    depth_ref,
    across_ref,
    back_ref,
    act_ref,
    up_ref,
    lines_ref,
    rows_ref,
    spec_ref,
    point_sems,
    cot_sems,
    act_sems,
    up_sems,
    table_sems,
):
    tables_in = start_tables(
        [(back_hbm, back_ref), (depth_hbm, depth_ref), (across_hbm, across_ref)], table_sems
    )
    start_parts(point_hbm, point_ref, point_sems, STEP)
    start_parts(cot_hbm, cot_ref, cot_sems, STEP)
    rows_gather(block_ref, rows_ref, spec_ref)
    for copy in tables_in:
        copy.wait()
    steps = point_ref.shape[0] // STEP

    @pl.loop(0, steps)
    def _(step):
        groups = [step * (STEP // GROUP) + g for g in range(STEP // GROUP)]
        spectral = synthesis(groups, spec_ref, back_ref[...], depth_ref[...], inverse_scale)
        part_copy(point_hbm, point_ref, point_sems, step, STEP).wait()
        part_copy(cot_hbm, cot_ref, cot_sems, step, STEP).wait()
        for g, group in enumerate(groups):
            slabs = []
            for oi in range(GROUP):
                index = group * GROUP + oi
                hidden = (
                    spectral[g * 128 : (g + 1) * 128, oi * 128 : (oi + 1) * 128]
                    + flat(point_ref[index]).astype(F32)
                    + bias_ref[index]
                )
                square = hidden * hidden
                gate = 0.5 + 0.5 * jnp.tanh(
                    hidden * (SQRT_TWO_PI + (SQRT_TWO_PI * CUBIC_COEF) * square)
                )
                slope = hidden * (2.0 * SQRT_TWO_PI + (6.0 * SQRT_TWO_PI * CUBIC_COEF) * square)
                derivative = gate + (gate - gate * gate) * slope
                upstream = (flat(cot_ref[index]).astype(F32) * derivative).astype(BF16)
                act_ref[index] = (hidden * gate).astype(BF16).reshape(act_ref.shape[1:])
                up_ref[index] = upstream.reshape(up_ref.shape[1:])
                slabs.append(upstream)
            depth_analysis(slabs, depth_ref[...], inverse_scale, group, lines_ref)
        part_copy(act_ref, act_hbm, act_sems, step, STEP).start()
        part_copy(up_ref, up_hbm, up_sems, step, STEP).start()

    rows_analysis(lines_ref, across_ref, rows_ref, out_ref)
    for step in range(steps):
        part_copy(act_ref, act_hbm, act_sems, step, STEP).wait()
        part_copy(up_ref, up_hbm, up_sems, step, STEP).wait()


def final_kernel(
    block_ref,
    point_hbm,
    depth_hbm,
    back_hbm,
    out_hbm,
    point_ref,
    depth_ref,
    back_ref,
    out_ref,
    rows_ref,
    spec_ref,
    point_sems,
    out_sems,
    table_sems,
):
    tables_in = start_tables([(back_hbm, back_ref), (depth_hbm, depth_ref)], table_sems)
    start_parts(point_hbm, point_ref, point_sems, STEP)
    rows_gather(block_ref, rows_ref, spec_ref)
    for copy in tables_in:
        copy.wait()
    steps = point_ref.shape[0] // STEP

    @pl.loop(0, steps)
    def _(step):
        groups = [step * (STEP // GROUP) + g for g in range(STEP // GROUP)]
        spectral = synthesis(groups, spec_ref, back_ref[...], depth_ref[...], None)
        part_copy(point_hbm, point_ref, point_sems, step, STEP).wait()
        for g, group in enumerate(groups):
            for ci in range(GROUP):
                index = group * GROUP + ci
                total = spectral[
                    g * 128 : (g + 1) * 128, ci * 128 : (ci + 1) * 128
                ] + flat(point_ref[index]).astype(F32)
                out_ref[index] = total.astype(BF16).reshape(out_ref.shape[1:])
        part_copy(out_ref, out_hbm, out_sems, step, STEP).start()

    for step in range(steps):
        part_copy(out_ref, out_hbm, out_sems, step, STEP).wait()


def point_kernel(
    transposed, weight_ref, field_hbm, out_hbm, field_ref, out_ref, wide_ref, in_sems, out_sems
):
    size = wide_ref.shape[0]
    planes = field_ref.shape[1]
    copies = []
    for plane in range(planes):
        part = (slice(None), pl.ds(plane, 1))
        copy = pltpu.make_async_copy(field_hbm.at[part], field_ref.at[part], in_sems.at[plane])
        copy.start()
        copies.append(copy)
    tall = (sublanes((size, 64)) // 16 == lanes((size, 64))).astype(BF16)
    weight = weight_ref[...]
    left = dot_nt(tall, weight) if transposed else dot_nn(tall, weight)
    left = left.astype(BF16)
    rows = size // 4
    same = sublanes((rows, size)) % 16 == lanes((rows, size)) % 16
    for quarter in range(4):
        spread = dot_nt(left[quarter * rows : (quarter + 1) * rows], tall)
        wide_ref[quarter * rows : (quarter + 1) * rows, :] = jnp.where(same, spread, 0.0).astype(
            BF16
        )
    sends = []
    for plane in range(planes):
        copies[plane].wait()
        for pair in range(2):
            right = jnp.concatenate(
                [
                    field_ref[:, plane, yc * 16 : (yc + 1) * 16, :].reshape(size, 128)
                    for yc in (2 * pair, 2 * pair + 1)
                ],
                axis=1,
            )
            result = dot_nn(wide_ref[...], right).astype(BF16)
            for k in range(2):
                yc = 2 * pair + k
                out_ref[:, plane, yc * 16 : (yc + 1) * 16, :] = result[
                    :, k * 128 : (k + 1) * 128
                ].reshape(size // 16, 16, 128)
        part = (slice(None), pl.ds(plane, 1))
        copy = pltpu.make_async_copy(out_ref.at[part], out_hbm.at[part], out_sems.at[plane])
        copy.start()
        sends.append(copy)
    for copy in sends:
        copy.wait()


def start_weights(weight_hbm, weight_ref, sems):
    copies = []
    for j in range(16):
        rows = weight_ref.shape[0] // 16
        part = pl.ds(j * rows, rows)
        copy = pltpu.make_async_copy(weight_hbm.at[part], weight_ref.at[part], sems.at[j])
        copy.start()
        copies.append(copy)
    return copies


def mode_pair(weight_ref, j, h, u):
    start = ((j * 2 + h) * MX + 8 * u) * 64
    return jnp.concatenate(
        [weight_ref[start : start + 256, :], weight_ref[start + 256 : start + 512, :]], axis=1
    )


def plane_sums(back_ref, mixed_ref, res_ref, out_ref):
    count = res_ref.shape[0] // 16
    for quarter in range(4):
        wide = jnp.concatenate([mixed_ref[quarter * 4 + k] for k in range(4)], axis=1)
        rows = dot_nn(back_ref[...], wide)
        for k in range(4):
            res_ref[pl.ds(quarter * 4 + k, count, stride=16), :] = rows[:, k * 128 : (k + 1) * 128]
    out_ref[...] = res_ref[...].astype(BF16)


def mode_kernel(
    scale,
    block_ref,
    weight_hbm,
    both_ref,
    plain_ref,
    back_ref,
    coeff_ref,
    out_ref,
    weight_ref,
    rows_ref,
    left_ref,
    mixed_ref,
    sems,
):
    copies = start_weights(weight_hbm, weight_ref, sems)
    count = rows_ref.shape[0] // 16
    rows_ref[...] = block_ref[...].astype(F32)
    low = lanes((128, 128)) < 64
    kxl = sublanes((128, 128)) % 4
    half = lanes((128, 128)) // 64
    first = (kxl == half).astype(BF16)
    second = (kxl == 2 + half).astype(BF16)
    low8 = lanes((8, 128)) < 64
    sign = jnp.where(sublanes((8, 128)) < 4, -1.0, 1.0)
    for quarter in range(4):
        wide = jnp.concatenate(
            [rows_ref[pl.ds(quarter * 4 + k, count, stride=16), :] for k in range(4)], axis=1
        ).astype(BF16)
        plain = (dot_nn(plain_ref[...], wide) * scale).astype(BF16)
        both = dot_nn(both_ref[...], wide) * scale
        for k in range(4):
            j = quarter * 4 + k
            coeff_ref[j] = plain[:, k * 128 : (k + 1) * 128]
            coeffs = both[:, k * 128 : (k + 1) * 128]
            swapped = swap_halves(coeffs)
            for h in range(2):
                twice = jnp.where(low if h == 0 else ~low, coeffs, swapped).astype(BF16)
                left_ref[j, h] = jnp.concatenate([twice * first, twice * second], axis=1)
    for j in range(16):
        if j % 4 == 0:
            for copy in copies[j : j + 4]:
                copy.wait()
        mixed = []
        for u in range(MX // 8):
            halves = [
                dot_nn(left_ref[j, h, u * 32 : (u + 1) * 32, :], mode_pair(weight_ref, j, h, u))
                for h in range(2)
            ]
            for t in range(2):
                low_h, high_h = [
                    part[t * 16 : (t + 1) * 16, t * 128 : (t + 1) * 128] for part in halves
                ]
                keep = jnp.where(low8, low_h[:8], sign * high_h[8:])
                move = jnp.where(low8, high_h[:8], sign * low_h[8:])
                mixed.append(keep + swap_halves(move))
        mixed_ref[j] = jnp.concatenate(mixed, axis=0).astype(BF16)
    plane_sums(back_ref, mixed_ref, rows_ref, out_ref)


def mode_grad_kernel(
    scale,
    block_ref,
    weight_hbm,
    straight_ref,
    back_ref,
    pair_ref,
    out_ref,
    weight_ref,
    rows_ref,
    mixed_ref,
    sems,
):
    copies = start_weights(weight_hbm, weight_ref, sems)
    count = rows_ref.shape[0] // 16
    rows_ref[...] = block_ref[...].astype(F32)
    low = lanes((64, 128)) < 64
    low16 = lanes((16, 128)) < 64
    row = sublanes((16, 128)) % 4
    upper = row < 2
    valid = lanes((16, 128)) // 64 == row % 2
    even = (sublanes((16, 128)) < 8).astype(BF16)
    odd = (sublanes((16, 128)) >= 8).astype(BF16)
    for j in range(16):
        section = rows_ref[pl.ds(j, count, stride=16), :]
        swapped = swap_halves(section)
        twice = jnp.concatenate(
            [jnp.where(low, section, swapped), jnp.where(low, swapped, section)], axis=1
        ).astype(BF16)
        turned = dot_nn(straight_ref[...], twice)
        for h in range(2):
            part = turned[:, h * 128 : (h + 1) * 128]
            pair_ref[2 * j + h] = jnp.where(low, part[:64], part[64:]).astype(BF16)
    for j in range(16):
        if j % 4 == 0:
            for copy in copies[j : j + 4]:
                copy.wait()
        mixed = []
        for u in range(MX // 8):
            found = []
            for h in range(2):
                pair = pair_ref[2 * j + h, u * 16 : (u + 1) * 16, :]
                rows = dot_nt(
                    jnp.concatenate([pair * even, pair * odd], axis=1),
                    mode_pair(weight_ref, j, h, u),
                )
                found.append(jnp.where(valid, jnp.where(upper, rows[:, :128], rows[:, 128:]), 0.0))
            keep = jnp.where(low16, found[0], found[1])
            move = jnp.where(low16, found[1], found[0])
            mixed.append(keep + swap_halves(move))
        mixed_ref[j] = (jnp.concatenate(mixed, axis=0) * scale).astype(BF16)
    plane_sums(back_ref, mixed_ref, rows_ref, out_ref)


def weight_grad_kernel(scale, coeff_ref, pair_ref, out_hbm, out_ref, mask_ref, sems):
    lane = lanes((128, 64))
    part = sublanes((128, 64)) // 64
    for t in range(MX // 4):
        mask_ref[t] = ((lane // 8 == t) & (lane % 4 // 2 == part)).astype(BF16)
    eye = (sublanes((128, 128)) == lanes((128, 128))).astype(BF16)
    even = (sublanes((64, 128)) % 2 == 0).astype(BF16)
    odd = (sublanes((64, 128)) % 2 == 1).astype(BF16)

    @pl.loop(0, 16)
    def _(j):
        turned = (dot_nt(eye, coeff_ref[j]) * scale).astype(BF16)
        for h in range(2):
            left = turned[h * 64 : (h + 1) * 64]
            left = jnp.concatenate([left, left], axis=0)
            pair = pair_ref[j * 2 + h]
            right = jnp.concatenate([pair * even, pair * odd], axis=1)
            for t in range(MX // 4):
                four = dot_nn(left * mask_ref[t], right).astype(BF16)
                mode = (j * 2 + h) * MX + 4 * t
                for k in range(4):
                    out_ref[mode + k] = four[
                        k // 2 * 64 : (k // 2 + 1) * 64, k % 2 * 128 : (k % 2 + 1) * 128
                    ]
        part_copy(out_ref, out_hbm, sems, j, 2 * MX).start()

    for j in range(16):
        part_copy(out_ref, out_hbm, sems, j, 2 * MX).wait()


def params(mib):
    return pltpu.CompilerParams(vmem_limit_bytes=mib * 1024 * 1024)


def cost(flops, moved):
    return pl.CostEstimate(flops=int(flops), bytes_accessed=int(moved), transcendentals=0)


def fast_body(features, cotangent, spectral_weight, channel_weight, channel_bias):
    channels, planes, lines, depth_len = features.shape
    devices = lax.axis_size("gx")
    owned_modes = spectral_weight.shape[0]
    wave_pairs = MY * MZ
    volume = planes * devices * lines * depth_len
    forward_scale = 1.0 / math.sqrt(volume)
    inverse_scale = 1.0 / math.sqrt(MX * wave_pairs)
    weight_scale = math.sqrt(MX * wave_pairs / volume)
    table = {name: jnp.asarray(value) for name, value in tables(devices, lines, depth_len).items()}
    block_rows = devices * 64
    block_shape = jax.ShapeDtypeStruct((block_rows, 128), BF16)
    vmem = pl.BlockSpec(memory_space=pltpu.VMEM)
    hbm = pl.BlockSpec(memory_space=pltpu.HBM)
    smem = pl.BlockSpec(memory_space=pltpu.SMEM)
    field_scratch = pltpu.VMEM(features.shape, BF16)
    field_shape = jax.ShapeDtypeStruct(features.shape, BF16)

    def sems(count):
        return pltpu.SemaphoreType.DMA((count,))

    def scratch(name):
        return pltpu.VMEM(table[name].shape, BF16)

    steps = channels // STEP
    lines_scratch = pltpu.VMEM((MZ, channels, 2 * planes * lines), F32)
    rows_scratch = pltpu.VMEM((block_rows, 128), F32)
    spec_scratch = pltpu.VMEM((channels // GROUP, MZ * GROUP, 128), F32)
    weight_rows = spectral_weight.reshape(owned_modes * channels, 2 * channels)
    field_bytes = features.size * 2

    def exchange(block):
        return lax.all_to_all(
            block.reshape(devices, 64, 128), "gx", 0, 0, tiled=True
        ).reshape(block_rows, 128)

    def point(field, transposed):
        return pl.pallas_call(
            functools.partial(point_kernel, transposed),
            out_shape=field_shape,
            in_specs=[vmem, hbm],
            out_specs=hbm,
            scratch_shapes=[
                field_scratch,
                field_scratch,
                pltpu.VMEM((channels * 16, channels * 16), BF16),
                sems(planes),
                sems(planes),
            ],
            compiler_params=params(VMEM_MIB),
            cost_estimate=cost(2 * 1024**3, 2 * field_bytes),
            name="channel_map_back" if transposed else "channel_map",
        )(channel_weight, field)

    block = pl.pallas_call(
        analysis_kernel,
        out_shape=block_shape,
        in_specs=[hbm, hbm, hbm],
        out_specs=vmem,
        scratch_shapes=[
            field_scratch,
            scratch("depth"),
            scratch("across_y"),
            lines_scratch,
            rows_scratch,
            sems(steps),
            sems(2),
        ],
        compiler_params=params(62),
        cost_estimate=cost(2 * 256 * 1024 * 1024, field_bytes),
        name="field_analysis",
    )(features, table["depth"], table["across_y"])
    block, pointwise = lax.optimization_barrier((exchange(block), point(features, False)))

    weight_scratch = pltpu.VMEM(weight_rows.shape, BF16)
    mixed_scratch = pltpu.VMEM((16, 64, 128), BF16)
    weight_sems = sems(16)
    coeffs, block = pl.pallas_call(
        functools.partial(mode_kernel, forward_scale),
        out_shape=[jax.ShapeDtypeStruct((16, 64, 128), BF16), block_shape],
        in_specs=[vmem, hbm, vmem, vmem, vmem],
        out_specs=[vmem, vmem],
        scratch_shapes=[
            weight_scratch,
            rows_scratch,
            pltpu.VMEM((16, 2, 128, 256), BF16),
            mixed_scratch,
            weight_sems,
        ],
        compiler_params=params(VMEM_MIB),
        cost_estimate=cost(256 * 2 * 16 * 256 * 128, 17 * 2**20),
        name="mode_product",
    )(block, weight_rows, table["both_x"], table["plain_x"], table["back_x"])
    block = exchange(block)

    activated, upstream, block = pl.pallas_call(
        functools.partial(middle_kernel, inverse_scale),
        out_shape=[field_shape, field_shape, block_shape],
        in_specs=[vmem, smem, hbm, hbm, hbm, hbm, hbm],
        out_specs=[hbm, hbm, vmem],
        scratch_shapes=[
            field_scratch,
            field_scratch,
            scratch("depth"),
            scratch("across_y"),
            scratch("back_y"),
            field_scratch,
            field_scratch,
            lines_scratch,
            rows_scratch,
            spec_scratch,
            sems(steps),
            sems(steps),
            sems(steps),
            sems(steps),
            sems(3),
        ],
        compiler_params=params(VMEM_MIB),
        cost_estimate=cost(2**30, 4 * field_bytes),
        name="gelu_and_gradient",
    )(
        block,
        channel_bias,
        pointwise,
        cotangent,
        table["depth"],
        table["across_y"],
        table["back_y"],
    )
    block = exchange(block)
    block, channel_back = lax.optimization_barrier((block, point(upstream, True)))

    pairs, block = pl.pallas_call(
        functools.partial(mode_grad_kernel, forward_scale),
        out_shape=[jax.ShapeDtypeStruct((32, 64, 128), BF16), block_shape],
        in_specs=[vmem, hbm, vmem, vmem],
        out_specs=[vmem, vmem],
        scratch_shapes=[weight_scratch, rows_scratch, mixed_scratch, weight_sems],
        compiler_params=params(VMEM_MIB),
        cost_estimate=cost(256 * 2 * 16 * 256 * 128, 17 * 2**20),
        name="mode_gradient",
    )(block, weight_rows, table["straight_x"], table["back_x"])
    block = exchange(block)

    spectral_grad = pl.pallas_call(
        functools.partial(weight_grad_kernel, weight_scale),
        out_shape=jax.ShapeDtypeStruct(spectral_weight.shape, BF16),
        in_specs=[vmem, vmem],
        out_specs=hbm,
        scratch_shapes=[
            pltpu.VMEM(spectral_weight.shape, BF16),
            pltpu.VMEM((MX // 4, 128, 64), BF16),
            sems(16),
        ],
        compiler_params=params(VMEM_MIB),
        cost_estimate=cost(512 * 2 * 64 * 64 * 256, 17 * 2**20),
        name="weight_gradient",
    )(coeffs, pairs)

    feature_grad = pl.pallas_call(
        final_kernel,
        out_shape=field_shape,
        in_specs=[vmem, hbm, hbm, hbm],
        out_specs=hbm,
        scratch_shapes=[
            field_scratch,
            scratch("depth"),
            scratch("back_y"),
            field_scratch,
            rows_scratch,
            spec_scratch,
            sems(steps),
            sems(steps),
            sems(2),
        ],
        compiler_params=params(VMEM_MIB),
        cost_estimate=cost(2**29, 2 * field_bytes),
        name="field_gradient",
    )(block, channel_back, table["depth"], table["back_y"])
    return (activated, feature_grad, spectral_grad)


def body(features, cotangent, spectral_weight, channel_weight, channel_bias):
    channels, planes, lines, depth_len = features.shape
    devices = lax.axis_size("gx")
    fits = (
        (channels, planes, lines, depth_len) == (64, PLANES, 64, 128)
        and spectral_weight.shape[0] == 2 * MZ * MX
        and devices * 2 == MY
        and devices * 2 == MX
    )
    run = fast_body if fits else general_body
    return run(features, cotangent, spectral_weight, channel_weight, channel_bias)


def solution(mesh):
    in_specs = (
        P("grp", "gx", None, None),
        P("grp", "gx", None, None),
        P("gx", None, None),
        P(),
        P(),
    )
    out_specs = (
        P("grp", "gx", None, None),
        P("grp", "gx", None, None),
        P(("grp", "gx"), None, None),
    )
    return jax.shard_map(body, mesh=mesh, in_specs=in_specs, out_specs=out_specs, check_vma=False)
```

```python
import functools
import math

import jax
import jax.numpy as jnp
import ml_dtypes
import numpy as np
from jax import lax
from jax.experimental import pallas as pl
from jax.experimental.pallas import tpu as pltpu
from jax.sharding import PartitionSpec as P

MX = 32
MY = 32
MZ = 16


SQRT_TWO_PI = math.sqrt(2.0 / math.pi)
CUBIC_COEF = 0.044715


def freq_index(retained, length):
    ladder = jnp.arange(retained, dtype=jnp.int32)
    return jnp.where(ladder < retained // 2, ladder, length - retained + ladder)


def cos_sin(wavenum, length):
    points = jnp.arange(length, dtype=jnp.int32)
    angles = (wavenum[:, None] * points[None, :] % length).astype(jnp.float32) * (
        2.0 * math.pi / length
    )
    return (jnp.cos(angles), jnp.sin(angles))


def analysis_pair(wavenum, length):
    cosine, sine_wave = cos_sin(wavenum, length)
    cosine, sine_wave = (cosine.T, sine_wave.T)
    return jnp.stack(
        [jnp.stack([cosine, -sine_wave], 1), jnp.stack([sine_wave, cosine], 1)], 1
    ).astype(jnp.bfloat16)


def synthesis_pair(wavenum, length):
    cosine, sine_wave = cos_sin(wavenum, length)
    return jnp.stack(
        [jnp.stack([cosine, sine_wave], 1), jnp.stack([-sine_wave, cosine], 1)], 1
    ).astype(jnp.bfloat16)


def depth_table(retained, length):
    cosine, sine_wave = cos_sin(jnp.arange(retained, dtype=jnp.int32), length)
    return jnp.concatenate([cosine, -sine_wave], 0).astype(jnp.bfloat16)


def gelu_parts(inputs):
    cubed_in = inputs * inputs * inputs
    tangent = jnp.tanh(SQRT_TWO_PI * (inputs + CUBIC_COEF * cubed_in))
    output = 0.5 * inputs * (1.0 + tangent)
    derivative = 0.5 * (1.0 + tangent) + 0.5 * inputs * (1.0 - tangent * tangent) * SQRT_TWO_PI * (
        1.0 + 3.0 * CUBIC_COEF * inputs * inputs
    )
    return (output, derivative)


def mode_product(coeffs, weights, channels):
    stacked = coeffs.reshape(coeffs.shape[0], 2, channels)
    halves = jnp.einsum("mac,mcj->amj", stacked, weights, preferred_element_type=jnp.float32)
    real_out = halves[0, :, :channels] - halves[1, :, channels:]
    imag_out = halves[0, :, channels:] + halves[1, :, :channels]
    return jnp.concatenate([real_out, imag_out], 1).astype(jnp.bfloat16)


def mode_grads(coeffs, weights, grad_modes, channels, weight_scale, input_scale):
    number = coeffs.shape[0]
    stacked = coeffs.reshape(number, 2, channels)
    grad_pairs = grad_modes.reshape(number, 2, channels)
    real_w = jnp.einsum("mac,mao->mco", stacked, grad_pairs, preferred_element_type=jnp.float32)
    imag_w = jnp.einsum(
        "mc,mo->mco", stacked[:, 0], grad_pairs[:, 1], preferred_element_type=jnp.float32
    ) - jnp.einsum(
        "mc,mo->mco", stacked[:, 1], grad_pairs[:, 0], preferred_element_type=jnp.float32
    )
    weight_grad = (jnp.concatenate([real_w, imag_w], 2) * weight_scale).astype(jnp.bfloat16)
    straight = jnp.concatenate([grad_pairs[:, 0], grad_pairs[:, 1]], 1)
    rotated = jnp.concatenate([grad_pairs[:, 1], -grad_pairs[:, 0]], 1)
    real_x = jnp.einsum("mcj,mj->mc", weights, straight, preferred_element_type=jnp.float32)
    imag_x = jnp.einsum("mcj,mj->mc", weights, rotated, preferred_element_type=jnp.float32)
    input_grad = (jnp.concatenate([real_x, imag_x], 1) * input_scale).astype(jnp.bfloat16)
    return (weight_grad, input_grad)


def general_body(features, cotangent, spectral_weight, channel_weight, channel_bias):
    channels, planes, lines, depth_len = features.shape
    devices = lax.axis_size("gx")
    all_planes = planes * devices
    owned_modes = spectral_weight.shape[0]
    wave_pairs = MY * MZ
    forward_scale = 1.0 / math.sqrt(all_planes * lines * depth_len)
    inverse_scale = 1.0 / math.sqrt(MX * wave_pairs)
    weight_scale = math.sqrt(MX * wave_pairs / (all_planes * lines * depth_len))
    depth_basis = depth_table(MZ, depth_len)
    across_y = analysis_pair(freq_index(MY, lines), lines)
    back_y = synthesis_pair(freq_index(MY, lines), lines)
    across_full = analysis_pair(freq_index(MX, all_planes), all_planes)
    back_full = synthesis_pair(freq_index(MX, all_planes), all_planes)
    depth_part = jnp.dot(features, depth_basis.T, preferred_element_type=jnp.float32).astype(
        jnp.bfloat16
    )
    plane_part = (
        jnp.einsum(
            "cxyaz,yabk->cxbkz",
            depth_part.reshape(channels, planes, lines, 2, MZ),
            across_y,
            preferred_element_type=jnp.float32,
        )
        .astype(jnp.bfloat16)
        .reshape(channels, planes, 2, wave_pairs)
    )
    all_rows = lax.all_to_all(plane_part, "gx", split_axis=3, concat_axis=1, tiled=True)
    mode_sums = jnp.einsum(
        "cxaq,xabk->qkbc", all_rows, across_full, preferred_element_type=jnp.float32
    ).reshape(owned_modes, 2 * channels)
    coeffs = (mode_sums * forward_scale).astype(jnp.bfloat16)
    spectral = mode_product(coeffs, spectral_weight, channels)
    planes_all = jnp.einsum(
        "qkao,kabx->oxbq",
        spectral.reshape(owned_modes // MX, MX, 2, channels),
        back_full,
        preferred_element_type=jnp.float32,
    ).astype(jnp.bfloat16)
    planes_back = lax.all_to_all(planes_all, "gx", split_axis=1, concat_axis=3, tiled=True)
    lines_back = (
        jnp.einsum(
            "oxakz,kaby->oxybz",
            planes_back.reshape(channels, planes, 2, MY, MZ),
            back_y,
            preferred_element_type=jnp.float32,
        )
        .astype(jnp.bfloat16)
        .reshape(channels, planes, lines, 2 * MZ)
    )
    spectral_term = (
        jnp.dot(lines_back, depth_basis, preferred_element_type=jnp.float32) * inverse_scale
    )
    pointwise = jnp.einsum(
        "oc,cxyz->oxyz", channel_weight, features, preferred_element_type=jnp.float32
    )
    hidden = spectral_term + pointwise + channel_bias[:, None, None, None]
    activated, derivative = gelu_parts(hidden)
    upstream = (cotangent.astype(jnp.float32) * derivative).astype(jnp.bfloat16)
    lines_grad = (
        jnp.dot(upstream, depth_basis.T, preferred_element_type=jnp.float32) * inverse_scale
    ).astype(jnp.bfloat16)
    rows_grad = (
        jnp.einsum(
            "oxybz,kaby->oxakz",
            lines_grad.reshape(channels, planes, lines, 2, MZ),
            back_y,
            preferred_element_type=jnp.float32,
        )
        .astype(jnp.bfloat16)
        .reshape(channels, planes, 2, wave_pairs)
    )
    all_grads = lax.all_to_all(rows_grad, "gx", split_axis=3, concat_axis=1, tiled=True)
    grad_sums = jnp.einsum(
        "oxbq,kabx->qkao", all_grads, back_full, preferred_element_type=jnp.float32
    ).reshape(owned_modes, 2 * channels)
    grad_modes = grad_sums.astype(jnp.bfloat16)
    spectral_grad, coeff_grad = mode_grads(
        coeffs, spectral_weight, grad_modes, channels, weight_scale, forward_scale
    )
    plane_all = jnp.einsum(
        "qkbc,xabk->cxaq",
        coeff_grad.reshape(owned_modes // MX, MX, 2, channels),
        across_full,
        preferred_element_type=jnp.float32,
    ).astype(jnp.bfloat16)
    plane_grad = lax.all_to_all(plane_all, "gx", split_axis=1, concat_axis=3, tiled=True)
    depth_grad = (
        jnp.einsum(
            "cxbkz,yabk->cxyaz",
            plane_grad.reshape(channels, planes, 2, MY, MZ),
            across_y,
            preferred_element_type=jnp.float32,
        )
        .astype(jnp.bfloat16)
        .reshape(channels, planes, lines, 2 * MZ)
    )
    channel_back = jnp.einsum(
        "oc,oxyz->cxyz", channel_weight, upstream, preferred_element_type=jnp.float32
    )
    feature_grad = (
        jnp.dot(depth_grad, depth_basis, preferred_element_type=jnp.float32) + channel_back
    ).astype(jnp.bfloat16)
    return (activated.astype(jnp.bfloat16), feature_grad, spectral_grad)


PLANES = 2
GROUP = 8
STEP = 16
VMEM_MIB = 28
NT = (((1,), (1,)), ((), ()))
F32 = jnp.float32
BF16 = jnp.bfloat16


def np_freq(retained, length):
    ladder = np.arange(retained)
    return np.where(ladder < retained // 2, ladder, length - retained + ladder)


def np_angles(wavenum, length):
    points = np.arange(length)
    return (wavenum[:, None] * points[None, :] % length) * (2.0 * math.pi / length)


def as_bf16(table):
    return np.asarray(table, np.float32).astype(ml_dtypes.bfloat16)


def rotation(angle, sign):
    cosine, sine_wave = np.cos(angle), sign * np.sin(angle)
    return np.stack([np.stack([cosine, -sine_wave]), np.stack([sine_wave, cosine])])


@functools.lru_cache(maxsize=None)
def tables(devices, lines, depth_len):
    planes_all = devices * PLANES
    angle = np_angles(np.arange(MZ), depth_len)
    depth = np.stack([np.cos(angle), -np.sin(angle)])
    eye = np.eye(GROUP)
    depth_block = np.einsum("akz,ij->akijz", depth, eye).reshape(2 * MZ * GROUP, GROUP * depth_len)
    plane_eye = np.eye(PLANES)
    angle = np_angles(np_freq(MY, lines), lines).reshape(devices, MY // devices, lines)
    across = np.einsum("badly,xw->ldbxawy", rotation(angle, -1.0), plane_eye)
    across = across.reshape(MY * 2 * PLANES, 2 * PLANES * lines)
    back = np.einsum("pbdly,xw->pxyldbw", rotation(angle, 1.0), plane_eye)
    back = back.reshape(2 * PLANES * lines, MY * 2 * PLANES)
    angle = np_angles(np_freq(MX, planes_all), planes_all).reshape(MX // 4, 4, devices, PLANES)
    forward = rotation(angle, -1.0)
    rows = np.einsum("batksx->tbksax", forward).reshape(MX // 4, 2, 4, devices * 2 * PLANES)
    plain = rows.reshape(2 * MX, -1)
    both = np.stack([rows, rows[:, ::-1]], 1).reshape(4 * MX, -1)
    turned = np.concatenate([rows[:, 1:], -rows[:, :1]], 1).reshape(2 * MX, -1)
    straight_rotated = np.concatenate([plain, turned], 0)
    inverse = np.einsum("batksx->sbxtak", rotation(angle, 1.0)).reshape(-1, 2 * MX)
    return {
        "depth": as_bf16(depth_block),
        "across_y": as_bf16(across),
        "back_y": as_bf16(back),
        "plain_x": as_bf16(plain),
        "both_x": as_bf16(both),
        "straight_x": as_bf16(straight_rotated),
        "back_x": as_bf16(inverse),
    }


def dot_nn(left, right):
    return jnp.dot(left, right, preferred_element_type=F32)


def dot_nt(left, right):
    return lax.dot_general(left, right, NT, preferred_element_type=F32)


def lanes(shape):
    return lax.broadcasted_iota(jnp.int32, shape, len(shape) - 1)


def sublanes(shape):
    return lax.broadcasted_iota(jnp.int32, shape, len(shape) - 2)


def swap_halves(block):
    return pltpu.roll(block, 64, 1)


def part_copy(source, target, sems, index, size):
    part = pl.ds(pl.multiple_of(index * size, size), size)
    return pltpu.make_async_copy(source.at[part], target.at[part], sems.at[index])


def start_parts(source, target, sems, size):
    for index in range(source.shape[0] // size):
        part_copy(source, target, sems, index, size).start()


def start_tables(pairs, sems):
    copies = []
    for index, (source, target) in enumerate(pairs):
        copy = pltpu.make_async_copy(source, target, sems.at[index])
        copy.start()
        copies.append(copy)
    return copies


def depth_analysis(slabs, depth, scale, group, lines_ref):
    wide = jnp.concatenate(slabs, axis=1)
    parts = dot_nt(depth, wide)
    if scale is not None:
        parts = parts * scale
    width = wide.shape[0]
    start = pl.multiple_of(group * GROUP, GROUP)
    for a in range(2):
        lines_ref[:, pl.ds(start, GROUP), a * width : (a + 1) * width] = parts[
            a * MZ * GROUP : (a + 1) * MZ * GROUP
        ].reshape(MZ, GROUP, width)


def rows_analysis(lines_ref, across_ref, rows_ref, out_ref):
    channels, width = lines_ref.shape[1], lines_ref.shape[2]
    across = across_ref[...]
    half = across.shape[0] // 2
    for kzh in range(MZ // 2):
        pair = lines_ref[2 * kzh : 2 * kzh + 2].reshape(2 * channels, width).astype(BF16)
        rows = dot_nt(across, pair)
        for kyl in range(2):
            rows_ref[pl.ds(kyl * 8 + kzh, half, stride=16), :] = rows[
                kyl * half : (kyl + 1) * half
            ]
    out_ref[...] = rows_ref[...].astype(BF16)


def rows_gather(block_ref, rows_ref, spec_ref):
    rows_ref[...] = block_ref[...].astype(F32)
    count = rows_ref.shape[0] // 16
    eye = (sublanes((128, 128)) == lanes((128, 128))).astype(BF16)
    for kzh in range(MZ // 2):
        both = jnp.concatenate(
            [rows_ref[pl.ds(kyl * 8 + kzh, count, stride=16), :] for kyl in range(2)], axis=0
        ).astype(BF16)
        turned = dot_nt(eye, both)
        for h in range(2):
            spec_ref[:, (2 * kzh + h) * GROUP : (2 * kzh + h + 1) * GROUP, :] = turned[
                h * 64 : (h + 1) * 64
            ].reshape(8, GROUP, turned.shape[1])


def synthesis(groups, spec_ref, back, depth, scale):
    wide = []
    for group in groups:
        lines = dot_nt(back, spec_ref[group].astype(BF16))
        if scale is not None:
            lines = lines * scale
        lines = lines.astype(BF16)
        half = lines.shape[0] // 2
        wide.append(jnp.concatenate([lines[:half], lines[half:]], axis=1))
    return dot_nn(jnp.concatenate(wide, axis=0), depth)


def flat(slab):
    return slab.reshape(slab.shape[0] * slab.shape[1], slab.shape[2])


def analysis_kernel(
    field_hbm,
    depth_hbm,
    across_hbm,
    out_ref,
    field_ref,
    depth_ref,
    across_ref,
    lines_ref,
    rows_ref,
    field_sems,
    table_sems,
):
    first, second = start_tables([(depth_hbm, depth_ref), (across_hbm, across_ref)], table_sems)
    start_parts(field_hbm, field_ref, field_sems, STEP)
    first.wait()

    @pl.loop(0, field_ref.shape[0] // STEP)
    def _(step):
        part_copy(field_hbm, field_ref, field_sems, step, STEP).wait()
        for g in range(STEP // GROUP):
            group = step * (STEP // GROUP) + g
            slabs = [flat(field_ref[group * GROUP + ci]) for ci in range(GROUP)]
            depth_analysis(slabs, depth_ref[...], None, group, lines_ref)

    second.wait()
    rows_analysis(lines_ref, across_ref, rows_ref, out_ref)


def middle_kernel(
    inverse_scale,
    block_ref,
    bias_ref,
    point_hbm,
    cot_hbm,
    depth_hbm,
    across_hbm,
    back_hbm,
    act_hbm,
    up_hbm,
    out_ref,
    point_ref,
    cot_ref,
    depth_ref,
    across_ref,
    back_ref,
    act_ref,
    up_ref,
    lines_ref,
    rows_ref,
    spec_ref,
    point_sems,
    cot_sems,
    act_sems,
    up_sems,
    table_sems,
):
    tables_in = start_tables(
        [(back_hbm, back_ref), (depth_hbm, depth_ref), (across_hbm, across_ref)], table_sems
    )
    start_parts(point_hbm, point_ref, point_sems, STEP)
    start_parts(cot_hbm, cot_ref, cot_sems, STEP)
    rows_gather(block_ref, rows_ref, spec_ref)
    for copy in tables_in:
        copy.wait()
    steps = point_ref.shape[0] // STEP

    @pl.loop(0, steps)
    def _(step):
        groups = [step * (STEP // GROUP) + g for g in range(STEP // GROUP)]
        spectral = synthesis(groups, spec_ref, back_ref[...], depth_ref[...], inverse_scale)
        part_copy(point_hbm, point_ref, point_sems, step, STEP).wait()
        part_copy(cot_hbm, cot_ref, cot_sems, step, STEP).wait()
        for g, group in enumerate(groups):
            slabs = []
            for oi in range(GROUP):
                index = group * GROUP + oi
                hidden = (
                    spectral[g * 128 : (g + 1) * 128, oi * 128 : (oi + 1) * 128]
                    + flat(point_ref[index]).astype(F32)
                    + bias_ref[index]
                )
                square = hidden * hidden
                gate = 0.5 + 0.5 * jnp.tanh(
                    hidden * (SQRT_TWO_PI + (SQRT_TWO_PI * CUBIC_COEF) * square)
                )
                slope = hidden * (2.0 * SQRT_TWO_PI + (6.0 * SQRT_TWO_PI * CUBIC_COEF) * square)
                derivative = gate + (gate - gate * gate) * slope
                upstream = (flat(cot_ref[index]).astype(F32) * derivative).astype(BF16)
                act_ref[index] = (hidden * gate).astype(BF16).reshape(act_ref.shape[1:])
                up_ref[index] = upstream.reshape(up_ref.shape[1:])
                slabs.append(upstream)
            depth_analysis(slabs, depth_ref[...], inverse_scale, group, lines_ref)
        part_copy(act_ref, act_hbm, act_sems, step, STEP).start()
        part_copy(up_ref, up_hbm, up_sems, step, STEP).start()

    rows_analysis(lines_ref, across_ref, rows_ref, out_ref)
    for step in range(steps):
        part_copy(act_ref, act_hbm, act_sems, step, STEP).wait()
        part_copy(up_ref, up_hbm, up_sems, step, STEP).wait()


def final_kernel(
    block_ref,
    point_hbm,
    depth_hbm,
    back_hbm,
    out_hbm,
    point_ref,
    depth_ref,
    back_ref,
    out_ref,
    rows_ref,
    spec_ref,
    point_sems,
    out_sems,
    table_sems,
):
    tables_in = start_tables([(back_hbm, back_ref), (depth_hbm, depth_ref)], table_sems)
    start_parts(point_hbm, point_ref, point_sems, STEP)
    rows_gather(block_ref, rows_ref, spec_ref)
    for copy in tables_in:
        copy.wait()
    steps = point_ref.shape[0] // STEP

    @pl.loop(0, steps)
    def _(step):
        groups = [step * (STEP // GROUP) + g for g in range(STEP // GROUP)]
        spectral = synthesis(groups, spec_ref, back_ref[...], depth_ref[...], None)
        part_copy(point_hbm, point_ref, point_sems, step, STEP).wait()
        for g, group in enumerate(groups):
            for ci in range(GROUP):
                index = group * GROUP + ci
                total = spectral[
                    g * 128 : (g + 1) * 128, ci * 128 : (ci + 1) * 128
                ] + flat(point_ref[index]).astype(F32)
                out_ref[index] = total.astype(BF16).reshape(out_ref.shape[1:])
        part_copy(out_ref, out_hbm, out_sems, step, STEP).start()

    for step in range(steps):
        part_copy(out_ref, out_hbm, out_sems, step, STEP).wait()


def load_and_point_kernel(
    weight_ref,
    field_hbm,
    modes_hbm,
    out_hbm,
    modes_ref,
    field_ref,
    out_ref,
    wide_ref,
    in_sems,
    out_sems,
    mode_sems,
):
    copies = start_weights(modes_hbm, modes_ref, mode_sems)
    point_kernel(
        False, weight_ref, field_hbm, out_hbm, field_ref, out_ref, wide_ref, in_sems, out_sems
    )
    for copy in copies:
        copy.wait()


def point_kernel(
    transposed, weight_ref, field_hbm, out_hbm, field_ref, out_ref, wide_ref, in_sems, out_sems
):
    size = wide_ref.shape[0]
    planes = field_ref.shape[1]
    copies = []
    for plane in range(planes):
        part = (slice(None), pl.ds(plane, 1))
        copy = pltpu.make_async_copy(field_hbm.at[part], field_ref.at[part], in_sems.at[plane])
        copy.start()
        copies.append(copy)
    tall = (sublanes((size, 64)) // 16 == lanes((size, 64))).astype(BF16)
    weight = weight_ref[...]
    left = dot_nt(tall, weight) if transposed else dot_nn(tall, weight)
    left = left.astype(BF16)
    rows = size // 4
    same = sublanes((rows, size)) % 16 == lanes((rows, size)) % 16
    for quarter in range(4):
        spread = dot_nt(left[quarter * rows : (quarter + 1) * rows], tall)
        wide_ref[quarter * rows : (quarter + 1) * rows, :] = jnp.where(same, spread, 0.0).astype(
            BF16
        )
    sends = []
    for plane in range(planes):
        copies[plane].wait()
        for pair in range(2):
            right = jnp.concatenate(
                [
                    field_ref[:, plane, yc * 16 : (yc + 1) * 16, :].reshape(size, 128)
                    for yc in (2 * pair, 2 * pair + 1)
                ],
                axis=1,
            )
            result = dot_nn(wide_ref[...], right).astype(BF16)
            for k in range(2):
                yc = 2 * pair + k
                out_ref[:, plane, yc * 16 : (yc + 1) * 16, :] = result[
                    :, k * 128 : (k + 1) * 128
                ].reshape(size // 16, 16, 128)
        part = (slice(None), pl.ds(plane, 1))
        copy = pltpu.make_async_copy(out_ref.at[part], out_hbm.at[part], out_sems.at[plane])
        copy.start()
        sends.append(copy)
    for copy in sends:
        copy.wait()


def start_weights(weight_hbm, weight_ref, sems):
    copies = []
    for j in range(16):
        rows = weight_ref.shape[0] // 16
        part = pl.ds(j * rows, rows)
        copy = pltpu.make_async_copy(weight_hbm.at[part], weight_ref.at[part], sems.at[j])
        copy.start()
        copies.append(copy)
    return copies


def mode_pair(weight_ref, j, h, u):
    start = ((j * 2 + h) * MX + 8 * u) * 64
    return jnp.concatenate(
        [weight_ref[start : start + 256, :], weight_ref[start + 256 : start + 512, :]], axis=1
    )


def plane_sums(back_ref, mixed_ref, res_ref, out_ref):
    count = res_ref.shape[0] // 16
    for quarter in range(4):
        wide = jnp.concatenate([mixed_ref[quarter * 4 + k] for k in range(4)], axis=1)
        rows = dot_nn(back_ref[...], wide)
        for k in range(4):
            res_ref[pl.ds(quarter * 4 + k, count, stride=16), :] = rows[:, k * 128 : (k + 1) * 128]
    out_ref[...] = res_ref[...].astype(BF16)


def mode_kernel(
    scale,
    block_ref,
    weight_ref,
    both_ref,
    plain_ref,
    back_ref,
    coeff_ref,
    out_ref,
    rows_ref,
    left_ref,
    mixed_ref,
):
    count = rows_ref.shape[0] // 16
    rows_ref[...] = block_ref[...].astype(F32)
    low = lanes((128, 128)) < 64
    kxl = sublanes((128, 128)) % 4
    half = lanes((128, 128)) // 64
    first = (kxl == half).astype(BF16)
    second = (kxl == 2 + half).astype(BF16)
    low8 = lanes((8, 128)) < 64
    sign = jnp.where(sublanes((8, 128)) < 4, -1.0, 1.0)
    for quarter in range(4):
        wide = jnp.concatenate(
            [rows_ref[pl.ds(quarter * 4 + k, count, stride=16), :] for k in range(4)], axis=1
        ).astype(BF16)
        plain = (dot_nn(plain_ref[...], wide) * scale).astype(BF16)
        both = dot_nn(both_ref[...], wide) * scale
        for k in range(4):
            j = quarter * 4 + k
            coeff_ref[j] = plain[:, k * 128 : (k + 1) * 128]
            coeffs = both[:, k * 128 : (k + 1) * 128]
            swapped = swap_halves(coeffs)
            for h in range(2):
                twice = jnp.where(low if h == 0 else ~low, coeffs, swapped).astype(BF16)
                left_ref[j, h] = jnp.concatenate([twice * first, twice * second], axis=1)
    for j in range(16):
        mixed = []
        for u in range(MX // 8):
            halves = [
                dot_nn(left_ref[j, h, u * 32 : (u + 1) * 32, :], mode_pair(weight_ref, j, h, u))
                for h in range(2)
            ]
            for t in range(2):
                low_h, high_h = [
                    part[t * 16 : (t + 1) * 16, t * 128 : (t + 1) * 128] for part in halves
                ]
                keep = jnp.where(low8, low_h[:8], sign * high_h[8:])
                move = jnp.where(low8, high_h[:8], sign * low_h[8:])
                mixed.append(keep + swap_halves(move))
        mixed_ref[j] = jnp.concatenate(mixed, axis=0).astype(BF16)
    plane_sums(back_ref, mixed_ref, rows_ref, out_ref)


def mode_grad_kernel(
    scale,
    block_ref,
    weight_ref,
    straight_ref,
    back_ref,
    pair_ref,
    out_ref,
    rows_ref,
    mixed_ref,
):
    count = rows_ref.shape[0] // 16
    rows_ref[...] = block_ref[...].astype(F32)
    low = lanes((64, 128)) < 64
    low16 = lanes((16, 128)) < 64
    row = sublanes((16, 128)) % 4
    upper = row < 2
    valid = lanes((16, 128)) // 64 == row % 2
    even = (sublanes((16, 128)) < 8).astype(BF16)
    odd = (sublanes((16, 128)) >= 8).astype(BF16)
    for j in range(16):
        section = rows_ref[pl.ds(j, count, stride=16), :]
        swapped = swap_halves(section)
        twice = jnp.concatenate(
            [jnp.where(low, section, swapped), jnp.where(low, swapped, section)], axis=1
        ).astype(BF16)
        turned = dot_nn(straight_ref[...], twice)
        for h in range(2):
            part = turned[:, h * 128 : (h + 1) * 128]
            pair_ref[2 * j + h] = jnp.where(low, part[:64], part[64:]).astype(BF16)
    for j in range(16):
        mixed = []
        for u in range(MX // 8):
            found = []
            for h in range(2):
                pair = pair_ref[2 * j + h, u * 16 : (u + 1) * 16, :]
                rows = dot_nt(
                    jnp.concatenate([pair * even, pair * odd], axis=1),
                    mode_pair(weight_ref, j, h, u),
                )
                found.append(jnp.where(valid, jnp.where(upper, rows[:, :128], rows[:, 128:]), 0.0))
            keep = jnp.where(low16, found[0], found[1])
            move = jnp.where(low16, found[1], found[0])
            mixed.append(keep + swap_halves(move))
        mixed_ref[j] = (jnp.concatenate(mixed, axis=0) * scale).astype(BF16)
    plane_sums(back_ref, mixed_ref, rows_ref, out_ref)


def weight_grad_kernel(scale, coeff_ref, pair_ref, out_hbm, out_ref, mask_ref, sems):
    lane = lanes((128, 128))
    part = sublanes((128, 128)) // 64
    for h in range(2):
        for t in range(MX // 4):
            mask_ref[h, t] = (
                (lane // 64 == h) & (lane % 64 // 8 == t) & (lane % 4 // 2 == part)
            ).astype(BF16)
    low = (lanes((64, 128)) < 64).astype(BF16)
    high = (lanes((64, 128)) >= 64).astype(BF16)
    pick = (lanes((64, 128)) % 64 == sublanes((64, 128))).astype(BF16)
    even = (sublanes((128, 128)) % 2 == 0).astype(BF16)
    odd = (sublanes((128, 128)) % 2 == 1).astype(BF16)

    @pl.loop(0, 16)
    def _(j):
        coeffs = coeff_ref[j]
        left = dot_nt(pick, jnp.concatenate([coeffs * low, coeffs * high], axis=0))
        left = (left * scale).astype(BF16)
        left = jnp.concatenate([left, left], axis=0)
        pair = jnp.concatenate([pair_ref[j * 2], pair_ref[j * 2 + 1]], axis=0)
        right = jnp.concatenate([pair * even, pair * odd], axis=1)
        for h in range(2):
            for t in range(MX // 4):
                four = dot_nn(left * mask_ref[h, t], right)
                mode = (j * 2 + h) * MX + 4 * t
                for k in range(4):
                    out_ref[mode + k] = four[
                        k // 2 * 64 : (k // 2 + 1) * 64, k % 2 * 128 : (k % 2 + 1) * 128
                    ].astype(BF16)
        part_copy(out_ref, out_hbm, sems, j, 2 * MX).start()

    for j in range(16):
        part_copy(out_ref, out_hbm, sems, j, 2 * MX).wait()


def params(mib):
    return pltpu.CompilerParams(vmem_limit_bytes=mib * 1024 * 1024)


def cost(flops, moved):
    return pl.CostEstimate(flops=int(flops), bytes_accessed=int(moved), transcendentals=0)


def fast_body(features, cotangent, spectral_weight, channel_weight, channel_bias):
    channels, planes, lines, depth_len = features.shape
    devices = lax.axis_size("gx")
    owned_modes = spectral_weight.shape[0]
    wave_pairs = MY * MZ
    volume = planes * devices * lines * depth_len
    forward_scale = 1.0 / math.sqrt(volume)
    inverse_scale = 1.0 / math.sqrt(MX * wave_pairs)
    weight_scale = math.sqrt(MX * wave_pairs / volume)
    table = {name: jnp.asarray(value) for name, value in tables(devices, lines, depth_len).items()}
    block_rows = devices * 64
    block_shape = jax.ShapeDtypeStruct((block_rows, 128), BF16)
    vmem = pl.BlockSpec(memory_space=pltpu.VMEM)
    hbm = pl.BlockSpec(memory_space=pltpu.HBM)
    smem = pl.BlockSpec(memory_space=pltpu.SMEM)
    field_scratch = pltpu.VMEM(features.shape, BF16)
    field_shape = jax.ShapeDtypeStruct(features.shape, BF16)

    def sems(count):
        return pltpu.SemaphoreType.DMA((count,))

    def scratch(name):
        return pltpu.VMEM(table[name].shape, BF16)

    def in_hbm(array):
        return pltpu.with_memory_space_constraint(array, pltpu.HBM)

    steps = channels // STEP
    lines_scratch = pltpu.VMEM((MZ, channels, 2 * planes * lines), F32)
    rows_scratch = pltpu.VMEM((block_rows, 128), F32)
    spec_scratch = pltpu.VMEM((channels // GROUP, MZ * GROUP, 128), F32)
    weight_rows = spectral_weight.reshape(owned_modes * channels, 2 * channels)
    field_bytes = features.size * 2

    def exchange(block):
        return lax.all_to_all(
            block.reshape(devices, 64, 128), "gx", 0, 0, tiled=True
        ).reshape(block_rows, 128)

    point_scratch = [
        field_scratch,
        field_scratch,
        pltpu.VMEM((channels * 16, channels * 16), BF16),
        sems(planes),
        sems(planes),
    ]

    block = pl.pallas_call(
        analysis_kernel,
        out_shape=block_shape,
        in_specs=[hbm, hbm, hbm],
        out_specs=vmem,
        scratch_shapes=[
            field_scratch,
            scratch("depth"),
            scratch("across_y"),
            lines_scratch,
            rows_scratch,
            sems(steps),
            sems(2),
        ],
        compiler_params=params(28),
        cost_estimate=cost(2 * 256 * 1024 * 1024, field_bytes),
        name="field_analysis",
    )(in_hbm(features), table["depth"], table["across_y"])
    pointwise, weight_rows = pl.pallas_call(
        load_and_point_kernel,
        out_shape=[
            pltpu.HBM(features.shape, BF16),
            pltpu.VMEM(weight_rows.shape, BF16),
        ],
        in_specs=[vmem, hbm, hbm],
        out_specs=[hbm, vmem],
        scratch_shapes=point_scratch + [sems(16)],
        compiler_params=params(28),
        cost_estimate=cost(2 * 1024**3, 2 * field_bytes + 2**24),
        name="channel_map",
    )(channel_weight, in_hbm(features), in_hbm(weight_rows))
    block, pointwise, weight_rows = lax.optimization_barrier(
        (exchange(block), pointwise, weight_rows)
    )
    weight_rows = pltpu.with_memory_space_constraint(weight_rows, pltpu.VMEM)

    mixed_scratch = pltpu.VMEM((16, 64, 128), BF16)
    coeffs, block = pl.pallas_call(
        functools.partial(mode_kernel, forward_scale),
        out_shape=[jax.ShapeDtypeStruct((16, 64, 128), BF16), block_shape],
        in_specs=[vmem, vmem, vmem, vmem, vmem],
        out_specs=[vmem, vmem],
        scratch_shapes=[
            rows_scratch,
            pltpu.VMEM((16, 2, 128, 256), BF16),
            mixed_scratch,
        ],
        compiler_params=params(24),
        cost_estimate=cost(256 * 2 * 16 * 256 * 128, 17 * 2**20),
        name="mode_product",
    )(block, weight_rows, table["both_x"], table["plain_x"], table["back_x"])
    block = exchange(block)

    activated, upstream, block = pl.pallas_call(
        functools.partial(middle_kernel, inverse_scale),
        out_shape=[field_shape, pltpu.HBM(features.shape, BF16), block_shape],
        in_specs=[vmem, smem, hbm, hbm, hbm, hbm, hbm],
        out_specs=[hbm, hbm, vmem],
        scratch_shapes=[
            field_scratch,
            field_scratch,
            scratch("depth"),
            scratch("across_y"),
            scratch("back_y"),
            field_scratch,
            field_scratch,
            lines_scratch,
            rows_scratch,
            spec_scratch,
            sems(steps),
            sems(steps),
            sems(steps),
            sems(steps),
            sems(3),
        ],
        compiler_params=params(VMEM_MIB),
        cost_estimate=cost(2**30, 4 * field_bytes),
        name="gelu_and_gradient",
    )(
        block,
        channel_bias,
        in_hbm(pointwise),
        in_hbm(cotangent),
        table["depth"],
        table["across_y"],
        table["back_y"],
    )
    channel_back = pl.pallas_call(
        functools.partial(point_kernel, True),
        out_shape=pltpu.HBM(features.shape, BF16),
        in_specs=[vmem, hbm],
        out_specs=hbm,
        scratch_shapes=point_scratch,
        compiler_params=params(28),
        cost_estimate=cost(2 * 1024**3, 2 * field_bytes),
        name="channel_map_back",
    )(channel_weight, in_hbm(upstream))
    block, channel_back = lax.optimization_barrier((exchange(block), channel_back))

    pairs, block = pl.pallas_call(
        functools.partial(mode_grad_kernel, forward_scale),
        out_shape=[jax.ShapeDtypeStruct((32, 64, 128), BF16), block_shape],
        in_specs=[vmem, vmem, vmem, vmem],
        out_specs=[vmem, vmem],
        scratch_shapes=[rows_scratch, mixed_scratch],
        compiler_params=params(24),
        cost_estimate=cost(256 * 2 * 16 * 256 * 128, 17 * 2**20),
        name="mode_gradient",
    )(block, weight_rows, table["straight_x"], table["back_x"])
    block = exchange(block)

    spectral_grad = pl.pallas_call(
        functools.partial(weight_grad_kernel, weight_scale),
        out_shape=jax.ShapeDtypeStruct(spectral_weight.shape, BF16),
        in_specs=[vmem, vmem],
        out_specs=hbm,
        scratch_shapes=[
            pltpu.VMEM(spectral_weight.shape, BF16),
            pltpu.VMEM((2, MX // 4, 128, 128), BF16),
            sems(16),
        ],
        compiler_params=params(VMEM_MIB),
        cost_estimate=cost(512 * 2 * 64 * 64 * 256, 17 * 2**20),
        name="weight_gradient",
    )(coeffs, pairs)

    feature_grad = pl.pallas_call(
        final_kernel,
        out_shape=field_shape,
        in_specs=[vmem, hbm, hbm, hbm],
        out_specs=hbm,
        scratch_shapes=[
            field_scratch,
            scratch("depth"),
            scratch("back_y"),
            field_scratch,
            rows_scratch,
            spec_scratch,
            sems(steps),
            sems(steps),
            sems(2),
        ],
        compiler_params=params(VMEM_MIB),
        cost_estimate=cost(2**29, 2 * field_bytes),
        name="field_gradient",
    )(block, in_hbm(channel_back), table["depth"], table["back_y"])
    return (activated, feature_grad, spectral_grad)


def body(features, cotangent, spectral_weight, channel_weight, channel_bias):
    channels, planes, lines, depth_len = features.shape
    devices = lax.axis_size("gx")
    fits = (
        (channels, planes, lines, depth_len) == (64, PLANES, 64, 128)
        and spectral_weight.shape[0] == 2 * MZ * MX
        and devices * 2 == MY
        and devices * 2 == MX
    )
    run = fast_body if fits else general_body
    return run(features, cotangent, spectral_weight, channel_weight, channel_bias)


def solution(mesh):
    in_specs = (
        P("grp", "gx", None, None),
        P("grp", "gx", None, None),
        P("gx", None, None),
        P(),
        P(),
    )
    out_specs = (
        P("grp", "gx", None, None),
        P("grp", "gx", None, None),
        P(("grp", "gx"), None, None),
    )
    return jax.shard_map(body, mesh=mesh, in_specs=in_specs, out_specs=out_specs, check_vma=False)
```

```python
import functools
import math

import jax
import jax.numpy as jnp
import ml_dtypes
import numpy as np
from jax import lax
from jax.experimental import pallas as pl
from jax.experimental.pallas import tpu as pltpu
from jax.sharding import PartitionSpec as P

MX = 32
MY = 32
MZ = 16


SQRT_TWO_PI = math.sqrt(2.0 / math.pi)
CUBIC_COEF = 0.044715


def freq_index(retained, length):
    ladder = jnp.arange(retained, dtype=jnp.int32)
    return jnp.where(ladder < retained // 2, ladder, length - retained + ladder)


def cos_sin(wavenum, length):
    points = jnp.arange(length, dtype=jnp.int32)
    angles = (wavenum[:, None] * points[None, :] % length).astype(jnp.float32) * (
        2.0 * math.pi / length
    )
    return (jnp.cos(angles), jnp.sin(angles))


def analysis_pair(wavenum, length):
    cosine, sine_wave = cos_sin(wavenum, length)
    cosine, sine_wave = (cosine.T, sine_wave.T)
    return jnp.stack(
        [jnp.stack([cosine, -sine_wave], 1), jnp.stack([sine_wave, cosine], 1)], 1
    ).astype(jnp.bfloat16)


def synthesis_pair(wavenum, length):
    cosine, sine_wave = cos_sin(wavenum, length)
    return jnp.stack(
        [jnp.stack([cosine, sine_wave], 1), jnp.stack([-sine_wave, cosine], 1)], 1
    ).astype(jnp.bfloat16)


def depth_table(retained, length):
    cosine, sine_wave = cos_sin(jnp.arange(retained, dtype=jnp.int32), length)
    return jnp.concatenate([cosine, -sine_wave], 0).astype(jnp.bfloat16)


def gelu_parts(inputs):
    cubed_in = inputs * inputs * inputs
    tangent = jnp.tanh(SQRT_TWO_PI * (inputs + CUBIC_COEF * cubed_in))
    output = 0.5 * inputs * (1.0 + tangent)
    derivative = 0.5 * (1.0 + tangent) + 0.5 * inputs * (1.0 - tangent * tangent) * SQRT_TWO_PI * (
        1.0 + 3.0 * CUBIC_COEF * inputs * inputs
    )
    return (output, derivative)


def mode_product(coeffs, weights, channels):
    stacked = coeffs.reshape(coeffs.shape[0], 2, channels)
    halves = jnp.einsum("mac,mcj->amj", stacked, weights, preferred_element_type=jnp.float32)
    real_out = halves[0, :, :channels] - halves[1, :, channels:]
    imag_out = halves[0, :, channels:] + halves[1, :, :channels]
    return jnp.concatenate([real_out, imag_out], 1).astype(jnp.bfloat16)


def mode_grads(coeffs, weights, grad_modes, channels, weight_scale, input_scale):
    number = coeffs.shape[0]
    stacked = coeffs.reshape(number, 2, channels)
    grad_pairs = grad_modes.reshape(number, 2, channels)
    real_w = jnp.einsum("mac,mao->mco", stacked, grad_pairs, preferred_element_type=jnp.float32)
    imag_w = jnp.einsum(
        "mc,mo->mco", stacked[:, 0], grad_pairs[:, 1], preferred_element_type=jnp.float32
    ) - jnp.einsum(
        "mc,mo->mco", stacked[:, 1], grad_pairs[:, 0], preferred_element_type=jnp.float32
    )
    weight_grad = (jnp.concatenate([real_w, imag_w], 2) * weight_scale).astype(jnp.bfloat16)
    straight = jnp.concatenate([grad_pairs[:, 0], grad_pairs[:, 1]], 1)
    rotated = jnp.concatenate([grad_pairs[:, 1], -grad_pairs[:, 0]], 1)
    real_x = jnp.einsum("mcj,mj->mc", weights, straight, preferred_element_type=jnp.float32)
    imag_x = jnp.einsum("mcj,mj->mc", weights, rotated, preferred_element_type=jnp.float32)
    input_grad = (jnp.concatenate([real_x, imag_x], 1) * input_scale).astype(jnp.bfloat16)
    return (weight_grad, input_grad)


def general_body(features, cotangent, spectral_weight, channel_weight, channel_bias):
    channels, planes, lines, depth_len = features.shape
    devices = lax.axis_size("gx")
    all_planes = planes * devices
    owned_modes = spectral_weight.shape[0]
    wave_pairs = MY * MZ
    forward_scale = 1.0 / math.sqrt(all_planes * lines * depth_len)
    inverse_scale = 1.0 / math.sqrt(MX * wave_pairs)
    weight_scale = math.sqrt(MX * wave_pairs / (all_planes * lines * depth_len))
    depth_basis = depth_table(MZ, depth_len)
    across_y = analysis_pair(freq_index(MY, lines), lines)
    back_y = synthesis_pair(freq_index(MY, lines), lines)
    across_full = analysis_pair(freq_index(MX, all_planes), all_planes)
    back_full = synthesis_pair(freq_index(MX, all_planes), all_planes)
    depth_part = jnp.dot(features, depth_basis.T, preferred_element_type=jnp.float32).astype(
        jnp.bfloat16
    )
    plane_part = (
        jnp.einsum(
            "cxyaz,yabk->cxbkz",
            depth_part.reshape(channels, planes, lines, 2, MZ),
            across_y,
            preferred_element_type=jnp.float32,
        )
        .astype(jnp.bfloat16)
        .reshape(channels, planes, 2, wave_pairs)
    )
    all_rows = lax.all_to_all(plane_part, "gx", split_axis=3, concat_axis=1, tiled=True)
    mode_sums = jnp.einsum(
        "cxaq,xabk->qkbc", all_rows, across_full, preferred_element_type=jnp.float32
    ).reshape(owned_modes, 2 * channels)
    coeffs = (mode_sums * forward_scale).astype(jnp.bfloat16)
    spectral = mode_product(coeffs, spectral_weight, channels)
    planes_all = jnp.einsum(
        "qkao,kabx->oxbq",
        spectral.reshape(owned_modes // MX, MX, 2, channels),
        back_full,
        preferred_element_type=jnp.float32,
    ).astype(jnp.bfloat16)
    planes_back = lax.all_to_all(planes_all, "gx", split_axis=1, concat_axis=3, tiled=True)
    lines_back = (
        jnp.einsum(
            "oxakz,kaby->oxybz",
            planes_back.reshape(channels, planes, 2, MY, MZ),
            back_y,
            preferred_element_type=jnp.float32,
        )
        .astype(jnp.bfloat16)
        .reshape(channels, planes, lines, 2 * MZ)
    )
    spectral_term = (
        jnp.dot(lines_back, depth_basis, preferred_element_type=jnp.float32) * inverse_scale
    )
    pointwise = jnp.einsum(
        "oc,cxyz->oxyz", channel_weight, features, preferred_element_type=jnp.float32
    )
    hidden = spectral_term + pointwise + channel_bias[:, None, None, None]
    activated, derivative = gelu_parts(hidden)
    upstream = (cotangent.astype(jnp.float32) * derivative).astype(jnp.bfloat16)
    lines_grad = (
        jnp.dot(upstream, depth_basis.T, preferred_element_type=jnp.float32) * inverse_scale
    ).astype(jnp.bfloat16)
    rows_grad = (
        jnp.einsum(
            "oxybz,kaby->oxakz",
            lines_grad.reshape(channels, planes, lines, 2, MZ),
            back_y,
            preferred_element_type=jnp.float32,
        )
        .astype(jnp.bfloat16)
        .reshape(channels, planes, 2, wave_pairs)
    )
    all_grads = lax.all_to_all(rows_grad, "gx", split_axis=3, concat_axis=1, tiled=True)
    grad_sums = jnp.einsum(
        "oxbq,kabx->qkao", all_grads, back_full, preferred_element_type=jnp.float32
    ).reshape(owned_modes, 2 * channels)
    grad_modes = grad_sums.astype(jnp.bfloat16)
    spectral_grad, coeff_grad = mode_grads(
        coeffs, spectral_weight, grad_modes, channels, weight_scale, forward_scale
    )
    plane_all = jnp.einsum(
        "qkbc,xabk->cxaq",
        coeff_grad.reshape(owned_modes // MX, MX, 2, channels),
        across_full,
        preferred_element_type=jnp.float32,
    ).astype(jnp.bfloat16)
    plane_grad = lax.all_to_all(plane_all, "gx", split_axis=1, concat_axis=3, tiled=True)
    depth_grad = (
        jnp.einsum(
            "cxbkz,yabk->cxyaz",
            plane_grad.reshape(channels, planes, 2, MY, MZ),
            across_y,
            preferred_element_type=jnp.float32,
        )
        .astype(jnp.bfloat16)
        .reshape(channels, planes, lines, 2 * MZ)
    )
    channel_back = jnp.einsum(
        "oc,oxyz->cxyz", channel_weight, upstream, preferred_element_type=jnp.float32
    )
    feature_grad = (
        jnp.dot(depth_grad, depth_basis, preferred_element_type=jnp.float32) + channel_back
    ).astype(jnp.bfloat16)
    return (activated.astype(jnp.bfloat16), feature_grad, spectral_grad)


PLANES = 2
GROUP = 8
STEP = 16
VMEM_MIB = 32
WIDE = jnp.bfloat16
NT = (((1,), (1,)), ((), ()))
F32 = jnp.float32
BF16 = jnp.bfloat16


def np_freq(retained, length):
    ladder = np.arange(retained)
    return np.where(ladder < retained // 2, ladder, length - retained + ladder)


def np_angles(wavenum, length):
    points = np.arange(length)
    return (wavenum[:, None] * points[None, :] % length) * (2.0 * math.pi / length)


def as_bf16(table):
    return np.asarray(table, np.float32).astype(ml_dtypes.bfloat16)


def rotation(angle, sign):
    cosine, sine_wave = np.cos(angle), sign * np.sin(angle)
    return np.stack([np.stack([cosine, -sine_wave]), np.stack([sine_wave, cosine])])


@functools.lru_cache(maxsize=None)
def tables(devices, lines, depth_len):
    planes_all = devices * PLANES
    angle = np_angles(np.arange(MZ), depth_len)
    depth = np.stack([np.cos(angle), -np.sin(angle)])
    eye = np.eye(GROUP)
    depth_block = np.einsum("akz,ij->akijz", depth, eye).reshape(2 * MZ * GROUP, GROUP * depth_len)
    plane_eye = np.eye(PLANES)
    angle = np_angles(np_freq(MY, lines), lines).reshape(devices, MY // devices, lines)
    across = np.einsum("badly,xw->ldbxawy", rotation(angle, -1.0), plane_eye)
    across = across.reshape(MY * 2 * PLANES, 2 * PLANES * lines)
    back = np.einsum("pbdly,xw->pxyldbw", rotation(angle, 1.0), plane_eye)
    back = back.reshape(2 * PLANES * lines, MY * 2 * PLANES)
    angle = np_angles(np_freq(MX, planes_all), planes_all).reshape(MX // 4, 4, devices, PLANES)
    forward = rotation(angle, -1.0)
    rows = np.einsum("batksx->tbksax", forward).reshape(MX // 4, 2, 4, devices * 2 * PLANES)
    plain = rows.reshape(2 * MX, -1)
    both = np.stack([rows, rows[:, ::-1]], 1).reshape(4 * MX, -1)
    turned = np.concatenate([rows[:, 1:], -rows[:, :1]], 1).reshape(2 * MX, -1)
    straight_rotated = np.concatenate([plain, turned], 0)
    inverse = np.einsum("batksx->sbxtak", rotation(angle, 1.0)).reshape(-1, 2 * MX)
    return {
        "depth": as_bf16(depth_block),
        "across_y": as_bf16(across),
        "back_y": as_bf16(back),
        "plain_x": as_bf16(plain),
        "both_x": as_bf16(both),
        "straight_x": as_bf16(straight_rotated),
        "back_x": as_bf16(inverse),
    }


def dot_nn(left, right):
    return jnp.dot(left, right, preferred_element_type=F32)


def dot_nt(left, right):
    return lax.dot_general(left, right, NT, preferred_element_type=F32)


def lanes(shape):
    return lax.broadcasted_iota(jnp.int32, shape, len(shape) - 1)


def sublanes(shape):
    return lax.broadcasted_iota(jnp.int32, shape, len(shape) - 2)


def swap_halves(block):
    return pltpu.roll(block, 64, 1)


def part_copy(source, target, sems, index, size):
    start = index * size if isinstance(index, int) else pl.multiple_of(index * size, size)
    part = pl.ds(start, size)
    return pltpu.make_async_copy(source.at[part], target.at[part], sems.at[index])


def start_parts(source, target, sems, size):
    for index in range(source.shape[0] // size):
        part_copy(source, target, sems, index, size).start()


def start_tables(pairs, sems):
    copies = []
    for index, (source, target) in enumerate(pairs):
        copy = pltpu.make_async_copy(source, target, sems.at[index])
        copy.start()
        copies.append(copy)
    return copies


def depth_analysis(slabs, depth, scale, group, lines_ref):
    wide = jnp.concatenate(slabs, axis=1)
    parts = dot_nt(depth, wide)
    if scale is not None:
        parts = parts * scale
    width = wide.shape[0]
    start = group * GROUP if isinstance(group, int) else pl.multiple_of(group * GROUP, GROUP)
    for a in range(2):
        lines_ref[:, pl.ds(start, GROUP), a * width : (a + 1) * width] = parts[
            a * MZ * GROUP : (a + 1) * MZ * GROUP
        ].reshape(MZ, GROUP, width)


def rows_analysis(lines_ref, across_ref, rows_ref, out_ref):
    channels, width = lines_ref.shape[1], lines_ref.shape[2]
    across = across_ref[...]
    half = across.shape[0] // 2
    for kzh in range(MZ // 2):
        pair = lines_ref[2 * kzh : 2 * kzh + 2].reshape(2 * channels, width).astype(BF16)
        rows = dot_nt(across, pair)
        for kyl in range(2):
            rows_ref[pl.ds(kyl * 8 + kzh, half, stride=16), :] = rows[
                kyl * half : (kyl + 1) * half
            ]
    out_ref[...] = rows_ref[...].astype(BF16)


def rows_gather(block_ref, rows_ref, spec_ref):
    rows_ref[...] = block_ref[...].astype(F32)
    count = rows_ref.shape[0] // 16
    eye = (sublanes((128, 128)) == lanes((128, 128))).astype(BF16)
    for kzh in range(MZ // 2):
        both = jnp.concatenate(
            [rows_ref[pl.ds(kyl * 8 + kzh, count, stride=16), :] for kyl in range(2)], axis=0
        ).astype(BF16)
        turned = dot_nt(eye, both)
        for h in range(2):
            spec_ref[:, (2 * kzh + h) * GROUP : (2 * kzh + h + 1) * GROUP, :] = turned[
                h * 64 : (h + 1) * 64
            ].reshape(8, GROUP, turned.shape[1])


def synthesis(groups, spec_ref, back, depth, scale):
    wide = []
    for group in groups:
        lines = dot_nt(back, spec_ref[group].astype(BF16))
        if scale is not None:
            lines = lines * scale
        lines = lines.astype(BF16)
        half = lines.shape[0] // 2
        wide.append(jnp.concatenate([lines[:half], lines[half:]], axis=1))
    return dot_nn(jnp.concatenate(wide, axis=0), depth)


def flat(slab):
    return slab.reshape(slab.shape[0] * slab.shape[1], slab.shape[2])


def analysis_kernel(
    field_hbm,
    depth_hbm,
    across_hbm,
    out_ref,
    field_ref,
    depth_ref,
    across_ref,
    lines_ref,
    rows_ref,
    field_sems,
    table_sems,
):
    first, second = start_tables([(depth_hbm, depth_ref), (across_hbm, across_ref)], table_sems)
    start_parts(field_hbm, field_ref, field_sems, STEP)
    first.wait()

    @pl.loop(0, field_ref.shape[0] // STEP)
    def _(step):
        part_copy(field_hbm, field_ref, field_sems, step, STEP).wait()
        for g in range(STEP // GROUP):
            group = step * (STEP // GROUP) + g
            slabs = [flat(field_ref[group * GROUP + ci]) for ci in range(GROUP)]
            depth_analysis(slabs, depth_ref[...], None, group, lines_ref)

    second.wait()
    rows_analysis(lines_ref, across_ref, rows_ref, out_ref)


def middle_kernel(
    inverse_scale,
    block_ref,
    bias_ref,
    point_hbm,
    cot_hbm,
    depth_hbm,
    across_hbm,
    back_hbm,
    act_hbm,
    up_hbm,
    out_ref,
    point_ref,
    cot_ref,
    depth_ref,
    across_ref,
    back_ref,
    act_ref,
    up_ref,
    lines_ref,
    rows_ref,
    spec_ref,
    wave_ref,
    point_sems,
    cot_sems,
    act_sems,
    up_sems,
    table_sems,
):
    tables_in = start_tables(
        [(back_hbm, back_ref), (depth_hbm, depth_ref), (across_hbm, across_ref)], table_sems
    )
    start_parts(point_hbm, point_ref, point_sems, STEP)
    start_parts(cot_hbm, cot_ref, cot_sems, STEP)
    rows_gather(block_ref, rows_ref, spec_ref)
    for copy in tables_in:
        copy.wait()
    steps = point_ref.shape[0] // STEP
    groups = point_ref.shape[0] // GROUP

    def synthesize(group):
        wave_ref[group % 2] = synthesis(
            [group], spec_ref, back_ref[...], depth_ref[...], inverse_scale
        )

    def activate(group):
        for oi in range(GROUP):
            index = group * GROUP + oi
            hidden = (
                wave_ref[group % 2, :, oi * 128 : (oi + 1) * 128]
                + flat(point_ref[index]).astype(F32)
                + bias_ref[index]
            )
            square = hidden * hidden
            gate = 0.5 + 0.5 * jnp.tanh(
                hidden * (SQRT_TWO_PI + (SQRT_TWO_PI * CUBIC_COEF) * square)
            )
            slope = hidden * (2.0 * SQRT_TWO_PI + (6.0 * SQRT_TWO_PI * CUBIC_COEF) * square)
            derivative = gate + (gate - gate * gate) * slope
            upstream = (flat(cot_ref[index]).astype(F32) * derivative).astype(BF16)
            act_ref[index] = (hidden * gate).astype(BF16).reshape(act_ref.shape[1:])
            up_ref[index] = upstream.reshape(up_ref.shape[1:])

    def analyse(group):
        slabs = [flat(up_ref[group * GROUP + oi]) for oi in range(GROUP)]
        depth_analysis(slabs, depth_ref[...], inverse_scale, group, lines_ref)

    synthesize(0)
    for group in range(groups + 1):
        if group % 2 == 0 and group < groups:
            part_copy(point_hbm, point_ref, point_sems, group // 2, STEP).wait()
            part_copy(cot_hbm, cot_ref, cot_sems, group // 2, STEP).wait()
        if group + 1 < groups:
            synthesize(group + 1)
        if group < groups:
            activate(group)
        if group > 0:
            analyse(group - 1)
        if group % 2 == 1:
            part_copy(act_ref, act_hbm, act_sems, group // 2, STEP).start()
            part_copy(up_ref, up_hbm, up_sems, group // 2, STEP).start()

    rows_analysis(lines_ref, across_ref, rows_ref, out_ref)
    for step in range(steps):
        part_copy(act_ref, act_hbm, act_sems, step, STEP).wait()
        part_copy(up_ref, up_hbm, up_sems, step, STEP).wait()


def final_kernel(
    block_ref,
    point_hbm,
    depth_hbm,
    back_hbm,
    out_hbm,
    point_ref,
    depth_ref,
    back_ref,
    out_ref,
    rows_ref,
    spec_ref,
    point_sems,
    out_sems,
    table_sems,
):
    tables_in = start_tables([(back_hbm, back_ref), (depth_hbm, depth_ref)], table_sems)
    start_parts(point_hbm, point_ref, point_sems, STEP)
    rows_gather(block_ref, rows_ref, spec_ref)
    for copy in tables_in:
        copy.wait()
    steps = point_ref.shape[0] // STEP

    @pl.loop(0, steps)
    def _(step):
        groups = [step * (STEP // GROUP) + g for g in range(STEP // GROUP)]
        spectral = synthesis(groups, spec_ref, back_ref[...], depth_ref[...], None)
        part_copy(point_hbm, point_ref, point_sems, step, STEP).wait()
        for g, group in enumerate(groups):
            for ci in range(GROUP):
                index = group * GROUP + ci
                total = spectral[
                    g * 128 : (g + 1) * 128, ci * 128 : (ci + 1) * 128
                ] + flat(point_ref[index]).astype(F32)
                out_ref[index] = total.astype(BF16).reshape(out_ref.shape[1:])
        part_copy(out_ref, out_hbm, out_sems, step, STEP).start()

    for step in range(steps):
        part_copy(out_ref, out_hbm, out_sems, step, STEP).wait()


def point_kernel(
    transposed, weight_ref, field_hbm, out_hbm, field_ref, out_ref, wide_ref, in_sems, out_sems
):
    size = wide_ref.shape[0]
    planes = field_ref.shape[1]
    copies = []
    for plane in range(planes):
        part = (slice(None), pl.ds(plane, 1))
        copy = pltpu.make_async_copy(field_hbm.at[part], field_ref.at[part], in_sems.at[plane])
        copy.start()
        copies.append(copy)
    tall = (sublanes((size, 64)) // 16 == lanes((size, 64))).astype(BF16)
    weight = weight_ref[...]
    left = dot_nt(tall, weight) if transposed else dot_nn(tall, weight)
    left = left.astype(BF16)
    rows = size // 4
    same = sublanes((rows, size)) % 16 == lanes((rows, size)) % 16
    for quarter in range(4):
        spread = dot_nt(left[quarter * rows : (quarter + 1) * rows], tall)
        wide_ref[quarter * rows : (quarter + 1) * rows, :] = jnp.where(same, spread, 0.0).astype(
            BF16
        )
    sends = []
    for plane in range(planes):
        copies[plane].wait()
        for pair in range(2):
            right = jnp.concatenate(
                [
                    field_ref[:, plane, yc * 16 : (yc + 1) * 16, :].reshape(size, 128)
                    for yc in (2 * pair, 2 * pair + 1)
                ],
                axis=1,
            )
            result = dot_nn(wide_ref[...], right).astype(BF16)
            for k in range(2):
                yc = 2 * pair + k
                out_ref[:, plane, yc * 16 : (yc + 1) * 16, :] = result[
                    :, k * 128 : (k + 1) * 128
                ].reshape(size // 16, 16, 128)
        part = (slice(None), pl.ds(plane, 1))
        copy = pltpu.make_async_copy(out_ref.at[part], out_hbm.at[part], out_sems.at[plane])
        copy.start()
        sends.append(copy)
    for copy in sends:
        copy.wait()


def start_weights(weight_hbm, weight_ref, sems):
    copies = []
    for j in range(16):
        rows = weight_ref.shape[0] // 16
        part = pl.ds(j * rows, rows)
        copy = pltpu.make_async_copy(weight_hbm.at[part], weight_ref.at[part], sems.at[j])
        copy.start()
        copies.append(copy)
    return copies


def mode_pair(weight_ref, j, h, u):
    start = ((j * 2 + h) * MX + 8 * u) * 64
    return jnp.concatenate(
        [weight_ref[start : start + 256, :], weight_ref[start + 256 : start + 512, :]], axis=1
    )


def plane_sums(back_ref, mixed_ref, res_ref, quarter):
    count = res_ref.shape[0] // 16
    wide = jnp.concatenate([mixed_ref[quarter * 4 + k] for k in range(4)], axis=1)
    rows = dot_nn(back_ref[...], wide)
    for k in range(4):
        res_ref[pl.ds(quarter * 4 + k, count, stride=16), :] = rows[:, k * 128 : (k + 1) * 128]


def mode_kernel(
    scale,
    block_ref,
    weight_hbm,
    both_ref,
    plain_ref,
    back_ref,
    coeff_ref,
    out_ref,
    weight_ref,
    rows_ref,
    res_ref,
    left_ref,
    mixed_ref,
    sems,
):
    copies = start_weights(weight_hbm, weight_ref, sems)
    count = rows_ref.shape[0] // 16
    rows_ref[...] = block_ref[...].astype(F32)
    low = lanes((128, 128)) < 64
    kxl = sublanes((128, 128)) % 4
    half = lanes((128, 128)) // 64
    first = (kxl == half).astype(BF16)
    second = (kxl == 2 + half).astype(BF16)
    low8 = lanes((8, 128)) < 64
    sign = jnp.where(sublanes((8, 128)) < 4, -1.0, 1.0)
    for quarter in range(4):
        wide = jnp.concatenate(
            [rows_ref[pl.ds(quarter * 4 + k, count, stride=16), :] for k in range(4)], axis=1
        ).astype(BF16)
        plain = (dot_nn(plain_ref[...], wide) * scale).astype(BF16)
        both = dot_nn(both_ref[...], wide) * scale
        for k in range(4):
            j = quarter * 4 + k
            coeff_ref[j] = plain[:, k * 128 : (k + 1) * 128]
            coeffs = both[:, k * 128 : (k + 1) * 128]
            swapped = swap_halves(coeffs)
            for h in range(2):
                twice = jnp.where(low if h == 0 else ~low, coeffs, swapped).astype(BF16)
                left_ref[j, h] = jnp.concatenate([twice * first, twice * second], axis=1)
    for j in range(16):
        if j % 4 == 0:
            for copy in copies[j : j + 4]:
                copy.wait()
        mixed = []
        for u in range(MX // 8):
            halves = [
                dot_nn(left_ref[j, h, u * 32 : (u + 1) * 32, :], mode_pair(weight_ref, j, h, u))
                for h in range(2)
            ]
            for t in range(2):
                low_h, high_h = [
                    part[t * 16 : (t + 1) * 16, t * 128 : (t + 1) * 128] for part in halves
                ]
                keep = jnp.where(low8, low_h[:8], sign * high_h[8:])
                move = jnp.where(low8, high_h[:8], sign * low_h[8:])
                mixed.append(keep + swap_halves(move))
        mixed_ref[j] = jnp.concatenate(mixed, axis=0).astype(BF16)
        if j % 4 == 3:
            plane_sums(back_ref, mixed_ref, res_ref, j // 4)
    out_ref[...] = res_ref[...].astype(BF16)


def mode_grad_kernel(
    scale,
    block_ref,
    weight_hbm,
    straight_ref,
    back_ref,
    pair_ref,
    out_ref,
    weight_ref,
    rows_ref,
    res_ref,
    mixed_ref,
    sems,
):
    copies = start_weights(weight_hbm, weight_ref, sems)
    count = rows_ref.shape[0] // 16
    rows_ref[...] = block_ref[...].astype(F32)
    low = lanes((64, 128)) < 64
    low16 = lanes((16, 128)) < 64
    row = sublanes((16, 128)) % 4
    upper = row < 2
    valid = lanes((16, 128)) // 64 == row % 2
    even = (sublanes((16, 128)) < 8).astype(BF16)
    odd = (sublanes((16, 128)) >= 8).astype(BF16)
    for j in range(16):
        section = rows_ref[pl.ds(j, count, stride=16), :]
        swapped = swap_halves(section)
        twice = jnp.concatenate(
            [jnp.where(low, section, swapped), jnp.where(low, swapped, section)], axis=1
        ).astype(BF16)
        turned = dot_nn(straight_ref[...], twice)
        for h in range(2):
            part = turned[:, h * 128 : (h + 1) * 128]
            pair_ref[2 * j + h] = jnp.where(low, part[:64], part[64:]).astype(BF16)
    for j in range(16):
        if j % 4 == 0:
            for copy in copies[j : j + 4]:
                copy.wait()
        mixed = []
        for u in range(MX // 8):
            found = []
            for h in range(2):
                pair = pair_ref[2 * j + h, u * 16 : (u + 1) * 16, :]
                rows = dot_nt(
                    jnp.concatenate([pair * even, pair * odd], axis=1),
                    mode_pair(weight_ref, j, h, u),
                )
                found.append(jnp.where(valid, jnp.where(upper, rows[:, :128], rows[:, 128:]), 0.0))
            keep = jnp.where(low16, found[0], found[1])
            move = jnp.where(low16, found[1], found[0])
            mixed.append(keep + swap_halves(move))
        mixed_ref[j] = (jnp.concatenate(mixed, axis=0) * scale).astype(BF16)
        if j % 4 == 3:
            plane_sums(back_ref, mixed_ref, res_ref, j // 4)
    out_ref[...] = res_ref[...].astype(BF16)


def weight_grad_kernel(scale, coeff_ref, pair_ref, out_hbm, out_ref, pairs_ref, sems):
    low = (lanes((64, 128)) < 64).astype(BF16)
    high = (lanes((64, 128)) >= 64).astype(BF16)
    pick = (lanes((64, 128)) % 64 == sublanes((64, 128))).astype(BF16)

    @pl.loop(0, 16)
    def _(j):
        coeffs = coeff_ref[j]
        left = dot_nt(pick, jnp.concatenate([coeffs * low, coeffs * high], axis=0))
        left = (left * scale).astype(WIDE)
        for h in range(2):
            pairs_ref[...] = pair_ref[j * 2 + h].astype(F32)
            for t in range(MX // 4):
                for k in range(4):
                    total = None
                    for b in range(2):
                        at = t * 8 + b * 4 + k
                        column = jnp.broadcast_to(
                            left[:, h * 64 + at : h * 64 + at + 1], (64, 128)
                        )
                        row = jnp.broadcast_to(pairs_ref[at : at + 1, :], (64, 128)).astype(WIDE)
                        total = column * row if total is None else total + column * row
                    out_ref[(j * 2 + h) * MX + 4 * t + k] = total.astype(BF16)
        part_copy(out_ref, out_hbm, sems, j, 2 * MX).start()

    for j in range(16):
        part_copy(out_ref, out_hbm, sems, j, 2 * MX).wait()


def params(mib):
    return pltpu.CompilerParams(vmem_limit_bytes=mib * 1024 * 1024)


def cost(flops, moved):
    return pl.CostEstimate(flops=int(flops), bytes_accessed=int(moved), transcendentals=0)


def fast_body(features, cotangent, spectral_weight, channel_weight, channel_bias):
    channels, planes, lines, depth_len = features.shape
    devices = lax.axis_size("gx")
    owned_modes = spectral_weight.shape[0]
    wave_pairs = MY * MZ
    volume = planes * devices * lines * depth_len
    forward_scale = 1.0 / math.sqrt(volume)
    inverse_scale = 1.0 / math.sqrt(MX * wave_pairs)
    weight_scale = math.sqrt(MX * wave_pairs / volume)
    table = {name: jnp.asarray(value) for name, value in tables(devices, lines, depth_len).items()}
    for name in ("depth", "across_y", "back_y"):
        table[name] = pltpu.with_memory_space_constraint(table[name], pltpu.HBM)
    block_rows = devices * 64
    block_shape = jax.ShapeDtypeStruct((block_rows, 128), BF16)
    vmem = pl.BlockSpec(memory_space=pltpu.VMEM)
    hbm = pl.BlockSpec(memory_space=pltpu.HBM)
    smem = pl.BlockSpec(memory_space=pltpu.SMEM)
    field_scratch = pltpu.VMEM(features.shape, BF16)
    field_shape = jax.ShapeDtypeStruct(features.shape, BF16)

    def sems(count):
        return pltpu.SemaphoreType.DMA((count,))

    def scratch(name):
        return pltpu.VMEM(table[name].shape, BF16)

    def in_hbm(array):
        return pltpu.with_memory_space_constraint(array, pltpu.HBM)

    steps = channels // STEP
    lines_scratch = pltpu.VMEM((MZ, channels, 2 * planes * lines), F32)
    rows_scratch = pltpu.VMEM((block_rows, 128), F32)
    spec_scratch = pltpu.VMEM((channels // GROUP, MZ * GROUP, 128), F32)
    weight_rows = pltpu.with_memory_space_constraint(
        spectral_weight.reshape(owned_modes * channels, 2 * channels), pltpu.HBM
    )
    field_bytes = features.size * 2

    def exchange(block):
        return lax.all_to_all(
            block.reshape(devices, 64, 128), "gx", 0, 0, tiled=True
        ).reshape(block_rows, 128)

    def point(field, transposed):
        return pl.pallas_call(
            functools.partial(point_kernel, transposed),
            out_shape=pltpu.HBM(features.shape, BF16),
            in_specs=[vmem, hbm],
            out_specs=hbm,
            scratch_shapes=[
                field_scratch,
                field_scratch,
                pltpu.VMEM((channels * 16, channels * 16), BF16),
                sems(planes),
                sems(planes),
            ],
            compiler_params=params(VMEM_MIB),
            cost_estimate=cost(2 * 1024**3, 2 * field_bytes),
            name="channel_map_back" if transposed else "channel_map",
        )(channel_weight, in_hbm(field))

    block = pl.pallas_call(
        analysis_kernel,
        out_shape=block_shape,
        in_specs=[hbm, hbm, hbm],
        out_specs=vmem,
        scratch_shapes=[
            field_scratch,
            scratch("depth"),
            scratch("across_y"),
            lines_scratch,
            rows_scratch,
            sems(steps),
            sems(2),
        ],
        compiler_params=params(VMEM_MIB),
        cost_estimate=cost(2 * 256 * 1024 * 1024, field_bytes),
        name="field_analysis",
    )(in_hbm(features), table["depth"], table["across_y"])
    block, pointwise = lax.optimization_barrier((exchange(block), point(features, False)))

    weight_scratch = pltpu.VMEM(weight_rows.shape, BF16)
    mixed_scratch = pltpu.VMEM((16, 64, 128), BF16)
    weight_sems = sems(16)
    coeffs, block = pl.pallas_call(
        functools.partial(mode_kernel, forward_scale),
        out_shape=[jax.ShapeDtypeStruct((16, 64, 128), BF16), block_shape],
        in_specs=[vmem, hbm, vmem, vmem, vmem],
        out_specs=[vmem, vmem],
        scratch_shapes=[
            weight_scratch,
            rows_scratch,
            rows_scratch,
            pltpu.VMEM((16, 2, 128, 256), BF16),
            mixed_scratch,
            weight_sems,
        ],
        compiler_params=params(VMEM_MIB),
        cost_estimate=cost(256 * 2 * 16 * 256 * 128, 17 * 2**20),
        name="mode_product",
    )(block, weight_rows, table["both_x"], table["plain_x"], table["back_x"])
    block = exchange(block)

    activated, upstream, block = pl.pallas_call(
        functools.partial(middle_kernel, inverse_scale),
        out_shape=[field_shape, pltpu.HBM(features.shape, BF16), block_shape],
        in_specs=[vmem, smem, hbm, hbm, hbm, hbm, hbm],
        out_specs=[hbm, hbm, vmem],
        scratch_shapes=[
            field_scratch,
            field_scratch,
            scratch("depth"),
            scratch("across_y"),
            scratch("back_y"),
            field_scratch,
            field_scratch,
            lines_scratch,
            rows_scratch,
            spec_scratch,
            pltpu.VMEM((2, planes * lines, GROUP * depth_len), F32),
            sems(steps),
            sems(steps),
            sems(steps),
            sems(steps),
            sems(3),
        ],
        compiler_params=params(VMEM_MIB),
        cost_estimate=cost(2**30, 4 * field_bytes),
        name="gelu_and_gradient",
    )(
        block,
        channel_bias,
        in_hbm(pointwise),
        in_hbm(cotangent),
        table["depth"],
        table["across_y"],
        table["back_y"],
    )
    block = exchange(block)
    block, channel_back = lax.optimization_barrier((block, point(upstream, True)))

    pairs, block = pl.pallas_call(
        functools.partial(mode_grad_kernel, forward_scale),
        out_shape=[jax.ShapeDtypeStruct((32, 64, 128), BF16), block_shape],
        in_specs=[vmem, hbm, vmem, vmem],
        out_specs=[vmem, vmem],
        scratch_shapes=[weight_scratch, rows_scratch, rows_scratch, mixed_scratch, weight_sems],
        compiler_params=params(VMEM_MIB),
        cost_estimate=cost(256 * 2 * 16 * 256 * 128, 17 * 2**20),
        name="mode_gradient",
    )(block, weight_rows, table["straight_x"], table["back_x"])
    block = exchange(block)

    spectral_grad = pl.pallas_call(
        functools.partial(weight_grad_kernel, weight_scale),
        out_shape=jax.ShapeDtypeStruct(spectral_weight.shape, BF16),
        in_specs=[vmem, vmem],
        out_specs=hbm,
        scratch_shapes=[
            pltpu.VMEM(spectral_weight.shape, BF16),
            pltpu.VMEM((64, 128), F32),
            sems(16),
        ],
        compiler_params=params(VMEM_MIB),
        cost_estimate=cost(512 * 2 * 64 * 64 * 256, 17 * 2**20),
        name="weight_gradient",
    )(coeffs, pairs)

    feature_grad = pl.pallas_call(
        final_kernel,
        out_shape=field_shape,
        in_specs=[vmem, hbm, hbm, hbm],
        out_specs=hbm,
        scratch_shapes=[
            field_scratch,
            scratch("depth"),
            scratch("back_y"),
            field_scratch,
            rows_scratch,
            spec_scratch,
            sems(steps),
            sems(steps),
            sems(2),
        ],
        compiler_params=params(VMEM_MIB),
        cost_estimate=cost(2**29, 2 * field_bytes),
        name="field_gradient",
    )(block, in_hbm(channel_back), table["depth"], table["back_y"])
    return (activated, feature_grad, spectral_grad)


def body(features, cotangent, spectral_weight, channel_weight, channel_bias):
    channels, planes, lines, depth_len = features.shape
    devices = lax.axis_size("gx")
    fits = (
        (channels, planes, lines, depth_len) == (64, PLANES, 64, 128)
        and spectral_weight.shape[0] == 2 * MZ * MX
        and devices * 2 == MY
        and devices * 2 == MX
    )
    run = fast_body if fits else general_body
    return run(features, cotangent, spectral_weight, channel_weight, channel_bias)


def solution(mesh):
    in_specs = (
        P("grp", "gx", None, None),
        P("grp", "gx", None, None),
        P("gx", None, None),
        P(),
        P(),
    )
    out_specs = (
        P("grp", "gx", None, None),
        P("grp", "gx", None, None),
        P(("grp", "gx"), None, None),
    )
    return jax.shard_map(body, mesh=mesh, in_specs=in_specs, out_specs=out_specs, check_vma=False)
```

```python
import functools
import math

import jax
import jax.numpy as jnp
import ml_dtypes
import numpy as np
from jax import lax
from jax.experimental import pallas as pl
from jax.experimental.pallas import tpu as pltpu
from jax.sharding import PartitionSpec as P

MX = 32
MY = 32
MZ = 16


SQRT_TWO_PI = math.sqrt(2.0 / math.pi)
CUBIC_COEF = 0.044715


def freq_index(retained, length):
    ladder = jnp.arange(retained, dtype=jnp.int32)
    return jnp.where(ladder < retained // 2, ladder, length - retained + ladder)


def cos_sin(wavenum, length):
    points = jnp.arange(length, dtype=jnp.int32)
    angles = (wavenum[:, None] * points[None, :] % length).astype(jnp.float32) * (
        2.0 * math.pi / length
    )
    return (jnp.cos(angles), jnp.sin(angles))


def analysis_pair(wavenum, length):
    cosine, sine_wave = cos_sin(wavenum, length)
    cosine, sine_wave = (cosine.T, sine_wave.T)
    return jnp.stack(
        [jnp.stack([cosine, -sine_wave], 1), jnp.stack([sine_wave, cosine], 1)], 1
    ).astype(jnp.bfloat16)


def synthesis_pair(wavenum, length):
    cosine, sine_wave = cos_sin(wavenum, length)
    return jnp.stack(
        [jnp.stack([cosine, sine_wave], 1), jnp.stack([-sine_wave, cosine], 1)], 1
    ).astype(jnp.bfloat16)


def depth_table(retained, length):
    cosine, sine_wave = cos_sin(jnp.arange(retained, dtype=jnp.int32), length)
    return jnp.concatenate([cosine, -sine_wave], 0).astype(jnp.bfloat16)


def gelu_parts(inputs):
    cubed_in = inputs * inputs * inputs
    tangent = jnp.tanh(SQRT_TWO_PI * (inputs + CUBIC_COEF * cubed_in))
    output = 0.5 * inputs * (1.0 + tangent)
    derivative = 0.5 * (1.0 + tangent) + 0.5 * inputs * (1.0 - tangent * tangent) * SQRT_TWO_PI * (
        1.0 + 3.0 * CUBIC_COEF * inputs * inputs
    )
    return (output, derivative)


def mode_product(coeffs, weights, channels):
    stacked = coeffs.reshape(coeffs.shape[0], 2, channels)
    halves = jnp.einsum("mac,mcj->amj", stacked, weights, preferred_element_type=jnp.float32)
    real_out = halves[0, :, :channels] - halves[1, :, channels:]
    imag_out = halves[0, :, channels:] + halves[1, :, :channels]
    return jnp.concatenate([real_out, imag_out], 1).astype(jnp.bfloat16)


def mode_grads(coeffs, weights, grad_modes, channels, weight_scale, input_scale):
    number = coeffs.shape[0]
    stacked = coeffs.reshape(number, 2, channels)
    grad_pairs = grad_modes.reshape(number, 2, channels)
    real_w = jnp.einsum("mac,mao->mco", stacked, grad_pairs, preferred_element_type=jnp.float32)
    imag_w = jnp.einsum(
        "mc,mo->mco", stacked[:, 0], grad_pairs[:, 1], preferred_element_type=jnp.float32
    ) - jnp.einsum(
        "mc,mo->mco", stacked[:, 1], grad_pairs[:, 0], preferred_element_type=jnp.float32
    )
    weight_grad = (jnp.concatenate([real_w, imag_w], 2) * weight_scale).astype(jnp.bfloat16)
    straight = jnp.concatenate([grad_pairs[:, 0], grad_pairs[:, 1]], 1)
    rotated = jnp.concatenate([grad_pairs[:, 1], -grad_pairs[:, 0]], 1)
    real_x = jnp.einsum("mcj,mj->mc", weights, straight, preferred_element_type=jnp.float32)
    imag_x = jnp.einsum("mcj,mj->mc", weights, rotated, preferred_element_type=jnp.float32)
    input_grad = (jnp.concatenate([real_x, imag_x], 1) * input_scale).astype(jnp.bfloat16)
    return (weight_grad, input_grad)


def general_body(features, cotangent, spectral_weight, channel_weight, channel_bias):
    channels, planes, lines, depth_len = features.shape
    devices = lax.axis_size("gx")
    all_planes = planes * devices
    owned_modes = spectral_weight.shape[0]
    wave_pairs = MY * MZ
    forward_scale = 1.0 / math.sqrt(all_planes * lines * depth_len)
    inverse_scale = 1.0 / math.sqrt(MX * wave_pairs)
    weight_scale = math.sqrt(MX * wave_pairs / (all_planes * lines * depth_len))
    depth_basis = depth_table(MZ, depth_len)
    across_y = analysis_pair(freq_index(MY, lines), lines)
    back_y = synthesis_pair(freq_index(MY, lines), lines)
    across_full = analysis_pair(freq_index(MX, all_planes), all_planes)
    back_full = synthesis_pair(freq_index(MX, all_planes), all_planes)
    depth_part = jnp.dot(features, depth_basis.T, preferred_element_type=jnp.float32).astype(
        jnp.bfloat16
    )
    plane_part = (
        jnp.einsum(
            "cxyaz,yabk->cxbkz",
            depth_part.reshape(channels, planes, lines, 2, MZ),
            across_y,
            preferred_element_type=jnp.float32,
        )
        .astype(jnp.bfloat16)
        .reshape(channels, planes, 2, wave_pairs)
    )
    all_rows = lax.all_to_all(plane_part, "gx", split_axis=3, concat_axis=1, tiled=True)
    mode_sums = jnp.einsum(
        "cxaq,xabk->qkbc", all_rows, across_full, preferred_element_type=jnp.float32
    ).reshape(owned_modes, 2 * channels)
    coeffs = (mode_sums * forward_scale).astype(jnp.bfloat16)
    spectral = mode_product(coeffs, spectral_weight, channels)
    planes_all = jnp.einsum(
        "qkao,kabx->oxbq",
        spectral.reshape(owned_modes // MX, MX, 2, channels),
        back_full,
        preferred_element_type=jnp.float32,
    ).astype(jnp.bfloat16)
    planes_back = lax.all_to_all(planes_all, "gx", split_axis=1, concat_axis=3, tiled=True)
    lines_back = (
        jnp.einsum(
            "oxakz,kaby->oxybz",
            planes_back.reshape(channels, planes, 2, MY, MZ),
            back_y,
            preferred_element_type=jnp.float32,
        )
        .astype(jnp.bfloat16)
        .reshape(channels, planes, lines, 2 * MZ)
    )
    spectral_term = (
        jnp.dot(lines_back, depth_basis, preferred_element_type=jnp.float32) * inverse_scale
    )
    pointwise = jnp.einsum(
        "oc,cxyz->oxyz", channel_weight, features, preferred_element_type=jnp.float32
    )
    hidden = spectral_term + pointwise + channel_bias[:, None, None, None]
    activated, derivative = gelu_parts(hidden)
    upstream = (cotangent.astype(jnp.float32) * derivative).astype(jnp.bfloat16)
    lines_grad = (
        jnp.dot(upstream, depth_basis.T, preferred_element_type=jnp.float32) * inverse_scale
    ).astype(jnp.bfloat16)
    rows_grad = (
        jnp.einsum(
            "oxybz,kaby->oxakz",
            lines_grad.reshape(channels, planes, lines, 2, MZ),
            back_y,
            preferred_element_type=jnp.float32,
        )
        .astype(jnp.bfloat16)
        .reshape(channels, planes, 2, wave_pairs)
    )
    all_grads = lax.all_to_all(rows_grad, "gx", split_axis=3, concat_axis=1, tiled=True)
    grad_sums = jnp.einsum(
        "oxbq,kabx->qkao", all_grads, back_full, preferred_element_type=jnp.float32
    ).reshape(owned_modes, 2 * channels)
    grad_modes = grad_sums.astype(jnp.bfloat16)
    spectral_grad, coeff_grad = mode_grads(
        coeffs, spectral_weight, grad_modes, channels, weight_scale, forward_scale
    )
    plane_all = jnp.einsum(
        "qkbc,xabk->cxaq",
        coeff_grad.reshape(owned_modes // MX, MX, 2, channels),
        across_full,
        preferred_element_type=jnp.float32,
    ).astype(jnp.bfloat16)
    plane_grad = lax.all_to_all(plane_all, "gx", split_axis=1, concat_axis=3, tiled=True)
    depth_grad = (
        jnp.einsum(
            "cxbkz,yabk->cxyaz",
            plane_grad.reshape(channels, planes, 2, MY, MZ),
            across_y,
            preferred_element_type=jnp.float32,
        )
        .astype(jnp.bfloat16)
        .reshape(channels, planes, lines, 2 * MZ)
    )
    channel_back = jnp.einsum(
        "oc,oxyz->cxyz", channel_weight, upstream, preferred_element_type=jnp.float32
    )
    feature_grad = (
        jnp.dot(depth_grad, depth_basis, preferred_element_type=jnp.float32) + channel_back
    ).astype(jnp.bfloat16)
    return (activated.astype(jnp.bfloat16), feature_grad, spectral_grad)


PLANES = 2
GROUP = 8
STEP = 16
VMEM_MIB = 32
VECTOR = 2
NT = (((1,), (1,)), ((), ()))
F32 = jnp.float32
BF16 = jnp.bfloat16


def np_freq(retained, length):
    ladder = np.arange(retained)
    return np.where(ladder < retained // 2, ladder, length - retained + ladder)


def np_angles(wavenum, length):
    points = np.arange(length)
    return (wavenum[:, None] * points[None, :] % length) * (2.0 * math.pi / length)


def as_bf16(table):
    return np.asarray(table, np.float32).astype(ml_dtypes.bfloat16)


def rotation(angle, sign):
    cosine, sine_wave = np.cos(angle), sign * np.sin(angle)
    return np.stack([np.stack([cosine, -sine_wave]), np.stack([sine_wave, cosine])])


@functools.lru_cache(maxsize=None)
def tables(devices, lines, depth_len):
    planes_all = devices * PLANES
    angle = np_angles(np.arange(MZ), depth_len)
    depth = np.stack([np.cos(angle), -np.sin(angle)])
    eye = np.eye(GROUP)
    depth_block = np.einsum("akz,ij->akijz", depth, eye).reshape(2 * MZ * GROUP, GROUP * depth_len)
    depth_pair = np.einsum("akz,ij->iakjz", depth, np.eye(2)).reshape(4 * MZ, 2 * depth_len)
    plane_eye = np.eye(PLANES)
    angle = np_angles(np_freq(MY, lines), lines).reshape(devices, MY // devices, lines)
    across = np.einsum("badly,xw->ldbxawy", rotation(angle, -1.0), plane_eye)
    across = across.reshape(MY * 2 * PLANES, 2 * PLANES * lines)
    back = np.einsum("pbdly,xw->pxyldbw", rotation(angle, 1.0), plane_eye)
    back = back.reshape(2 * PLANES * lines, MY * 2 * PLANES)
    angle = np_angles(np_freq(MX, planes_all), planes_all).reshape(MX // 4, 4, devices, PLANES)
    forward = rotation(angle, -1.0)
    rows = np.einsum("batksx->tbksax", forward).reshape(MX // 4, 2, 4, devices * 2 * PLANES)
    plain = rows.reshape(2 * MX, -1)
    both = np.stack([rows, rows[:, ::-1]], 1).reshape(4 * MX, -1)
    turned = np.concatenate([rows[:, 1:], -rows[:, :1]], 1).reshape(2 * MX, -1)
    straight_rotated = np.concatenate([plain, turned], 0)
    inverse = np.einsum("batksx->sbxtak", rotation(angle, 1.0)).reshape(-1, 2 * MX)
    return {
        "depth": as_bf16(depth_block),
        "depth_pair": as_bf16(depth_pair),
        "across_y": as_bf16(across),
        "back_y": as_bf16(back),
        "plain_x": as_bf16(plain),
        "both_x": as_bf16(both),
        "straight_x": as_bf16(straight_rotated),
        "back_x": as_bf16(inverse),
    }


def dot_nn(left, right):
    return jnp.dot(left, right, preferred_element_type=F32)


def dot_nt(left, right):
    return lax.dot_general(left, right, NT, preferred_element_type=F32)


def lanes(shape):
    return lax.broadcasted_iota(jnp.int32, shape, len(shape) - 1)


def sublanes(shape):
    return lax.broadcasted_iota(jnp.int32, shape, len(shape) - 2)


def swap_halves(block):
    return pltpu.roll(block, 64, 1)


def part_copy(source, target, sems, index, size):
    start = index * size if isinstance(index, int) else pl.multiple_of(index * size, size)
    part = pl.ds(start, size)
    return pltpu.make_async_copy(source.at[part], target.at[part], sems.at[index])


def start_parts(source, target, sems, size):
    for index in range(source.shape[0] // size):
        part_copy(source, target, sems, index, size).start()


def start_tables(pairs, sems):
    copies = []
    for index, (source, target) in enumerate(pairs):
        copy = pltpu.make_async_copy(source, target, sems.at[index])
        copy.start()
        copies.append(copy)
    return copies


def depth_analysis(slabs, depth_pair, scale, group, lines_ref):
    for quad in range(2):
        four = slabs[quad * 4 : quad * 4 + 4]
        wide = jnp.concatenate(
            [jnp.concatenate(four[2 * pair : 2 * pair + 2], axis=1) for pair in range(2)], axis=0
        )
        parts = dot_nt(depth_pair, wide)
        if scale is not None:
            parts = parts * scale
        half = wide.shape[0] // 2
        for pair in range(2):
            start = (group * GROUP + quad * 4 + pair * 2) * 2 * MZ
            if not isinstance(start, int):
                start = pl.multiple_of(start, 4 * MZ)
            lines_ref[pl.ds(start, 4 * MZ), :] = parts[:, pair * half : (pair + 1) * half]


def rows_analysis(lines_ref, across_ref, rows_ref, out_ref):
    channels = lines_ref.shape[0] // (2 * MZ)
    across = across_ref[...]
    half = across.shape[0] // 2
    for kzh in range(MZ // 2):
        pair = jnp.concatenate(
            [
                jnp.concatenate(
                    [
                        lines_ref[pl.ds(a * MZ + 2 * kzh + h, channels, stride=2 * MZ), :]
                        for a in range(2)
                    ],
                    axis=1,
                )
                for h in range(2)
            ],
            axis=0,
        ).astype(BF16)
        rows = dot_nt(across, pair)
        for kyl in range(2):
            rows_ref[pl.ds(kyl * 8 + kzh, half, stride=16), :] = rows[
                kyl * half : (kyl + 1) * half
            ]
    out_ref[...] = rows_ref[...].astype(BF16)


def rows_gather(block_ref, rows_ref, spec_ref):
    rows_ref[...] = block_ref[...].astype(F32)
    count = rows_ref.shape[0] // 16
    eye = (sublanes((128, 128)) == lanes((128, 128))).astype(BF16)
    for kzh in range(MZ // 2):
        both = jnp.concatenate(
            [rows_ref[pl.ds(kyl * 8 + kzh, count, stride=16), :] for kyl in range(2)], axis=0
        ).astype(BF16)
        turned = dot_nt(eye, both)
        for h in range(2):
            spec_ref[:, (2 * kzh + h) * GROUP : (2 * kzh + h + 1) * GROUP, :] = turned[
                h * 64 : (h + 1) * 64
            ].reshape(8, GROUP, turned.shape[1])


def lines_synthesis(step, spec_ref, back, scale):
    count = STEP // GROUP
    both = jnp.concatenate([spec_ref[step * count + g] for g in range(count)], axis=0)
    lines = dot_nt(back, both.astype(BF16))
    if scale is not None:
        lines = lines * scale
    lines = lines.astype(BF16)
    half = lines.shape[0] // 2
    return [
        jnp.concatenate(
            [lines[p * half : (p + 1) * half, g * 128 : (g + 1) * 128] for p in range(2)], axis=1
        )
        for g in range(count)
    ]


def flat(slab):
    return slab.reshape(slab.shape[0] * slab.shape[1], slab.shape[2])


def analysis_kernel(
    field_hbm,
    pair_hbm,
    across_hbm,
    out_ref,
    field_ref,
    pair_ref,
    across_ref,
    lines_ref,
    rows_ref,
    field_sems,
    table_sems,
):
    first, second = start_tables([(pair_hbm, pair_ref), (across_hbm, across_ref)], table_sems)
    start_parts(field_hbm, field_ref, field_sems, STEP)
    first.wait()

    @pl.loop(0, field_ref.shape[0] // STEP)
    def _(step):
        part_copy(field_hbm, field_ref, field_sems, step, STEP).wait()
        for g in range(STEP // GROUP):
            group = step * (STEP // GROUP) + g
            slabs = [flat(field_ref[group * GROUP + ci]) for ci in range(GROUP)]
            depth_analysis(slabs, pair_ref[...], None, group, lines_ref)

    second.wait()
    rows_analysis(lines_ref, across_ref, rows_ref, out_ref)


def middle_kernel(
    inverse_scale,
    block_ref,
    bias_ref,
    point_hbm,
    cot_hbm,
    depth_hbm,
    pair_hbm,
    across_hbm,
    back_hbm,
    act_hbm,
    up_hbm,
    out_ref,
    point_ref,
    cot_ref,
    depth_ref,
    pair_ref,
    across_ref,
    back_ref,
    act_ref,
    up_ref,
    lines_ref,
    rows_ref,
    spec_ref,
    point_sems,
    cot_sems,
    act_sems,
    up_sems,
    table_sems,
):
    tables_in = start_tables(
        [
            (back_hbm, back_ref),
            (depth_hbm, depth_ref),
            (pair_hbm, pair_ref),
            (across_hbm, across_ref),
        ],
        table_sems,
    )
    start_parts(point_hbm, point_ref, point_sems, STEP)
    start_parts(cot_hbm, cot_ref, cot_sems, STEP)
    rows_gather(block_ref, rows_ref, spec_ref)
    for copy in tables_in:
        copy.wait()
    steps = point_ref.shape[0] // STEP

    @pl.loop(0, steps)
    def _(step):
        part_copy(point_hbm, point_ref, point_sems, step, STEP).wait()
        part_copy(cot_hbm, cot_ref, cot_sems, step, STEP).wait()
        for g, wide in enumerate(lines_synthesis(step, spec_ref, back_ref[...], inverse_scale)):
            group = step * (STEP // GROUP) + g
            spectral = dot_nn(wide, depth_ref[...])
            slabs = []
            for oi in range(GROUP):
                index = group * GROUP + oi
                hidden = (
                    spectral[:, oi * 128 : (oi + 1) * 128]
                    + flat(point_ref[index]).astype(F32)
                    + bias_ref[index]
                )
                square = hidden * hidden
                gate = 0.5 + 0.5 * jnp.tanh(
                    hidden * (SQRT_TWO_PI + (SQRT_TWO_PI * CUBIC_COEF) * square)
                )
                slope = hidden * (2.0 * SQRT_TWO_PI + (6.0 * SQRT_TWO_PI * CUBIC_COEF) * square)
                derivative = gate + (gate - gate * gate) * slope
                upstream = (flat(cot_ref[index]).astype(F32) * derivative).astype(BF16)
                act_ref[index] = (hidden * gate).astype(BF16).reshape(act_ref.shape[1:])
                up_ref[index] = upstream.reshape(up_ref.shape[1:])
                slabs.append(upstream)
            depth_analysis(slabs, pair_ref[...], inverse_scale, group, lines_ref)
        part_copy(act_ref, act_hbm, act_sems, step, STEP).start()
        part_copy(up_ref, up_hbm, up_sems, step, STEP).start()

    rows_analysis(lines_ref, across_ref, rows_ref, out_ref)
    for step in range(steps):
        part_copy(act_ref, act_hbm, act_sems, step, STEP).wait()
        part_copy(up_ref, up_hbm, up_sems, step, STEP).wait()


def final_kernel(
    block_ref,
    point_hbm,
    depth_hbm,
    back_hbm,
    out_hbm,
    point_ref,
    depth_ref,
    back_ref,
    out_ref,
    rows_ref,
    spec_ref,
    point_sems,
    out_sems,
    table_sems,
):
    tables_in = start_tables([(back_hbm, back_ref), (depth_hbm, depth_ref)], table_sems)
    start_parts(point_hbm, point_ref, point_sems, STEP)
    rows_gather(block_ref, rows_ref, spec_ref)
    for copy in tables_in:
        copy.wait()
    steps = point_ref.shape[0] // STEP

    @pl.loop(0, steps)
    def _(step):
        part_copy(point_hbm, point_ref, point_sems, step, STEP).wait()
        for g, wide in enumerate(lines_synthesis(step, spec_ref, back_ref[...], None)):
            spectral = dot_nn(wide, depth_ref[...])
            for ci in range(GROUP):
                index = (step * (STEP // GROUP) + g) * GROUP + ci
                total = spectral[:, ci * 128 : (ci + 1) * 128] + flat(point_ref[index]).astype(F32)
                out_ref[index] = total.astype(BF16).reshape(out_ref.shape[1:])
        part_copy(out_ref, out_hbm, out_sems, step, STEP).start()

    for step in range(steps):
        part_copy(out_ref, out_hbm, out_sems, step, STEP).wait()


def point_kernel(
    transposed, weight_ref, field_hbm, out_hbm, field_ref, out_ref, wide_ref, in_sems, out_sems
):
    size = wide_ref.shape[0]
    planes = field_ref.shape[1]
    copies = []
    for plane in range(planes):
        part = (slice(None), pl.ds(plane, 1))
        copy = pltpu.make_async_copy(field_hbm.at[part], field_ref.at[part], in_sems.at[plane])
        copy.start()
        copies.append(copy)
    tall = (sublanes((size, 64)) // 16 == lanes((size, 64))).astype(BF16)
    weight = weight_ref[...]
    left = dot_nt(tall, weight) if transposed else dot_nn(tall, weight)
    left = left.astype(BF16)
    rows = size // 4
    same = sublanes((rows, size)) % 16 == lanes((rows, size)) % 16
    for quarter in range(4):
        spread = dot_nt(left[quarter * rows : (quarter + 1) * rows], tall)
        wide_ref[quarter * rows : (quarter + 1) * rows, :] = jnp.where(same, spread, 0.0).astype(
            BF16
        )
    sends = []
    for plane in range(planes):
        copies[plane].wait()
        for pair in range(2):
            right = jnp.concatenate(
                [
                    field_ref[:, plane, yc * 16 : (yc + 1) * 16, :].reshape(size, 128)
                    for yc in (2 * pair, 2 * pair + 1)
                ],
                axis=1,
            )
            result = dot_nn(wide_ref[...], right).astype(BF16)
            for k in range(2):
                yc = 2 * pair + k
                out_ref[:, plane, yc * 16 : (yc + 1) * 16, :] = result[
                    :, k * 128 : (k + 1) * 128
                ].reshape(size // 16, 16, 128)
        part = (slice(None), pl.ds(plane, 1))
        copy = pltpu.make_async_copy(out_ref.at[part], out_hbm.at[part], out_sems.at[plane])
        copy.start()
        sends.append(copy)
    for copy in sends:
        copy.wait()


def start_weights(weight_hbm, weight_ref, sems):
    copies = []
    for j in range(16):
        rows = weight_ref.shape[0] // 16
        part = pl.ds(j * rows, rows)
        copy = pltpu.make_async_copy(weight_hbm.at[part], weight_ref.at[part], sems.at[j])
        copy.start()
        copies.append(copy)
    return copies


def mode_pair(weight_ref, j, h, u):
    start = ((j * 2 + h) * MX + 8 * u) * 64
    return jnp.concatenate(
        [weight_ref[start : start + 256, :], weight_ref[start + 256 : start + 512, :]], axis=1
    )


def plane_sums(back_ref, mixed_ref, res_ref, quarter):
    count = res_ref.shape[0] // 16
    wide = jnp.concatenate([mixed_ref[quarter * 4 + k] for k in range(4)], axis=1)
    rows = dot_nn(back_ref[...], wide)
    for k in range(4):
        res_ref[pl.ds(quarter * 4 + k, count, stride=16), :] = rows[:, k * 128 : (k + 1) * 128]


def mode_kernel(
    scale,
    block_ref,
    weight_hbm,
    both_ref,
    plain_ref,
    back_ref,
    coeff_hbm,
    out_ref,
    coeff_ref,
    weight_ref,
    rows_ref,
    res_ref,
    left_ref,
    mixed_ref,
    sems,
    coeff_sems,
):
    copies = start_weights(weight_hbm, weight_ref, sems)
    count = rows_ref.shape[0] // 16
    rows_ref[...] = block_ref[...].astype(F32)
    low = lanes((128, 128)) < 64
    kxl = sublanes((128, 128)) % 4
    half = lanes((128, 128)) // 64
    first = (kxl == half).astype(BF16)
    second = (kxl == 2 + half).astype(BF16)
    low8 = lanes((8, 128)) < 64
    sign = jnp.where(sublanes((8, 128)) < 4, -1.0, 1.0)
    for quarter in range(4):
        wide = jnp.concatenate(
            [rows_ref[pl.ds(quarter * 4 + k, count, stride=16), :] for k in range(4)], axis=1
        ).astype(BF16)
        plain = (dot_nn(plain_ref[...], wide) * scale).astype(BF16)
        both = dot_nn(both_ref[...], wide) * scale
        for k in range(4):
            j = quarter * 4 + k
            coeff_ref[j] = plain[:, k * 128 : (k + 1) * 128]
            coeffs = both[:, k * 128 : (k + 1) * 128]
            swapped = swap_halves(coeffs)
            for h in range(2):
                twice = jnp.where(low if h == 0 else ~low, coeffs, swapped).astype(BF16)
                left_ref[j, h] = jnp.concatenate([twice * first, twice * second], axis=1)
    send = pltpu.make_async_copy(coeff_ref, coeff_hbm, coeff_sems.at[0])
    send.start()
    for j in range(16):
        if j % 4 == 0:
            for copy in copies[j : j + 4]:
                copy.wait()
        mixed = []
        for u in range(MX // 8):
            halves = [
                dot_nn(left_ref[j, h, u * 32 : (u + 1) * 32, :], mode_pair(weight_ref, j, h, u))
                for h in range(2)
            ]
            for t in range(2):
                low_h, high_h = [
                    part[t * 16 : (t + 1) * 16, t * 128 : (t + 1) * 128] for part in halves
                ]
                keep = jnp.where(low8, low_h[:8], sign * high_h[8:])
                move = jnp.where(low8, high_h[:8], sign * low_h[8:])
                mixed.append(keep + swap_halves(move))
        mixed_ref[j] = jnp.concatenate(mixed, axis=0).astype(BF16)
        if j % 4 == 3:
            plane_sums(back_ref, mixed_ref, res_ref, j // 4)
    out_ref[...] = res_ref[...].astype(BF16)
    send.wait()


def mode_grad_kernel(
    scale,
    block_ref,
    weight_hbm,
    straight_ref,
    back_ref,
    pair_hbm,
    out_ref,
    pair_ref,
    weight_ref,
    rows_ref,
    res_ref,
    mixed_ref,
    sems,
    pair_sems,
):
    copies = start_weights(weight_hbm, weight_ref, sems)
    count = rows_ref.shape[0] // 16
    rows_ref[...] = block_ref[...].astype(F32)
    low = lanes((64, 128)) < 64
    low16 = lanes((16, 128)) < 64
    row = sublanes((16, 128)) % 4
    upper = row < 2
    valid = lanes((16, 128)) // 64 == row % 2
    even = (sublanes((16, 128)) < 8).astype(BF16)
    odd = (sublanes((16, 128)) >= 8).astype(BF16)
    for j in range(16):
        section = rows_ref[pl.ds(j, count, stride=16), :]
        swapped = swap_halves(section)
        twice = jnp.concatenate(
            [jnp.where(low, section, swapped), jnp.where(low, swapped, section)], axis=1
        ).astype(BF16)
        turned = dot_nn(straight_ref[...], twice)
        for h in range(2):
            part = turned[:, h * 128 : (h + 1) * 128]
            pair_ref[2 * j + h] = jnp.where(low, part[:64], part[64:]).astype(BF16)
    send = pltpu.make_async_copy(pair_ref, pair_hbm, pair_sems.at[0])
    send.start()
    for j in range(16):
        if j % 4 == 0:
            for copy in copies[j : j + 4]:
                copy.wait()
        mixed = []
        for u in range(MX // 8):
            found = []
            for h in range(2):
                pair = pair_ref[2 * j + h, u * 16 : (u + 1) * 16, :]
                rows = dot_nt(
                    jnp.concatenate([pair * even, pair * odd], axis=1),
                    mode_pair(weight_ref, j, h, u),
                )
                found.append(jnp.where(valid, jnp.where(upper, rows[:, :128], rows[:, 128:]), 0.0))
            keep = jnp.where(low16, found[0], found[1])
            move = jnp.where(low16, found[1], found[0])
            mixed.append(keep + swap_halves(move))
        mixed_ref[j] = (jnp.concatenate(mixed, axis=0) * scale).astype(BF16)
        if j % 4 == 3:
            plane_sums(back_ref, mixed_ref, res_ref, j // 4)
    out_ref[...] = res_ref[...].astype(BF16)
    send.wait()


def weight_grad_kernel(scale, coeff_ref, pair_ref, out_hbm, out_ref, mask_ref, pairs_ref, sems):
    lane = lanes((128, 64))
    part = sublanes((128, 64)) // 64
    for t in range(MX // 4 - VECTOR):
        mask_ref[t] = ((lane // 8 == t) & (lane % 4 // 2 == part)).astype(BF16)
    eye = (sublanes((128, 128)) == lanes((128, 128))).astype(BF16)
    even = (sublanes((64, 128)) % 2 == 0).astype(BF16)
    odd = (sublanes((64, 128)) % 2 == 1).astype(BF16)

    @pl.loop(0, 16)
    def _(j):
        turned = (dot_nt(eye, coeff_ref[j]) * scale).astype(BF16)
        for h in range(2):
            one = turned[h * 64 : (h + 1) * 64]
            left = jnp.concatenate([one, one], axis=0)
            pair = pair_ref[j * 2 + h]
            pairs_ref[h] = pair.astype(F32)
            right = jnp.concatenate([pair * even, pair * odd], axis=1)
            for t in range(MX // 4):
                mode = (j * 2 + h) * MX + 4 * t
                if t < MX // 4 - VECTOR:
                    four = dot_nn(left * mask_ref[t], right)
                    for k in range(4):
                        out_ref[mode + k] = four[
                            k // 2 * 64 : (k // 2 + 1) * 64, k % 2 * 128 : (k % 2 + 1) * 128
                        ].astype(BF16)
                    continue
                for k in range(4):
                    total = None
                    for b in range(2):
                        at = t * 8 + b * 4 + k
                        column = jnp.broadcast_to(one[:, at : at + 1], (64, 128))
                        row = jnp.broadcast_to(pairs_ref[h, at : at + 1, :], (64, 128)).astype(BF16)
                        total = column * row if total is None else total + column * row
                    out_ref[mode + k] = total
        part_copy(out_ref, out_hbm, sems, j, 2 * MX).start()

    for j in range(16):
        part_copy(out_ref, out_hbm, sems, j, 2 * MX).wait()


def params(mib):
    return pltpu.CompilerParams(vmem_limit_bytes=mib * 1024 * 1024)


def cost(flops, moved):
    return pl.CostEstimate(flops=int(flops), bytes_accessed=int(moved), transcendentals=0)


def fast_body(features, cotangent, spectral_weight, channel_weight, channel_bias):
    channels, planes, lines, depth_len = features.shape
    devices = lax.axis_size("gx")
    owned_modes = spectral_weight.shape[0]
    wave_pairs = MY * MZ
    volume = planes * devices * lines * depth_len
    forward_scale = 1.0 / math.sqrt(volume)
    inverse_scale = 1.0 / math.sqrt(MX * wave_pairs)
    weight_scale = math.sqrt(MX * wave_pairs / volume)
    table = {name: jnp.asarray(value) for name, value in tables(devices, lines, depth_len).items()}
    for name in ("depth", "depth_pair", "across_y", "back_y"):
        table[name] = pltpu.with_memory_space_constraint(table[name], pltpu.HBM)
    block_rows = devices * 64
    block_shape = jax.ShapeDtypeStruct((block_rows, 128), BF16)
    vmem = pl.BlockSpec(memory_space=pltpu.VMEM)
    hbm = pl.BlockSpec(memory_space=pltpu.HBM)
    smem = pl.BlockSpec(memory_space=pltpu.SMEM)
    field_scratch = pltpu.VMEM(features.shape, BF16)
    field_shape = jax.ShapeDtypeStruct(features.shape, BF16)

    def sems(count):
        return pltpu.SemaphoreType.DMA((count,))

    def scratch(name):
        return pltpu.VMEM(table[name].shape, BF16)

    def in_hbm(array):
        return pltpu.with_memory_space_constraint(array, pltpu.HBM)

    steps = channels // STEP
    lines_scratch = pltpu.VMEM((channels * 2 * MZ, planes * lines), F32)
    rows_scratch = pltpu.VMEM((block_rows, 128), F32)
    spec_scratch = pltpu.VMEM((channels // GROUP, MZ * GROUP, 128), F32)
    weight_rows = pltpu.with_memory_space_constraint(
        spectral_weight.reshape(owned_modes * channels, 2 * channels), pltpu.HBM
    )
    field_bytes = features.size * 2

    def exchange(block):
        return lax.all_to_all(
            block.reshape(devices, 64, 128), "gx", 0, 0, tiled=True
        ).reshape(block_rows, 128)

    def point(field, transposed):
        return pl.pallas_call(
            functools.partial(point_kernel, transposed),
            out_shape=pltpu.HBM(features.shape, BF16),
            in_specs=[vmem, hbm],
            out_specs=hbm,
            scratch_shapes=[
                field_scratch,
                field_scratch,
                pltpu.VMEM((channels * 16, channels * 16), BF16),
                sems(planes),
                sems(planes),
            ],
            compiler_params=params(VMEM_MIB),
            cost_estimate=cost(2 * 1024**3, 2 * field_bytes),
            name="channel_map_back" if transposed else "channel_map",
        )(channel_weight, in_hbm(field))

    block = pl.pallas_call(
        analysis_kernel,
        out_shape=block_shape,
        in_specs=[hbm, hbm, hbm],
        out_specs=vmem,
        scratch_shapes=[
            field_scratch,
            scratch("depth_pair"),
            scratch("across_y"),
            lines_scratch,
            rows_scratch,
            sems(steps),
            sems(2),
        ],
        compiler_params=params(VMEM_MIB),
        cost_estimate=cost(2 * 256 * 1024 * 1024, field_bytes),
        name="field_analysis",
    )(in_hbm(features), table["depth_pair"], table["across_y"])
    block, pointwise = lax.optimization_barrier((exchange(block), point(features, False)))

    weight_scratch = pltpu.VMEM(weight_rows.shape, BF16)
    mixed_scratch = pltpu.VMEM((16, 64, 128), BF16)
    weight_sems = sems(16)
    coeffs, block = pl.pallas_call(
        functools.partial(mode_kernel, forward_scale),
        out_shape=[pltpu.HBM((16, 64, 128), BF16), block_shape],
        in_specs=[vmem, hbm, vmem, vmem, vmem],
        out_specs=[hbm, vmem],
        scratch_shapes=[
            pltpu.VMEM((16, 64, 128), BF16),
            weight_scratch,
            rows_scratch,
            rows_scratch,
            pltpu.VMEM((16, 2, 128, 256), BF16),
            mixed_scratch,
            weight_sems,
            sems(1),
        ],
        compiler_params=params(VMEM_MIB),
        cost_estimate=cost(256 * 2 * 16 * 256 * 128, 17 * 2**20),
        name="mode_product",
    )(block, weight_rows, table["both_x"], table["plain_x"], table["back_x"])
    block = exchange(block)

    activated, upstream, block = pl.pallas_call(
        functools.partial(middle_kernel, inverse_scale),
        out_shape=[field_shape, pltpu.HBM(features.shape, BF16), block_shape],
        in_specs=[vmem, smem, hbm, hbm, hbm, hbm, hbm, hbm],
        out_specs=[hbm, hbm, vmem],
        scratch_shapes=[
            field_scratch,
            field_scratch,
            scratch("depth"),
            scratch("depth_pair"),
            scratch("across_y"),
            scratch("back_y"),
            field_scratch,
            field_scratch,
            lines_scratch,
            rows_scratch,
            spec_scratch,
            sems(steps),
            sems(steps),
            sems(steps),
            sems(steps),
            sems(4),
        ],
        compiler_params=params(VMEM_MIB),
        cost_estimate=cost(2**30, 4 * field_bytes),
        name="gelu_and_gradient",
    )(
        block,
        channel_bias,
        in_hbm(pointwise),
        in_hbm(cotangent),
        table["depth"],
        table["depth_pair"],
        table["across_y"],
        table["back_y"],
    )
    block = exchange(block)
    block, channel_back = lax.optimization_barrier((block, point(upstream, True)))

    pairs, block = pl.pallas_call(
        functools.partial(mode_grad_kernel, forward_scale),
        out_shape=[pltpu.HBM((32, 64, 128), BF16), block_shape],
        in_specs=[vmem, hbm, vmem, vmem],
        out_specs=[hbm, vmem],
        scratch_shapes=[
            pltpu.VMEM((32, 64, 128), BF16),
            weight_scratch,
            rows_scratch,
            rows_scratch,
            mixed_scratch,
            weight_sems,
            sems(1),
        ],
        compiler_params=params(VMEM_MIB),
        cost_estimate=cost(256 * 2 * 16 * 256 * 128, 17 * 2**20),
        name="mode_gradient",
    )(block, weight_rows, table["straight_x"], table["back_x"])
    block = exchange(block)

    spectral_grad = pl.pallas_call(
        functools.partial(weight_grad_kernel, weight_scale),
        out_shape=jax.ShapeDtypeStruct(spectral_weight.shape, BF16),
        in_specs=[vmem, vmem],
        out_specs=hbm,
        scratch_shapes=[
            pltpu.VMEM(spectral_weight.shape, BF16),
            pltpu.VMEM((MX // 4, 128, 64), BF16),
            pltpu.VMEM((2, 64, 128), F32),
            sems(16),
        ],
        compiler_params=params(VMEM_MIB),
        cost_estimate=cost(512 * 2 * 64 * 64 * 256, 17 * 2**20),
        name="weight_gradient",
    )(coeffs, pairs)

    feature_grad = pl.pallas_call(
        final_kernel,
        out_shape=field_shape,
        in_specs=[vmem, hbm, hbm, hbm],
        out_specs=hbm,
        scratch_shapes=[
            field_scratch,
            scratch("depth"),
            scratch("back_y"),
            field_scratch,
            rows_scratch,
            spec_scratch,
            sems(steps),
            sems(steps),
            sems(2),
        ],
        compiler_params=params(VMEM_MIB),
        cost_estimate=cost(2**29, 2 * field_bytes),
        name="field_gradient",
    )(block, in_hbm(channel_back), table["depth"], table["back_y"])
    return (activated, feature_grad, spectral_grad)


def body(features, cotangent, spectral_weight, channel_weight, channel_bias):
    channels, planes, lines, depth_len = features.shape
    devices = lax.axis_size("gx")
    fits = (
        (channels, planes, lines, depth_len) == (64, PLANES, 64, 128)
        and spectral_weight.shape[0] == 2 * MZ * MX
        and devices * 2 == MY
        and devices * 2 == MX
    )
    run = fast_body if fits else general_body
    return run(features, cotangent, spectral_weight, channel_weight, channel_bias)


def solution(mesh):
    in_specs = (
        P("grp", "gx", None, None),
        P("grp", "gx", None, None),
        P("gx", None, None),
        P(),
        P(),
    )
    out_specs = (
        P("grp", "gx", None, None),
        P("grp", "gx", None, None),
        P(("grp", "gx"), None, None),
    )
    return jax.shard_map(body, mesh=mesh, in_specs=in_specs, out_specs=out_specs, check_vma=False)
```

```python
import functools
import math

import jax
import jax.numpy as jnp
import ml_dtypes
import numpy as np
from jax import lax
from jax.experimental import pallas as pl
from jax.experimental.pallas import tpu as pltpu
from jax.sharding import PartitionSpec as P

MX = 32
MY = 32
MZ = 16


SQRT_TWO_PI = math.sqrt(2.0 / math.pi)
CUBIC_COEF = 0.044715


def freq_index(retained, length):
    ladder = jnp.arange(retained, dtype=jnp.int32)
    return jnp.where(ladder < retained // 2, ladder, length - retained + ladder)


def cos_sin(wavenum, length):
    points = jnp.arange(length, dtype=jnp.int32)
    angles = (wavenum[:, None] * points[None, :] % length).astype(jnp.float32) * (
        2.0 * math.pi / length
    )
    return (jnp.cos(angles), jnp.sin(angles))


def analysis_pair(wavenum, length):
    cosine, sine_wave = cos_sin(wavenum, length)
    cosine, sine_wave = (cosine.T, sine_wave.T)
    return jnp.stack(
        [jnp.stack([cosine, -sine_wave], 1), jnp.stack([sine_wave, cosine], 1)], 1
    ).astype(jnp.bfloat16)


def synthesis_pair(wavenum, length):
    cosine, sine_wave = cos_sin(wavenum, length)
    return jnp.stack(
        [jnp.stack([cosine, sine_wave], 1), jnp.stack([-sine_wave, cosine], 1)], 1
    ).astype(jnp.bfloat16)


def depth_table(retained, length):
    cosine, sine_wave = cos_sin(jnp.arange(retained, dtype=jnp.int32), length)
    return jnp.concatenate([cosine, -sine_wave], 0).astype(jnp.bfloat16)


def gelu_parts(inputs):
    cubed_in = inputs * inputs * inputs
    tangent = jnp.tanh(SQRT_TWO_PI * (inputs + CUBIC_COEF * cubed_in))
    output = 0.5 * inputs * (1.0 + tangent)
    derivative = 0.5 * (1.0 + tangent) + 0.5 * inputs * (1.0 - tangent * tangent) * SQRT_TWO_PI * (
        1.0 + 3.0 * CUBIC_COEF * inputs * inputs
    )
    return (output, derivative)


def mode_product(coeffs, weights, channels):
    stacked = coeffs.reshape(coeffs.shape[0], 2, channels)
    halves = jnp.einsum("mac,mcj->amj", stacked, weights, preferred_element_type=jnp.float32)
    real_out = halves[0, :, :channels] - halves[1, :, channels:]
    imag_out = halves[0, :, channels:] + halves[1, :, :channels]
    return jnp.concatenate([real_out, imag_out], 1).astype(jnp.bfloat16)


def mode_grads(coeffs, weights, grad_modes, channels, weight_scale, input_scale):
    number = coeffs.shape[0]
    stacked = coeffs.reshape(number, 2, channels)
    grad_pairs = grad_modes.reshape(number, 2, channels)
    real_w = jnp.einsum("mac,mao->mco", stacked, grad_pairs, preferred_element_type=jnp.float32)
    imag_w = jnp.einsum(
        "mc,mo->mco", stacked[:, 0], grad_pairs[:, 1], preferred_element_type=jnp.float32
    ) - jnp.einsum(
        "mc,mo->mco", stacked[:, 1], grad_pairs[:, 0], preferred_element_type=jnp.float32
    )
    weight_grad = (jnp.concatenate([real_w, imag_w], 2) * weight_scale).astype(jnp.bfloat16)
    straight = jnp.concatenate([grad_pairs[:, 0], grad_pairs[:, 1]], 1)
    rotated = jnp.concatenate([grad_pairs[:, 1], -grad_pairs[:, 0]], 1)
    real_x = jnp.einsum("mcj,mj->mc", weights, straight, preferred_element_type=jnp.float32)
    imag_x = jnp.einsum("mcj,mj->mc", weights, rotated, preferred_element_type=jnp.float32)
    input_grad = (jnp.concatenate([real_x, imag_x], 1) * input_scale).astype(jnp.bfloat16)
    return (weight_grad, input_grad)


def general_body(features, cotangent, spectral_weight, channel_weight, channel_bias):
    channels, planes, lines, depth_len = features.shape
    devices = lax.axis_size("gx")
    all_planes = planes * devices
    owned_modes = spectral_weight.shape[0]
    wave_pairs = MY * MZ
    forward_scale = 1.0 / math.sqrt(all_planes * lines * depth_len)
    inverse_scale = 1.0 / math.sqrt(MX * wave_pairs)
    weight_scale = math.sqrt(MX * wave_pairs / (all_planes * lines * depth_len))
    depth_basis = depth_table(MZ, depth_len)
    across_y = analysis_pair(freq_index(MY, lines), lines)
    back_y = synthesis_pair(freq_index(MY, lines), lines)
    across_full = analysis_pair(freq_index(MX, all_planes), all_planes)
    back_full = synthesis_pair(freq_index(MX, all_planes), all_planes)
    depth_part = jnp.dot(features, depth_basis.T, preferred_element_type=jnp.float32).astype(
        jnp.bfloat16
    )
    plane_part = (
        jnp.einsum(
            "cxyaz,yabk->cxbkz",
            depth_part.reshape(channels, planes, lines, 2, MZ),
            across_y,
            preferred_element_type=jnp.float32,
        )
        .astype(jnp.bfloat16)
        .reshape(channels, planes, 2, wave_pairs)
    )
    all_rows = lax.all_to_all(plane_part, "gx", split_axis=3, concat_axis=1, tiled=True)
    mode_sums = jnp.einsum(
        "cxaq,xabk->qkbc", all_rows, across_full, preferred_element_type=jnp.float32
    ).reshape(owned_modes, 2 * channels)
    coeffs = (mode_sums * forward_scale).astype(jnp.bfloat16)
    spectral = mode_product(coeffs, spectral_weight, channels)
    planes_all = jnp.einsum(
        "qkao,kabx->oxbq",
        spectral.reshape(owned_modes // MX, MX, 2, channels),
        back_full,
        preferred_element_type=jnp.float32,
    ).astype(jnp.bfloat16)
    planes_back = lax.all_to_all(planes_all, "gx", split_axis=1, concat_axis=3, tiled=True)
    lines_back = (
        jnp.einsum(
            "oxakz,kaby->oxybz",
            planes_back.reshape(channels, planes, 2, MY, MZ),
            back_y,
            preferred_element_type=jnp.float32,
        )
        .astype(jnp.bfloat16)
        .reshape(channels, planes, lines, 2 * MZ)
    )
    spectral_term = (
        jnp.dot(lines_back, depth_basis, preferred_element_type=jnp.float32) * inverse_scale
    )
    pointwise = jnp.einsum(
        "oc,cxyz->oxyz", channel_weight, features, preferred_element_type=jnp.float32
    )
    hidden = spectral_term + pointwise + channel_bias[:, None, None, None]
    activated, derivative = gelu_parts(hidden)
    upstream = (cotangent.astype(jnp.float32) * derivative).astype(jnp.bfloat16)
    lines_grad = (
        jnp.dot(upstream, depth_basis.T, preferred_element_type=jnp.float32) * inverse_scale
    ).astype(jnp.bfloat16)
    rows_grad = (
        jnp.einsum(
            "oxybz,kaby->oxakz",
            lines_grad.reshape(channels, planes, lines, 2, MZ),
            back_y,
            preferred_element_type=jnp.float32,
        )
        .astype(jnp.bfloat16)
        .reshape(channels, planes, 2, wave_pairs)
    )
    all_grads = lax.all_to_all(rows_grad, "gx", split_axis=3, concat_axis=1, tiled=True)
    grad_sums = jnp.einsum(
        "oxbq,kabx->qkao", all_grads, back_full, preferred_element_type=jnp.float32
    ).reshape(owned_modes, 2 * channels)
    grad_modes = grad_sums.astype(jnp.bfloat16)
    spectral_grad, coeff_grad = mode_grads(
        coeffs, spectral_weight, grad_modes, channels, weight_scale, forward_scale
    )
    plane_all = jnp.einsum(
        "qkbc,xabk->cxaq",
        coeff_grad.reshape(owned_modes // MX, MX, 2, channels),
        across_full,
        preferred_element_type=jnp.float32,
    ).astype(jnp.bfloat16)
    plane_grad = lax.all_to_all(plane_all, "gx", split_axis=1, concat_axis=3, tiled=True)
    depth_grad = (
        jnp.einsum(
            "cxbkz,yabk->cxyaz",
            plane_grad.reshape(channels, planes, 2, MY, MZ),
            across_y,
            preferred_element_type=jnp.float32,
        )
        .astype(jnp.bfloat16)
        .reshape(channels, planes, lines, 2 * MZ)
    )
    channel_back = jnp.einsum(
        "oc,oxyz->cxyz", channel_weight, upstream, preferred_element_type=jnp.float32
    )
    feature_grad = (
        jnp.dot(depth_grad, depth_basis, preferred_element_type=jnp.float32) + channel_back
    ).astype(jnp.bfloat16)
    return (activated.astype(jnp.bfloat16), feature_grad, spectral_grad)


PLANES = 2
GROUP = 8
STEP = 16
VMEM_MIB = 32
VECTOR = 2
WAITS = {0: 4, 4: 4, 8: 4, 12: 2, 14: 1, 15: 1}
NT = (((1,), (1,)), ((), ()))
F32 = jnp.float32
BF16 = jnp.bfloat16


def np_freq(retained, length):
    ladder = np.arange(retained)
    return np.where(ladder < retained // 2, ladder, length - retained + ladder)


def np_angles(wavenum, length):
    points = np.arange(length)
    return (wavenum[:, None] * points[None, :] % length) * (2.0 * math.pi / length)


def as_bf16(table):
    return np.asarray(table, np.float32).astype(ml_dtypes.bfloat16)


def rotation(angle, sign):
    cosine, sine_wave = np.cos(angle), sign * np.sin(angle)
    return np.stack([np.stack([cosine, -sine_wave]), np.stack([sine_wave, cosine])])


@functools.lru_cache(maxsize=None)
def tables(devices, lines, depth_len):
    planes_all = devices * PLANES
    angle = np_angles(np.arange(MZ), depth_len)
    depth = np.stack([np.cos(angle), -np.sin(angle)])
    eye = np.eye(GROUP)
    depth_block = np.einsum("akz,ij->akijz", depth, eye).reshape(2 * MZ * GROUP, GROUP * depth_len)
    depth_pair = np.einsum("akz,ij->iakjz", depth, np.eye(2)).reshape(4 * MZ, 2 * depth_len)
    plane_eye = np.eye(PLANES)
    angle = np_angles(np_freq(MY, lines), lines).reshape(devices, MY // devices, lines)
    across = np.einsum("badly,xw->ldbxawy", rotation(angle, -1.0), plane_eye)
    across = across.reshape(MY * 2 * PLANES, 2 * PLANES * lines)
    back = np.einsum("pbdly,xw->pxyldbw", rotation(angle, 1.0), plane_eye)
    back = back.reshape(2 * PLANES * lines, MY * 2 * PLANES)
    angle = np_angles(np_freq(MX, planes_all), planes_all).reshape(MX // 4, 4, devices, PLANES)
    forward = rotation(angle, -1.0)
    rows = np.einsum("batksx->tbksax", forward).reshape(MX // 4, 2, 4, devices * 2 * PLANES)
    plain = rows.reshape(2 * MX, -1)
    both = np.stack([rows, rows[:, ::-1]], 1).reshape(4 * MX, -1)
    turned = np.concatenate([rows[:, 1:], -rows[:, :1]], 1).reshape(2 * MX, -1)
    straight_rotated = np.concatenate([plain, turned], 0)
    inverse = np.einsum("batksx->sbxtak", rotation(angle, 1.0)).reshape(-1, 2 * MX)
    return {
        "depth": as_bf16(depth_block),
        "depth_pair": as_bf16(depth_pair),
        "across_y": as_bf16(across),
        "back_y": as_bf16(back),
        "plain_x": as_bf16(plain),
        "both_x": as_bf16(both),
        "straight_x": as_bf16(straight_rotated),
        "back_x": as_bf16(inverse),
    }


def dot_nn(left, right):
    return jnp.dot(left, right, preferred_element_type=F32)


def dot_nt(left, right):
    return lax.dot_general(left, right, NT, preferred_element_type=F32)


def lanes(shape):
    return lax.broadcasted_iota(jnp.int32, shape, len(shape) - 1)


def sublanes(shape):
    return lax.broadcasted_iota(jnp.int32, shape, len(shape) - 2)


def swap_halves(block):
    return pltpu.roll(block, 64, 1)


def part_copy(source, target, sems, index, size):
    start = index * size if isinstance(index, int) else pl.multiple_of(index * size, size)
    part = pl.ds(start, size)
    return pltpu.make_async_copy(source.at[part], target.at[part], sems.at[index])


def start_parts(source, target, sems, size):
    for index in range(source.shape[0] // size):
        part_copy(source, target, sems, index, size).start()


def start_tables(pairs, sems):
    copies = []
    for index, (source, target) in enumerate(pairs):
        copy = pltpu.make_async_copy(source, target, sems.at[index])
        copy.start()
        copies.append(copy)
    return copies


def depth_quad(slabs, quad, depth_pair, scale, group, lines_ref):
    four = slabs[quad * 4 : quad * 4 + 4]
    wide = jnp.concatenate(
        [jnp.concatenate(four[2 * pair : 2 * pair + 2], axis=1) for pair in range(2)], axis=0
    )
    parts = dot_nt(depth_pair, wide)
    if scale is not None:
        parts = parts * scale
    half = wide.shape[0] // 2
    for pair in range(2):
        start = (group * GROUP + quad * 4 + pair * 2) * 2 * MZ
        if not isinstance(start, int):
            start = pl.multiple_of(start, 4 * MZ)
        lines_ref[pl.ds(start, 4 * MZ), :] = parts[:, pair * half : (pair + 1) * half]


def depth_analysis(slabs, depth_pair, scale, group, lines_ref):
    for quad in range(2):
        depth_quad(slabs, quad, depth_pair, scale, group, lines_ref)


def rows_analysis(lines_ref, across_ref, rows_ref, out_ref):
    channels = lines_ref.shape[0] // (2 * MZ)
    across = across_ref[...]
    half = across.shape[0] // 2
    for kzh in range(MZ // 2):
        pair = jnp.concatenate(
            [
                jnp.concatenate(
                    [
                        lines_ref[pl.ds(a * MZ + 2 * kzh + h, channels, stride=2 * MZ), :]
                        for a in range(2)
                    ],
                    axis=1,
                )
                for h in range(2)
            ],
            axis=0,
        ).astype(BF16)
        rows = dot_nt(across, pair)
        for kyl in range(2):
            rows_ref[pl.ds(kyl * 8 + kzh, half, stride=16), :] = rows[
                kyl * half : (kyl + 1) * half
            ]
    out_ref[...] = rows_ref[...].astype(BF16)


def rows_gather(block_ref, rows_ref, spec_ref):
    rows_ref[...] = block_ref[...].astype(F32)
    count = rows_ref.shape[0] // 16
    eye = (sublanes((128, 128)) == lanes((128, 128))).astype(BF16)
    for kzh in range(MZ // 2):
        both = jnp.concatenate(
            [rows_ref[pl.ds(kyl * 8 + kzh, count, stride=16), :] for kyl in range(2)], axis=0
        ).astype(BF16)
        turned = dot_nt(eye, both)
        for h in range(2):
            spec_ref[:, (2 * kzh + h) * GROUP : (2 * kzh + h + 1) * GROUP, :] = turned[
                h * 64 : (h + 1) * 64
            ].reshape(8, GROUP, turned.shape[1])


def lines_synthesis(step, spec_ref, back, scale):
    count = STEP // GROUP
    both = jnp.concatenate([spec_ref[step * count + g] for g in range(count)], axis=0)
    lines = dot_nt(back, both.astype(BF16))
    if scale is not None:
        lines = lines * scale
    lines = lines.astype(BF16)
    half = lines.shape[0] // 2
    return [
        jnp.concatenate(
            [lines[p * half : (p + 1) * half, g * 128 : (g + 1) * 128] for p in range(2)], axis=1
        )
        for g in range(count)
    ]


def flat(slab):
    return slab.reshape(slab.shape[0] * slab.shape[1], slab.shape[2])


def analysis_kernel(
    field_hbm,
    pair_hbm,
    across_hbm,
    out_ref,
    field_ref,
    pair_ref,
    across_ref,
    lines_ref,
    rows_ref,
    field_sems,
    table_sems,
):
    first, second = start_tables([(pair_hbm, pair_ref), (across_hbm, across_ref)], table_sems)
    start_parts(field_hbm, field_ref, field_sems, STEP)
    first.wait()

    @pl.loop(0, field_ref.shape[0] // STEP)
    def _(step):
        part_copy(field_hbm, field_ref, field_sems, step, STEP).wait()
        for g in range(STEP // GROUP):
            group = step * (STEP // GROUP) + g
            slabs = [flat(field_ref[group * GROUP + ci]) for ci in range(GROUP)]
            depth_analysis(slabs, pair_ref[...], None, group, lines_ref)

    second.wait()
    rows_analysis(lines_ref, across_ref, rows_ref, out_ref)


def middle_kernel(
    inverse_scale,
    block_ref,
    bias_ref,
    point_hbm,
    cot_hbm,
    depth_hbm,
    pair_hbm,
    across_hbm,
    back_hbm,
    act_hbm,
    up_hbm,
    out_ref,
    point_ref,
    cot_ref,
    depth_ref,
    pair_ref,
    across_ref,
    back_ref,
    act_ref,
    up_ref,
    lines_ref,
    rows_ref,
    spec_ref,
    point_sems,
    cot_sems,
    act_sems,
    up_sems,
    table_sems,
):
    tables_in = start_tables(
        [
            (back_hbm, back_ref),
            (depth_hbm, depth_ref),
            (pair_hbm, pair_ref),
            (across_hbm, across_ref),
        ],
        table_sems,
    )
    start_parts(point_hbm, point_ref, point_sems, STEP)
    start_parts(cot_hbm, cot_ref, cot_sems, STEP)
    rows_gather(block_ref, rows_ref, spec_ref)
    for copy in tables_in:
        copy.wait()
    steps = point_ref.shape[0] // STEP
    groups = point_ref.shape[0] // GROUP
    per_step = STEP // GROUP

    def activate(index, spectral):
        hidden = spectral + flat(point_ref[index]).astype(F32) + bias_ref[index]
        square = hidden * hidden
        gate = 0.5 + 0.5 * jnp.tanh(hidden * (SQRT_TWO_PI + (SQRT_TWO_PI * CUBIC_COEF) * square))
        slope = hidden * (2.0 * SQRT_TWO_PI + (6.0 * SQRT_TWO_PI * CUBIC_COEF) * square)
        derivative = gate + (gate - gate * gate) * slope
        upstream = (flat(cot_ref[index]).astype(F32) * derivative).astype(BF16)
        act_ref[index] = (hidden * gate).astype(BF16).reshape(act_ref.shape[1:])
        up_ref[index] = upstream.reshape(up_ref.shape[1:])
        return upstream

    def quarter(wide, at):
        return dot_nn(wide, depth_ref[:, at * 256 : (at + 1) * 256])

    wides = lines_synthesis(0, spec_ref, back_ref[...], inverse_scale)
    spectral = [quarter(wides[0], at) for at in range(4)]
    last = None
    for group in range(groups):
        step = group // per_step
        if group % per_step == 0:
            part_copy(point_hbm, point_ref, point_sems, step, STEP).wait()
            part_copy(cot_hbm, cot_ref, cot_sems, step, STEP).wait()
            if step + 1 < steps:
                wides += lines_synthesis(step + 1, spec_ref, back_ref[...], inverse_scale)
        following, slabs = [], []
        for at in range(4):
            if group + 1 < groups:
                following.append(quarter(wides[group + 1], at))
            for k in range(2):
                oi = 2 * at + k
                slabs.append(
                    activate(group * GROUP + oi, spectral[at][:, k * 128 : (k + 1) * 128])
                )
            if last is not None and at % 2 == 0:
                depth_quad(last, at // 2, pair_ref[...], inverse_scale, group - 1, lines_ref)
        if group % per_step == per_step - 1:
            part_copy(act_ref, act_hbm, act_sems, step, STEP).start()
            part_copy(up_ref, up_hbm, up_sems, step, STEP).start()
        spectral, last = following, slabs
    depth_analysis(last, pair_ref[...], inverse_scale, groups - 1, lines_ref)
    rows_analysis(lines_ref, across_ref, rows_ref, out_ref)
    for step in range(steps):
        part_copy(act_ref, act_hbm, act_sems, step, STEP).wait()
        part_copy(up_ref, up_hbm, up_sems, step, STEP).wait()


def final_kernel(
    block_ref,
    point_hbm,
    depth_hbm,
    back_hbm,
    out_hbm,
    point_ref,
    depth_ref,
    back_ref,
    out_ref,
    rows_ref,
    spec_ref,
    point_sems,
    out_sems,
    table_sems,
):
    tables_in = start_tables([(back_hbm, back_ref), (depth_hbm, depth_ref)], table_sems)
    start_parts(point_hbm, point_ref, point_sems, STEP)
    rows_gather(block_ref, rows_ref, spec_ref)
    for copy in tables_in:
        copy.wait()
    steps = point_ref.shape[0] // STEP

    @pl.loop(0, steps)
    def _(step):
        part_copy(point_hbm, point_ref, point_sems, step, STEP).wait()
        for g, wide in enumerate(lines_synthesis(step, spec_ref, back_ref[...], None)):
            spectral = dot_nn(wide, depth_ref[...])
            for ci in range(GROUP):
                index = (step * (STEP // GROUP) + g) * GROUP + ci
                total = spectral[:, ci * 128 : (ci + 1) * 128] + flat(point_ref[index]).astype(F32)
                out_ref[index] = total.astype(BF16).reshape(out_ref.shape[1:])
        part_copy(out_ref, out_hbm, out_sems, step, STEP).start()

    for step in range(steps):
        part_copy(out_ref, out_hbm, out_sems, step, STEP).wait()


def point_kernel(
    transposed, weight_ref, field_hbm, out_hbm, field_ref, out_ref, wide_ref, in_sems, out_sems
):
    size = wide_ref.shape[0]
    planes = field_ref.shape[1]
    copies = []
    for plane in range(planes):
        part = (slice(None), pl.ds(plane, 1))
        copy = pltpu.make_async_copy(field_hbm.at[part], field_ref.at[part], in_sems.at[plane])
        copy.start()
        copies.append(copy)
    tall = (sublanes((size, 64)) // 16 == lanes((size, 64))).astype(BF16)
    weight = weight_ref[...]
    left = dot_nt(tall, weight) if transposed else dot_nn(tall, weight)
    left = left.astype(BF16)
    rows = size // 4
    same = sublanes((rows, size)) % 16 == lanes((rows, size)) % 16
    for quarter in range(4):
        spread = dot_nt(left[quarter * rows : (quarter + 1) * rows], tall)
        wide_ref[quarter * rows : (quarter + 1) * rows, :] = jnp.where(same, spread, 0.0).astype(
            BF16
        )
    sends = []
    for plane in range(planes):
        copies[plane].wait()
        for pair in range(2):
            right = jnp.concatenate(
                [
                    field_ref[:, plane, yc * 16 : (yc + 1) * 16, :].reshape(size, 128)
                    for yc in (2 * pair, 2 * pair + 1)
                ],
                axis=1,
            )
            result = dot_nn(wide_ref[...], right).astype(BF16)
            for k in range(2):
                yc = 2 * pair + k
                out_ref[:, plane, yc * 16 : (yc + 1) * 16, :] = result[
                    :, k * 128 : (k + 1) * 128
                ].reshape(size // 16, 16, 128)
        part = (slice(None), pl.ds(plane, 1))
        copy = pltpu.make_async_copy(out_ref.at[part], out_hbm.at[part], out_sems.at[plane])
        copy.start()
        sends.append(copy)
    for copy in sends:
        copy.wait()


def start_weights(weight_hbm, weight_ref, sems):
    copies = []
    for j in range(16):
        rows = weight_ref.shape[0] // 16
        part = pl.ds(j * rows, rows)
        copy = pltpu.make_async_copy(weight_hbm.at[part], weight_ref.at[part], sems.at[j])
        copy.start()
        copies.append(copy)
    return copies


def mode_pair(weight_ref, j, h, u):
    start = ((j * 2 + h) * MX + 8 * u) * 64
    return jnp.concatenate(
        [weight_ref[start : start + 256, :], weight_ref[start + 256 : start + 512, :]], axis=1
    )


def plane_sums(back_ref, mixed_ref, res_ref, quarter):
    count = res_ref.shape[0] // 16
    wide = jnp.concatenate([mixed_ref[quarter * 4 + k] for k in range(4)], axis=1)
    rows = dot_nn(back_ref[...], wide)
    for k in range(4):
        res_ref[pl.ds(quarter * 4 + k, count, stride=16), :] = rows[:, k * 128 : (k + 1) * 128]


def mode_kernel(
    scale,
    block_ref,
    weight_hbm,
    both_ref,
    plain_ref,
    back_ref,
    coeff_hbm,
    out_ref,
    coeff_ref,
    weight_ref,
    rows_ref,
    res_ref,
    left_ref,
    mixed_ref,
    sems,
    coeff_sems,
):
    copies = start_weights(weight_hbm, weight_ref, sems)
    count = rows_ref.shape[0] // 16
    rows_ref[...] = block_ref[...].astype(F32)
    low = lanes((128, 128)) < 64
    kxl = sublanes((128, 128)) % 4
    half = lanes((128, 128)) // 64
    first = (kxl == half).astype(BF16)
    second = (kxl == 2 + half).astype(BF16)
    low8 = lanes((8, 128)) < 64
    sign = jnp.where(sublanes((8, 128)) < 4, -1.0, 1.0)
    for quarter in range(4):
        wide = jnp.concatenate(
            [rows_ref[pl.ds(quarter * 4 + k, count, stride=16), :] for k in range(4)], axis=1
        ).astype(BF16)
        plain = (dot_nn(plain_ref[...], wide) * scale).astype(BF16)
        both = dot_nn(both_ref[...], wide) * scale
        for k in range(4):
            j = quarter * 4 + k
            coeff_ref[j] = plain[:, k * 128 : (k + 1) * 128]
            coeffs = both[:, k * 128 : (k + 1) * 128]
            swapped = swap_halves(coeffs)
            for h in range(2):
                twice = jnp.where(low if h == 0 else ~low, coeffs, swapped).astype(BF16)
                left_ref[j, h] = jnp.concatenate([twice * first, twice * second], axis=1)
    send = pltpu.make_async_copy(coeff_ref, coeff_hbm, coeff_sems.at[0])
    send.start()
    for j in range(16):
        for copy in copies[j : j + WAITS.get(j, 0)]:
            copy.wait()
        mixed = []
        for u in range(MX // 8):
            halves = [
                dot_nn(left_ref[j, h, u * 32 : (u + 1) * 32, :], mode_pair(weight_ref, j, h, u))
                for h in range(2)
            ]
            for t in range(2):
                low_h, high_h = [
                    part[t * 16 : (t + 1) * 16, t * 128 : (t + 1) * 128] for part in halves
                ]
                keep = jnp.where(low8, low_h[:8], sign * high_h[8:])
                move = jnp.where(low8, high_h[:8], sign * low_h[8:])
                mixed.append(keep + swap_halves(move))
        mixed_ref[j] = jnp.concatenate(mixed, axis=0).astype(BF16)
        if j % 4 == 3:
            plane_sums(back_ref, mixed_ref, res_ref, j // 4)
    out_ref[...] = res_ref[...].astype(BF16)
    send.wait()


def mode_grad_kernel(
    scale,
    block_ref,
    weight_hbm,
    straight_ref,
    back_ref,
    coeff_hbm,
    pair_ref,
    coeff_ref,
    out_ref,
    weight_ref,
    rows_ref,
    res_ref,
    mixed_ref,
    sems,
    coeff_sems,
):
    send = pltpu.make_async_copy(coeff_hbm, coeff_ref, coeff_sems.at[0])
    send.start()
    copies = start_weights(weight_hbm, weight_ref, sems)
    count = rows_ref.shape[0] // 16
    rows_ref[...] = block_ref[...].astype(F32)
    low = lanes((64, 128)) < 64
    low16 = lanes((16, 128)) < 64
    row = sublanes((16, 128)) % 4
    upper = row < 2
    valid = lanes((16, 128)) // 64 == row % 2
    even = (sublanes((16, 128)) < 8).astype(BF16)
    odd = (sublanes((16, 128)) >= 8).astype(BF16)
    for j in range(16):
        section = rows_ref[pl.ds(j, count, stride=16), :]
        swapped = swap_halves(section)
        twice = jnp.concatenate(
            [jnp.where(low, section, swapped), jnp.where(low, swapped, section)], axis=1
        ).astype(BF16)
        turned = dot_nn(straight_ref[...], twice)
        for h in range(2):
            part = turned[:, h * 128 : (h + 1) * 128]
            pair_ref[2 * j + h] = jnp.where(low, part[:64], part[64:]).astype(BF16)
    for j in range(16):
        for copy in copies[j : j + WAITS.get(j, 0)]:
            copy.wait()
        mixed = []
        for u in range(MX // 8):
            found = []
            for h in range(2):
                pair = pair_ref[2 * j + h, u * 16 : (u + 1) * 16, :]
                rows = dot_nt(
                    jnp.concatenate([pair * even, pair * odd], axis=1),
                    mode_pair(weight_ref, j, h, u),
                )
                found.append(jnp.where(valid, jnp.where(upper, rows[:, :128], rows[:, 128:]), 0.0))
            keep = jnp.where(low16, found[0], found[1])
            move = jnp.where(low16, found[1], found[0])
            mixed.append(keep + swap_halves(move))
        mixed_ref[j] = (jnp.concatenate(mixed, axis=0) * scale).astype(BF16)
        if j % 4 == 3:
            plane_sums(back_ref, mixed_ref, res_ref, j // 4)
    out_ref[...] = res_ref[...].astype(BF16)
    send.wait()


def weight_grad_kernel(scale, coeff_ref, pair_ref, out_hbm, out_ref, mask_ref, pairs_ref, sems):
    lane = lanes((128, 64))
    part = sublanes((128, 64)) // 64
    for t in range(MX // 4 - VECTOR):
        mask_ref[t] = ((lane // 8 == t) & (lane % 4 // 2 == part)).astype(BF16)
    eye = (sublanes((128, 128)) == lanes((128, 128))).astype(BF16)
    even = (sublanes((64, 128)) % 2 == 0).astype(BF16)
    odd = (sublanes((64, 128)) % 2 == 1).astype(BF16)

    @pl.loop(0, 16)
    def _(j):
        turned = (dot_nt(eye, coeff_ref[j]) * scale).astype(BF16)
        for h in range(2):
            one = turned[h * 64 : (h + 1) * 64]
            left = jnp.concatenate([one, one], axis=0)
            pair = pair_ref[j * 2 + h]
            pairs_ref[h] = pair.astype(F32)
            right = jnp.concatenate([pair * even, pair * odd], axis=1)
            for t in range(MX // 4):
                mode = (j * 2 + h) * MX + 4 * t
                if t < MX // 4 - VECTOR:
                    four = dot_nn(left * mask_ref[t], right)
                    for k in range(4):
                        out_ref[mode + k] = four[
                            k // 2 * 64 : (k // 2 + 1) * 64, k % 2 * 128 : (k % 2 + 1) * 128
                        ].astype(BF16)
                    continue
                for k in range(4):
                    total = None
                    for b in range(2):
                        at = t * 8 + b * 4 + k
                        column = jnp.broadcast_to(one[:, at : at + 1], (64, 128))
                        row = jnp.broadcast_to(pairs_ref[h, at : at + 1, :], (64, 128)).astype(BF16)
                        total = column * row if total is None else total + column * row
                    out_ref[mode + k] = total
        part_copy(out_ref, out_hbm, sems, j, 2 * MX).start()

    for j in range(16):
        part_copy(out_ref, out_hbm, sems, j, 2 * MX).wait()


def params(mib):
    return pltpu.CompilerParams(vmem_limit_bytes=mib * 1024 * 1024)


def cost(flops, moved):
    return pl.CostEstimate(flops=int(flops), bytes_accessed=int(moved), transcendentals=0)


def fast_body(features, cotangent, spectral_weight, channel_weight, channel_bias):
    channels, planes, lines, depth_len = features.shape
    devices = lax.axis_size("gx")
    owned_modes = spectral_weight.shape[0]
    wave_pairs = MY * MZ
    volume = planes * devices * lines * depth_len
    forward_scale = 1.0 / math.sqrt(volume)
    inverse_scale = 1.0 / math.sqrt(MX * wave_pairs)
    weight_scale = math.sqrt(MX * wave_pairs / volume)
    table = {name: jnp.asarray(value) for name, value in tables(devices, lines, depth_len).items()}
    for name in ("depth", "depth_pair", "across_y", "back_y"):
        table[name] = pltpu.with_memory_space_constraint(table[name], pltpu.HBM)
    block_rows = devices * 64
    block_shape = jax.ShapeDtypeStruct((block_rows, 128), BF16)
    vmem = pl.BlockSpec(memory_space=pltpu.VMEM)
    hbm = pl.BlockSpec(memory_space=pltpu.HBM)
    smem = pl.BlockSpec(memory_space=pltpu.SMEM)
    field_scratch = pltpu.VMEM(features.shape, BF16)
    field_shape = jax.ShapeDtypeStruct(features.shape, BF16)

    def sems(count):
        return pltpu.SemaphoreType.DMA((count,))

    def scratch(name):
        return pltpu.VMEM(table[name].shape, BF16)

    def in_hbm(array):
        return pltpu.with_memory_space_constraint(array, pltpu.HBM)

    steps = channels // STEP
    lines_scratch = pltpu.VMEM((channels * 2 * MZ, planes * lines), F32)
    rows_scratch = pltpu.VMEM((block_rows, 128), F32)
    spec_scratch = pltpu.VMEM((channels // GROUP, MZ * GROUP, 128), F32)
    weight_rows = pltpu.with_memory_space_constraint(
        spectral_weight.reshape(owned_modes * channels, 2 * channels), pltpu.HBM
    )
    field_bytes = features.size * 2

    def exchange(block):
        return lax.all_to_all(
            block.reshape(devices, 64, 128), "gx", 0, 0, tiled=True
        ).reshape(block_rows, 128)

    def point(field, transposed):
        return pl.pallas_call(
            functools.partial(point_kernel, transposed),
            out_shape=pltpu.HBM(features.shape, BF16),
            in_specs=[vmem, hbm],
            out_specs=hbm,
            scratch_shapes=[
                field_scratch,
                field_scratch,
                pltpu.VMEM((channels * 16, channels * 16), BF16),
                sems(planes),
                sems(planes),
            ],
            compiler_params=params(VMEM_MIB),
            cost_estimate=cost(2 * 1024**3, 2 * field_bytes),
            name="channel_map_back" if transposed else "channel_map",
        )(channel_weight, in_hbm(field))

    block = pl.pallas_call(
        analysis_kernel,
        out_shape=block_shape,
        in_specs=[hbm, hbm, hbm],
        out_specs=vmem,
        scratch_shapes=[
            field_scratch,
            scratch("depth_pair"),
            scratch("across_y"),
            lines_scratch,
            rows_scratch,
            sems(steps),
            sems(2),
        ],
        compiler_params=params(VMEM_MIB),
        cost_estimate=cost(2 * 256 * 1024 * 1024, field_bytes),
        name="field_analysis",
    )(in_hbm(features), table["depth_pair"], table["across_y"])
    block, pointwise = lax.optimization_barrier((exchange(block), point(features, False)))

    weight_scratch = pltpu.VMEM(weight_rows.shape, BF16)
    mixed_scratch = pltpu.VMEM((16, 64, 128), BF16)
    weight_sems = sems(16)
    coeffs, block = pl.pallas_call(
        functools.partial(mode_kernel, forward_scale),
        out_shape=[pltpu.HBM((16, 64, 128), BF16), block_shape],
        in_specs=[vmem, hbm, vmem, vmem, vmem],
        out_specs=[hbm, vmem],
        scratch_shapes=[
            pltpu.VMEM((16, 64, 128), BF16),
            weight_scratch,
            rows_scratch,
            rows_scratch,
            pltpu.VMEM((16, 2, 128, 256), BF16),
            mixed_scratch,
            weight_sems,
            sems(1),
        ],
        compiler_params=params(VMEM_MIB),
        cost_estimate=cost(256 * 2 * 16 * 256 * 128, 17 * 2**20),
        name="mode_product",
    )(block, weight_rows, table["both_x"], table["plain_x"], table["back_x"])
    block = exchange(block)

    activated, upstream, block = pl.pallas_call(
        functools.partial(middle_kernel, inverse_scale),
        out_shape=[field_shape, pltpu.HBM(features.shape, BF16), block_shape],
        in_specs=[vmem, smem, hbm, hbm, hbm, hbm, hbm, hbm],
        out_specs=[hbm, hbm, vmem],
        scratch_shapes=[
            field_scratch,
            field_scratch,
            scratch("depth"),
            scratch("depth_pair"),
            scratch("across_y"),
            scratch("back_y"),
            field_scratch,
            field_scratch,
            lines_scratch,
            rows_scratch,
            spec_scratch,
            sems(steps),
            sems(steps),
            sems(steps),
            sems(steps),
            sems(4),
        ],
        compiler_params=params(VMEM_MIB),
        cost_estimate=cost(2**30, 4 * field_bytes),
        name="gelu_and_gradient",
    )(
        block,
        channel_bias,
        in_hbm(pointwise),
        in_hbm(cotangent),
        table["depth"],
        table["depth_pair"],
        table["across_y"],
        table["back_y"],
    )
    block = exchange(block)
    block, channel_back = lax.optimization_barrier((block, point(upstream, True)))

    pairs, coeffs, block = pl.pallas_call(
        functools.partial(mode_grad_kernel, forward_scale),
        out_shape=[
            pltpu.VMEM((32, 64, 128), BF16),
            pltpu.VMEM((16, 64, 128), BF16),
            block_shape,
        ],
        in_specs=[vmem, hbm, vmem, vmem, hbm],
        out_specs=[vmem, vmem, vmem],
        scratch_shapes=[
            weight_scratch,
            rows_scratch,
            rows_scratch,
            mixed_scratch,
            weight_sems,
            sems(1),
        ],
        compiler_params=params(VMEM_MIB),
        cost_estimate=cost(256 * 2 * 16 * 256 * 128, 17 * 2**20),
        name="mode_gradient",
    )(block, weight_rows, table["straight_x"], table["back_x"], in_hbm(coeffs))
    block = exchange(block)

    spectral_grad = pl.pallas_call(
        functools.partial(weight_grad_kernel, weight_scale),
        out_shape=jax.ShapeDtypeStruct(spectral_weight.shape, BF16),
        in_specs=[vmem, vmem],
        out_specs=hbm,
        scratch_shapes=[
            pltpu.VMEM(spectral_weight.shape, BF16),
            pltpu.VMEM((MX // 4, 128, 64), BF16),
            pltpu.VMEM((2, 64, 128), F32),
            sems(16),
        ],
        compiler_params=params(VMEM_MIB),
        cost_estimate=cost(512 * 2 * 64 * 64 * 256, 17 * 2**20),
        name="weight_gradient",
    )(
        pltpu.with_memory_space_constraint(coeffs, pltpu.VMEM),
        pltpu.with_memory_space_constraint(pairs, pltpu.VMEM),
    )

    feature_grad = pl.pallas_call(
        final_kernel,
        out_shape=field_shape,
        in_specs=[vmem, hbm, hbm, hbm],
        out_specs=hbm,
        scratch_shapes=[
            field_scratch,
            scratch("depth"),
            scratch("back_y"),
            field_scratch,
            rows_scratch,
            spec_scratch,
            sems(steps),
            sems(steps),
            sems(2),
        ],
        compiler_params=params(VMEM_MIB),
        cost_estimate=cost(2**29, 2 * field_bytes),
        name="field_gradient",
    )(block, in_hbm(channel_back), table["depth"], table["back_y"])
    return (activated, feature_grad, spectral_grad)


def body(features, cotangent, spectral_weight, channel_weight, channel_bias):
    channels, planes, lines, depth_len = features.shape
    devices = lax.axis_size("gx")
    fits = (
        (channels, planes, lines, depth_len) == (64, PLANES, 64, 128)
        and spectral_weight.shape[0] == 2 * MZ * MX
        and devices * 2 == MY
        and devices * 2 == MX
    )
    run = fast_body if fits else general_body
    return run(features, cotangent, spectral_weight, channel_weight, channel_bias)


def solution(mesh):
    in_specs = (
        P("grp", "gx", None, None),
        P("grp", "gx", None, None),
        P("gx", None, None),
        P(),
        P(),
    )
    out_specs = (
        P("grp", "gx", None, None),
        P("grp", "gx", None, None),
        P(("grp", "gx"), None, None),
    )
    return jax.shard_map(body, mesh=mesh, in_specs=in_specs, out_specs=out_specs, check_vma=False)
```

```python
import functools
import math

import jax
import jax.numpy as jnp
import ml_dtypes
import numpy as np
from jax import lax
from jax.experimental import pallas as pl
from jax.experimental.pallas import tpu as pltpu
from jax.sharding import PartitionSpec as P

MX = 32
MY = 32
MZ = 16


SQRT_TWO_PI = math.sqrt(2.0 / math.pi)
CUBIC_COEF = 0.044715


def freq_index(retained, length):
    ladder = jnp.arange(retained, dtype=jnp.int32)
    return jnp.where(ladder < retained // 2, ladder, length - retained + ladder)


def cos_sin(wavenum, length):
    points = jnp.arange(length, dtype=jnp.int32)
    angles = (wavenum[:, None] * points[None, :] % length).astype(jnp.float32) * (
        2.0 * math.pi / length
    )
    return (jnp.cos(angles), jnp.sin(angles))


def analysis_pair(wavenum, length):
    cosine, sine_wave = cos_sin(wavenum, length)
    cosine, sine_wave = (cosine.T, sine_wave.T)
    return jnp.stack(
        [jnp.stack([cosine, -sine_wave], 1), jnp.stack([sine_wave, cosine], 1)], 1
    ).astype(jnp.bfloat16)


def synthesis_pair(wavenum, length):
    cosine, sine_wave = cos_sin(wavenum, length)
    return jnp.stack(
        [jnp.stack([cosine, sine_wave], 1), jnp.stack([-sine_wave, cosine], 1)], 1
    ).astype(jnp.bfloat16)


def depth_table(retained, length):
    cosine, sine_wave = cos_sin(jnp.arange(retained, dtype=jnp.int32), length)
    return jnp.concatenate([cosine, -sine_wave], 0).astype(jnp.bfloat16)


def gelu_parts(inputs):
    cubed_in = inputs * inputs * inputs
    tangent = jnp.tanh(SQRT_TWO_PI * (inputs + CUBIC_COEF * cubed_in))
    output = 0.5 * inputs * (1.0 + tangent)
    derivative = 0.5 * (1.0 + tangent) + 0.5 * inputs * (1.0 - tangent * tangent) * SQRT_TWO_PI * (
        1.0 + 3.0 * CUBIC_COEF * inputs * inputs
    )
    return (output, derivative)


def mode_product(coeffs, weights, channels):
    stacked = coeffs.reshape(coeffs.shape[0], 2, channels)
    halves = jnp.einsum("mac,mcj->amj", stacked, weights, preferred_element_type=jnp.float32)
    real_out = halves[0, :, :channels] - halves[1, :, channels:]
    imag_out = halves[0, :, channels:] + halves[1, :, :channels]
    return jnp.concatenate([real_out, imag_out], 1).astype(jnp.bfloat16)


def mode_grads(coeffs, weights, grad_modes, channels, weight_scale, input_scale):
    number = coeffs.shape[0]
    stacked = coeffs.reshape(number, 2, channels)
    grad_pairs = grad_modes.reshape(number, 2, channels)
    real_w = jnp.einsum("mac,mao->mco", stacked, grad_pairs, preferred_element_type=jnp.float32)
    imag_w = jnp.einsum(
        "mc,mo->mco", stacked[:, 0], grad_pairs[:, 1], preferred_element_type=jnp.float32
    ) - jnp.einsum(
        "mc,mo->mco", stacked[:, 1], grad_pairs[:, 0], preferred_element_type=jnp.float32
    )
    weight_grad = (jnp.concatenate([real_w, imag_w], 2) * weight_scale).astype(jnp.bfloat16)
    straight = jnp.concatenate([grad_pairs[:, 0], grad_pairs[:, 1]], 1)
    rotated = jnp.concatenate([grad_pairs[:, 1], -grad_pairs[:, 0]], 1)
    real_x = jnp.einsum("mcj,mj->mc", weights, straight, preferred_element_type=jnp.float32)
    imag_x = jnp.einsum("mcj,mj->mc", weights, rotated, preferred_element_type=jnp.float32)
    input_grad = (jnp.concatenate([real_x, imag_x], 1) * input_scale).astype(jnp.bfloat16)
    return (weight_grad, input_grad)


def general_body(features, cotangent, spectral_weight, channel_weight, channel_bias):
    channels, planes, lines, depth_len = features.shape
    devices = lax.axis_size("gx")
    all_planes = planes * devices
    owned_modes = spectral_weight.shape[0]
    wave_pairs = MY * MZ
    forward_scale = 1.0 / math.sqrt(all_planes * lines * depth_len)
    inverse_scale = 1.0 / math.sqrt(MX * wave_pairs)
    weight_scale = math.sqrt(MX * wave_pairs / (all_planes * lines * depth_len))
    depth_basis = depth_table(MZ, depth_len)
    across_y = analysis_pair(freq_index(MY, lines), lines)
    back_y = synthesis_pair(freq_index(MY, lines), lines)
    across_full = analysis_pair(freq_index(MX, all_planes), all_planes)
    back_full = synthesis_pair(freq_index(MX, all_planes), all_planes)
    depth_part = jnp.dot(features, depth_basis.T, preferred_element_type=jnp.float32).astype(
        jnp.bfloat16
    )
    plane_part = (
        jnp.einsum(
            "cxyaz,yabk->cxbkz",
            depth_part.reshape(channels, planes, lines, 2, MZ),
            across_y,
            preferred_element_type=jnp.float32,
        )
        .astype(jnp.bfloat16)
        .reshape(channels, planes, 2, wave_pairs)
    )
    all_rows = lax.all_to_all(plane_part, "gx", split_axis=3, concat_axis=1, tiled=True)
    mode_sums = jnp.einsum(
        "cxaq,xabk->qkbc", all_rows, across_full, preferred_element_type=jnp.float32
    ).reshape(owned_modes, 2 * channels)
    coeffs = (mode_sums * forward_scale).astype(jnp.bfloat16)
    spectral = mode_product(coeffs, spectral_weight, channels)
    planes_all = jnp.einsum(
        "qkao,kabx->oxbq",
        spectral.reshape(owned_modes // MX, MX, 2, channels),
        back_full,
        preferred_element_type=jnp.float32,
    ).astype(jnp.bfloat16)
    planes_back = lax.all_to_all(planes_all, "gx", split_axis=1, concat_axis=3, tiled=True)
    lines_back = (
        jnp.einsum(
            "oxakz,kaby->oxybz",
            planes_back.reshape(channels, planes, 2, MY, MZ),
            back_y,
            preferred_element_type=jnp.float32,
        )
        .astype(jnp.bfloat16)
        .reshape(channels, planes, lines, 2 * MZ)
    )
    spectral_term = (
        jnp.dot(lines_back, depth_basis, preferred_element_type=jnp.float32) * inverse_scale
    )
    pointwise = jnp.einsum(
        "oc,cxyz->oxyz", channel_weight, features, preferred_element_type=jnp.float32
    )
    hidden = spectral_term + pointwise + channel_bias[:, None, None, None]
    activated, derivative = gelu_parts(hidden)
    upstream = (cotangent.astype(jnp.float32) * derivative).astype(jnp.bfloat16)
    lines_grad = (
        jnp.dot(upstream, depth_basis.T, preferred_element_type=jnp.float32) * inverse_scale
    ).astype(jnp.bfloat16)
    rows_grad = (
        jnp.einsum(
            "oxybz,kaby->oxakz",
            lines_grad.reshape(channels, planes, lines, 2, MZ),
            back_y,
            preferred_element_type=jnp.float32,
        )
        .astype(jnp.bfloat16)
        .reshape(channels, planes, 2, wave_pairs)
    )
    all_grads = lax.all_to_all(rows_grad, "gx", split_axis=3, concat_axis=1, tiled=True)
    grad_sums = jnp.einsum(
        "oxbq,kabx->qkao", all_grads, back_full, preferred_element_type=jnp.float32
    ).reshape(owned_modes, 2 * channels)
    grad_modes = grad_sums.astype(jnp.bfloat16)
    spectral_grad, coeff_grad = mode_grads(
        coeffs, spectral_weight, grad_modes, channels, weight_scale, forward_scale
    )
    plane_all = jnp.einsum(
        "qkbc,xabk->cxaq",
        coeff_grad.reshape(owned_modes // MX, MX, 2, channels),
        across_full,
        preferred_element_type=jnp.float32,
    ).astype(jnp.bfloat16)
    plane_grad = lax.all_to_all(plane_all, "gx", split_axis=1, concat_axis=3, tiled=True)
    depth_grad = (
        jnp.einsum(
            "cxbkz,yabk->cxyaz",
            plane_grad.reshape(channels, planes, 2, MY, MZ),
            across_y,
            preferred_element_type=jnp.float32,
        )
        .astype(jnp.bfloat16)
        .reshape(channels, planes, lines, 2 * MZ)
    )
    channel_back = jnp.einsum(
        "oc,oxyz->cxyz", channel_weight, upstream, preferred_element_type=jnp.float32
    )
    feature_grad = (
        jnp.dot(depth_grad, depth_basis, preferred_element_type=jnp.float32) + channel_back
    ).astype(jnp.bfloat16)
    return (activated.astype(jnp.bfloat16), feature_grad, spectral_grad)


PLANES = 2
GROUP = 8
STEP = 16
VMEM_MIB = 32
VECTOR = 2
HEAD = 4
WAITS = {4: 4, 8: 4, 12: 4}
NT = (((1,), (1,)), ((), ()))
F32 = jnp.float32
BF16 = jnp.bfloat16


def np_freq(retained, length):
    ladder = np.arange(retained)
    return np.where(ladder < retained // 2, ladder, length - retained + ladder)


def np_angles(wavenum, length):
    points = np.arange(length)
    return (wavenum[:, None] * points[None, :] % length) * (2.0 * math.pi / length)


def as_bf16(table):
    return np.asarray(table, np.float32).astype(ml_dtypes.bfloat16)


def rotation(angle, sign):
    cosine, sine_wave = np.cos(angle), sign * np.sin(angle)
    return np.stack([np.stack([cosine, -sine_wave]), np.stack([sine_wave, cosine])])


@functools.lru_cache(maxsize=None)
def tables(devices, lines, depth_len):
    planes_all = devices * PLANES
    angle = np_angles(np.arange(MZ), depth_len)
    depth = np.stack([np.cos(angle), -np.sin(angle)])
    eye = np.eye(GROUP)
    depth_block = np.einsum("akz,ij->akijz", depth, eye).reshape(2 * MZ * GROUP, GROUP * depth_len)
    depth_pair = np.einsum("akz,ij->iakjz", depth, np.eye(2)).reshape(4 * MZ, 2 * depth_len)
    plane_eye = np.eye(PLANES)
    angle = np_angles(np_freq(MY, lines), lines).reshape(devices, MY // devices, lines)
    across = np.einsum("badly,xw->ldbxawy", rotation(angle, -1.0), plane_eye)
    across = across.reshape(MY * 2 * PLANES, 2 * PLANES * lines)
    back = np.einsum("pbdly,xw->pxyldbw", rotation(angle, 1.0), plane_eye)
    back = back.reshape(2 * PLANES * lines, MY * 2 * PLANES)
    angle = np_angles(np_freq(MX, planes_all), planes_all).reshape(MX // 4, 4, devices, PLANES)
    forward = rotation(angle, -1.0)
    rows = np.einsum("batksx->tbksax", forward).reshape(MX // 4, 2, 4, devices * 2 * PLANES)
    plain = rows.reshape(2 * MX, -1)
    both = np.stack([rows, rows[:, ::-1]], 1).reshape(4 * MX, -1)
    turned = np.concatenate([rows[:, 1:], -rows[:, :1]], 1).reshape(2 * MX, -1)
    straight_rotated = np.concatenate([plain, turned], 0)
    inverse = np.einsum("batksx->sbxtak", rotation(angle, 1.0)).reshape(-1, 2 * MX)
    return {
        "depth": as_bf16(depth_block),
        "depth_pair": as_bf16(depth_pair),
        "across_y": as_bf16(across),
        "back_y": as_bf16(back),
        "plain_x": as_bf16(plain),
        "both_x": as_bf16(both),
        "straight_x": as_bf16(straight_rotated),
        "back_x": as_bf16(inverse),
    }


def dot_nn(left, right):
    return jnp.dot(left, right, preferred_element_type=F32)


def dot_nt(left, right):
    return lax.dot_general(left, right, NT, preferred_element_type=F32)


def lanes(shape):
    return lax.broadcasted_iota(jnp.int32, shape, len(shape) - 1)


def sublanes(shape):
    return lax.broadcasted_iota(jnp.int32, shape, len(shape) - 2)


def swap_halves(block):
    return pltpu.roll(block, 64, 1)


def part_copy(source, target, sems, index, size):
    start = index * size if isinstance(index, int) else pl.multiple_of(index * size, size)
    part = pl.ds(start, size)
    return pltpu.make_async_copy(source.at[part], target.at[part], sems.at[index])


def start_parts(source, target, sems, size):
    for index in range(source.shape[0] // size):
        part_copy(source, target, sems, index, size).start()


def start_tables(pairs, sems):
    copies = []
    for index, (source, target) in enumerate(pairs):
        copy = pltpu.make_async_copy(source, target, sems.at[index])
        copy.start()
        copies.append(copy)
    return copies


def depth_quad(slabs, quad, depth_pair, scale, group, lines_ref):
    four = slabs[quad * 4 : quad * 4 + 4]
    wide = jnp.concatenate(
        [jnp.concatenate(four[2 * pair : 2 * pair + 2], axis=1) for pair in range(2)], axis=0
    )
    parts = dot_nt(depth_pair, wide)
    if scale is not None:
        parts = parts * scale
    half = wide.shape[0] // 2
    for pair in range(2):
        start = (group * GROUP + quad * 4 + pair * 2) * 2 * MZ
        if not isinstance(start, int):
            start = pl.multiple_of(start, 4 * MZ)
        lines_ref[pl.ds(start, 4 * MZ), :] = parts[:, pair * half : (pair + 1) * half]


def depth_analysis(slabs, depth_pair, scale, group, lines_ref):
    for quad in range(2):
        depth_quad(slabs, quad, depth_pair, scale, group, lines_ref)


def rows_analysis(lines_ref, across_ref, rows_ref, out_ref):
    channels = lines_ref.shape[0] // (2 * MZ)
    across = across_ref[...]
    half = across.shape[0] // 2
    for first in range(0, MZ // 2, 2):
        pair = jnp.concatenate(
            [
                jnp.concatenate(
                    [
                        lines_ref[pl.ds(a * MZ + kz, channels, stride=2 * MZ), :]
                        for a in range(2)
                    ],
                    axis=1,
                )
                for kz in range(2 * first, 2 * first + 4)
            ],
            axis=0,
        ).astype(BF16)
        rows = dot_nt(across, pair)
        for k in range(2):
            for kyl in range(2):
                rows_ref[pl.ds(kyl * 8 + first + k, half, stride=16), :] = rows[
                    kyl * half : (kyl + 1) * half, k * 128 : (k + 1) * 128
                ]
    out_ref[...] = rows_ref[...].astype(BF16)


def rows_gather(block_ref, rows_ref, spec_ref):
    rows_ref[...] = block_ref[...].astype(F32)
    count = rows_ref.shape[0] // 16
    eye = (sublanes((128, 128)) == lanes((128, 128))).astype(BF16)
    for first in range(0, MZ // 2, 2):
        both = jnp.concatenate(
            [
                rows_ref[pl.ds(kyl * 8 + first + k, count, stride=16), :]
                for k in range(2)
                for kyl in range(2)
            ],
            axis=0,
        ).astype(BF16)
        turned = dot_nt(eye, both)
        half = turned.shape[1] // 2
        for k in range(2):
            for h in range(2):
                at = (2 * (first + k) + h) * GROUP
                spec_ref[:, at : at + GROUP, :] = turned[
                    h * 64 : (h + 1) * 64, k * half : (k + 1) * half
                ].reshape(8, GROUP, half)


def lines_synthesis(step, spec_ref, back, scale):
    count = STEP // GROUP
    both = jnp.concatenate([spec_ref[step * count + g] for g in range(count)], axis=0)
    lines = dot_nt(back, both.astype(BF16))
    if scale is not None:
        lines = lines * scale
    lines = lines.astype(BF16)
    half = lines.shape[0] // 2
    return [
        jnp.concatenate(
            [lines[p * half : (p + 1) * half, g * 128 : (g + 1) * 128] for p in range(2)], axis=1
        )
        for g in range(count)
    ]


def flat(slab):
    return slab.reshape(slab.shape[0] * slab.shape[1], slab.shape[2])


def analysis_kernel(
    field_hbm,
    pair_hbm,
    across_hbm,
    out_ref,
    field_ref,
    pair_ref,
    across_ref,
    lines_ref,
    rows_ref,
    field_sems,
    table_sems,
):
    first, second = start_tables([(pair_hbm, pair_ref), (across_hbm, across_ref)], table_sems)
    start_parts(field_hbm, field_ref, field_sems, STEP)
    first.wait()

    @pl.loop(0, field_ref.shape[0] // STEP)
    def _(step):
        part_copy(field_hbm, field_ref, field_sems, step, STEP).wait()
        for g in range(STEP // GROUP):
            group = step * (STEP // GROUP) + g
            slabs = [flat(field_ref[group * GROUP + ci]) for ci in range(GROUP)]
            depth_analysis(slabs, pair_ref[...], None, group, lines_ref)

    second.wait()
    rows_analysis(lines_ref, across_ref, rows_ref, out_ref)


def middle_kernel(
    inverse_scale,
    block_ref,
    bias_ref,
    point_hbm,
    cot_hbm,
    depth_hbm,
    pair_hbm,
    across_hbm,
    back_hbm,
    act_hbm,
    up_hbm,
    out_ref,
    point_ref,
    cot_ref,
    depth_ref,
    pair_ref,
    across_ref,
    back_ref,
    act_ref,
    up_ref,
    lines_ref,
    rows_ref,
    spec_ref,
    point_sems,
    cot_sems,
    act_sems,
    up_sems,
    table_sems,
):
    tables_in = start_tables(
        [
            (back_hbm, back_ref),
            (depth_hbm, depth_ref),
            (pair_hbm, pair_ref),
            (across_hbm, across_ref),
        ],
        table_sems,
    )
    start_parts(point_hbm, point_ref, point_sems, STEP)
    start_parts(cot_hbm, cot_ref, cot_sems, STEP)
    rows_gather(block_ref, rows_ref, spec_ref)
    for copy in tables_in:
        copy.wait()
    steps = point_ref.shape[0] // STEP
    groups = point_ref.shape[0] // GROUP
    per_step = STEP // GROUP

    def activate(index, spectral):
        hidden = spectral + flat(point_ref[index]).astype(F32) + bias_ref[index]
        square = hidden * hidden
        gate = 0.5 + 0.5 * jnp.tanh(hidden * (SQRT_TWO_PI + (SQRT_TWO_PI * CUBIC_COEF) * square))
        slope = hidden * (2.0 * SQRT_TWO_PI + (6.0 * SQRT_TWO_PI * CUBIC_COEF) * square)
        derivative = gate + (gate - gate * gate) * slope
        upstream = (flat(cot_ref[index]).astype(F32) * derivative).astype(BF16)
        act_ref[index] = (hidden * gate).astype(BF16).reshape(act_ref.shape[1:])
        up_ref[index] = upstream.reshape(up_ref.shape[1:])
        return upstream

    def quarter(wide, at):
        return dot_nn(wide, depth_ref[:, at * 256 : (at + 1) * 256])

    wides = lines_synthesis(0, spec_ref, back_ref[...], inverse_scale)
    spectral = [quarter(wides[0], at) for at in range(4)]
    last = None
    for group in range(groups):
        step = group // per_step
        if group % per_step == 0:
            part_copy(point_hbm, point_ref, point_sems, step, STEP).wait()
            part_copy(cot_hbm, cot_ref, cot_sems, step, STEP).wait()
            if step + 1 < steps:
                wides += lines_synthesis(step + 1, spec_ref, back_ref[...], inverse_scale)
        following, slabs = [], []
        for at in range(4):
            if group + 1 < groups:
                following.append(quarter(wides[group + 1], at))
            for k in range(2):
                oi = 2 * at + k
                slabs.append(
                    activate(group * GROUP + oi, spectral[at][:, k * 128 : (k + 1) * 128])
                )
            if last is not None and at % 2 == 0:
                depth_quad(last, at // 2, pair_ref[...], inverse_scale, group - 1, lines_ref)
        if group % per_step == per_step - 1:
            part_copy(act_ref, act_hbm, act_sems, step, STEP).start()
            part_copy(up_ref, up_hbm, up_sems, step, STEP).start()
        spectral, last = following, slabs
    depth_analysis(last, pair_ref[...], inverse_scale, groups - 1, lines_ref)
    rows_analysis(lines_ref, across_ref, rows_ref, out_ref)
    for step in range(steps):
        part_copy(act_ref, act_hbm, act_sems, step, STEP).wait()
        part_copy(up_ref, up_hbm, up_sems, step, STEP).wait()


def final_kernel(
    block_ref,
    point_hbm,
    depth_hbm,
    back_hbm,
    out_hbm,
    point_ref,
    depth_ref,
    back_ref,
    out_ref,
    rows_ref,
    spec_ref,
    point_sems,
    out_sems,
    table_sems,
):
    tables_in = start_tables([(back_hbm, back_ref), (depth_hbm, depth_ref)], table_sems)
    start_parts(point_hbm, point_ref, point_sems, STEP)
    rows_gather(block_ref, rows_ref, spec_ref)
    for copy in tables_in:
        copy.wait()
    steps = point_ref.shape[0] // STEP
    groups = point_ref.shape[0] // GROUP
    per_step = STEP // GROUP

    def quarter(wide, at):
        return dot_nn(wide, depth_ref[:, at * 256 : (at + 1) * 256])

    wides = lines_synthesis(0, spec_ref, back_ref[...], None)
    spectral = [quarter(wides[0], at) for at in range(4)]
    for group in range(groups):
        step = group // per_step
        if group % per_step == 0:
            part_copy(point_hbm, point_ref, point_sems, step, STEP).wait()
            if step + 1 < steps:
                wides += lines_synthesis(step + 1, spec_ref, back_ref[...], None)
        following = []
        for at in range(4):
            if group + 1 < groups:
                following.append(quarter(wides[group + 1], at))
            for k in range(2):
                index = group * GROUP + 2 * at + k
                total = spectral[at][:, k * 128 : (k + 1) * 128] + flat(point_ref[index]).astype(F32)
                out_ref[index] = total.astype(BF16).reshape(out_ref.shape[1:])
        if group % per_step == per_step - 1:
            part_copy(out_ref, out_hbm, out_sems, step, STEP).start()
        spectral = following

    for step in range(steps):
        part_copy(out_ref, out_hbm, out_sems, step, STEP).wait()


def point_kernel(
    transposed,
    weight_ref,
    field_hbm,
    modes_hbm,
    out_hbm,
    head_ref,
    field_ref,
    out_ref,
    wide_ref,
    in_sems,
    out_sems,
    head_sems,
):
    size = wide_ref.shape[0]
    planes = field_ref.shape[1]
    copies = []
    for plane in range(planes):
        part = (slice(None), pl.ds(plane, 1))
        copy = pltpu.make_async_copy(field_hbm.at[part], field_ref.at[part], in_sems.at[plane])
        copy.start()
        copies.append(copy)
    heads = start_weights(modes_hbm, head_ref, head_sems, 0)
    tall = (sublanes((size, 64)) // 16 == lanes((size, 64))).astype(BF16)
    weight = weight_ref[...]
    left = dot_nt(tall, weight) if transposed else dot_nn(tall, weight)
    left = left.astype(BF16)
    rows = size // 4
    same = sublanes((rows, size)) % 16 == lanes((rows, size)) % 16
    for quarter in range(4):
        spread = dot_nt(left[quarter * rows : (quarter + 1) * rows], tall)
        wide_ref[quarter * rows : (quarter + 1) * rows, :] = jnp.where(same, spread, 0.0).astype(
            BF16
        )
    sends = []
    for plane in range(planes):
        copies[plane].wait()
        for pair in range(2):
            right = jnp.concatenate(
                [
                    field_ref[:, plane, yc * 16 : (yc + 1) * 16, :].reshape(size, 128)
                    for yc in (2 * pair, 2 * pair + 1)
                ],
                axis=1,
            )
            result = dot_nn(wide_ref[...], right).astype(BF16)
            for k in range(2):
                yc = 2 * pair + k
                out_ref[:, plane, yc * 16 : (yc + 1) * 16, :] = result[
                    :, k * 128 : (k + 1) * 128
                ].reshape(size // 16, 16, 128)
        part = (slice(None), pl.ds(plane, 1))
        copy = pltpu.make_async_copy(out_ref.at[part], out_hbm.at[part], out_sems.at[plane])
        copy.start()
        sends.append(copy)
    for copy in sends + heads:
        copy.wait()


def start_weights(weight_hbm, weight_ref, sems, first):
    rows = weight_hbm.shape[0] // 16
    copies = []
    for index in range(weight_ref.shape[0] // rows):
        copy = pltpu.make_async_copy(
            weight_hbm.at[pl.ds((first + index) * rows, rows)],
            weight_ref.at[pl.ds(index * rows, rows)],
            sems.at[index],
        )
        copy.start()
        copies.append(copy)
    return copies


def mode_pair(head_ref, weight_ref, j, h, u):
    source = head_ref if j < HEAD else weight_ref
    start = (((j if j < HEAD else j - HEAD) * 2 + h) * MX + 8 * u) * 64
    return jnp.concatenate(
        [source[start : start + 256, :], source[start + 256 : start + 512, :]], axis=1
    )


def plane_sums(back_ref, mixed_ref, res_ref, quarter):
    count = res_ref.shape[0] // 16
    wide = jnp.concatenate([mixed_ref[quarter * 4 + k] for k in range(4)], axis=1)
    rows = dot_nn(back_ref[...], wide)
    for k in range(4):
        res_ref[pl.ds(quarter * 4 + k, count, stride=16), :] = rows[:, k * 128 : (k + 1) * 128]


def mode_kernel(
    scale,
    block_ref,
    head_ref,
    weight_hbm,
    both_ref,
    plain_ref,
    back_ref,
    coeff_hbm,
    out_ref,
    coeff_ref,
    weight_ref,
    rows_ref,
    res_ref,
    left_ref,
    mixed_ref,
    sems,
    coeff_sems,
):
    copies = start_weights(weight_hbm, weight_ref, sems, HEAD)
    count = rows_ref.shape[0] // 16
    rows_ref[...] = block_ref[...].astype(F32)
    low = lanes((128, 128)) < 64
    kxl = sublanes((128, 128)) % 4
    half = lanes((128, 128)) // 64
    first = (kxl == half).astype(BF16)
    second = (kxl == 2 + half).astype(BF16)
    low8 = lanes((8, 128)) < 64
    sign = jnp.where(sublanes((8, 128)) < 4, -1.0, 1.0)
    for quarter in range(4):
        wide = jnp.concatenate(
            [rows_ref[pl.ds(quarter * 4 + k, count, stride=16), :] for k in range(4)], axis=1
        ).astype(BF16)
        plain = (dot_nn(plain_ref[...], wide) * scale).astype(BF16)
        both = dot_nn(both_ref[...], wide) * scale
        for k in range(4):
            j = quarter * 4 + k
            coeff_ref[j] = plain[:, k * 128 : (k + 1) * 128]
            coeffs = both[:, k * 128 : (k + 1) * 128]
            swapped = swap_halves(coeffs)
            for h in range(2):
                twice = jnp.where(low if h == 0 else ~low, coeffs, swapped).astype(BF16)
                left_ref[j, h] = jnp.concatenate([twice * first, twice * second], axis=1)
    send = pltpu.make_async_copy(coeff_ref, coeff_hbm, coeff_sems.at[0])
    send.start()
    for j in range(16):
        for copy in copies[j - HEAD : j - HEAD + WAITS.get(j, 0)]:
            copy.wait()
        mixed = []
        for u in range(MX // 8):
            halves = [
                dot_nn(left_ref[j, h, u * 32 : (u + 1) * 32, :], mode_pair(head_ref, weight_ref, j, h, u))
                for h in range(2)
            ]
            for t in range(2):
                low_h, high_h = [
                    part[t * 16 : (t + 1) * 16, t * 128 : (t + 1) * 128] for part in halves
                ]
                keep = jnp.where(low8, low_h[:8], sign * high_h[8:])
                move = jnp.where(low8, high_h[:8], sign * low_h[8:])
                mixed.append(keep + swap_halves(move))
        mixed_ref[j] = jnp.concatenate(mixed, axis=0).astype(BF16)
        if j % 4 == 3:
            plane_sums(back_ref, mixed_ref, res_ref, j // 4)
    out_ref[...] = res_ref[...].astype(BF16)
    send.wait()


def mode_grad_kernel(
    scale,
    block_ref,
    head_ref,
    weight_hbm,
    straight_ref,
    back_ref,
    coeff_hbm,
    pair_ref,
    coeff_ref,
    out_ref,
    weight_ref,
    rows_ref,
    res_ref,
    mixed_ref,
    sems,
    coeff_sems,
):
    send = pltpu.make_async_copy(coeff_hbm, coeff_ref, coeff_sems.at[0])
    send.start()
    copies = start_weights(weight_hbm, weight_ref, sems, HEAD)
    count = rows_ref.shape[0] // 16
    rows_ref[...] = block_ref[...].astype(F32)
    low = lanes((64, 128)) < 64
    low16 = lanes((16, 128)) < 64
    row = sublanes((16, 128)) % 4
    upper = row < 2
    valid = lanes((16, 128)) // 64 == row % 2
    even = (sublanes((16, 128)) < 8).astype(BF16)
    odd = (sublanes((16, 128)) >= 8).astype(BF16)
    for j in range(16):
        section = rows_ref[pl.ds(j, count, stride=16), :]
        swapped = swap_halves(section)
        twice = jnp.concatenate(
            [jnp.where(low, section, swapped), jnp.where(low, swapped, section)], axis=1
        ).astype(BF16)
        turned = dot_nn(straight_ref[...], twice)
        for h in range(2):
            part = turned[:, h * 128 : (h + 1) * 128]
            pair_ref[2 * j + h] = jnp.where(low, part[:64], part[64:]).astype(BF16)
    for j in range(16):
        for copy in copies[j - HEAD : j - HEAD + WAITS.get(j, 0)]:
            copy.wait()
        mixed = []
        for u in range(MX // 8):
            found = []
            for h in range(2):
                pair = pair_ref[2 * j + h, u * 16 : (u + 1) * 16, :]
                rows = dot_nt(
                    jnp.concatenate([pair * even, pair * odd], axis=1),
                    mode_pair(head_ref, weight_ref, j, h, u),
                )
                found.append(jnp.where(valid, jnp.where(upper, rows[:, :128], rows[:, 128:]), 0.0))
            keep = jnp.where(low16, found[0], found[1])
            move = jnp.where(low16, found[1], found[0])
            mixed.append(keep + swap_halves(move))
        mixed_ref[j] = (jnp.concatenate(mixed, axis=0) * scale).astype(BF16)
    for quarter in range(4):
        plane_sums(back_ref, mixed_ref, res_ref, quarter)
    out_ref[...] = res_ref[...].astype(BF16)
    send.wait()


def weight_grad_kernel(scale, coeff_ref, pair_ref, out_hbm, out_ref, mask_ref, pairs_ref, sems):
    lane = lanes((128, 64))
    part = sublanes((128, 64)) // 64
    for t in range(MX // 4 - VECTOR):
        mask_ref[t] = ((lane // 8 == t) & (lane % 4 // 2 == part)).astype(BF16)
    eye = (sublanes((128, 128)) == lanes((128, 128))).astype(BF16)
    even = (sublanes((64, 128)) % 2 == 0).astype(BF16)
    odd = (sublanes((64, 128)) % 2 == 1).astype(BF16)

    @pl.loop(0, 16)
    def _(j):
        turned = (dot_nt(eye, coeff_ref[j]) * scale).astype(BF16)
        for h in range(2):
            one = turned[h * 64 : (h + 1) * 64]
            left = jnp.concatenate([one, one], axis=0)
            pair = pair_ref[j * 2 + h]
            pairs_ref[h] = pair.astype(F32)
            right = jnp.concatenate([pair * even, pair * odd], axis=1)
            for t in range(MX // 4):
                mode = (j * 2 + h) * MX + 4 * t
                if t < MX // 4 - VECTOR:
                    four = dot_nn(left * mask_ref[t], right)
                    for k in range(4):
                        out_ref[mode + k] = four[
                            k // 2 * 64 : (k // 2 + 1) * 64, k % 2 * 128 : (k % 2 + 1) * 128
                        ].astype(BF16)
                    continue
                for k in range(4):
                    total = None
                    for b in range(2):
                        at = t * 8 + b * 4 + k
                        column = jnp.broadcast_to(one[:, at : at + 1], (64, 128))
                        row = jnp.broadcast_to(pairs_ref[h, at : at + 1, :], (64, 128)).astype(BF16)
                        total = column * row if total is None else total + column * row
                    out_ref[mode + k] = total
        part_copy(out_ref, out_hbm, sems, j, 2 * MX).start()

    for j in range(16):
        part_copy(out_ref, out_hbm, sems, j, 2 * MX).wait()


def params(mib):
    return pltpu.CompilerParams(vmem_limit_bytes=mib * 1024 * 1024)


def cost(flops, moved):
    return pl.CostEstimate(flops=int(flops), bytes_accessed=int(moved), transcendentals=0)


def fast_body(features, cotangent, spectral_weight, channel_weight, channel_bias):
    channels, planes, lines, depth_len = features.shape
    devices = lax.axis_size("gx")
    owned_modes = spectral_weight.shape[0]
    wave_pairs = MY * MZ
    volume = planes * devices * lines * depth_len
    forward_scale = 1.0 / math.sqrt(volume)
    inverse_scale = 1.0 / math.sqrt(MX * wave_pairs)
    weight_scale = math.sqrt(MX * wave_pairs / volume)
    table = {name: jnp.asarray(value) for name, value in tables(devices, lines, depth_len).items()}
    for name in ("depth", "depth_pair", "across_y", "back_y"):
        table[name] = pltpu.with_memory_space_constraint(table[name], pltpu.HBM)
    block_rows = devices * 64
    block_shape = jax.ShapeDtypeStruct((block_rows, 128), BF16)
    vmem = pl.BlockSpec(memory_space=pltpu.VMEM)
    hbm = pl.BlockSpec(memory_space=pltpu.HBM)
    smem = pl.BlockSpec(memory_space=pltpu.SMEM)
    field_scratch = pltpu.VMEM(features.shape, BF16)
    field_shape = jax.ShapeDtypeStruct(features.shape, BF16)

    def sems(count):
        return pltpu.SemaphoreType.DMA((count,))

    def scratch(name):
        return pltpu.VMEM(table[name].shape, BF16)

    def in_hbm(array):
        return pltpu.with_memory_space_constraint(array, pltpu.HBM)

    def in_vmem(array):
        return pltpu.with_memory_space_constraint(array, pltpu.VMEM)

    steps = channels // STEP
    lines_scratch = pltpu.VMEM((channels * 2 * MZ, planes * lines), F32)
    rows_scratch = pltpu.VMEM((block_rows, 128), F32)
    spec_scratch = pltpu.VMEM((channels // GROUP, MZ * GROUP, 128), F32)
    weight_rows = pltpu.with_memory_space_constraint(
        spectral_weight.reshape(owned_modes * channels, 2 * channels), pltpu.HBM
    )
    field_bytes = features.size * 2

    def exchange(block):
        return lax.all_to_all(
            block.reshape(devices, 64, 128), "gx", 0, 0, tiled=True
        ).reshape(block_rows, 128)

    def point(field, transposed):
        return pl.pallas_call(
            functools.partial(point_kernel, transposed),
            out_shape=[
                pltpu.HBM(features.shape, BF16),
                pltpu.VMEM((weight_rows.shape[0] * HEAD // 16, weight_rows.shape[1]), BF16),
            ],
            in_specs=[vmem, hbm, hbm],
            out_specs=[hbm, vmem],
            scratch_shapes=[
                field_scratch,
                field_scratch,
                pltpu.VMEM((channels * 16, channels * 16), BF16),
                sems(planes),
                sems(planes),
                sems(HEAD),
            ],
            compiler_params=params(VMEM_MIB),
            cost_estimate=cost(2 * 1024**3, 2 * field_bytes),
            name="channel_map_back" if transposed else "channel_map",
        )(channel_weight, in_hbm(field), weight_rows)

    block = pl.pallas_call(
        analysis_kernel,
        out_shape=block_shape,
        in_specs=[hbm, hbm, hbm],
        out_specs=vmem,
        scratch_shapes=[
            field_scratch,
            scratch("depth_pair"),
            scratch("across_y"),
            lines_scratch,
            rows_scratch,
            sems(steps),
            sems(2),
        ],
        compiler_params=params(VMEM_MIB),
        cost_estimate=cost(2 * 256 * 1024 * 1024, field_bytes),
        name="field_analysis",
    )(in_hbm(features), table["depth_pair"], table["across_y"])
    pointwise, head = point(features, False)
    block, pointwise, head = lax.optimization_barrier((exchange(block), pointwise, head))

    weight_scratch = pltpu.VMEM(
        (weight_rows.shape[0] * (16 - HEAD) // 16, weight_rows.shape[1]), BF16
    )
    mixed_scratch = pltpu.VMEM((16, 64, 128), BF16)
    weight_sems = sems(16 - HEAD)
    coeffs, block = pl.pallas_call(
        functools.partial(mode_kernel, forward_scale),
        out_shape=[pltpu.HBM((16, 64, 128), BF16), block_shape],
        in_specs=[vmem, vmem, hbm, vmem, vmem, vmem],
        out_specs=[hbm, vmem],
        scratch_shapes=[
            pltpu.VMEM((16, 64, 128), BF16),
            weight_scratch,
            rows_scratch,
            rows_scratch,
            pltpu.VMEM((16, 2, 128, 256), BF16),
            mixed_scratch,
            weight_sems,
            sems(1),
        ],
        compiler_params=params(VMEM_MIB),
        cost_estimate=cost(256 * 2 * 16 * 256 * 128, 17 * 2**20),
        name="mode_product",
    )(block, in_vmem(head), weight_rows, table["both_x"], table["plain_x"], table["back_x"])
    block = exchange(block)

    activated, upstream, block = pl.pallas_call(
        functools.partial(middle_kernel, inverse_scale),
        out_shape=[field_shape, pltpu.HBM(features.shape, BF16), block_shape],
        in_specs=[vmem, smem, hbm, hbm, hbm, hbm, hbm, hbm],
        out_specs=[hbm, hbm, vmem],
        scratch_shapes=[
            field_scratch,
            field_scratch,
            scratch("depth"),
            scratch("depth_pair"),
            scratch("across_y"),
            scratch("back_y"),
            field_scratch,
            field_scratch,
            lines_scratch,
            rows_scratch,
            spec_scratch,
            sems(steps),
            sems(steps),
            sems(steps),
            sems(steps),
            sems(4),
        ],
        compiler_params=params(VMEM_MIB),
        cost_estimate=cost(2**30, 4 * field_bytes),
        name="gelu_and_gradient",
    )(
        block,
        channel_bias,
        in_hbm(pointwise),
        in_hbm(cotangent),
        table["depth"],
        table["depth_pair"],
        table["across_y"],
        table["back_y"],
    )
    channel_back, head = point(upstream, True)
    block, channel_back, head = lax.optimization_barrier((exchange(block), channel_back, head))

    pairs, coeffs, block = pl.pallas_call(
        functools.partial(mode_grad_kernel, forward_scale),
        out_shape=[
            pltpu.VMEM((32, 64, 128), BF16),
            pltpu.VMEM((16, 64, 128), BF16),
            block_shape,
        ],
        in_specs=[vmem, vmem, hbm, vmem, vmem, hbm],
        out_specs=[vmem, vmem, vmem],
        scratch_shapes=[
            weight_scratch,
            rows_scratch,
            rows_scratch,
            mixed_scratch,
            weight_sems,
            sems(1),
        ],
        compiler_params=params(VMEM_MIB),
        cost_estimate=cost(256 * 2 * 16 * 256 * 128, 17 * 2**20),
        name="mode_gradient",
    )(block, in_vmem(head), weight_rows, table["straight_x"], table["back_x"], in_hbm(coeffs))
    block = exchange(block)

    spectral_grad = pl.pallas_call(
        functools.partial(weight_grad_kernel, weight_scale),
        out_shape=jax.ShapeDtypeStruct(spectral_weight.shape, BF16),
        in_specs=[vmem, vmem],
        out_specs=hbm,
        scratch_shapes=[
            pltpu.VMEM(spectral_weight.shape, BF16),
            pltpu.VMEM((MX // 4, 128, 64), BF16),
            pltpu.VMEM((2, 64, 128), F32),
            sems(16),
        ],
        compiler_params=params(VMEM_MIB),
        cost_estimate=cost(512 * 2 * 64 * 64 * 256, 17 * 2**20),
        name="weight_gradient",
    )(
        in_vmem(coeffs),
        in_vmem(pairs),
    )

    feature_grad = pl.pallas_call(
        final_kernel,
        out_shape=field_shape,
        in_specs=[vmem, hbm, hbm, hbm],
        out_specs=hbm,
        scratch_shapes=[
            field_scratch,
            scratch("depth"),
            scratch("back_y"),
            field_scratch,
            rows_scratch,
            spec_scratch,
            sems(steps),
            sems(steps),
            sems(2),
        ],
        compiler_params=params(VMEM_MIB),
        cost_estimate=cost(2**29, 2 * field_bytes),
        name="field_gradient",
    )(block, in_hbm(channel_back), table["depth"], table["back_y"])
    return (activated, feature_grad, spectral_grad)


def body(features, cotangent, spectral_weight, channel_weight, channel_bias):
    channels, planes, lines, depth_len = features.shape
    devices = lax.axis_size("gx")
    fits = (
        (channels, planes, lines, depth_len) == (64, PLANES, 64, 128)
        and spectral_weight.shape[0] == 2 * MZ * MX
        and devices * 2 == MY
        and devices * 2 == MX
    )
    run = fast_body if fits else general_body
    return run(features, cotangent, spectral_weight, channel_weight, channel_bias)


def solution(mesh):
    in_specs = (
        P("grp", "gx", None, None),
        P("grp", "gx", None, None),
        P("gx", None, None),
        P(),
        P(),
    )
    out_specs = (
        P("grp", "gx", None, None),
        P("grp", "gx", None, None),
        P(("grp", "gx"), None, None),
    )
    return jax.shard_map(body, mesh=mesh, in_specs=in_specs, out_specs=out_specs, check_vma=False)
```

```python
import functools
import math

import jax
import jax.numpy as jnp
import ml_dtypes
import numpy as np
from jax import lax
from jax.experimental import pallas as pl
from jax.experimental.pallas import tpu as pltpu
from jax.sharding import PartitionSpec as P

MX = 32
MY = 32
MZ = 16


SQRT_TWO_PI = math.sqrt(2.0 / math.pi)
CUBIC_COEF = 0.044715


def freq_index(retained, length):
    ladder = jnp.arange(retained, dtype=jnp.int32)
    return jnp.where(ladder < retained // 2, ladder, length - retained + ladder)


def cos_sin(wavenum, length):
    points = jnp.arange(length, dtype=jnp.int32)
    angles = (wavenum[:, None] * points[None, :] % length).astype(jnp.float32) * (
        2.0 * math.pi / length
    )
    return (jnp.cos(angles), jnp.sin(angles))


def analysis_pair(wavenum, length):
    cosine, sine_wave = cos_sin(wavenum, length)
    cosine, sine_wave = (cosine.T, sine_wave.T)
    return jnp.stack(
        [jnp.stack([cosine, -sine_wave], 1), jnp.stack([sine_wave, cosine], 1)], 1
    ).astype(jnp.bfloat16)


def synthesis_pair(wavenum, length):
    cosine, sine_wave = cos_sin(wavenum, length)
    return jnp.stack(
        [jnp.stack([cosine, sine_wave], 1), jnp.stack([-sine_wave, cosine], 1)], 1
    ).astype(jnp.bfloat16)


def depth_table(retained, length):
    cosine, sine_wave = cos_sin(jnp.arange(retained, dtype=jnp.int32), length)
    return jnp.concatenate([cosine, -sine_wave], 0).astype(jnp.bfloat16)


def gelu_parts(inputs):
    cubed_in = inputs * inputs * inputs
    tangent = jnp.tanh(SQRT_TWO_PI * (inputs + CUBIC_COEF * cubed_in))
    output = 0.5 * inputs * (1.0 + tangent)
    derivative = 0.5 * (1.0 + tangent) + 0.5 * inputs * (1.0 - tangent * tangent) * SQRT_TWO_PI * (
        1.0 + 3.0 * CUBIC_COEF * inputs * inputs
    )
    return (output, derivative)


def mode_product(coeffs, weights, channels):
    stacked = coeffs.reshape(coeffs.shape[0], 2, channels)
    halves = jnp.einsum("mac,mcj->amj", stacked, weights, preferred_element_type=jnp.float32)
    real_out = halves[0, :, :channels] - halves[1, :, channels:]
    imag_out = halves[0, :, channels:] + halves[1, :, :channels]
    return jnp.concatenate([real_out, imag_out], 1).astype(jnp.bfloat16)


def mode_grads(coeffs, weights, grad_modes, channels, weight_scale, input_scale):
    number = coeffs.shape[0]
    stacked = coeffs.reshape(number, 2, channels)
    grad_pairs = grad_modes.reshape(number, 2, channels)
    real_w = jnp.einsum("mac,mao->mco", stacked, grad_pairs, preferred_element_type=jnp.float32)
    imag_w = jnp.einsum(
        "mc,mo->mco", stacked[:, 0], grad_pairs[:, 1], preferred_element_type=jnp.float32
    ) - jnp.einsum(
        "mc,mo->mco", stacked[:, 1], grad_pairs[:, 0], preferred_element_type=jnp.float32
    )
    weight_grad = (jnp.concatenate([real_w, imag_w], 2) * weight_scale).astype(jnp.bfloat16)
    straight = jnp.concatenate([grad_pairs[:, 0], grad_pairs[:, 1]], 1)
    rotated = jnp.concatenate([grad_pairs[:, 1], -grad_pairs[:, 0]], 1)
    real_x = jnp.einsum("mcj,mj->mc", weights, straight, preferred_element_type=jnp.float32)
    imag_x = jnp.einsum("mcj,mj->mc", weights, rotated, preferred_element_type=jnp.float32)
    input_grad = (jnp.concatenate([real_x, imag_x], 1) * input_scale).astype(jnp.bfloat16)
    return (weight_grad, input_grad)


def general_body(features, cotangent, spectral_weight, channel_weight, channel_bias):
    channels, planes, lines, depth_len = features.shape
    devices = lax.axis_size("gx")
    all_planes = planes * devices
    owned_modes = spectral_weight.shape[0]
    wave_pairs = MY * MZ
    forward_scale = 1.0 / math.sqrt(all_planes * lines * depth_len)
    inverse_scale = 1.0 / math.sqrt(MX * wave_pairs)
    weight_scale = math.sqrt(MX * wave_pairs / (all_planes * lines * depth_len))
    depth_basis = depth_table(MZ, depth_len)
    across_y = analysis_pair(freq_index(MY, lines), lines)
    back_y = synthesis_pair(freq_index(MY, lines), lines)
    across_full = analysis_pair(freq_index(MX, all_planes), all_planes)
    back_full = synthesis_pair(freq_index(MX, all_planes), all_planes)
    depth_part = jnp.dot(features, depth_basis.T, preferred_element_type=jnp.float32).astype(
        jnp.bfloat16
    )
    plane_part = (
        jnp.einsum(
            "cxyaz,yabk->cxbkz",
            depth_part.reshape(channels, planes, lines, 2, MZ),
            across_y,
            preferred_element_type=jnp.float32,
        )
        .astype(jnp.bfloat16)
        .reshape(channels, planes, 2, wave_pairs)
    )
    all_rows = lax.all_to_all(plane_part, "gx", split_axis=3, concat_axis=1, tiled=True)
    mode_sums = jnp.einsum(
        "cxaq,xabk->qkbc", all_rows, across_full, preferred_element_type=jnp.float32
    ).reshape(owned_modes, 2 * channels)
    coeffs = (mode_sums * forward_scale).astype(jnp.bfloat16)
    spectral = mode_product(coeffs, spectral_weight, channels)
    planes_all = jnp.einsum(
        "qkao,kabx->oxbq",
        spectral.reshape(owned_modes // MX, MX, 2, channels),
        back_full,
        preferred_element_type=jnp.float32,
    ).astype(jnp.bfloat16)
    planes_back = lax.all_to_all(planes_all, "gx", split_axis=1, concat_axis=3, tiled=True)
    lines_back = (
        jnp.einsum(
            "oxakz,kaby->oxybz",
            planes_back.reshape(channels, planes, 2, MY, MZ),
            back_y,
            preferred_element_type=jnp.float32,
        )
        .astype(jnp.bfloat16)
        .reshape(channels, planes, lines, 2 * MZ)
    )
    spectral_term = (
        jnp.dot(lines_back, depth_basis, preferred_element_type=jnp.float32) * inverse_scale
    )
    pointwise = jnp.einsum(
        "oc,cxyz->oxyz", channel_weight, features, preferred_element_type=jnp.float32
    )
    hidden = spectral_term + pointwise + channel_bias[:, None, None, None]
    activated, derivative = gelu_parts(hidden)
    upstream = (cotangent.astype(jnp.float32) * derivative).astype(jnp.bfloat16)
    lines_grad = (
        jnp.dot(upstream, depth_basis.T, preferred_element_type=jnp.float32) * inverse_scale
    ).astype(jnp.bfloat16)
    rows_grad = (
        jnp.einsum(
            "oxybz,kaby->oxakz",
            lines_grad.reshape(channels, planes, lines, 2, MZ),
            back_y,
            preferred_element_type=jnp.float32,
        )
        .astype(jnp.bfloat16)
        .reshape(channels, planes, 2, wave_pairs)
    )
    all_grads = lax.all_to_all(rows_grad, "gx", split_axis=3, concat_axis=1, tiled=True)
    grad_sums = jnp.einsum(
        "oxbq,kabx->qkao", all_grads, back_full, preferred_element_type=jnp.float32
    ).reshape(owned_modes, 2 * channels)
    grad_modes = grad_sums.astype(jnp.bfloat16)
    spectral_grad, coeff_grad = mode_grads(
        coeffs, spectral_weight, grad_modes, channels, weight_scale, forward_scale
    )
    plane_all = jnp.einsum(
        "qkbc,xabk->cxaq",
        coeff_grad.reshape(owned_modes // MX, MX, 2, channels),
        across_full,
        preferred_element_type=jnp.float32,
    ).astype(jnp.bfloat16)
    plane_grad = lax.all_to_all(plane_all, "gx", split_axis=1, concat_axis=3, tiled=True)
    depth_grad = (
        jnp.einsum(
            "cxbkz,yabk->cxyaz",
            plane_grad.reshape(channels, planes, 2, MY, MZ),
            across_y,
            preferred_element_type=jnp.float32,
        )
        .astype(jnp.bfloat16)
        .reshape(channels, planes, lines, 2 * MZ)
    )
    channel_back = jnp.einsum(
        "oc,oxyz->cxyz", channel_weight, upstream, preferred_element_type=jnp.float32
    )
    feature_grad = (
        jnp.dot(depth_grad, depth_basis, preferred_element_type=jnp.float32) + channel_back
    ).astype(jnp.bfloat16)
    return (activated.astype(jnp.bfloat16), feature_grad, spectral_grad)


PLANES = 2
GROUP = 8
STEP = 16
VMEM_MIB = 32
VECTOR = 2
HEAD = 2
WAITS = {2: 2, 4: 4, 8: 4, 12: 4}
NT = (((1,), (1,)), ((), ()))
F32 = jnp.float32
BF16 = jnp.bfloat16


def np_freq(retained, length):
    ladder = np.arange(retained)
    return np.where(ladder < retained // 2, ladder, length - retained + ladder)


def np_angles(wavenum, length):
    points = np.arange(length)
    return (wavenum[:, None] * points[None, :] % length) * (2.0 * math.pi / length)


def as_bf16(table):
    return np.asarray(table, np.float32).astype(ml_dtypes.bfloat16)


def rotation(angle, sign):
    cosine, sine_wave = np.cos(angle), sign * np.sin(angle)
    return np.stack([np.stack([cosine, -sine_wave]), np.stack([sine_wave, cosine])])


@functools.lru_cache(maxsize=None)
def tables(devices, lines, depth_len):
    planes_all = devices * PLANES
    angle = np_angles(np.arange(MZ), depth_len)
    depth = np.stack([np.cos(angle), -np.sin(angle)])
    eye = np.eye(GROUP)
    depth_block = np.einsum("akz,ij->akijz", depth, eye).reshape(2 * MZ * GROUP, GROUP * depth_len)
    depth_pair = np.einsum("akz,ij->iakjz", depth, np.eye(2)).reshape(4 * MZ, 2 * depth_len)
    plane_eye = np.eye(PLANES)
    angle = np_angles(np_freq(MY, lines), lines).reshape(devices, MY // devices, lines)
    across = np.einsum("badly,xw->ldbxawy", rotation(angle, -1.0), plane_eye)
    across = across.reshape(MY * 2 * PLANES, 2 * PLANES * lines)
    back = np.einsum("pbdly,xw->pxyldbw", rotation(angle, 1.0), plane_eye)
    back = back.reshape(2 * PLANES * lines, MY * 2 * PLANES)
    angle = np_angles(np_freq(MX, planes_all), planes_all).reshape(MX // 4, 4, devices, PLANES)
    forward = rotation(angle, -1.0)
    rows = np.einsum("batksx->tbksax", forward).reshape(MX // 4, 2, 4, devices * 2 * PLANES)
    plain = rows.reshape(2 * MX, -1)
    both = np.stack([rows, rows[:, ::-1]], 1).reshape(4 * MX, -1)
    turned = np.concatenate([rows[:, 1:], -rows[:, :1]], 1).reshape(2 * MX, -1)
    straight_rotated = np.concatenate([plain, turned], 0)
    inverse = np.einsum("batksx->sbxtak", rotation(angle, 1.0)).reshape(-1, 2 * MX)
    return {
        "depth": as_bf16(depth_block),
        "depth_pair": as_bf16(depth_pair),
        "across_y": as_bf16(across),
        "back_y": as_bf16(back),
        "plain_x": as_bf16(plain),
        "both_x": as_bf16(both),
        "straight_x": as_bf16(straight_rotated),
        "back_x": as_bf16(inverse),
    }


def dot_nn(left, right):
    return jnp.dot(left, right, preferred_element_type=F32)


def dot_nt(left, right):
    return lax.dot_general(left, right, NT, preferred_element_type=F32)


def lanes(shape):
    return lax.broadcasted_iota(jnp.int32, shape, len(shape) - 1)


def sublanes(shape):
    return lax.broadcasted_iota(jnp.int32, shape, len(shape) - 2)


def swap_halves(block):
    return pltpu.roll(block, 64, 1)


def part_copy(source, target, sems, index, size):
    start = index * size if isinstance(index, int) else pl.multiple_of(index * size, size)
    part = pl.ds(start, size)
    return pltpu.make_async_copy(source.at[part], target.at[part], sems.at[index])


def start_parts(source, target, sems, size):
    for index in range(source.shape[0] // size):
        part_copy(source, target, sems, index, size).start()


def start_tables(pairs, sems):
    copies = []
    for index, (source, target) in enumerate(pairs):
        copy = pltpu.make_async_copy(source, target, sems.at[index])
        copy.start()
        copies.append(copy)
    return copies


def depth_quad(slabs, quad, depth_pair, scale, group, lines_ref):
    four = slabs[quad * 4 : quad * 4 + 4]
    wide = jnp.concatenate(
        [jnp.concatenate(four[2 * pair : 2 * pair + 2], axis=1) for pair in range(2)], axis=0
    )
    parts = dot_nt(depth_pair, wide)
    if scale is not None:
        parts = parts * scale
    half = wide.shape[0] // 2
    for pair in range(2):
        start = (group * GROUP + quad * 4 + pair * 2) * 2 * MZ
        if not isinstance(start, int):
            start = pl.multiple_of(start, 4 * MZ)
        lines_ref[pl.ds(start, 4 * MZ), :] = parts[:, pair * half : (pair + 1) * half]


def depth_analysis(slabs, depth_pair, scale, group, lines_ref):
    for quad in range(2):
        depth_quad(slabs, quad, depth_pair, scale, group, lines_ref)


def rows_analysis(lines_ref, across_ref, rows_ref, out_ref):
    channels = lines_ref.shape[0] // (2 * MZ)
    across = across_ref[...]
    half = across.shape[0] // 2
    for first in range(0, MZ // 2, 2):
        pair = jnp.concatenate(
            [
                jnp.concatenate(
                    [
                        lines_ref[pl.ds(a * MZ + kz, channels, stride=2 * MZ), :]
                        for a in range(2)
                    ],
                    axis=1,
                )
                for kz in range(2 * first, 2 * first + 4)
            ],
            axis=0,
        ).astype(BF16)
        rows = dot_nt(across, pair)
        for k in range(2):
            for kyl in range(2):
                rows_ref[pl.ds(kyl * 8 + first + k, half, stride=16), :] = rows[
                    kyl * half : (kyl + 1) * half, k * 128 : (k + 1) * 128
                ]
    out_ref[...] = rows_ref[...].astype(BF16)


def rows_gather(block_ref, rows_ref, spec_ref):
    rows_ref[...] = block_ref[...].astype(F32)
    count = rows_ref.shape[0] // 16
    eye = (sublanes((128, 128)) == lanes((128, 128))).astype(BF16)
    for first in range(0, MZ // 2, 2):
        both = jnp.concatenate(
            [
                rows_ref[pl.ds(kyl * 8 + first + k, count, stride=16), :]
                for k in range(2)
                for kyl in range(2)
            ],
            axis=0,
        ).astype(BF16)
        turned = dot_nt(eye, both)
        half = turned.shape[1] // 2
        for k in range(2):
            for h in range(2):
                at = (2 * (first + k) + h) * GROUP
                spec_ref[:, at : at + GROUP, :] = turned[
                    h * 64 : (h + 1) * 64, k * half : (k + 1) * half
                ].reshape(8, GROUP, half)


def lines_synthesis(step, spec_ref, back, scale):
    count = STEP // GROUP
    both = jnp.concatenate([spec_ref[step * count + g] for g in range(count)], axis=0)
    lines = dot_nt(back, both.astype(BF16))
    if scale is not None:
        lines = lines * scale
    lines = lines.astype(BF16)
    half = lines.shape[0] // 2
    return [
        jnp.concatenate(
            [lines[p * half : (p + 1) * half, g * 128 : (g + 1) * 128] for p in range(2)], axis=1
        )
        for g in range(count)
    ]


def flat(slab):
    return slab.reshape(slab.shape[0] * slab.shape[1], slab.shape[2])


def analysis_kernel(
    field_hbm,
    pair_hbm,
    across_hbm,
    out_ref,
    field_ref,
    pair_ref,
    across_ref,
    lines_ref,
    rows_ref,
    field_sems,
    table_sems,
):
    first, second = start_tables([(pair_hbm, pair_ref), (across_hbm, across_ref)], table_sems)
    start_parts(field_hbm, field_ref, field_sems, STEP)
    first.wait()

    for step in range(field_ref.shape[0] // STEP):
        part_copy(field_hbm, field_ref, field_sems, step, STEP).wait()
        for g in range(STEP // GROUP):
            group = step * (STEP // GROUP) + g
            slabs = [flat(field_ref[group * GROUP + ci]) for ci in range(GROUP)]
            depth_analysis(slabs, pair_ref[...], None, group, lines_ref)

    second.wait()
    rows_analysis(lines_ref, across_ref, rows_ref, out_ref)


def middle_kernel(
    inverse_scale,
    block_ref,
    bias_ref,
    point_hbm,
    cot_hbm,
    depth_hbm,
    pair_hbm,
    across_hbm,
    back_hbm,
    act_hbm,
    up_hbm,
    out_ref,
    point_ref,
    cot_ref,
    depth_ref,
    pair_ref,
    across_ref,
    back_ref,
    act_ref,
    up_ref,
    lines_ref,
    rows_ref,
    spec_ref,
    point_sems,
    cot_sems,
    act_sems,
    up_sems,
    table_sems,
):
    tables_in = start_tables(
        [
            (back_hbm, back_ref),
            (depth_hbm, depth_ref),
            (pair_hbm, pair_ref),
            (across_hbm, across_ref),
        ],
        table_sems,
    )
    start_parts(point_hbm, point_ref, point_sems, STEP)
    start_parts(cot_hbm, cot_ref, cot_sems, STEP)
    rows_gather(block_ref, rows_ref, spec_ref)
    for copy in tables_in:
        copy.wait()
    steps = point_ref.shape[0] // STEP
    groups = point_ref.shape[0] // GROUP
    per_step = STEP // GROUP

    def activate(index, spectral):
        hidden = spectral + flat(point_ref[index]).astype(F32) + bias_ref[index]
        square = hidden * hidden
        gate = 0.5 + 0.5 * jnp.tanh(hidden * (SQRT_TWO_PI + (SQRT_TWO_PI * CUBIC_COEF) * square))
        slope = hidden * (2.0 * SQRT_TWO_PI + (6.0 * SQRT_TWO_PI * CUBIC_COEF) * square)
        derivative = gate + (gate - gate * gate) * slope
        upstream = (flat(cot_ref[index]).astype(F32) * derivative).astype(BF16)
        act_ref[index] = (hidden * gate).astype(BF16).reshape(act_ref.shape[1:])
        up_ref[index] = upstream.reshape(up_ref.shape[1:])
        return upstream

    def quarter(wide, at):
        return dot_nn(wide, depth_ref[:, at * 256 : (at + 1) * 256])

    wides = lines_synthesis(0, spec_ref, back_ref[...], inverse_scale)
    spectral = [quarter(wides[0], at) for at in range(4)]
    last = None
    for group in range(groups):
        step = group // per_step
        if group % per_step == 0:
            part_copy(point_hbm, point_ref, point_sems, step, STEP).wait()
            part_copy(cot_hbm, cot_ref, cot_sems, step, STEP).wait()
            if step + 1 < steps:
                wides += lines_synthesis(step + 1, spec_ref, back_ref[...], inverse_scale)
        following, slabs = [], []
        for at in range(4):
            if group + 1 < groups:
                following.append(quarter(wides[group + 1], at))
            for k in range(2):
                oi = 2 * at + k
                slabs.append(
                    activate(group * GROUP + oi, spectral[at][:, k * 128 : (k + 1) * 128])
                )
            if last is not None and at % 2 == 0:
                depth_quad(last, at // 2, pair_ref[...], inverse_scale, group - 1, lines_ref)
        if group % per_step == per_step - 1:
            part_copy(act_ref, act_hbm, act_sems, step, STEP).start()
            part_copy(up_ref, up_hbm, up_sems, step, STEP).start()
        spectral, last = following, slabs
    depth_analysis(last, pair_ref[...], inverse_scale, groups - 1, lines_ref)
    rows_analysis(lines_ref, across_ref, rows_ref, out_ref)
    for step in range(steps):
        part_copy(act_ref, act_hbm, act_sems, step, STEP).wait()
        part_copy(up_ref, up_hbm, up_sems, step, STEP).wait()


def final_kernel(
    block_ref,
    point_hbm,
    depth_hbm,
    back_hbm,
    out_hbm,
    point_ref,
    depth_ref,
    back_ref,
    out_ref,
    rows_ref,
    spec_ref,
    point_sems,
    out_sems,
    table_sems,
):
    tables_in = start_tables([(back_hbm, back_ref), (depth_hbm, depth_ref)], table_sems)
    start_parts(point_hbm, point_ref, point_sems, STEP)
    rows_gather(block_ref, rows_ref, spec_ref)
    for copy in tables_in:
        copy.wait()
    steps = point_ref.shape[0] // STEP
    groups = point_ref.shape[0] // GROUP
    per_step = STEP // GROUP

    def quarter(wide, at):
        return dot_nn(wide, depth_ref[:, at * 256 : (at + 1) * 256])

    wides = lines_synthesis(0, spec_ref, back_ref[...], None)
    spectral = [quarter(wides[0], at) for at in range(4)]
    for group in range(groups):
        step = group // per_step
        if group % per_step == 0:
            part_copy(point_hbm, point_ref, point_sems, step, STEP).wait()
            if step + 1 < steps:
                wides += lines_synthesis(step + 1, spec_ref, back_ref[...], None)
        following = []
        for at in range(4):
            if group + 1 < groups:
                following.append(quarter(wides[group + 1], at))
            for k in range(2):
                index = group * GROUP + 2 * at + k
                total = spectral[at][:, k * 128 : (k + 1) * 128] + flat(point_ref[index]).astype(F32)
                out_ref[index] = total.astype(BF16).reshape(out_ref.shape[1:])
        if group % per_step == per_step - 1:
            part_copy(out_ref, out_hbm, out_sems, step, STEP).start()
        spectral = following

    for step in range(steps):
        part_copy(out_ref, out_hbm, out_sems, step, STEP).wait()


def point_kernel(
    transposed,
    weight_ref,
    field_hbm,
    modes_hbm,
    out_hbm,
    head_ref,
    field_ref,
    out_ref,
    wide_ref,
    in_sems,
    out_sems,
    head_sems,
):
    size = wide_ref.shape[0]
    planes = field_ref.shape[1]
    copies = []
    for plane in range(planes):
        part = (slice(None), pl.ds(plane, 1))
        copy = pltpu.make_async_copy(field_hbm.at[part], field_ref.at[part], in_sems.at[plane])
        copy.start()
        copies.append(copy)
    heads = start_weights(modes_hbm, head_ref, head_sems, 0)
    tall = (sublanes((size, 64)) // 16 == lanes((size, 64))).astype(BF16)
    weight = weight_ref[...]
    left = dot_nt(tall, weight) if transposed else dot_nn(tall, weight)
    left = left.astype(BF16)
    rows = size // 4
    same = sublanes((rows, size)) % 16 == lanes((rows, size)) % 16
    for quarter in range(4):
        spread = dot_nt(left[quarter * rows : (quarter + 1) * rows], tall)
        wide_ref[quarter * rows : (quarter + 1) * rows, :] = jnp.where(same, spread, 0.0).astype(
            BF16
        )
    sends = []
    for plane in range(planes):
        copies[plane].wait()
        for pair in range(2):
            right = jnp.concatenate(
                [
                    field_ref[:, plane, yc * 16 : (yc + 1) * 16, :].reshape(size, 128)
                    for yc in (2 * pair, 2 * pair + 1)
                ],
                axis=1,
            )
            result = dot_nn(wide_ref[...], right).astype(BF16)
            for k in range(2):
                yc = 2 * pair + k
                out_ref[:, plane, yc * 16 : (yc + 1) * 16, :] = result[
                    :, k * 128 : (k + 1) * 128
                ].reshape(size // 16, 16, 128)
        part = (slice(None), pl.ds(plane, 1))
        copy = pltpu.make_async_copy(out_ref.at[part], out_hbm.at[part], out_sems.at[plane])
        copy.start()
        sends.append(copy)
    for copy in sends + heads:
        copy.wait()


def start_weights(weight_hbm, weight_ref, sems, first):
    rows = weight_hbm.shape[0] // 16
    copies = []
    for index in range(weight_ref.shape[0] // rows):
        copy = pltpu.make_async_copy(
            weight_hbm.at[pl.ds((first + index) * rows, rows)],
            weight_ref.at[pl.ds(index * rows, rows)],
            sems.at[index],
        )
        copy.start()
        copies.append(copy)
    return copies


def mode_pair(head_ref, weight_ref, j, h, u):
    source = head_ref if j < HEAD else weight_ref
    start = (((j if j < HEAD else j - HEAD) * 2 + h) * MX + 8 * u) * 64
    return jnp.concatenate(
        [source[start : start + 256, :], source[start + 256 : start + 512, :]], axis=1
    )


def plane_sums(back_ref, mixed_ref, res_ref, quarter):
    count = res_ref.shape[0] // 16
    wide = jnp.concatenate([mixed_ref[quarter * 4 + k] for k in range(4)], axis=1)
    rows = dot_nn(back_ref[...], wide)
    for k in range(4):
        res_ref[pl.ds(quarter * 4 + k, count, stride=16), :] = rows[:, k * 128 : (k + 1) * 128]


def mode_kernel(
    scale,
    block_ref,
    head_ref,
    weight_hbm,
    both_ref,
    plain_ref,
    back_ref,
    coeff_hbm,
    out_ref,
    coeff_ref,
    weight_ref,
    rows_ref,
    res_ref,
    left_ref,
    mixed_ref,
    sems,
    coeff_sems,
):
    copies = start_weights(weight_hbm, weight_ref, sems, HEAD)
    count = rows_ref.shape[0] // 16
    rows_ref[...] = block_ref[...].astype(F32)
    low = lanes((128, 128)) < 64
    kxl = sublanes((128, 128)) % 4
    half = lanes((128, 128)) // 64
    first = (kxl == half).astype(BF16)
    second = (kxl == 2 + half).astype(BF16)
    low8 = lanes((8, 128)) < 64
    sign = jnp.where(sublanes((8, 128)) < 4, -1.0, 1.0)
    for quarter in range(4):
        wide = jnp.concatenate(
            [rows_ref[pl.ds(quarter * 4 + k, count, stride=16), :] for k in range(4)], axis=1
        ).astype(BF16)
        plain = (dot_nn(plain_ref[...], wide) * scale).astype(BF16)
        both = dot_nn(both_ref[...], wide) * scale
        for k in range(4):
            j = quarter * 4 + k
            coeff_ref[j] = plain[:, k * 128 : (k + 1) * 128]
            coeffs = both[:, k * 128 : (k + 1) * 128]
            swapped = swap_halves(coeffs)
            for h in range(2):
                twice = jnp.where(low if h == 0 else ~low, coeffs, swapped).astype(BF16)
                left_ref[j, h] = jnp.concatenate([twice * first, twice * second], axis=1)
    send = pltpu.make_async_copy(coeff_ref, coeff_hbm, coeff_sems.at[0])
    send.start()
    for j in range(16):
        for copy in copies[j - HEAD : j - HEAD + WAITS.get(j, 0)]:
            copy.wait()
        mixed = []
        for u in range(MX // 8):
            halves = [
                dot_nn(left_ref[j, h, u * 32 : (u + 1) * 32, :], mode_pair(head_ref, weight_ref, j, h, u))
                for h in range(2)
            ]
            for t in range(2):
                low_h, high_h = [
                    part[t * 16 : (t + 1) * 16, t * 128 : (t + 1) * 128] for part in halves
                ]
                keep = jnp.where(low8, low_h[:8], sign * high_h[8:])
                move = jnp.where(low8, high_h[:8], sign * low_h[8:])
                mixed.append(keep + swap_halves(move))
        mixed_ref[j] = jnp.concatenate(mixed, axis=0).astype(BF16)
        if j % 4 == 3:
            plane_sums(back_ref, mixed_ref, res_ref, j // 4)
    out_ref[...] = res_ref[...].astype(BF16)
    send.wait()


def mode_grad_kernel(
    scale,
    block_ref,
    head_ref,
    weight_hbm,
    straight_ref,
    back_ref,
    coeff_hbm,
    pair_ref,
    coeff_ref,
    out_ref,
    weight_ref,
    rows_ref,
    res_ref,
    mixed_ref,
    sems,
    coeff_sems,
):
    send = pltpu.make_async_copy(coeff_hbm, coeff_ref, coeff_sems.at[0])
    send.start()
    copies = start_weights(weight_hbm, weight_ref, sems, HEAD)
    count = rows_ref.shape[0] // 16
    rows_ref[...] = block_ref[...].astype(F32)
    low = lanes((64, 128)) < 64
    low16 = lanes((16, 128)) < 64
    row = sublanes((16, 128)) % 4
    upper = row < 2
    valid = lanes((16, 128)) // 64 == row % 2
    even = (sublanes((16, 128)) < 8).astype(BF16)
    odd = (sublanes((16, 128)) >= 8).astype(BF16)
    for j in range(16):
        section = rows_ref[pl.ds(j, count, stride=16), :]
        swapped = swap_halves(section)
        twice = jnp.concatenate(
            [jnp.where(low, section, swapped), jnp.where(low, swapped, section)], axis=1
        ).astype(BF16)
        turned = dot_nn(straight_ref[...], twice)
        for h in range(2):
            part = turned[:, h * 128 : (h + 1) * 128]
            pair_ref[2 * j + h] = jnp.where(low, part[:64], part[64:]).astype(BF16)
    for j in range(16):
        for copy in copies[j - HEAD : j - HEAD + WAITS.get(j, 0)]:
            copy.wait()
        mixed = []
        for u in range(MX // 8):
            found = []
            for h in range(2):
                pair = pair_ref[2 * j + h, u * 16 : (u + 1) * 16, :]
                rows = dot_nt(
                    jnp.concatenate([pair * even, pair * odd], axis=1),
                    mode_pair(head_ref, weight_ref, j, h, u),
                )
                found.append(jnp.where(valid, jnp.where(upper, rows[:, :128], rows[:, 128:]), 0.0))
            keep = jnp.where(low16, found[0], found[1])
            move = jnp.where(low16, found[1], found[0])
            mixed.append(keep + swap_halves(move))
        mixed_ref[j] = (jnp.concatenate(mixed, axis=0) * scale).astype(BF16)
    for quarter in range(4):
        plane_sums(back_ref, mixed_ref, res_ref, quarter)
    out_ref[...] = res_ref[...].astype(BF16)
    send.wait()


def weight_grad_kernel(
    scale, coeff_ref, pair_ref, out_hbm, out_ref, mask_ref, turned_ref, pairs_ref, sems
):
    lane = lanes((128, 64))
    part = sublanes((128, 64)) // 64
    for t in range(MX // 4 - VECTOR):
        mask_ref[t] = ((lane // 8 == t) & (lane % 4 // 2 == part)).astype(BF16)
    eye = (sublanes((128, 128)) == lanes((128, 128))).astype(BF16)
    for j in range(16):
        turned_ref[j] = (dot_nt(eye, coeff_ref[j]) * scale).astype(BF16)
        for h in range(2):
            pairs_ref[2 * j + h] = pair_ref[2 * j + h].astype(F32)
    even = (sublanes((64, 128)) % 2 == 0).astype(BF16)
    odd = (sublanes((64, 128)) % 2 == 1).astype(BF16)

    def one_pair(j):
        for h in range(2):
            one = turned_ref[j, h * 64 : (h + 1) * 64, :]
            left = jnp.concatenate([one, one], axis=0)
            pair = pair_ref[j * 2 + h]
            right = jnp.concatenate([pair * even, pair * odd], axis=1)
            for t in range(MX // 4):
                mode = (j * 2 + h) * MX + 4 * t
                if t < MX // 4 - VECTOR:
                    four = dot_nn(left * mask_ref[t], right)
                    for k in range(4):
                        out_ref[mode + k] = four[
                            k // 2 * 64 : (k // 2 + 1) * 64, k % 2 * 128 : (k % 2 + 1) * 128
                        ].astype(BF16)
                    continue
                for k in range(4):
                    total = None
                    for b in range(2):
                        at = t * 8 + b * 4 + k
                        column = jnp.broadcast_to(one[:, at : at + 1], (64, 128))
                        row = jnp.broadcast_to(
                            pairs_ref[j * 2 + h, at : at + 1, :], (64, 128)
                        ).astype(BF16)
                        total = column * row if total is None else total + column * row
                    out_ref[mode + k] = total
        part_copy(out_ref, out_hbm, sems, j, 2 * MX).start()

    @pl.loop(0, 4)
    def _(trip):
        for k in range(4):
            one_pair(trip * 4 + k)

    for j in range(16):
        part_copy(out_ref, out_hbm, sems, j, 2 * MX).wait()


def params(mib):
    return pltpu.CompilerParams(vmem_limit_bytes=mib * 1024 * 1024)


def cost(flops, moved):
    return pl.CostEstimate(flops=int(flops), bytes_accessed=int(moved), transcendentals=0)


def fast_body(features, cotangent, spectral_weight, channel_weight, channel_bias):
    channels, planes, lines, depth_len = features.shape
    devices = lax.axis_size("gx")
    owned_modes = spectral_weight.shape[0]
    wave_pairs = MY * MZ
    volume = planes * devices * lines * depth_len
    forward_scale = 1.0 / math.sqrt(volume)
    inverse_scale = 1.0 / math.sqrt(MX * wave_pairs)
    weight_scale = math.sqrt(MX * wave_pairs / volume)
    table = {name: jnp.asarray(value) for name, value in tables(devices, lines, depth_len).items()}
    for name in ("depth", "depth_pair", "across_y", "back_y"):
        table[name] = pltpu.with_memory_space_constraint(table[name], pltpu.HBM)
    block_rows = devices * 64
    block_shape = jax.ShapeDtypeStruct((block_rows, 128), BF16)
    vmem = pl.BlockSpec(memory_space=pltpu.VMEM)
    hbm = pl.BlockSpec(memory_space=pltpu.HBM)
    smem = pl.BlockSpec(memory_space=pltpu.SMEM)
    field_scratch = pltpu.VMEM(features.shape, BF16)
    field_shape = jax.ShapeDtypeStruct(features.shape, BF16)

    def sems(count):
        return pltpu.SemaphoreType.DMA((count,))

    def scratch(name):
        return pltpu.VMEM(table[name].shape, BF16)

    def in_hbm(array):
        return pltpu.with_memory_space_constraint(array, pltpu.HBM)

    def in_vmem(array):
        return pltpu.with_memory_space_constraint(array, pltpu.VMEM)

    steps = channels // STEP
    lines_scratch = pltpu.VMEM((channels * 2 * MZ, planes * lines), F32)
    rows_scratch = pltpu.VMEM((block_rows, 128), F32)
    spec_scratch = pltpu.VMEM((channels // GROUP, MZ * GROUP, 128), F32)
    weight_rows = pltpu.with_memory_space_constraint(
        spectral_weight.reshape(owned_modes * channels, 2 * channels), pltpu.HBM
    )
    field_bytes = features.size * 2

    def exchange(block):
        return lax.all_to_all(
            block.reshape(devices, 64, 128), "gx", 0, 0, tiled=True
        ).reshape(block_rows, 128)

    def point(field, transposed):
        return pl.pallas_call(
            functools.partial(point_kernel, transposed),
            out_shape=[
                pltpu.HBM(features.shape, BF16),
                pltpu.VMEM((weight_rows.shape[0] * HEAD // 16, weight_rows.shape[1]), BF16),
            ],
            in_specs=[vmem, hbm, hbm],
            out_specs=[hbm, vmem],
            scratch_shapes=[
                field_scratch,
                field_scratch,
                pltpu.VMEM((channels * 16, channels * 16), BF16),
                sems(planes),
                sems(planes),
                sems(HEAD),
            ],
            compiler_params=params(VMEM_MIB),
            cost_estimate=cost(2 * 1024**3, 2 * field_bytes),
            name="channel_map_back" if transposed else "channel_map",
        )(channel_weight, in_hbm(field), weight_rows)

    block = pl.pallas_call(
        analysis_kernel,
        out_shape=block_shape,
        in_specs=[hbm, hbm, hbm],
        out_specs=vmem,
        scratch_shapes=[
            field_scratch,
            scratch("depth_pair"),
            scratch("across_y"),
            lines_scratch,
            rows_scratch,
            sems(steps),
            sems(2),
        ],
        compiler_params=params(VMEM_MIB),
        cost_estimate=cost(2 * 256 * 1024 * 1024, field_bytes),
        name="field_analysis",
    )(in_hbm(features), table["depth_pair"], table["across_y"])
    pointwise, head = point(features, False)
    block, pointwise, head = lax.optimization_barrier((exchange(block), pointwise, head))

    weight_scratch = pltpu.VMEM(
        (weight_rows.shape[0] * (16 - HEAD) // 16, weight_rows.shape[1]), BF16
    )
    mixed_scratch = pltpu.VMEM((16, 64, 128), BF16)
    weight_sems = sems(16 - HEAD)
    coeffs, block = pl.pallas_call(
        functools.partial(mode_kernel, forward_scale),
        out_shape=[pltpu.HBM((16, 64, 128), BF16), block_shape],
        in_specs=[vmem, vmem, hbm, vmem, vmem, vmem],
        out_specs=[hbm, vmem],
        scratch_shapes=[
            pltpu.VMEM((16, 64, 128), BF16),
            weight_scratch,
            rows_scratch,
            rows_scratch,
            pltpu.VMEM((16, 2, 128, 256), BF16),
            mixed_scratch,
            weight_sems,
            sems(1),
        ],
        compiler_params=params(VMEM_MIB),
        cost_estimate=cost(256 * 2 * 16 * 256 * 128, 17 * 2**20),
        name="mode_product",
    )(block, in_vmem(head), weight_rows, table["both_x"], table["plain_x"], table["back_x"])
    block = exchange(block)

    activated, upstream, block = pl.pallas_call(
        functools.partial(middle_kernel, inverse_scale),
        out_shape=[field_shape, pltpu.HBM(features.shape, BF16), block_shape],
        in_specs=[vmem, smem, hbm, hbm, hbm, hbm, hbm, hbm],
        out_specs=[hbm, hbm, vmem],
        scratch_shapes=[
            field_scratch,
            field_scratch,
            scratch("depth"),
            scratch("depth_pair"),
            scratch("across_y"),
            scratch("back_y"),
            field_scratch,
            field_scratch,
            lines_scratch,
            rows_scratch,
            spec_scratch,
            sems(steps),
            sems(steps),
            sems(steps),
            sems(steps),
            sems(4),
        ],
        compiler_params=params(VMEM_MIB),
        cost_estimate=cost(2**30, 4 * field_bytes),
        name="gelu_and_gradient",
    )(
        block,
        channel_bias,
        in_hbm(pointwise),
        in_hbm(cotangent),
        table["depth"],
        table["depth_pair"],
        table["across_y"],
        table["back_y"],
    )
    channel_back, head = point(upstream, True)
    block, channel_back, head = lax.optimization_barrier((exchange(block), channel_back, head))

    pairs, coeffs, block = pl.pallas_call(
        functools.partial(mode_grad_kernel, forward_scale),
        out_shape=[
            pltpu.VMEM((32, 64, 128), BF16),
            pltpu.VMEM((16, 64, 128), BF16),
            block_shape,
        ],
        in_specs=[vmem, vmem, hbm, vmem, vmem, hbm],
        out_specs=[vmem, vmem, vmem],
        scratch_shapes=[
            weight_scratch,
            rows_scratch,
            rows_scratch,
            mixed_scratch,
            weight_sems,
            sems(1),
        ],
        compiler_params=params(VMEM_MIB),
        cost_estimate=cost(256 * 2 * 16 * 256 * 128, 17 * 2**20),
        name="mode_gradient",
    )(block, in_vmem(head), weight_rows, table["straight_x"], table["back_x"], in_hbm(coeffs))
    block = exchange(block)

    spectral_grad = pl.pallas_call(
        functools.partial(weight_grad_kernel, weight_scale),
        out_shape=jax.ShapeDtypeStruct(spectral_weight.shape, BF16),
        in_specs=[vmem, vmem],
        out_specs=hbm,
        scratch_shapes=[
            pltpu.VMEM(spectral_weight.shape, BF16),
            pltpu.VMEM((MX // 4, 128, 64), BF16),
            pltpu.VMEM((16, 128, 64), BF16),
            pltpu.VMEM((32, 64, 128), F32),
            sems(16),
        ],
        compiler_params=params(VMEM_MIB),
        cost_estimate=cost(512 * 2 * 64 * 64 * 256, 17 * 2**20),
        name="weight_gradient",
    )(
        in_vmem(coeffs),
        in_vmem(pairs),
    )

    feature_grad = pl.pallas_call(
        final_kernel,
        out_shape=field_shape,
        in_specs=[vmem, hbm, hbm, hbm],
        out_specs=hbm,
        scratch_shapes=[
            field_scratch,
            scratch("depth"),
            scratch("back_y"),
            field_scratch,
            rows_scratch,
            spec_scratch,
            sems(steps),
            sems(steps),
            sems(2),
        ],
        compiler_params=params(VMEM_MIB),
        cost_estimate=cost(2**29, 2 * field_bytes),
        name="field_gradient",
    )(block, in_hbm(channel_back), table["depth"], table["back_y"])
    return (activated, feature_grad, spectral_grad)


def body(features, cotangent, spectral_weight, channel_weight, channel_bias):
    channels, planes, lines, depth_len = features.shape
    devices = lax.axis_size("gx")
    fits = (
        (channels, planes, lines, depth_len) == (64, PLANES, 64, 128)
        and spectral_weight.shape[0] == 2 * MZ * MX
        and devices * 2 == MY
        and devices * 2 == MX
    )
    run = fast_body if fits else general_body
    return run(features, cotangent, spectral_weight, channel_weight, channel_bias)


def solution(mesh):
    in_specs = (
        P("grp", "gx", None, None),
        P("grp", "gx", None, None),
        P("gx", None, None),
        P(),
        P(),
    )
    out_specs = (
        P("grp", "gx", None, None),
        P("grp", "gx", None, None),
        P(("grp", "gx"), None, None),
    )
    return jax.shard_map(body, mesh=mesh, in_specs=in_specs, out_specs=out_specs, check_vma=False)
```

```python
import functools
import math

import jax
import jax.numpy as jnp
import ml_dtypes
import numpy as np
from jax import lax
from jax.experimental import pallas as pl
from jax.experimental.pallas import tpu as pltpu
from jax.sharding import PartitionSpec as P

MX = 32
MY = 32
MZ = 16


SQRT_TWO_PI = math.sqrt(2.0 / math.pi)
CUBIC_COEF = 0.044715


def freq_index(retained, length):
    ladder = jnp.arange(retained, dtype=jnp.int32)
    return jnp.where(ladder < retained // 2, ladder, length - retained + ladder)


def cos_sin(wavenum, length):
    points = jnp.arange(length, dtype=jnp.int32)
    angles = (wavenum[:, None] * points[None, :] % length).astype(jnp.float32) * (
        2.0 * math.pi / length
    )
    return (jnp.cos(angles), jnp.sin(angles))


def analysis_pair(wavenum, length):
    cosine, sine_wave = cos_sin(wavenum, length)
    cosine, sine_wave = (cosine.T, sine_wave.T)
    return jnp.stack(
        [jnp.stack([cosine, -sine_wave], 1), jnp.stack([sine_wave, cosine], 1)], 1
    ).astype(jnp.bfloat16)


def synthesis_pair(wavenum, length):
    cosine, sine_wave = cos_sin(wavenum, length)
    return jnp.stack(
        [jnp.stack([cosine, sine_wave], 1), jnp.stack([-sine_wave, cosine], 1)], 1
    ).astype(jnp.bfloat16)


def depth_table(retained, length):
    cosine, sine_wave = cos_sin(jnp.arange(retained, dtype=jnp.int32), length)
    return jnp.concatenate([cosine, -sine_wave], 0).astype(jnp.bfloat16)


def gelu_parts(inputs):
    cubed_in = inputs * inputs * inputs
    tangent = jnp.tanh(SQRT_TWO_PI * (inputs + CUBIC_COEF * cubed_in))
    output = 0.5 * inputs * (1.0 + tangent)
    derivative = 0.5 * (1.0 + tangent) + 0.5 * inputs * (1.0 - tangent * tangent) * SQRT_TWO_PI * (
        1.0 + 3.0 * CUBIC_COEF * inputs * inputs
    )
    return (output, derivative)


def mode_product(coeffs, weights, channels):
    stacked = coeffs.reshape(coeffs.shape[0], 2, channels)
    halves = jnp.einsum("mac,mcj->amj", stacked, weights, preferred_element_type=jnp.float32)
    real_out = halves[0, :, :channels] - halves[1, :, channels:]
    imag_out = halves[0, :, channels:] + halves[1, :, :channels]
    return jnp.concatenate([real_out, imag_out], 1).astype(jnp.bfloat16)


def mode_grads(coeffs, weights, grad_modes, channels, weight_scale, input_scale):
    number = coeffs.shape[0]
    stacked = coeffs.reshape(number, 2, channels)
    grad_pairs = grad_modes.reshape(number, 2, channels)
    real_w = jnp.einsum("mac,mao->mco", stacked, grad_pairs, preferred_element_type=jnp.float32)
    imag_w = jnp.einsum(
        "mc,mo->mco", stacked[:, 0], grad_pairs[:, 1], preferred_element_type=jnp.float32
    ) - jnp.einsum(
        "mc,mo->mco", stacked[:, 1], grad_pairs[:, 0], preferred_element_type=jnp.float32
    )
    weight_grad = (jnp.concatenate([real_w, imag_w], 2) * weight_scale).astype(jnp.bfloat16)
    straight = jnp.concatenate([grad_pairs[:, 0], grad_pairs[:, 1]], 1)
    rotated = jnp.concatenate([grad_pairs[:, 1], -grad_pairs[:, 0]], 1)
    real_x = jnp.einsum("mcj,mj->mc", weights, straight, preferred_element_type=jnp.float32)
    imag_x = jnp.einsum("mcj,mj->mc", weights, rotated, preferred_element_type=jnp.float32)
    input_grad = (jnp.concatenate([real_x, imag_x], 1) * input_scale).astype(jnp.bfloat16)
    return (weight_grad, input_grad)


def general_body(features, cotangent, spectral_weight, channel_weight, channel_bias):
    channels, planes, lines, depth_len = features.shape
    devices = lax.axis_size("gx")
    all_planes = planes * devices
    owned_modes = spectral_weight.shape[0]
    wave_pairs = MY * MZ
    forward_scale = 1.0 / math.sqrt(all_planes * lines * depth_len)
    inverse_scale = 1.0 / math.sqrt(MX * wave_pairs)
    weight_scale = math.sqrt(MX * wave_pairs / (all_planes * lines * depth_len))
    depth_basis = depth_table(MZ, depth_len)
    across_y = analysis_pair(freq_index(MY, lines), lines)
    back_y = synthesis_pair(freq_index(MY, lines), lines)
    across_full = analysis_pair(freq_index(MX, all_planes), all_planes)
    back_full = synthesis_pair(freq_index(MX, all_planes), all_planes)
    depth_part = jnp.dot(features, depth_basis.T, preferred_element_type=jnp.float32).astype(
        jnp.bfloat16
    )
    plane_part = (
        jnp.einsum(
            "cxyaz,yabk->cxbkz",
            depth_part.reshape(channels, planes, lines, 2, MZ),
            across_y,
            preferred_element_type=jnp.float32,
        )
        .astype(jnp.bfloat16)
        .reshape(channels, planes, 2, wave_pairs)
    )
    all_rows = lax.all_to_all(plane_part, "gx", split_axis=3, concat_axis=1, tiled=True)
    mode_sums = jnp.einsum(
        "cxaq,xabk->qkbc", all_rows, across_full, preferred_element_type=jnp.float32
    ).reshape(owned_modes, 2 * channels)
    coeffs = (mode_sums * forward_scale).astype(jnp.bfloat16)
    spectral = mode_product(coeffs, spectral_weight, channels)
    planes_all = jnp.einsum(
        "qkao,kabx->oxbq",
        spectral.reshape(owned_modes // MX, MX, 2, channels),
        back_full,
        preferred_element_type=jnp.float32,
    ).astype(jnp.bfloat16)
    planes_back = lax.all_to_all(planes_all, "gx", split_axis=1, concat_axis=3, tiled=True)
    lines_back = (
        jnp.einsum(
            "oxakz,kaby->oxybz",
            planes_back.reshape(channels, planes, 2, MY, MZ),
            back_y,
            preferred_element_type=jnp.float32,
        )
        .astype(jnp.bfloat16)
        .reshape(channels, planes, lines, 2 * MZ)
    )
    spectral_term = (
        jnp.dot(lines_back, depth_basis, preferred_element_type=jnp.float32) * inverse_scale
    )
    pointwise = jnp.einsum(
        "oc,cxyz->oxyz", channel_weight, features, preferred_element_type=jnp.float32
    )
    hidden = spectral_term + pointwise + channel_bias[:, None, None, None]
    activated, derivative = gelu_parts(hidden)
    upstream = (cotangent.astype(jnp.float32) * derivative).astype(jnp.bfloat16)
    lines_grad = (
        jnp.dot(upstream, depth_basis.T, preferred_element_type=jnp.float32) * inverse_scale
    ).astype(jnp.bfloat16)
    rows_grad = (
        jnp.einsum(
            "oxybz,kaby->oxakz",
            lines_grad.reshape(channels, planes, lines, 2, MZ),
            back_y,
            preferred_element_type=jnp.float32,
        )
        .astype(jnp.bfloat16)
        .reshape(channels, planes, 2, wave_pairs)
    )
    all_grads = lax.all_to_all(rows_grad, "gx", split_axis=3, concat_axis=1, tiled=True)
    grad_sums = jnp.einsum(
        "oxbq,kabx->qkao", all_grads, back_full, preferred_element_type=jnp.float32
    ).reshape(owned_modes, 2 * channels)
    grad_modes = grad_sums.astype(jnp.bfloat16)
    spectral_grad, coeff_grad = mode_grads(
        coeffs, spectral_weight, grad_modes, channels, weight_scale, forward_scale
    )
    plane_all = jnp.einsum(
        "qkbc,xabk->cxaq",
        coeff_grad.reshape(owned_modes // MX, MX, 2, channels),
        across_full,
        preferred_element_type=jnp.float32,
    ).astype(jnp.bfloat16)
    plane_grad = lax.all_to_all(plane_all, "gx", split_axis=1, concat_axis=3, tiled=True)
    depth_grad = (
        jnp.einsum(
            "cxbkz,yabk->cxyaz",
            plane_grad.reshape(channels, planes, 2, MY, MZ),
            across_y,
            preferred_element_type=jnp.float32,
        )
        .astype(jnp.bfloat16)
        .reshape(channels, planes, lines, 2 * MZ)
    )
    channel_back = jnp.einsum(
        "oc,oxyz->cxyz", channel_weight, upstream, preferred_element_type=jnp.float32
    )
    feature_grad = (
        jnp.dot(depth_grad, depth_basis, preferred_element_type=jnp.float32) + channel_back
    ).astype(jnp.bfloat16)
    return (activated.astype(jnp.bfloat16), feature_grad, spectral_grad)


PLANES = 2
GROUP = 8
STEP = 16
VMEM_MIB = 32
VECTOR = 2
HEAD = 2
FLIGHT = 6
NT = (((1,), (1,)), ((), ()))
F32 = jnp.float32
BF16 = jnp.bfloat16


def np_freq(retained, length):
    ladder = np.arange(retained)
    return np.where(ladder < retained // 2, ladder, length - retained + ladder)


def np_angles(wavenum, length):
    points = np.arange(length)
    return (wavenum[:, None] * points[None, :] % length) * (2.0 * math.pi / length)


def as_bf16(table):
    return np.asarray(table, np.float32).astype(ml_dtypes.bfloat16)


def rotation(angle, sign):
    cosine, sine_wave = np.cos(angle), sign * np.sin(angle)
    return np.stack([np.stack([cosine, -sine_wave]), np.stack([sine_wave, cosine])])


@functools.lru_cache(maxsize=None)
def tables(devices, lines, depth_len):
    planes_all = devices * PLANES
    angle = np_angles(np.arange(MZ), depth_len)
    depth = np.stack([np.cos(angle), -np.sin(angle)])
    eye = np.eye(GROUP)
    depth_block = np.einsum("akz,ij->akijz", depth, eye).reshape(2 * MZ * GROUP, GROUP * depth_len)
    depth_pair = np.einsum("akz,ij->iakjz", depth, np.eye(2)).reshape(4 * MZ, 2 * depth_len)
    plane_eye = np.eye(PLANES)
    angle = np_angles(np_freq(MY, lines), lines).reshape(devices, MY // devices, lines)
    across = np.einsum("badly,xw->ldbxawy", rotation(angle, -1.0), plane_eye)
    across = across.reshape(MY * 2 * PLANES, 2 * PLANES * lines)
    back = np.einsum("pbdly,xw->pxyldbw", rotation(angle, 1.0), plane_eye)
    back = back.reshape(2 * PLANES * lines, MY * 2 * PLANES)
    angle = np_angles(np_freq(MX, planes_all), planes_all).reshape(MX // 4, 4, devices, PLANES)
    forward = rotation(angle, -1.0)
    rows = np.einsum("batksx->tbksax", forward).reshape(MX // 4, 2, 4, devices * 2 * PLANES)
    plain = rows.reshape(2 * MX, -1)
    both = np.stack([rows, rows[:, ::-1]], 1).reshape(4 * MX, -1)
    turned = np.concatenate([rows[:, 1:], -rows[:, :1]], 1).reshape(2 * MX, -1)
    straight_rotated = np.concatenate([plain, turned], 0)
    inverse = np.einsum("batksx->sbxtak", rotation(angle, 1.0)).reshape(-1, 2 * MX)
    return {
        "depth": as_bf16(depth_block),
        "depth_pair": as_bf16(depth_pair),
        "across_y": as_bf16(across),
        "back_y": as_bf16(back),
        "plain_x": as_bf16(plain),
        "both_x": as_bf16(both),
        "straight_x": as_bf16(straight_rotated),
        "back_x": as_bf16(inverse),
    }


def dot_nn(left, right):
    return jnp.dot(left, right, preferred_element_type=F32)


def dot_nt(left, right):
    return lax.dot_general(left, right, NT, preferred_element_type=F32)


def lanes(shape):
    return lax.broadcasted_iota(jnp.int32, shape, len(shape) - 1)


def sublanes(shape):
    return lax.broadcasted_iota(jnp.int32, shape, len(shape) - 2)


def swap_halves(block):
    return pltpu.roll(block, 64, 1)


def part_copy(source, target, sems, index, size):
    start = index * size if isinstance(index, int) else pl.multiple_of(index * size, size)
    part = pl.ds(start, size)
    return pltpu.make_async_copy(source.at[part], target.at[part], sems.at[index])


def start_parts(source, target, sems, size, first, last):
    for index in range(first, min(last, source.shape[0] // size)):
        part_copy(source, target, sems, index, size).start()


def start_tables(pairs, sems):
    copies = []
    for index, (source, target) in enumerate(pairs):
        copy = pltpu.make_async_copy(source, target, sems.at[index])
        copy.start()
        copies.append(copy)
    return copies


def depth_quad(slabs, quad, depth_pair, scale, group, lines_ref):
    four = slabs[quad * 4 : quad * 4 + 4]
    wide = jnp.concatenate(
        [jnp.concatenate(four[2 * pair : 2 * pair + 2], axis=1) for pair in range(2)], axis=0
    )
    parts = dot_nt(depth_pair, wide)
    if scale is not None:
        parts = parts * scale
    half = wide.shape[0] // 2
    for pair in range(2):
        start = (group * GROUP + quad * 4 + pair * 2) * 2 * MZ
        if not isinstance(start, int):
            start = pl.multiple_of(start, 4 * MZ)
        lines_ref[pl.ds(start, 4 * MZ), :] = parts[:, pair * half : (pair + 1) * half]


def depth_analysis(slabs, depth_pair, scale, group, lines_ref):
    for quad in range(2):
        depth_quad(slabs, quad, depth_pair, scale, group, lines_ref)


def rows_analysis(lines_ref, across_ref, rows_ref, out_ref):
    channels = lines_ref.shape[0] // (2 * MZ)
    across = across_ref[...]
    half = across.shape[0] // 2
    for first in range(0, MZ // 2, 2):
        pair = jnp.concatenate(
            [
                jnp.concatenate(
                    [
                        lines_ref[pl.ds(a * MZ + kz, channels, stride=2 * MZ), :]
                        for a in range(2)
                    ],
                    axis=1,
                )
                for kz in range(2 * first, 2 * first + 4)
            ],
            axis=0,
        ).astype(BF16)
        rows = dot_nt(across, pair)
        for k in range(2):
            for kyl in range(2):
                rows_ref[pl.ds(kyl * 8 + first + k, half, stride=16), :] = rows[
                    kyl * half : (kyl + 1) * half, k * 128 : (k + 1) * 128
                ]
    out_ref[...] = rows_ref[...].astype(BF16)


def rows_gather(block_ref, rows_ref, spec_ref):
    rows_ref[...] = block_ref[...].astype(F32)
    count = rows_ref.shape[0] // 16
    eye = (sublanes((128, 128)) == lanes((128, 128))).astype(BF16)
    for first in range(0, MZ // 2, 2):
        both = jnp.concatenate(
            [
                rows_ref[pl.ds(kyl * 8 + first + k, count, stride=16), :]
                for k in range(2)
                for kyl in range(2)
            ],
            axis=0,
        ).astype(BF16)
        turned = dot_nt(eye, both)
        half = turned.shape[1] // 2
        for k in range(2):
            for h in range(2):
                at = (2 * (first + k) + h) * GROUP
                spec_ref[:, at : at + GROUP, :] = turned[
                    h * 64 : (h + 1) * 64, k * half : (k + 1) * half
                ].reshape(8, GROUP, half)


def lines_synthesis(step, spec_ref, back, scale):
    count = STEP // GROUP
    both = jnp.concatenate([spec_ref[step * count + g] for g in range(count)], axis=0)
    lines = dot_nt(back, both.astype(BF16))
    if scale is not None:
        lines = lines * scale
    lines = lines.astype(BF16)
    half = lines.shape[0] // 2
    return [
        jnp.concatenate(
            [lines[p * half : (p + 1) * half, g * 128 : (g + 1) * 128] for p in range(2)], axis=1
        )
        for g in range(count)
    ]


def flat(slab):
    return slab.reshape(slab.shape[0] * slab.shape[1], slab.shape[2])


def analysis_kernel(
    field_hbm,
    pair_hbm,
    across_hbm,
    out_ref,
    field_ref,
    pair_ref,
    across_ref,
    lines_ref,
    rows_ref,
    field_sems,
    table_sems,
):
    first, second = start_tables([(pair_hbm, pair_ref), (across_hbm, across_ref)], table_sems)
    start_parts(field_hbm, field_ref, field_sems, STEP, 0, 2)
    first.wait()

    for step in range(field_ref.shape[0] // STEP):
        part_copy(field_hbm, field_ref, field_sems, step, STEP).wait()
        start_parts(field_hbm, field_ref, field_sems, STEP, step + 2, step + 3)
        for g in range(STEP // GROUP):
            group = step * (STEP // GROUP) + g
            slabs = [flat(field_ref[group * GROUP + ci]) for ci in range(GROUP)]
            depth_analysis(slabs, pair_ref[...], None, group, lines_ref)

    second.wait()
    rows_analysis(lines_ref, across_ref, rows_ref, out_ref)


def middle_kernel(
    inverse_scale,
    block_ref,
    bias_ref,
    point_hbm,
    cot_hbm,
    depth_hbm,
    pair_hbm,
    across_hbm,
    back_hbm,
    act_hbm,
    up_hbm,
    out_ref,
    point_ref,
    cot_ref,
    depth_ref,
    pair_ref,
    across_ref,
    back_ref,
    act_ref,
    up_ref,
    lines_ref,
    rows_ref,
    spec_ref,
    point_sems,
    cot_sems,
    act_sems,
    up_sems,
    table_sems,
):
    tables_in = start_tables(
        [
            (back_hbm, back_ref),
            (depth_hbm, depth_ref),
            (pair_hbm, pair_ref),
            (across_hbm, across_ref),
        ],
        table_sems,
    )
    start_parts(point_hbm, point_ref, point_sems, STEP, 0, 1)
    start_parts(cot_hbm, cot_ref, cot_sems, STEP, 0, 1)
    rows_gather(block_ref, rows_ref, spec_ref)
    start_parts(point_hbm, point_ref, point_sems, STEP, 1, 2)
    start_parts(cot_hbm, cot_ref, cot_sems, STEP, 1, 2)
    for copy in tables_in:
        copy.wait()
    steps = point_ref.shape[0] // STEP
    groups = point_ref.shape[0] // GROUP
    per_step = STEP // GROUP

    def activate(index, spectral):
        hidden = spectral + flat(point_ref[index]).astype(F32) + bias_ref[index]
        square = hidden * hidden
        gate = 0.5 + 0.5 * jnp.tanh(hidden * (SQRT_TWO_PI + (SQRT_TWO_PI * CUBIC_COEF) * square))
        slope = hidden * (2.0 * SQRT_TWO_PI + (6.0 * SQRT_TWO_PI * CUBIC_COEF) * square)
        derivative = gate + (gate - gate * gate) * slope
        upstream = (flat(cot_ref[index]).astype(F32) * derivative).astype(BF16)
        act_ref[index] = (hidden * gate).astype(BF16).reshape(act_ref.shape[1:])
        up_ref[index] = upstream.reshape(up_ref.shape[1:])
        return upstream

    def quarter(wide, at):
        return dot_nn(wide, depth_ref[:, at * 256 : (at + 1) * 256])

    wides = lines_synthesis(0, spec_ref, back_ref[...], inverse_scale)
    spectral = [quarter(wides[0], at) for at in range(4)]
    last = None
    for group in range(groups):
        step = group // per_step
        if group % per_step == 0:
            part_copy(point_hbm, point_ref, point_sems, step, STEP).wait()
            part_copy(cot_hbm, cot_ref, cot_sems, step, STEP).wait()
            start_parts(point_hbm, point_ref, point_sems, STEP, step + 2, step + 3)
            start_parts(cot_hbm, cot_ref, cot_sems, STEP, step + 2, step + 3)
            if step + 1 < steps:
                wides += lines_synthesis(step + 1, spec_ref, back_ref[...], inverse_scale)
        following, slabs = [], []
        for at in range(4):
            if group + 1 < groups:
                following.append(quarter(wides[group + 1], at))
            for k in range(2):
                oi = 2 * at + k
                slabs.append(
                    activate(group * GROUP + oi, spectral[at][:, k * 128 : (k + 1) * 128])
                )
            if last is not None and at % 2 == 0:
                depth_quad(last, at // 2, pair_ref[...], inverse_scale, group - 1, lines_ref)
        if group % per_step == per_step - 1:
            part_copy(act_ref, act_hbm, act_sems, step, STEP).start()
            part_copy(up_ref, up_hbm, up_sems, step, STEP).start()
        spectral, last = following, slabs
    depth_analysis(last, pair_ref[...], inverse_scale, groups - 1, lines_ref)
    rows_analysis(lines_ref, across_ref, rows_ref, out_ref)
    for step in range(steps):
        part_copy(act_ref, act_hbm, act_sems, step, STEP).wait()
        part_copy(up_ref, up_hbm, up_sems, step, STEP).wait()


def final_kernel(
    block_ref,
    point_hbm,
    depth_hbm,
    back_hbm,
    out_hbm,
    point_ref,
    depth_ref,
    back_ref,
    out_ref,
    rows_ref,
    spec_ref,
    point_sems,
    out_sems,
    table_sems,
):
    tables_in = start_tables([(back_hbm, back_ref), (depth_hbm, depth_ref)], table_sems)
    start_parts(point_hbm, point_ref, point_sems, STEP, 0, 1)
    rows_gather(block_ref, rows_ref, spec_ref)
    start_parts(point_hbm, point_ref, point_sems, STEP, 1, 4)
    for copy in tables_in:
        copy.wait()
    steps = point_ref.shape[0] // STEP
    groups = point_ref.shape[0] // GROUP
    per_step = STEP // GROUP

    def quarter(wide, at):
        return dot_nn(wide, depth_ref[:, at * 256 : (at + 1) * 256])

    wides = lines_synthesis(0, spec_ref, back_ref[...], None)
    spectral = [quarter(wides[0], at) for at in range(4)]
    for group in range(groups):
        step = group // per_step
        if group % per_step == 0:
            part_copy(point_hbm, point_ref, point_sems, step, STEP).wait()
            if step + 1 < steps:
                wides += lines_synthesis(step + 1, spec_ref, back_ref[...], None)
        following = []
        for at in range(4):
            if group + 1 < groups:
                following.append(quarter(wides[group + 1], at))
            for k in range(2):
                index = group * GROUP + 2 * at + k
                total = spectral[at][:, k * 128 : (k + 1) * 128] + flat(point_ref[index]).astype(F32)
                out_ref[index] = total.astype(BF16).reshape(out_ref.shape[1:])
        if group % per_step == per_step - 1:
            part_copy(out_ref, out_hbm, out_sems, step, STEP).start()
        spectral = following

    for step in range(steps):
        part_copy(out_ref, out_hbm, out_sems, step, STEP).wait()


def point_kernel(
    transposed,
    weight_ref,
    field_hbm,
    modes_hbm,
    out_hbm,
    head_ref,
    field_ref,
    out_ref,
    wide_ref,
    in_sems,
    out_sems,
    head_sems,
):
    size = wide_ref.shape[0]
    planes = field_ref.shape[1]
    copies = []
    for plane in range(planes):
        part = (slice(None), pl.ds(plane, 1))
        copy = pltpu.make_async_copy(field_hbm.at[part], field_ref.at[part], in_sems.at[plane])
        copy.start()
        copies.append(copy)
    heads = weight_copies(modes_hbm, head_ref, head_sems, 0)
    for copy in heads:
        copy.start()
    tall = (sublanes((size, 64)) // 16 == lanes((size, 64))).astype(BF16)
    weight = weight_ref[...]
    left = dot_nt(tall, weight) if transposed else dot_nn(tall, weight)
    left = left.astype(BF16)
    rows = size // 4
    same = sublanes((rows, size)) % 16 == lanes((rows, size)) % 16
    for quarter in range(4):
        spread = dot_nt(left[quarter * rows : (quarter + 1) * rows], tall)
        wide_ref[quarter * rows : (quarter + 1) * rows, :] = jnp.where(same, spread, 0.0).astype(
            BF16
        )
    sends = []
    for plane in range(planes):
        copies[plane].wait()
        for pair in range(2):
            right = jnp.concatenate(
                [
                    field_ref[:, plane, yc * 16 : (yc + 1) * 16, :].reshape(size, 128)
                    for yc in (2 * pair, 2 * pair + 1)
                ],
                axis=1,
            )
            result = dot_nn(wide_ref[...], right).astype(BF16)
            for k in range(2):
                yc = 2 * pair + k
                out_ref[:, plane, yc * 16 : (yc + 1) * 16, :] = result[
                    :, k * 128 : (k + 1) * 128
                ].reshape(size // 16, 16, 128)
        part = (slice(None), pl.ds(plane, 1))
        copy = pltpu.make_async_copy(out_ref.at[part], out_hbm.at[part], out_sems.at[plane])
        copy.start()
        sends.append(copy)
    for copy in sends + heads:
        copy.wait()


def weight_copies(weight_hbm, weight_ref, sems, first):
    rows = weight_hbm.shape[0] // 16
    copies = []
    for index in range(weight_ref.shape[0] // rows):
        copy = pltpu.make_async_copy(
            weight_hbm.at[pl.ds((first + index) * rows, rows)],
            weight_ref.at[pl.ds(index * rows, rows)],
            sems.at[index],
        )
        copies.append(copy)
    return copies


def next_weights(copies, j):
    if j < HEAD or j % 2:
        return
    for index in (j - HEAD, j - HEAD + 1):
        copies[index].wait()
        if index + FLIGHT < len(copies):
            copies[index + FLIGHT].start()


def mode_pair(head_ref, weight_ref, j, h, u):
    source = head_ref if j < HEAD else weight_ref
    start = (((j if j < HEAD else j - HEAD) * 2 + h) * MX + 8 * u) * 64
    return jnp.concatenate(
        [source[start : start + 256, :], source[start + 256 : start + 512, :]], axis=1
    )


def plane_sums(back_ref, mixed_ref, res_ref, quarter):
    count = res_ref.shape[0] // 16
    wide = jnp.concatenate([mixed_ref[quarter * 4 + k] for k in range(4)], axis=1)
    rows = dot_nn(back_ref[...], wide)
    for k in range(4):
        res_ref[pl.ds(quarter * 4 + k, count, stride=16), :] = rows[:, k * 128 : (k + 1) * 128]


def mode_kernel(
    scale,
    block_ref,
    head_ref,
    weight_hbm,
    both_ref,
    plain_ref,
    back_ref,
    coeff_hbm,
    out_ref,
    coeff_ref,
    weight_ref,
    rows_ref,
    res_ref,
    left_ref,
    mixed_ref,
    sems,
    coeff_sems,
):
    copies = weight_copies(weight_hbm, weight_ref, sems, HEAD)
    for copy in copies[:FLIGHT]:
        copy.start()
    count = rows_ref.shape[0] // 16
    rows_ref[...] = block_ref[...].astype(F32)
    low = lanes((128, 128)) < 64
    kxl = sublanes((128, 128)) % 4
    half = lanes((128, 128)) // 64
    first = (kxl == half).astype(BF16)
    second = (kxl == 2 + half).astype(BF16)
    low8 = lanes((8, 128)) < 64
    sign = jnp.where(sublanes((8, 128)) < 4, -1.0, 1.0)
    for quarter in range(4):
        wide = jnp.concatenate(
            [rows_ref[pl.ds(quarter * 4 + k, count, stride=16), :] for k in range(4)], axis=1
        ).astype(BF16)
        plain = (dot_nn(plain_ref[...], wide) * scale).astype(BF16)
        both = dot_nn(both_ref[...], wide) * scale
        for k in range(4):
            j = quarter * 4 + k
            coeff_ref[j] = plain[:, k * 128 : (k + 1) * 128]
            coeffs = both[:, k * 128 : (k + 1) * 128]
            swapped = swap_halves(coeffs)
            for h in range(2):
                twice = jnp.where(low if h == 0 else ~low, coeffs, swapped).astype(BF16)
                left_ref[j, h] = jnp.concatenate([twice * first, twice * second], axis=1)
    send = pltpu.make_async_copy(coeff_ref, coeff_hbm, coeff_sems.at[0])
    send.start()
    for j in range(16):
        next_weights(copies, j)
        mixed = []
        for u in range(MX // 8):
            halves = [
                dot_nn(left_ref[j, h, u * 32 : (u + 1) * 32, :], mode_pair(head_ref, weight_ref, j, h, u))
                for h in range(2)
            ]
            for t in range(2):
                low_h, high_h = [
                    part[t * 16 : (t + 1) * 16, t * 128 : (t + 1) * 128] for part in halves
                ]
                keep = jnp.where(low8, low_h[:8], sign * high_h[8:])
                move = jnp.where(low8, high_h[:8], sign * low_h[8:])
                mixed.append(keep + swap_halves(move))
        mixed_ref[j] = jnp.concatenate(mixed, axis=0).astype(BF16)
        if j > 4 and j % 4 == 1:
            plane_sums(back_ref, mixed_ref, res_ref, j // 4 - 1)
    plane_sums(back_ref, mixed_ref, res_ref, 3)
    out_ref[...] = res_ref[...].astype(BF16)
    send.wait()


def mode_grad_kernel(
    scale,
    block_ref,
    head_ref,
    weight_hbm,
    straight_ref,
    back_ref,
    coeff_hbm,
    pair_ref,
    coeff_ref,
    out_ref,
    weight_ref,
    rows_ref,
    res_ref,
    mixed_ref,
    sems,
    coeff_sems,
):
    send = pltpu.make_async_copy(coeff_hbm, coeff_ref, coeff_sems.at[0])
    send.start()
    copies = weight_copies(weight_hbm, weight_ref, sems, HEAD)
    for copy in copies[:FLIGHT]:
        copy.start()
    count = rows_ref.shape[0] // 16
    rows_ref[...] = block_ref[...].astype(F32)
    low = lanes((64, 128)) < 64
    low16 = lanes((16, 128)) < 64
    row = sublanes((16, 128)) % 4
    upper = row < 2
    valid = lanes((16, 128)) // 64 == row % 2
    even = (sublanes((16, 128)) < 8).astype(BF16)
    odd = (sublanes((16, 128)) >= 8).astype(BF16)
    for j in range(16):
        section = rows_ref[pl.ds(j, count, stride=16), :]
        swapped = swap_halves(section)
        twice = jnp.concatenate(
            [jnp.where(low, section, swapped), jnp.where(low, swapped, section)], axis=1
        ).astype(BF16)
        turned = dot_nn(straight_ref[...], twice)
        for h in range(2):
            part = turned[:, h * 128 : (h + 1) * 128]
            pair_ref[2 * j + h] = jnp.where(low, part[:64], part[64:]).astype(BF16)
    for j in range(16):
        next_weights(copies, j)
        mixed = []
        for u in range(MX // 8):
            found = []
            for h in range(2):
                pair = pair_ref[2 * j + h, u * 16 : (u + 1) * 16, :]
                rows = dot_nt(
                    jnp.concatenate([pair * even, pair * odd], axis=1),
                    mode_pair(head_ref, weight_ref, j, h, u),
                )
                found.append(jnp.where(valid, jnp.where(upper, rows[:, :128], rows[:, 128:]), 0.0))
            keep = jnp.where(low16, found[0], found[1])
            move = jnp.where(low16, found[1], found[0])
            mixed.append(keep + swap_halves(move))
        mixed_ref[j] = (jnp.concatenate(mixed, axis=0) * scale).astype(BF16)
        if j > 4 and j % 4 == 1:
            plane_sums(back_ref, mixed_ref, res_ref, j // 4 - 1)
    plane_sums(back_ref, mixed_ref, res_ref, 3)
    out_ref[...] = res_ref[...].astype(BF16)
    send.wait()


def weight_grad_kernel(
    scale, coeff_ref, pair_ref, out_hbm, out_ref, mask_ref, turned_ref, pairs_ref, sems
):
    lane = lanes((128, 64))
    part = sublanes((128, 64)) // 64
    for t in range(MX // 4 - VECTOR):
        mask_ref[t] = ((lane // 8 == t) & (lane % 4 // 2 == part)).astype(BF16)
    eye = (sublanes((128, 128)) == lanes((128, 128))).astype(BF16)
    for j in range(16):
        turned_ref[j] = (dot_nt(eye, coeff_ref[j]) * scale).astype(BF16)
        for h in range(2):
            pairs_ref[2 * j + h] = pair_ref[2 * j + h].astype(F32)
    even = (sublanes((64, 128)) % 2 == 0).astype(BF16)
    odd = (sublanes((64, 128)) % 2 == 1).astype(BF16)

    def one_pair(j):
        for h in range(2):
            one = turned_ref[j, h * 64 : (h + 1) * 64, :]
            left = jnp.concatenate([one, one], axis=0)
            pair = pair_ref[j * 2 + h]
            right = jnp.concatenate([pair * even, pair * odd], axis=1)
            for t in range(MX // 4):
                mode = (j * 2 + h) * MX + 4 * t
                if t < MX // 4 - VECTOR:
                    four = dot_nn(left * mask_ref[t], right)
                    for k in range(4):
                        out_ref[mode + k] = four[
                            k // 2 * 64 : (k // 2 + 1) * 64, k % 2 * 128 : (k % 2 + 1) * 128
                        ].astype(BF16)
                    continue
                for k in range(4):
                    total = None
                    for b in range(2):
                        at = t * 8 + b * 4 + k
                        column = jnp.broadcast_to(one[:, at : at + 1], (64, 128))
                        row = jnp.broadcast_to(
                            pairs_ref[j * 2 + h, at : at + 1, :], (64, 128)
                        ).astype(BF16)
                        total = column * row if total is None else total + column * row
                    out_ref[mode + k] = total
        part_copy(out_ref, out_hbm, sems, j, 2 * MX).start()

    @pl.loop(0, 4)
    def _(trip):
        for k in range(4):
            one_pair(trip * 4 + k)

    for j in range(16):
        part_copy(out_ref, out_hbm, sems, j, 2 * MX).wait()


def params(mib):
    return pltpu.CompilerParams(vmem_limit_bytes=mib * 1024 * 1024)


def cost(flops, moved):
    return pl.CostEstimate(flops=int(flops), bytes_accessed=int(moved), transcendentals=0)


def fast_body(features, cotangent, spectral_weight, channel_weight, channel_bias):
    channels, planes, lines, depth_len = features.shape
    devices = lax.axis_size("gx")
    owned_modes = spectral_weight.shape[0]
    wave_pairs = MY * MZ
    volume = planes * devices * lines * depth_len
    forward_scale = 1.0 / math.sqrt(volume)
    inverse_scale = 1.0 / math.sqrt(MX * wave_pairs)
    weight_scale = math.sqrt(MX * wave_pairs / volume)
    table = {name: jnp.asarray(value) for name, value in tables(devices, lines, depth_len).items()}
    for name in ("depth", "depth_pair", "across_y", "back_y"):
        table[name] = pltpu.with_memory_space_constraint(table[name], pltpu.HBM)
    block_rows = devices * 64
    block_shape = jax.ShapeDtypeStruct((block_rows, 128), BF16)
    vmem = pl.BlockSpec(memory_space=pltpu.VMEM)
    hbm = pl.BlockSpec(memory_space=pltpu.HBM)
    smem = pl.BlockSpec(memory_space=pltpu.SMEM)
    field_scratch = pltpu.VMEM(features.shape, BF16)
    field_shape = jax.ShapeDtypeStruct(features.shape, BF16)

    def sems(count):
        return pltpu.SemaphoreType.DMA((count,))

    def scratch(name):
        return pltpu.VMEM(table[name].shape, BF16)

    def in_hbm(array):
        return pltpu.with_memory_space_constraint(array, pltpu.HBM)

    def in_vmem(array):
        return pltpu.with_memory_space_constraint(array, pltpu.VMEM)

    steps = channels // STEP
    lines_scratch = pltpu.VMEM((channels * 2 * MZ, planes * lines), F32)
    rows_scratch = pltpu.VMEM((block_rows, 128), F32)
    spec_scratch = pltpu.VMEM((channels // GROUP, MZ * GROUP, 128), F32)
    weight_rows = pltpu.with_memory_space_constraint(
        spectral_weight.reshape(owned_modes * channels, 2 * channels), pltpu.HBM
    )
    field_bytes = features.size * 2

    def exchange(block):
        return lax.all_to_all(
            block.reshape(devices, 64, 128), "gx", 0, 0, tiled=True
        ).reshape(block_rows, 128)

    def point(field, transposed):
        return pl.pallas_call(
            functools.partial(point_kernel, transposed),
            out_shape=[
                pltpu.HBM(features.shape, BF16),
                pltpu.VMEM((weight_rows.shape[0] * HEAD // 16, weight_rows.shape[1]), BF16),
            ],
            in_specs=[vmem, hbm, hbm],
            out_specs=[hbm, vmem],
            scratch_shapes=[
                field_scratch,
                field_scratch,
                pltpu.VMEM((channels * 16, channels * 16), BF16),
                sems(planes),
                sems(planes),
                sems(HEAD),
            ],
            compiler_params=params(VMEM_MIB),
            cost_estimate=cost(2 * 1024**3, 2 * field_bytes),
            name="channel_map_back" if transposed else "channel_map",
        )(channel_weight, in_hbm(field), weight_rows)

    block = pl.pallas_call(
        analysis_kernel,
        out_shape=block_shape,
        in_specs=[hbm, hbm, hbm],
        out_specs=vmem,
        scratch_shapes=[
            field_scratch,
            scratch("depth_pair"),
            scratch("across_y"),
            lines_scratch,
            rows_scratch,
            sems(steps),
            sems(2),
        ],
        compiler_params=params(VMEM_MIB),
        cost_estimate=cost(2 * 256 * 1024 * 1024, field_bytes),
        name="field_analysis",
    )(in_hbm(features), table["depth_pair"], table["across_y"])
    pointwise, head = point(features, False)
    block, pointwise, head = lax.optimization_barrier((exchange(block), pointwise, head))

    weight_scratch = pltpu.VMEM(
        (weight_rows.shape[0] * (16 - HEAD) // 16, weight_rows.shape[1]), BF16
    )
    mixed_scratch = pltpu.VMEM((16, 64, 128), BF16)
    weight_sems = sems(16 - HEAD)
    coeffs, block = pl.pallas_call(
        functools.partial(mode_kernel, forward_scale),
        out_shape=[pltpu.HBM((16, 64, 128), BF16), block_shape],
        in_specs=[vmem, vmem, hbm, vmem, vmem, vmem],
        out_specs=[hbm, vmem],
        scratch_shapes=[
            pltpu.VMEM((16, 64, 128), BF16),
            weight_scratch,
            rows_scratch,
            rows_scratch,
            pltpu.VMEM((16, 2, 128, 256), BF16),
            mixed_scratch,
            weight_sems,
            sems(1),
        ],
        compiler_params=params(VMEM_MIB),
        cost_estimate=cost(256 * 2 * 16 * 256 * 128, 17 * 2**20),
        name="mode_product",
    )(block, in_vmem(head), weight_rows, table["both_x"], table["plain_x"], table["back_x"])
    block = exchange(block)

    activated, upstream, block = pl.pallas_call(
        functools.partial(middle_kernel, inverse_scale),
        out_shape=[field_shape, pltpu.HBM(features.shape, BF16), block_shape],
        in_specs=[vmem, smem, hbm, hbm, hbm, hbm, hbm, hbm],
        out_specs=[hbm, hbm, vmem],
        scratch_shapes=[
            field_scratch,
            field_scratch,
            scratch("depth"),
            scratch("depth_pair"),
            scratch("across_y"),
            scratch("back_y"),
            field_scratch,
            field_scratch,
            lines_scratch,
            rows_scratch,
            spec_scratch,
            sems(steps),
            sems(steps),
            sems(steps),
            sems(steps),
            sems(4),
        ],
        compiler_params=params(VMEM_MIB),
        cost_estimate=cost(2**30, 4 * field_bytes),
        name="gelu_and_gradient",
    )(
        block,
        channel_bias,
        in_hbm(pointwise),
        in_hbm(cotangent),
        table["depth"],
        table["depth_pair"],
        table["across_y"],
        table["back_y"],
    )
    channel_back, head = point(upstream, True)
    block, channel_back, head = lax.optimization_barrier((exchange(block), channel_back, head))

    pairs, coeffs, block = pl.pallas_call(
        functools.partial(mode_grad_kernel, forward_scale),
        out_shape=[
            pltpu.VMEM((32, 64, 128), BF16),
            pltpu.VMEM((16, 64, 128), BF16),
            block_shape,
        ],
        in_specs=[vmem, vmem, hbm, vmem, vmem, hbm],
        out_specs=[vmem, vmem, vmem],
        scratch_shapes=[
            weight_scratch,
            rows_scratch,
            rows_scratch,
            mixed_scratch,
            weight_sems,
            sems(1),
        ],
        compiler_params=params(VMEM_MIB),
        cost_estimate=cost(256 * 2 * 16 * 256 * 128, 17 * 2**20),
        name="mode_gradient",
    )(block, in_vmem(head), weight_rows, table["straight_x"], table["back_x"], in_hbm(coeffs))
    block = exchange(block)

    spectral_grad = pl.pallas_call(
        functools.partial(weight_grad_kernel, weight_scale),
        out_shape=jax.ShapeDtypeStruct(spectral_weight.shape, BF16),
        in_specs=[vmem, vmem],
        out_specs=hbm,
        scratch_shapes=[
            pltpu.VMEM(spectral_weight.shape, BF16),
            pltpu.VMEM((MX // 4, 128, 64), BF16),
            pltpu.VMEM((16, 128, 64), BF16),
            pltpu.VMEM((32, 64, 128), F32),
            sems(16),
        ],
        compiler_params=params(VMEM_MIB),
        cost_estimate=cost(512 * 2 * 64 * 64 * 256, 17 * 2**20),
        name="weight_gradient",
    )(
        in_vmem(coeffs),
        in_vmem(pairs),
    )

    feature_grad = pl.pallas_call(
        final_kernel,
        out_shape=field_shape,
        in_specs=[vmem, hbm, hbm, hbm],
        out_specs=hbm,
        scratch_shapes=[
            field_scratch,
            scratch("depth"),
            scratch("back_y"),
            field_scratch,
            rows_scratch,
            spec_scratch,
            sems(steps),
            sems(steps),
            sems(2),
        ],
        compiler_params=params(VMEM_MIB),
        cost_estimate=cost(2**29, 2 * field_bytes),
        name="field_gradient",
    )(block, in_hbm(channel_back), table["depth"], table["back_y"])
    return (activated, feature_grad, spectral_grad)


def body(features, cotangent, spectral_weight, channel_weight, channel_bias):
    channels, planes, lines, depth_len = features.shape
    devices = lax.axis_size("gx")
    fits = (
        (channels, planes, lines, depth_len) == (64, PLANES, 64, 128)
        and spectral_weight.shape[0] == 2 * MZ * MX
        and devices * 2 == MY
        and devices * 2 == MX
    )
    run = fast_body if fits else general_body
    return run(features, cotangent, spectral_weight, channel_weight, channel_bias)


def solution(mesh):
    in_specs = (
        P("grp", "gx", None, None),
        P("grp", "gx", None, None),
        P("gx", None, None),
        P(),
        P(),
    )
    out_specs = (
        P("grp", "gx", None, None),
        P("grp", "gx", None, None),
        P(("grp", "gx"), None, None),
    )
    return jax.shard_map(body, mesh=mesh, in_specs=in_specs, out_specs=out_specs, check_vma=False)
```

```python
import functools
import math

import jax
import jax.numpy as jnp
import ml_dtypes
import numpy as np
from jax import lax
from jax.experimental import pallas as pl
from jax.experimental.pallas import tpu as pltpu
from jax.sharding import PartitionSpec as P

MX = 32
MY = 32
MZ = 16


SQRT_TWO_PI = math.sqrt(2.0 / math.pi)
CUBIC_COEF = 0.044715


def freq_index(retained, length):
    ladder = jnp.arange(retained, dtype=jnp.int32)
    return jnp.where(ladder < retained // 2, ladder, length - retained + ladder)


def cos_sin(wavenum, length):
    points = jnp.arange(length, dtype=jnp.int32)
    angles = (wavenum[:, None] * points[None, :] % length).astype(jnp.float32) * (
        2.0 * math.pi / length
    )
    return (jnp.cos(angles), jnp.sin(angles))


def analysis_pair(wavenum, length):
    cosine, sine_wave = cos_sin(wavenum, length)
    cosine, sine_wave = (cosine.T, sine_wave.T)
    return jnp.stack(
        [jnp.stack([cosine, -sine_wave], 1), jnp.stack([sine_wave, cosine], 1)], 1
    ).astype(jnp.bfloat16)


def synthesis_pair(wavenum, length):
    cosine, sine_wave = cos_sin(wavenum, length)
    return jnp.stack(
        [jnp.stack([cosine, sine_wave], 1), jnp.stack([-sine_wave, cosine], 1)], 1
    ).astype(jnp.bfloat16)


def depth_table(retained, length):
    cosine, sine_wave = cos_sin(jnp.arange(retained, dtype=jnp.int32), length)
    return jnp.concatenate([cosine, -sine_wave], 0).astype(jnp.bfloat16)


def gelu_parts(inputs):
    cubed_in = inputs * inputs * inputs
    tangent = jnp.tanh(SQRT_TWO_PI * (inputs + CUBIC_COEF * cubed_in))
    output = 0.5 * inputs * (1.0 + tangent)
    derivative = 0.5 * (1.0 + tangent) + 0.5 * inputs * (1.0 - tangent * tangent) * SQRT_TWO_PI * (
        1.0 + 3.0 * CUBIC_COEF * inputs * inputs
    )
    return (output, derivative)


def mode_product(coeffs, weights, channels):
    stacked = coeffs.reshape(coeffs.shape[0], 2, channels)
    halves = jnp.einsum("mac,mcj->amj", stacked, weights, preferred_element_type=jnp.float32)
    real_out = halves[0, :, :channels] - halves[1, :, channels:]
    imag_out = halves[0, :, channels:] + halves[1, :, :channels]
    return jnp.concatenate([real_out, imag_out], 1).astype(jnp.bfloat16)


def mode_grads(coeffs, weights, grad_modes, channels, weight_scale, input_scale):
    number = coeffs.shape[0]
    stacked = coeffs.reshape(number, 2, channels)
    grad_pairs = grad_modes.reshape(number, 2, channels)
    real_w = jnp.einsum("mac,mao->mco", stacked, grad_pairs, preferred_element_type=jnp.float32)
    imag_w = jnp.einsum(
        "mc,mo->mco", stacked[:, 0], grad_pairs[:, 1], preferred_element_type=jnp.float32
    ) - jnp.einsum(
        "mc,mo->mco", stacked[:, 1], grad_pairs[:, 0], preferred_element_type=jnp.float32
    )
    weight_grad = (jnp.concatenate([real_w, imag_w], 2) * weight_scale).astype(jnp.bfloat16)
    straight = jnp.concatenate([grad_pairs[:, 0], grad_pairs[:, 1]], 1)
    rotated = jnp.concatenate([grad_pairs[:, 1], -grad_pairs[:, 0]], 1)
    real_x = jnp.einsum("mcj,mj->mc", weights, straight, preferred_element_type=jnp.float32)
    imag_x = jnp.einsum("mcj,mj->mc", weights, rotated, preferred_element_type=jnp.float32)
    input_grad = (jnp.concatenate([real_x, imag_x], 1) * input_scale).astype(jnp.bfloat16)
    return (weight_grad, input_grad)


def general_body(features, cotangent, spectral_weight, channel_weight, channel_bias):
    channels, planes, lines, depth_len = features.shape
    devices = lax.axis_size("gx")
    all_planes = planes * devices
    owned_modes = spectral_weight.shape[0]
    wave_pairs = MY * MZ
    forward_scale = 1.0 / math.sqrt(all_planes * lines * depth_len)
    inverse_scale = 1.0 / math.sqrt(MX * wave_pairs)
    weight_scale = math.sqrt(MX * wave_pairs / (all_planes * lines * depth_len))
    depth_basis = depth_table(MZ, depth_len)
    across_y = analysis_pair(freq_index(MY, lines), lines)
    back_y = synthesis_pair(freq_index(MY, lines), lines)
    across_full = analysis_pair(freq_index(MX, all_planes), all_planes)
    back_full = synthesis_pair(freq_index(MX, all_planes), all_planes)
    depth_part = jnp.dot(features, depth_basis.T, preferred_element_type=jnp.float32).astype(
        jnp.bfloat16
    )
    plane_part = (
        jnp.einsum(
            "cxyaz,yabk->cxbkz",
            depth_part.reshape(channels, planes, lines, 2, MZ),
            across_y,
            preferred_element_type=jnp.float32,
        )
        .astype(jnp.bfloat16)
        .reshape(channels, planes, 2, wave_pairs)
    )
    all_rows = lax.all_to_all(plane_part, "gx", split_axis=3, concat_axis=1, tiled=True)
    mode_sums = jnp.einsum(
        "cxaq,xabk->qkbc", all_rows, across_full, preferred_element_type=jnp.float32
    ).reshape(owned_modes, 2 * channels)
    coeffs = (mode_sums * forward_scale).astype(jnp.bfloat16)
    spectral = mode_product(coeffs, spectral_weight, channels)
    planes_all = jnp.einsum(
        "qkao,kabx->oxbq",
        spectral.reshape(owned_modes // MX, MX, 2, channels),
        back_full,
        preferred_element_type=jnp.float32,
    ).astype(jnp.bfloat16)
    planes_back = lax.all_to_all(planes_all, "gx", split_axis=1, concat_axis=3, tiled=True)
    lines_back = (
        jnp.einsum(
            "oxakz,kaby->oxybz",
            planes_back.reshape(channels, planes, 2, MY, MZ),
            back_y,
            preferred_element_type=jnp.float32,
        )
        .astype(jnp.bfloat16)
        .reshape(channels, planes, lines, 2 * MZ)
    )
    spectral_term = (
        jnp.dot(lines_back, depth_basis, preferred_element_type=jnp.float32) * inverse_scale
    )
    pointwise = jnp.einsum(
        "oc,cxyz->oxyz", channel_weight, features, preferred_element_type=jnp.float32
    )
    hidden = spectral_term + pointwise + channel_bias[:, None, None, None]
    activated, derivative = gelu_parts(hidden)
    upstream = (cotangent.astype(jnp.float32) * derivative).astype(jnp.bfloat16)
    lines_grad = (
        jnp.dot(upstream, depth_basis.T, preferred_element_type=jnp.float32) * inverse_scale
    ).astype(jnp.bfloat16)
    rows_grad = (
        jnp.einsum(
            "oxybz,kaby->oxakz",
            lines_grad.reshape(channels, planes, lines, 2, MZ),
            back_y,
            preferred_element_type=jnp.float32,
        )
        .astype(jnp.bfloat16)
        .reshape(channels, planes, 2, wave_pairs)
    )
    all_grads = lax.all_to_all(rows_grad, "gx", split_axis=3, concat_axis=1, tiled=True)
    grad_sums = jnp.einsum(
        "oxbq,kabx->qkao", all_grads, back_full, preferred_element_type=jnp.float32
    ).reshape(owned_modes, 2 * channels)
    grad_modes = grad_sums.astype(jnp.bfloat16)
    spectral_grad, coeff_grad = mode_grads(
        coeffs, spectral_weight, grad_modes, channels, weight_scale, forward_scale
    )
    plane_all = jnp.einsum(
        "qkbc,xabk->cxaq",
        coeff_grad.reshape(owned_modes // MX, MX, 2, channels),
        across_full,
        preferred_element_type=jnp.float32,
    ).astype(jnp.bfloat16)
    plane_grad = lax.all_to_all(plane_all, "gx", split_axis=1, concat_axis=3, tiled=True)
    depth_grad = (
        jnp.einsum(
            "cxbkz,yabk->cxyaz",
            plane_grad.reshape(channels, planes, 2, MY, MZ),
            across_y,
            preferred_element_type=jnp.float32,
        )
        .astype(jnp.bfloat16)
        .reshape(channels, planes, lines, 2 * MZ)
    )
    channel_back = jnp.einsum(
        "oc,oxyz->cxyz", channel_weight, upstream, preferred_element_type=jnp.float32
    )
    feature_grad = (
        jnp.dot(depth_grad, depth_basis, preferred_element_type=jnp.float32) + channel_back
    ).astype(jnp.bfloat16)
    return (activated.astype(jnp.bfloat16), feature_grad, spectral_grad)


PLANES = 2
GROUP = 8
STEP = 16
VMEM_MIB = 32
VECTOR = 3
HEAD = 3
FLIGHT = 6
NT = (((1,), (1,)), ((), ()))
F32 = jnp.float32
BF16 = jnp.bfloat16


def np_freq(retained, length):
    ladder = np.arange(retained)
    return np.where(ladder < retained // 2, ladder, length - retained + ladder)


def np_angles(wavenum, length):
    points = np.arange(length)
    return (wavenum[:, None] * points[None, :] % length) * (2.0 * math.pi / length)


def as_bf16(table):
    return np.asarray(table, np.float32).astype(ml_dtypes.bfloat16)


def rotation(angle, sign):
    cosine, sine_wave = np.cos(angle), sign * np.sin(angle)
    return np.stack([np.stack([cosine, -sine_wave]), np.stack([sine_wave, cosine])])


@functools.lru_cache(maxsize=None)
def tables(devices, lines, depth_len):
    planes_all = devices * PLANES
    angle = np_angles(np.arange(MZ), depth_len)
    depth = np.stack([np.cos(angle), -np.sin(angle)])
    eye = np.eye(GROUP)
    depth_block = np.einsum("akz,ij->akijz", depth, eye).reshape(2 * MZ * GROUP, GROUP * depth_len)
    depth_pair = np.einsum("akz,ij->iakjz", depth, np.eye(2)).reshape(4 * MZ, 2 * depth_len)
    plane_eye = np.eye(PLANES)
    angle = np_angles(np_freq(MY, lines), lines).reshape(devices, MY // devices, lines)
    across = np.einsum("badly,xw->ldbxawy", rotation(angle, -1.0), plane_eye)
    across = across.reshape(MY * 2 * PLANES, 2 * PLANES * lines)
    back = np.einsum("pbdly,xw->pxyldbw", rotation(angle, 1.0), plane_eye)
    back = back.reshape(2 * PLANES * lines, MY * 2 * PLANES)
    angle = np_angles(np_freq(MX, planes_all), planes_all).reshape(MX // 4, 4, devices, PLANES)
    forward = rotation(angle, -1.0)
    rows = np.einsum("batksx->tbksax", forward).reshape(MX // 4, 2, 4, devices * 2 * PLANES)
    plain = rows.reshape(2 * MX, -1)
    both = np.stack([rows, rows[:, ::-1]], 1).reshape(4 * MX, -1)
    turned = np.concatenate([rows[:, 1:], -rows[:, :1]], 1).reshape(2 * MX, -1)
    straight_rotated = np.concatenate([plain, turned], 0)
    inverse = np.einsum("batksx->sbxtak", rotation(angle, 1.0)).reshape(-1, 2 * MX)
    return {
        "depth": as_bf16(depth_block),
        "depth_pair": as_bf16(depth_pair),
        "across_y": as_bf16(across),
        "back_y": as_bf16(back),
        "plain_x": as_bf16(plain),
        "both_x": as_bf16(both),
        "straight_x": as_bf16(straight_rotated),
        "back_x": as_bf16(inverse),
    }


def dot_nn(left, right):
    return jnp.dot(left, right, preferred_element_type=F32)


def dot_nt(left, right):
    return lax.dot_general(left, right, NT, preferred_element_type=F32)


def lanes(shape):
    return lax.broadcasted_iota(jnp.int32, shape, len(shape) - 1)


def sublanes(shape):
    return lax.broadcasted_iota(jnp.int32, shape, len(shape) - 2)


def swap_halves(block):
    return pltpu.roll(block, 64, 1)


def part_copy(source, target, sems, index, size):
    start = index * size if isinstance(index, int) else pl.multiple_of(index * size, size)
    part = pl.ds(start, size)
    return pltpu.make_async_copy(source.at[part], target.at[part], sems.at[index])


def start_parts(source, target, sems, size, first, last):
    for index in range(first, min(last, source.shape[0] // size)):
        part_copy(source, target, sems, index, size).start()


def start_tables(pairs, sems):
    copies = []
    for index, (source, target) in enumerate(pairs):
        copy = pltpu.make_async_copy(source, target, sems.at[index])
        copy.start()
        copies.append(copy)
    return copies


def depth_quad(slabs, quad, depth_pair, scale, group, lines_ref):
    four = slabs[quad * 4 : quad * 4 + 4]
    wide = jnp.concatenate(
        [jnp.concatenate(four[2 * pair : 2 * pair + 2], axis=1) for pair in range(2)], axis=0
    )
    parts = dot_nt(depth_pair, wide)
    if scale is not None:
        parts = parts * scale
    half = wide.shape[0] // 2
    for pair in range(2):
        start = (group * GROUP + quad * 4 + pair * 2) * 2 * MZ
        if not isinstance(start, int):
            start = pl.multiple_of(start, 4 * MZ)
        lines_ref[pl.ds(start, 4 * MZ), :] = parts[:, pair * half : (pair + 1) * half]


def depth_analysis(slabs, depth_pair, scale, group, lines_ref):
    for quad in range(2):
        depth_quad(slabs, quad, depth_pair, scale, group, lines_ref)


def rows_analysis(lines_ref, across_ref, rows_ref, out_ref):
    channels = lines_ref.shape[0] // (2 * MZ)
    across = across_ref[...]
    half = across.shape[0] // 2
    for first in range(0, MZ // 2, 2):
        pair = jnp.concatenate(
            [
                jnp.concatenate(
                    [
                        lines_ref[pl.ds(a * MZ + kz, channels, stride=2 * MZ), :]
                        for a in range(2)
                    ],
                    axis=1,
                )
                for kz in range(2 * first, 2 * first + 4)
            ],
            axis=0,
        ).astype(BF16)
        rows = dot_nt(across, pair)
        for k in range(2):
            for kyl in range(2):
                rows_ref[pl.ds(kyl * 8 + first + k, half, stride=16), :] = rows[
                    kyl * half : (kyl + 1) * half, k * 128 : (k + 1) * 128
                ]
    out_ref[...] = rows_ref[...].astype(BF16)


def rows_gather(block_ref, rows_ref, spec_ref):
    rows_ref[...] = block_ref[...].astype(F32)
    count = rows_ref.shape[0] // 16
    eye = (sublanes((128, 128)) == lanes((128, 128))).astype(BF16)
    for first in range(0, MZ // 2, 2):
        both = jnp.concatenate(
            [
                rows_ref[pl.ds(kyl * 8 + first + k, count, stride=16), :]
                for k in range(2)
                for kyl in range(2)
            ],
            axis=0,
        ).astype(BF16)
        turned = dot_nt(eye, both)
        half = turned.shape[1] // 2
        for k in range(2):
            for h in range(2):
                at = (2 * (first + k) + h) * GROUP
                spec_ref[:, at : at + GROUP, :] = turned[
                    h * 64 : (h + 1) * 64, k * half : (k + 1) * half
                ].reshape(8, GROUP, half)


def lines_synthesis(step, spec_ref, back, scale):
    count = STEP // GROUP
    both = jnp.concatenate([spec_ref[step * count + g] for g in range(count)], axis=0)
    lines = dot_nt(back, both.astype(BF16))
    if scale is not None:
        lines = lines * scale
    lines = lines.astype(BF16)
    half = lines.shape[0] // 2
    return [
        jnp.concatenate(
            [lines[p * half : (p + 1) * half, g * 128 : (g + 1) * 128] for p in range(2)], axis=1
        )
        for g in range(count)
    ]


def flat(slab):
    return slab.reshape(slab.shape[0] * slab.shape[1], slab.shape[2])


def analysis_kernel(
    field_hbm,
    pair_hbm,
    across_hbm,
    out_ref,
    field_ref,
    pair_ref,
    across_ref,
    lines_ref,
    rows_ref,
    field_sems,
    table_sems,
):
    first, second = start_tables([(pair_hbm, pair_ref), (across_hbm, across_ref)], table_sems)
    start_parts(field_hbm, field_ref, field_sems, STEP, 0, field_ref.shape[0] // STEP)
    first.wait()

    for step in range(field_ref.shape[0] // STEP):
        part_copy(field_hbm, field_ref, field_sems, step, STEP).wait()
        for g in range(STEP // GROUP):
            group = step * (STEP // GROUP) + g
            slabs = [flat(field_ref[group * GROUP + ci]) for ci in range(GROUP)]
            depth_analysis(slabs, pair_ref[...], None, group, lines_ref)

    second.wait()
    rows_analysis(lines_ref, across_ref, rows_ref, out_ref)


def middle_kernel(
    inverse_scale,
    block_ref,
    bias_ref,
    point_hbm,
    cot_hbm,
    depth_hbm,
    pair_hbm,
    across_hbm,
    back_hbm,
    act_hbm,
    up_hbm,
    out_ref,
    point_ref,
    cot_ref,
    depth_ref,
    pair_ref,
    across_ref,
    back_ref,
    act_ref,
    up_ref,
    lines_ref,
    rows_ref,
    spec_ref,
    point_sems,
    cot_sems,
    act_sems,
    up_sems,
    table_sems,
):
    tables_in = start_tables(
        [
            (back_hbm, back_ref),
            (depth_hbm, depth_ref),
            (pair_hbm, pair_ref),
            (across_hbm, across_ref),
        ],
        table_sems,
    )
    start_parts(point_hbm, point_ref, point_sems, STEP, 0, 1)
    start_parts(cot_hbm, cot_ref, cot_sems, STEP, 0, 1)
    rows_gather(block_ref, rows_ref, spec_ref)
    start_parts(point_hbm, point_ref, point_sems, STEP, 1, 2)
    start_parts(cot_hbm, cot_ref, cot_sems, STEP, 1, 2)
    for copy in tables_in:
        copy.wait()
    steps = point_ref.shape[0] // STEP
    groups = point_ref.shape[0] // GROUP
    per_step = STEP // GROUP

    def activate(index, spectral):
        hidden = spectral + flat(point_ref[index]).astype(F32) + bias_ref[index]
        square = hidden * hidden
        gate = 0.5 + 0.5 * jnp.tanh(hidden * (SQRT_TWO_PI + (SQRT_TWO_PI * CUBIC_COEF) * square))
        slope = hidden * (2.0 * SQRT_TWO_PI + (6.0 * SQRT_TWO_PI * CUBIC_COEF) * square)
        derivative = gate + (gate - gate * gate) * slope
        upstream = (flat(cot_ref[index]).astype(F32) * derivative).astype(BF16)
        act_ref[index] = (hidden * gate).astype(BF16).reshape(act_ref.shape[1:])
        up_ref[index] = upstream.reshape(up_ref.shape[1:])
        return upstream

    def quarter(wide, at):
        return dot_nn(wide, depth_ref[:, at * 256 : (at + 1) * 256])

    wides = lines_synthesis(0, spec_ref, back_ref[...], inverse_scale)
    spectral = [quarter(wides[0], at) for at in range(4)]
    last = None
    for group in range(groups):
        step = group // per_step
        if group % per_step == 0:
            part_copy(point_hbm, point_ref, point_sems, step, STEP).wait()
            part_copy(cot_hbm, cot_ref, cot_sems, step, STEP).wait()
            start_parts(point_hbm, point_ref, point_sems, STEP, step + 2, step + 3)
            start_parts(cot_hbm, cot_ref, cot_sems, STEP, step + 2, step + 3)
            if step + 1 < steps:
                wides += lines_synthesis(step + 1, spec_ref, back_ref[...], inverse_scale)
        following, slabs = [], []
        for at in range(4):
            if group + 1 < groups:
                following.append(quarter(wides[group + 1], at))
            for k in range(2):
                oi = 2 * at + k
                slabs.append(
                    activate(group * GROUP + oi, spectral[at][:, k * 128 : (k + 1) * 128])
                )
            if last is not None and at % 2 == 0:
                depth_quad(last, at // 2, pair_ref[...], inverse_scale, group - 1, lines_ref)
        if group % per_step == per_step - 1:
            part_copy(act_ref, act_hbm, act_sems, step, STEP).start()
            part_copy(up_ref, up_hbm, up_sems, step, STEP).start()
        spectral, last = following, slabs
    depth_analysis(last, pair_ref[...], inverse_scale, groups - 1, lines_ref)
    rows_analysis(lines_ref, across_ref, rows_ref, out_ref)
    for step in range(steps):
        part_copy(act_ref, act_hbm, act_sems, step, STEP).wait()
        part_copy(up_ref, up_hbm, up_sems, step, STEP).wait()


def final_kernel(
    block_ref,
    point_hbm,
    depth_hbm,
    back_hbm,
    out_hbm,
    point_ref,
    depth_ref,
    back_ref,
    out_ref,
    rows_ref,
    spec_ref,
    point_sems,
    out_sems,
    table_sems,
):
    tables_in = start_tables([(back_hbm, back_ref), (depth_hbm, depth_ref)], table_sems)
    start_parts(point_hbm, point_ref, point_sems, STEP, 0, 1)
    rows_gather(block_ref, rows_ref, spec_ref)
    start_parts(point_hbm, point_ref, point_sems, STEP, 1, 4)
    for copy in tables_in:
        copy.wait()
    steps = point_ref.shape[0] // STEP
    groups = point_ref.shape[0] // GROUP
    per_step = STEP // GROUP

    def quarter(wide, at):
        return dot_nn(wide, depth_ref[:, at * 256 : (at + 1) * 256])

    wides = lines_synthesis(0, spec_ref, back_ref[...], None)
    spectral = [quarter(wides[0], at) for at in range(4)]
    for group in range(groups):
        step = group // per_step
        if group % per_step == 0:
            part_copy(point_hbm, point_ref, point_sems, step, STEP).wait()
            if step + 1 < steps:
                wides += lines_synthesis(step + 1, spec_ref, back_ref[...], None)
        following = []
        for at in range(4):
            if group + 1 < groups:
                following.append(quarter(wides[group + 1], at))
            for k in range(2):
                index = group * GROUP + 2 * at + k
                total = spectral[at][:, k * 128 : (k + 1) * 128] + flat(point_ref[index]).astype(F32)
                out_ref[index] = total.astype(BF16).reshape(out_ref.shape[1:])
        if group % per_step == per_step - 1:
            part_copy(out_ref, out_hbm, out_sems, step, STEP).start()
        spectral = following

    for step in range(steps):
        part_copy(out_ref, out_hbm, out_sems, step, STEP).wait()


def point_turn_kernel(
    scale,
    weight_ref,
    field_hbm,
    modes_hbm,
    coeff_hbm,
    out_hbm,
    head_ref,
    turned_hbm,
    *refs,
):
    refs, (coeff_ref, turned_ref, turn_sems) = refs[:-3], refs[-3:]
    take = pltpu.make_async_copy(coeff_hbm, coeff_ref, turn_sems.at[0])
    take.start()
    point_kernel(True, weight_ref, field_hbm, modes_hbm, out_hbm, head_ref, *refs)
    take.wait()
    eye = (sublanes((128, 128)) == lanes((128, 128))).astype(BF16)
    for j in range(16):
        turned_ref[j] = (dot_nt(eye, coeff_ref[j]) * scale).astype(BF16)
    give = pltpu.make_async_copy(turned_ref, turned_hbm, turn_sems.at[1])
    give.start()
    give.wait()


def point_kernel(
    transposed,
    weight_ref,
    field_hbm,
    modes_hbm,
    out_hbm,
    head_ref,
    field_ref,
    out_ref,
    wide_ref,
    in_sems,
    out_sems,
    head_sems,
):
    size = wide_ref.shape[0]
    planes = field_ref.shape[1]
    copies = []
    for plane in range(planes):
        part = (slice(None), pl.ds(plane, 1))
        copy = pltpu.make_async_copy(field_hbm.at[part], field_ref.at[part], in_sems.at[plane])
        copy.start()
        copies.append(copy)
    heads = weight_copies(modes_hbm, head_ref, head_sems, 0)
    for copy in heads:
        copy.start()
    tall = (sublanes((size, 64)) // 16 == lanes((size, 64))).astype(BF16)
    weight = weight_ref[...]
    left = dot_nt(tall, weight) if transposed else dot_nn(tall, weight)
    left = left.astype(BF16)
    rows = size // 4
    same = sublanes((rows, size)) % 16 == lanes((rows, size)) % 16
    for quarter in range(4):
        spread = dot_nt(left[quarter * rows : (quarter + 1) * rows], tall)
        wide_ref[quarter * rows : (quarter + 1) * rows, :] = jnp.where(same, spread, 0.0).astype(
            BF16
        )
    sends = []
    for plane in range(planes):
        copies[plane].wait()
        for pair in range(2):
            right = jnp.concatenate(
                [
                    field_ref[:, plane, yc * 16 : (yc + 1) * 16, :].reshape(size, 128)
                    for yc in (2 * pair, 2 * pair + 1)
                ],
                axis=1,
            )
            result = dot_nn(wide_ref[...], right).astype(BF16)
            for k in range(2):
                yc = 2 * pair + k
                out_ref[:, plane, yc * 16 : (yc + 1) * 16, :] = result[
                    :, k * 128 : (k + 1) * 128
                ].reshape(size // 16, 16, 128)
        part = (slice(None), pl.ds(plane, 1))
        copy = pltpu.make_async_copy(out_ref.at[part], out_hbm.at[part], out_sems.at[plane])
        copy.start()
        sends.append(copy)
    for copy in sends + heads:
        copy.wait()


def weight_copies(weight_hbm, weight_ref, sems, first):
    rows = weight_hbm.shape[0] // 16
    copies = []
    for index in range(weight_ref.shape[0] // rows):
        copy = pltpu.make_async_copy(
            weight_hbm.at[pl.ds((first + index) * rows, rows)],
            weight_ref.at[pl.ds(index * rows, rows)],
            sems.at[index],
        )
        copies.append(copy)
    return copies


def next_weights(copies, j):
    if j < HEAD or (j - HEAD) % 2:
        return
    for index in range(j - HEAD, min(j - HEAD + 2, len(copies))):
        copies[index].wait()
        if index + FLIGHT < len(copies):
            copies[index + FLIGHT].start()


def mode_pair(head_ref, weight_ref, j, h, u):
    source = head_ref if j < HEAD else weight_ref
    start = (((j if j < HEAD else j - HEAD) * 2 + h) * MX + 8 * u) * 64
    return jnp.concatenate(
        [source[start : start + 256, :], source[start + 256 : start + 512, :]], axis=1
    )


def plane_sums(back_ref, mixed_ref, res_ref, quarter):
    count = res_ref.shape[0] // 16
    wide = jnp.concatenate([mixed_ref[quarter * 4 + k] for k in range(4)], axis=1)
    rows = dot_nn(back_ref[...], wide)
    for k in range(4):
        res_ref[pl.ds(quarter * 4 + k, count, stride=16), :] = rows[:, k * 128 : (k + 1) * 128]


def mode_kernel(
    scale,
    block_ref,
    head_ref,
    weight_hbm,
    both_ref,
    plain_ref,
    back_ref,
    coeff_hbm,
    out_ref,
    coeff_ref,
    weight_ref,
    rows_ref,
    res_ref,
    left_ref,
    mixed_ref,
    sems,
    coeff_sems,
):
    copies = weight_copies(weight_hbm, weight_ref, sems, HEAD)
    for copy in copies[:FLIGHT]:
        copy.start()
    count = rows_ref.shape[0] // 16
    rows_ref[...] = block_ref[...].astype(F32)
    low = lanes((128, 128)) < 64
    kxl = sublanes((128, 128)) % 4
    half = lanes((128, 128)) // 64
    first = (kxl == half).astype(BF16)
    second = (kxl == 2 + half).astype(BF16)
    low8 = lanes((8, 128)) < 64
    sign = jnp.where(sublanes((8, 128)) < 4, -1.0, 1.0)
    for quarter in range(4):
        wide = jnp.concatenate(
            [rows_ref[pl.ds(quarter * 4 + k, count, stride=16), :] for k in range(4)], axis=1
        ).astype(BF16)
        plain = (dot_nn(plain_ref[...], wide) * scale).astype(BF16)
        both = dot_nn(both_ref[...], wide) * scale
        for k in range(4):
            j = quarter * 4 + k
            coeff_ref[j] = plain[:, k * 128 : (k + 1) * 128]
            coeffs = both[:, k * 128 : (k + 1) * 128]
            swapped = swap_halves(coeffs)
            for h in range(2):
                twice = jnp.where(low if h == 0 else ~low, coeffs, swapped).astype(BF16)
                left_ref[j, h] = jnp.concatenate([twice * first, twice * second], axis=1)
    send = pltpu.make_async_copy(coeff_ref, coeff_hbm, coeff_sems.at[0])
    send.start()
    for j in range(16):
        next_weights(copies, j)
        mixed = []
        for u in range(MX // 8):
            halves = [
                dot_nn(left_ref[j, h, u * 32 : (u + 1) * 32, :], mode_pair(head_ref, weight_ref, j, h, u))
                for h in range(2)
            ]
            for t in range(2):
                low_h, high_h = [
                    part[t * 16 : (t + 1) * 16, t * 128 : (t + 1) * 128] for part in halves
                ]
                keep = jnp.where(low8, low_h[:8], sign * high_h[8:])
                move = jnp.where(low8, high_h[:8], sign * low_h[8:])
                mixed.append(keep + swap_halves(move))
        mixed_ref[j] = jnp.concatenate(mixed, axis=0).astype(BF16)
        if j > 4 and j % 4 == 1:
            plane_sums(back_ref, mixed_ref, res_ref, j // 4 - 1)
    plane_sums(back_ref, mixed_ref, res_ref, 3)
    out_ref[...] = res_ref[...].astype(BF16)
    send.wait()


def mode_grad_kernel(
    scale,
    block_ref,
    head_ref,
    weight_hbm,
    straight_ref,
    back_ref,
    turned_hbm,
    pair_ref,
    turned_ref,
    out_ref,
    weight_ref,
    rows_ref,
    res_ref,
    mixed_ref,
    sems,
    turned_sems,
):
    send = pltpu.make_async_copy(turned_hbm, turned_ref, turned_sems.at[0])
    copies = weight_copies(weight_hbm, weight_ref, sems, HEAD)
    for copy in copies[:FLIGHT]:
        copy.start()
    send.start()
    count = rows_ref.shape[0] // 16
    rows_ref[...] = block_ref[...].astype(F32)
    low = lanes((64, 128)) < 64
    low16 = lanes((16, 128)) < 64
    row = sublanes((16, 128)) % 4
    upper = row < 2
    valid = lanes((16, 128)) // 64 == row % 2
    even = (sublanes((16, 128)) < 8).astype(BF16)
    odd = (sublanes((16, 128)) >= 8).astype(BF16)
    for j in range(16):
        section = rows_ref[pl.ds(j, count, stride=16), :]
        swapped = swap_halves(section)
        twice = jnp.concatenate(
            [jnp.where(low, section, swapped), jnp.where(low, swapped, section)], axis=1
        ).astype(BF16)
        turned = dot_nn(straight_ref[...], twice)
        for h in range(2):
            part = turned[:, h * 128 : (h + 1) * 128]
            pair_ref[2 * j + h] = jnp.where(low, part[:64], part[64:]).astype(BF16)
    for j in range(16):
        next_weights(copies, j)
        mixed = []
        for u in range(MX // 8):
            found = []
            for h in range(2):
                pair = pair_ref[2 * j + h, u * 16 : (u + 1) * 16, :]
                rows = dot_nt(
                    jnp.concatenate([pair * even, pair * odd], axis=1),
                    mode_pair(head_ref, weight_ref, j, h, u),
                )
                found.append(jnp.where(valid, jnp.where(upper, rows[:, :128], rows[:, 128:]), 0.0))
            keep = jnp.where(low16, found[0], found[1])
            move = jnp.where(low16, found[1], found[0])
            mixed.append(keep + swap_halves(move))
        mixed_ref[j] = (jnp.concatenate(mixed, axis=0) * scale).astype(BF16)
        if j > 4 and j % 4 == 1:
            plane_sums(back_ref, mixed_ref, res_ref, j // 4 - 1)
    plane_sums(back_ref, mixed_ref, res_ref, 3)
    out_ref[...] = res_ref[...].astype(BF16)
    send.wait()


def weight_grad_kernel(
    turned_ref, pair_ref, out_hbm, out_ref, mask_ref, pairs_ref, sems
):
    lane = lanes((128, 64))
    part = sublanes((128, 64)) // 64
    for t in range(MX // 4 - VECTOR):
        mask_ref[t] = ((lane // 8 == t) & (lane % 4 // 2 == part)).astype(BF16)
    for index in range(32):
        pairs_ref[index] = pair_ref[index].astype(F32)
    even = (sublanes((64, 128)) % 2 == 0).astype(BF16)
    odd = (sublanes((64, 128)) % 2 == 1).astype(BF16)

    def one_pair(j):
        for h in range(2):
            one = turned_ref[j, h * 64 : (h + 1) * 64, :]
            left = jnp.concatenate([one, one], axis=0)
            pair = pair_ref[j * 2 + h]
            right = jnp.concatenate([pair * even, pair * odd], axis=1)
            for t in range(MX // 4):
                mode = (j * 2 + h) * MX + 4 * t
                if t < MX // 4 - VECTOR:
                    four = dot_nn(left * mask_ref[t], right)
                    for k in range(4):
                        out_ref[mode + k] = four[
                            k // 2 * 64 : (k // 2 + 1) * 64, k % 2 * 128 : (k % 2 + 1) * 128
                        ].astype(BF16)
                    continue
                for k in range(4):
                    total = None
                    for b in range(2):
                        at = t * 8 + b * 4 + k
                        column = jnp.broadcast_to(one[:, at : at + 1], (64, 128))
                        row = jnp.broadcast_to(
                            pairs_ref[j * 2 + h, at : at + 1, :], (64, 128)
                        ).astype(BF16)
                        total = column * row if total is None else total + column * row
                    out_ref[mode + k] = total
        part_copy(out_ref, out_hbm, sems, j, 2 * MX).start()

    @pl.loop(0, 4)
    def _(trip):
        for k in range(4):
            one_pair(trip * 4 + k)

    for j in range(16):
        part_copy(out_ref, out_hbm, sems, j, 2 * MX).wait()


def params(mib):
    return pltpu.CompilerParams(vmem_limit_bytes=mib * 1024 * 1024)


def cost(flops, moved):
    return pl.CostEstimate(flops=int(flops), bytes_accessed=int(moved), transcendentals=0)


def fast_body(features, cotangent, spectral_weight, channel_weight, channel_bias):
    channels, planes, lines, depth_len = features.shape
    devices = lax.axis_size("gx")
    owned_modes = spectral_weight.shape[0]
    wave_pairs = MY * MZ
    volume = planes * devices * lines * depth_len
    forward_scale = 1.0 / math.sqrt(volume)
    inverse_scale = 1.0 / math.sqrt(MX * wave_pairs)
    weight_scale = math.sqrt(MX * wave_pairs / volume)
    table = {name: jnp.asarray(value) for name, value in tables(devices, lines, depth_len).items()}
    for name in ("depth", "depth_pair", "across_y", "back_y"):
        table[name] = pltpu.with_memory_space_constraint(table[name], pltpu.HBM)
    block_rows = devices * 64
    block_shape = jax.ShapeDtypeStruct((block_rows, 128), BF16)
    vmem = pl.BlockSpec(memory_space=pltpu.VMEM)
    hbm = pl.BlockSpec(memory_space=pltpu.HBM)
    smem = pl.BlockSpec(memory_space=pltpu.SMEM)
    field_scratch = pltpu.VMEM(features.shape, BF16)
    field_shape = jax.ShapeDtypeStruct(features.shape, BF16)

    def sems(count):
        return pltpu.SemaphoreType.DMA((count,))

    def scratch(name):
        return pltpu.VMEM(table[name].shape, BF16)

    def in_hbm(array):
        return pltpu.with_memory_space_constraint(array, pltpu.HBM)

    def in_vmem(array):
        return pltpu.with_memory_space_constraint(array, pltpu.VMEM)

    steps = channels // STEP
    lines_scratch = pltpu.VMEM((channels * 2 * MZ, planes * lines), F32)
    rows_scratch = pltpu.VMEM((block_rows, 128), F32)
    spec_scratch = pltpu.VMEM((channels // GROUP, MZ * GROUP, 128), F32)
    weight_rows = pltpu.with_memory_space_constraint(
        spectral_weight.reshape(owned_modes * channels, 2 * channels), pltpu.HBM
    )
    field_bytes = features.size * 2

    def exchange(block):
        return lax.all_to_all(
            block.reshape(devices, 64, 128), "gx", 0, 0, tiled=True
        ).reshape(block_rows, 128)

    point_scratch = [
        field_scratch,
        field_scratch,
        pltpu.VMEM((channels * 16, channels * 16), BF16),
        sems(planes),
        sems(planes),
        sems(HEAD),
    ]
    point_out = [
        pltpu.HBM(features.shape, BF16),
        pltpu.VMEM((weight_rows.shape[0] * HEAD // 16, weight_rows.shape[1]), BF16),
    ]
    turned_shape = (16, 2 * channels, 64)

    block = pl.pallas_call(
        analysis_kernel,
        out_shape=block_shape,
        in_specs=[hbm, hbm, hbm],
        out_specs=vmem,
        scratch_shapes=[
            field_scratch,
            scratch("depth_pair"),
            scratch("across_y"),
            lines_scratch,
            rows_scratch,
            sems(steps),
            sems(2),
        ],
        compiler_params=params(VMEM_MIB),
        cost_estimate=cost(2 * 256 * 1024 * 1024, field_bytes),
        name="field_analysis",
    )(in_hbm(features), table["depth_pair"], table["across_y"])
    pointwise, head = pl.pallas_call(
        functools.partial(point_kernel, False),
        out_shape=point_out,
        in_specs=[vmem, hbm, hbm],
        out_specs=[hbm, vmem],
        scratch_shapes=point_scratch,
        compiler_params=params(VMEM_MIB),
        cost_estimate=cost(2 * 1024**3, 2 * field_bytes),
        name="channel_map",
    )(channel_weight, in_hbm(features), weight_rows)
    block, pointwise, head = lax.optimization_barrier((exchange(block), pointwise, head))

    weight_scratch = pltpu.VMEM(
        (weight_rows.shape[0] * (16 - HEAD) // 16, weight_rows.shape[1]), BF16
    )
    mixed_scratch = pltpu.VMEM((16, 64, 128), BF16)
    weight_sems = sems(16 - HEAD)
    coeffs, block = pl.pallas_call(
        functools.partial(mode_kernel, forward_scale),
        out_shape=[pltpu.HBM((16, 64, 128), BF16), block_shape],
        in_specs=[vmem, vmem, hbm, vmem, vmem, vmem],
        out_specs=[hbm, vmem],
        scratch_shapes=[
            pltpu.VMEM((16, 64, 128), BF16),
            weight_scratch,
            rows_scratch,
            rows_scratch,
            pltpu.VMEM((16, 2, 128, 256), BF16),
            mixed_scratch,
            weight_sems,
            sems(1),
        ],
        compiler_params=params(VMEM_MIB),
        cost_estimate=cost(256 * 2 * 16 * 256 * 128, 17 * 2**20),
        name="mode_product",
    )(block, in_vmem(head), weight_rows, table["both_x"], table["plain_x"], table["back_x"])
    block = exchange(block)

    activated, upstream, block = pl.pallas_call(
        functools.partial(middle_kernel, inverse_scale),
        out_shape=[field_shape, pltpu.HBM(features.shape, BF16), block_shape],
        in_specs=[vmem, smem, hbm, hbm, hbm, hbm, hbm, hbm],
        out_specs=[hbm, hbm, vmem],
        scratch_shapes=[
            field_scratch,
            field_scratch,
            scratch("depth"),
            scratch("depth_pair"),
            scratch("across_y"),
            scratch("back_y"),
            field_scratch,
            field_scratch,
            lines_scratch,
            rows_scratch,
            spec_scratch,
            sems(steps),
            sems(steps),
            sems(steps),
            sems(steps),
            sems(4),
        ],
        compiler_params=params(VMEM_MIB),
        cost_estimate=cost(2**30, 4 * field_bytes),
        name="gelu_and_gradient",
    )(
        block,
        channel_bias,
        in_hbm(pointwise),
        in_hbm(cotangent),
        table["depth"],
        table["depth_pair"],
        table["across_y"],
        table["back_y"],
    )
    channel_back, head, turned = pl.pallas_call(
        functools.partial(point_turn_kernel, weight_scale),
        out_shape=point_out + [pltpu.HBM(turned_shape, BF16)],
        in_specs=[vmem, hbm, hbm, hbm],
        out_specs=[hbm, vmem, hbm],
        scratch_shapes=point_scratch
        + [pltpu.VMEM((16, 64, 128), BF16), pltpu.VMEM(turned_shape, BF16), sems(2)],
        compiler_params=params(VMEM_MIB),
        cost_estimate=cost(2 * 1024**3, 2 * field_bytes),
        name="channel_map_back",
    )(channel_weight, in_hbm(upstream), weight_rows, in_hbm(coeffs))
    block, channel_back, head, turned = lax.optimization_barrier(
        (exchange(block), channel_back, head, turned)
    )

    pairs, turned, block = pl.pallas_call(
        functools.partial(mode_grad_kernel, forward_scale),
        out_shape=[
            pltpu.VMEM((32, 64, 128), BF16),
            pltpu.VMEM(turned_shape, BF16),
            block_shape,
        ],
        in_specs=[vmem, vmem, hbm, vmem, vmem, hbm],
        out_specs=[vmem, vmem, vmem],
        scratch_shapes=[
            weight_scratch,
            rows_scratch,
            rows_scratch,
            mixed_scratch,
            weight_sems,
            sems(1),
        ],
        compiler_params=params(VMEM_MIB),
        cost_estimate=cost(256 * 2 * 16 * 256 * 128, 17 * 2**20),
        name="mode_gradient",
    )(block, in_vmem(head), weight_rows, table["straight_x"], table["back_x"], in_hbm(turned))
    block = exchange(block)

    spectral_grad = pl.pallas_call(
        weight_grad_kernel,
        out_shape=jax.ShapeDtypeStruct(spectral_weight.shape, BF16),
        in_specs=[vmem, vmem],
        out_specs=hbm,
        scratch_shapes=[
            pltpu.VMEM(spectral_weight.shape, BF16),
            pltpu.VMEM((MX // 4, 128, 64), BF16),
            pltpu.VMEM((32, 64, 128), F32),
            sems(16),
        ],
        compiler_params=params(VMEM_MIB),
        cost_estimate=cost(512 * 2 * 64 * 64 * 256, 17 * 2**20),
        name="weight_gradient",
    )(
        in_vmem(turned),
        in_vmem(pairs),
    )

    feature_grad = pl.pallas_call(
        final_kernel,
        out_shape=field_shape,
        in_specs=[vmem, hbm, hbm, hbm],
        out_specs=hbm,
        scratch_shapes=[
            field_scratch,
            scratch("depth"),
            scratch("back_y"),
            field_scratch,
            rows_scratch,
            spec_scratch,
            sems(steps),
            sems(steps),
            sems(2),
        ],
        compiler_params=params(VMEM_MIB),
        cost_estimate=cost(2**29, 2 * field_bytes),
        name="field_gradient",
    )(block, in_hbm(channel_back), table["depth"], table["back_y"])
    return (activated, feature_grad, spectral_grad)


def body(features, cotangent, spectral_weight, channel_weight, channel_bias):
    channels, planes, lines, depth_len = features.shape
    devices = lax.axis_size("gx")
    fits = (
        (channels, planes, lines, depth_len) == (64, PLANES, 64, 128)
        and spectral_weight.shape[0] == 2 * MZ * MX
        and devices * 2 == MY
        and devices * 2 == MX
    )
    run = fast_body if fits else general_body
    return run(features, cotangent, spectral_weight, channel_weight, channel_bias)


def solution(mesh):
    in_specs = (
        P("grp", "gx", None, None),
        P("grp", "gx", None, None),
        P("gx", None, None),
        P(),
        P(),
    )
    out_specs = (
        P("grp", "gx", None, None),
        P("grp", "gx", None, None),
        P(("grp", "gx"), None, None),
    )
    return jax.shard_map(body, mesh=mesh, in_specs=in_specs, out_specs=out_specs, check_vma=False)
```

```python
import functools
import math

import jax
import jax.numpy as jnp
import ml_dtypes
import numpy as np
from jax import lax
from jax.experimental import pallas as pl
from jax.experimental.pallas import tpu as pltpu
from jax.sharding import PartitionSpec as P

MX = 32
MY = 32
MZ = 16


SQRT_TWO_PI = math.sqrt(2.0 / math.pi)
CUBIC_COEF = 0.044715


def freq_index(retained, length):
    ladder = jnp.arange(retained, dtype=jnp.int32)
    return jnp.where(ladder < retained // 2, ladder, length - retained + ladder)


def cos_sin(wavenum, length):
    points = jnp.arange(length, dtype=jnp.int32)
    angles = (wavenum[:, None] * points[None, :] % length).astype(jnp.float32) * (
        2.0 * math.pi / length
    )
    return (jnp.cos(angles), jnp.sin(angles))


def analysis_pair(wavenum, length):
    cosine, sine_wave = cos_sin(wavenum, length)
    cosine, sine_wave = (cosine.T, sine_wave.T)
    return jnp.stack(
        [jnp.stack([cosine, -sine_wave], 1), jnp.stack([sine_wave, cosine], 1)], 1
    ).astype(jnp.bfloat16)


def synthesis_pair(wavenum, length):
    cosine, sine_wave = cos_sin(wavenum, length)
    return jnp.stack(
        [jnp.stack([cosine, sine_wave], 1), jnp.stack([-sine_wave, cosine], 1)], 1
    ).astype(jnp.bfloat16)


def depth_table(retained, length):
    cosine, sine_wave = cos_sin(jnp.arange(retained, dtype=jnp.int32), length)
    return jnp.concatenate([cosine, -sine_wave], 0).astype(jnp.bfloat16)


def gelu_parts(inputs):
    cubed_in = inputs * inputs * inputs
    tangent = jnp.tanh(SQRT_TWO_PI * (inputs + CUBIC_COEF * cubed_in))
    output = 0.5 * inputs * (1.0 + tangent)
    derivative = 0.5 * (1.0 + tangent) + 0.5 * inputs * (1.0 - tangent * tangent) * SQRT_TWO_PI * (
        1.0 + 3.0 * CUBIC_COEF * inputs * inputs
    )
    return (output, derivative)


def mode_product(coeffs, weights, channels):
    stacked = coeffs.reshape(coeffs.shape[0], 2, channels)
    halves = jnp.einsum("mac,mcj->amj", stacked, weights, preferred_element_type=jnp.float32)
    real_out = halves[0, :, :channels] - halves[1, :, channels:]
    imag_out = halves[0, :, channels:] + halves[1, :, :channels]
    return jnp.concatenate([real_out, imag_out], 1).astype(jnp.bfloat16)


def mode_grads(coeffs, weights, grad_modes, channels, weight_scale, input_scale):
    number = coeffs.shape[0]
    stacked = coeffs.reshape(number, 2, channels)
    grad_pairs = grad_modes.reshape(number, 2, channels)
    real_w = jnp.einsum("mac,mao->mco", stacked, grad_pairs, preferred_element_type=jnp.float32)
    imag_w = jnp.einsum(
        "mc,mo->mco", stacked[:, 0], grad_pairs[:, 1], preferred_element_type=jnp.float32
    ) - jnp.einsum(
        "mc,mo->mco", stacked[:, 1], grad_pairs[:, 0], preferred_element_type=jnp.float32
    )
    weight_grad = (jnp.concatenate([real_w, imag_w], 2) * weight_scale).astype(jnp.bfloat16)
    straight = jnp.concatenate([grad_pairs[:, 0], grad_pairs[:, 1]], 1)
    rotated = jnp.concatenate([grad_pairs[:, 1], -grad_pairs[:, 0]], 1)
    real_x = jnp.einsum("mcj,mj->mc", weights, straight, preferred_element_type=jnp.float32)
    imag_x = jnp.einsum("mcj,mj->mc", weights, rotated, preferred_element_type=jnp.float32)
    input_grad = (jnp.concatenate([real_x, imag_x], 1) * input_scale).astype(jnp.bfloat16)
    return (weight_grad, input_grad)


def general_body(features, cotangent, spectral_weight, channel_weight, channel_bias):
    channels, planes, lines, depth_len = features.shape
    devices = lax.axis_size("gx")
    all_planes = planes * devices
    owned_modes = spectral_weight.shape[0]
    wave_pairs = MY * MZ
    forward_scale = 1.0 / math.sqrt(all_planes * lines * depth_len)
    inverse_scale = 1.0 / math.sqrt(MX * wave_pairs)
    weight_scale = math.sqrt(MX * wave_pairs / (all_planes * lines * depth_len))
    depth_basis = depth_table(MZ, depth_len)
    across_y = analysis_pair(freq_index(MY, lines), lines)
    back_y = synthesis_pair(freq_index(MY, lines), lines)
    across_full = analysis_pair(freq_index(MX, all_planes), all_planes)
    back_full = synthesis_pair(freq_index(MX, all_planes), all_planes)
    depth_part = jnp.dot(features, depth_basis.T, preferred_element_type=jnp.float32).astype(
        jnp.bfloat16
    )
    plane_part = (
        jnp.einsum(
            "cxyaz,yabk->cxbkz",
            depth_part.reshape(channels, planes, lines, 2, MZ),
            across_y,
            preferred_element_type=jnp.float32,
        )
        .astype(jnp.bfloat16)
        .reshape(channels, planes, 2, wave_pairs)
    )
    all_rows = lax.all_to_all(plane_part, "gx", split_axis=3, concat_axis=1, tiled=True)
    mode_sums = jnp.einsum(
        "cxaq,xabk->qkbc", all_rows, across_full, preferred_element_type=jnp.float32
    ).reshape(owned_modes, 2 * channels)
    coeffs = (mode_sums * forward_scale).astype(jnp.bfloat16)
    spectral = mode_product(coeffs, spectral_weight, channels)
    planes_all = jnp.einsum(
        "qkao,kabx->oxbq",
        spectral.reshape(owned_modes // MX, MX, 2, channels),
        back_full,
        preferred_element_type=jnp.float32,
    ).astype(jnp.bfloat16)
    planes_back = lax.all_to_all(planes_all, "gx", split_axis=1, concat_axis=3, tiled=True)
    lines_back = (
        jnp.einsum(
            "oxakz,kaby->oxybz",
            planes_back.reshape(channels, planes, 2, MY, MZ),
            back_y,
            preferred_element_type=jnp.float32,
        )
        .astype(jnp.bfloat16)
        .reshape(channels, planes, lines, 2 * MZ)
    )
    spectral_term = (
        jnp.dot(lines_back, depth_basis, preferred_element_type=jnp.float32) * inverse_scale
    )
    pointwise = jnp.einsum(
        "oc,cxyz->oxyz", channel_weight, features, preferred_element_type=jnp.float32
    )
    hidden = spectral_term + pointwise + channel_bias[:, None, None, None]
    activated, derivative = gelu_parts(hidden)
    upstream = (cotangent.astype(jnp.float32) * derivative).astype(jnp.bfloat16)
    lines_grad = (
        jnp.dot(upstream, depth_basis.T, preferred_element_type=jnp.float32) * inverse_scale
    ).astype(jnp.bfloat16)
    rows_grad = (
        jnp.einsum(
            "oxybz,kaby->oxakz",
            lines_grad.reshape(channels, planes, lines, 2, MZ),
            back_y,
            preferred_element_type=jnp.float32,
        )
        .astype(jnp.bfloat16)
        .reshape(channels, planes, 2, wave_pairs)
    )
    all_grads = lax.all_to_all(rows_grad, "gx", split_axis=3, concat_axis=1, tiled=True)
    grad_sums = jnp.einsum(
        "oxbq,kabx->qkao", all_grads, back_full, preferred_element_type=jnp.float32
    ).reshape(owned_modes, 2 * channels)
    grad_modes = grad_sums.astype(jnp.bfloat16)
    spectral_grad, coeff_grad = mode_grads(
        coeffs, spectral_weight, grad_modes, channels, weight_scale, forward_scale
    )
    plane_all = jnp.einsum(
        "qkbc,xabk->cxaq",
        coeff_grad.reshape(owned_modes // MX, MX, 2, channels),
        across_full,
        preferred_element_type=jnp.float32,
    ).astype(jnp.bfloat16)
    plane_grad = lax.all_to_all(plane_all, "gx", split_axis=1, concat_axis=3, tiled=True)
    depth_grad = (
        jnp.einsum(
            "cxbkz,yabk->cxyaz",
            plane_grad.reshape(channels, planes, 2, MY, MZ),
            across_y,
            preferred_element_type=jnp.float32,
        )
        .astype(jnp.bfloat16)
        .reshape(channels, planes, lines, 2 * MZ)
    )
    channel_back = jnp.einsum(
        "oc,oxyz->cxyz", channel_weight, upstream, preferred_element_type=jnp.float32
    )
    feature_grad = (
        jnp.dot(depth_grad, depth_basis, preferred_element_type=jnp.float32) + channel_back
    ).astype(jnp.bfloat16)
    return (activated.astype(jnp.bfloat16), feature_grad, spectral_grad)


PLANES = 2
GROUP = 8
STEP = 16
VMEM_MIB = 32
VECTOR = 1
HEAD = 3
FLIGHT = 6
NT = (((1,), (1,)), ((), ()))
F32 = jnp.float32
BF16 = jnp.bfloat16


def np_freq(retained, length):
    ladder = np.arange(retained)
    return np.where(ladder < retained // 2, ladder, length - retained + ladder)


def np_angles(wavenum, length):
    points = np.arange(length)
    return (wavenum[:, None] * points[None, :] % length) * (2.0 * math.pi / length)


def as_bf16(table):
    return np.asarray(table, np.float32).astype(ml_dtypes.bfloat16)


def rotation(angle, sign):
    cosine, sine_wave = np.cos(angle), sign * np.sin(angle)
    return np.stack([np.stack([cosine, -sine_wave]), np.stack([sine_wave, cosine])])


@functools.lru_cache(maxsize=None)
def tables(devices, lines, depth_len):
    planes_all = devices * PLANES
    angle = np_angles(np.arange(MZ), depth_len)
    depth = np.stack([np.cos(angle), -np.sin(angle)])
    eye = np.eye(GROUP)
    depth_block = np.einsum("akz,ij->akijz", depth, eye).reshape(2 * MZ * GROUP, GROUP * depth_len)
    depth_pair = np.einsum("akz,ij->iakjz", depth, np.eye(2)).reshape(4 * MZ, 2 * depth_len)
    plane_eye = np.eye(PLANES)
    angle = np_angles(np_freq(MY, lines), lines).reshape(devices, MY // devices, lines)
    across = np.einsum("badly,xw->ldbxawy", rotation(angle, -1.0), plane_eye)
    across = across.reshape(MY * 2 * PLANES, 2 * PLANES * lines)
    back = np.einsum("pbdly,xw->pxyldbw", rotation(angle, 1.0), plane_eye)
    back = back.reshape(2 * PLANES * lines, MY * 2 * PLANES)
    angle = np_angles(np_freq(MX, planes_all), planes_all).reshape(MX // 4, 4, devices, PLANES)
    forward = rotation(angle, -1.0)
    rows = np.einsum("batksx->tbksax", forward).reshape(MX // 4, 2, 4, devices * 2 * PLANES)
    plain = rows.reshape(2 * MX, -1)
    both = np.stack([rows, rows[:, ::-1]], 1).reshape(4 * MX, -1)
    turned = np.concatenate([rows[:, 1:], -rows[:, :1]], 1).reshape(2 * MX, -1)
    straight_rotated = np.concatenate([plain, turned], 0)
    inverse = np.einsum("batksx->sbxtak", rotation(angle, 1.0)).reshape(-1, 2 * MX)
    return {
        "depth": as_bf16(depth_block),
        "depth_pair": as_bf16(depth_pair),
        "across_y": as_bf16(across),
        "back_y": as_bf16(back),
        "plain_x": as_bf16(plain),
        "both_x": as_bf16(both),
        "straight_x": as_bf16(straight_rotated),
        "back_x": as_bf16(inverse),
    }


def dot_nn(left, right):
    return jnp.dot(left, right, preferred_element_type=F32)


def dot_nt(left, right):
    return lax.dot_general(left, right, NT, preferred_element_type=F32)


def lanes(shape):
    return lax.broadcasted_iota(jnp.int32, shape, len(shape) - 1)


def sublanes(shape):
    return lax.broadcasted_iota(jnp.int32, shape, len(shape) - 2)


def swap_halves(block):
    return pltpu.roll(block, 64, 1)


def part_copy(source, target, sems, index, size):
    start = index * size if isinstance(index, int) else pl.multiple_of(index * size, size)
    part = pl.ds(start, size)
    return pltpu.make_async_copy(source.at[part], target.at[part], sems.at[index])


def start_parts(source, target, sems, size, first, last):
    for index in range(first, min(last, source.shape[0] // size)):
        part_copy(source, target, sems, index, size).start()


def start_tables(pairs, sems):
    copies = []
    for index, (source, target) in enumerate(pairs):
        copy = pltpu.make_async_copy(source, target, sems.at[index])
        copy.start()
        copies.append(copy)
    return copies


def depth_quad(slabs, quad, depth_pair, scale, group, lines_ref):
    four = slabs[quad * 4 : quad * 4 + 4]
    wide = jnp.concatenate(
        [jnp.concatenate(four[2 * pair : 2 * pair + 2], axis=1) for pair in range(2)], axis=0
    )
    parts = dot_nt(depth_pair, wide)
    if scale is not None:
        parts = parts * scale
    half = wide.shape[0] // 2
    for pair in range(2):
        start = (group * GROUP + quad * 4 + pair * 2) * 2 * MZ
        if not isinstance(start, int):
            start = pl.multiple_of(start, 4 * MZ)
        lines_ref[pl.ds(start, 4 * MZ), :] = parts[:, pair * half : (pair + 1) * half]


def depth_analysis(slabs, depth_pair, scale, group, lines_ref):
    for quad in range(2):
        depth_quad(slabs, quad, depth_pair, scale, group, lines_ref)


def rows_analysis(lines_ref, across_ref, rows_ref, out_ref):
    channels = lines_ref.shape[0] // (2 * MZ)
    across = across_ref[...]
    half = across.shape[0] // 2
    for first in range(0, MZ // 2, 2):
        pair = jnp.concatenate(
            [
                jnp.concatenate(
                    [
                        lines_ref[pl.ds(a * MZ + kz, channels, stride=2 * MZ), :]
                        for a in range(2)
                    ],
                    axis=1,
                )
                for kz in range(2 * first, 2 * first + 4)
            ],
            axis=0,
        ).astype(BF16)
        rows = dot_nt(across, pair)
        for k in range(2):
            for kyl in range(2):
                rows_ref[pl.ds(kyl * 8 + first + k, half, stride=16), :] = rows[
                    kyl * half : (kyl + 1) * half, k * 128 : (k + 1) * 128
                ]
    out_ref[...] = rows_ref[...].astype(BF16)


def rows_gather(block_ref, rows_ref, spec_ref):
    rows_ref[...] = block_ref[...].astype(F32)
    count = rows_ref.shape[0] // 16
    eye = (sublanes((128, 128)) == lanes((128, 128))).astype(BF16)
    for first in range(0, MZ // 2, 2):
        both = jnp.concatenate(
            [
                rows_ref[pl.ds(kyl * 8 + first + k, count, stride=16), :]
                for k in range(2)
                for kyl in range(2)
            ],
            axis=0,
        ).astype(BF16)
        turned = dot_nt(eye, both)
        half = turned.shape[1] // 2
        for k in range(2):
            for h in range(2):
                at = (2 * (first + k) + h) * GROUP
                spec_ref[:, at : at + GROUP, :] = turned[
                    h * 64 : (h + 1) * 64, k * half : (k + 1) * half
                ].reshape(8, GROUP, half)


def lines_synthesis(step, spec_ref, back, scale):
    count = STEP // GROUP
    both = jnp.concatenate([spec_ref[step * count + g] for g in range(count)], axis=0)
    lines = dot_nt(back, both.astype(BF16))
    if scale is not None:
        lines = lines * scale
    lines = lines.astype(BF16)
    half = lines.shape[0] // 2
    return [
        jnp.concatenate(
            [lines[p * half : (p + 1) * half, g * 128 : (g + 1) * 128] for p in range(2)], axis=1
        )
        for g in range(count)
    ]


def flat(slab):
    return slab.reshape(slab.shape[0] * slab.shape[1], slab.shape[2])


def analysis_kernel(
    field_hbm,
    pair_hbm,
    across_hbm,
    out_ref,
    field_ref,
    pair_ref,
    across_ref,
    lines_ref,
    rows_ref,
    field_sems,
    table_sems,
):
    first, second = start_tables([(pair_hbm, pair_ref), (across_hbm, across_ref)], table_sems)
    start_parts(field_hbm, field_ref, field_sems, STEP, 0, field_ref.shape[0] // STEP)
    first.wait()

    for step in range(field_ref.shape[0] // STEP):
        part_copy(field_hbm, field_ref, field_sems, step, STEP).wait()
        for g in range(STEP // GROUP):
            group = step * (STEP // GROUP) + g
            slabs = [flat(field_ref[group * GROUP + ci]) for ci in range(GROUP)]
            depth_analysis(slabs, pair_ref[...], None, group, lines_ref)

    second.wait()
    rows_analysis(lines_ref, across_ref, rows_ref, out_ref)


def middle_kernel(
    inverse_scale,
    block_ref,
    bias_ref,
    point_hbm,
    cot_hbm,
    depth_hbm,
    pair_hbm,
    across_hbm,
    back_hbm,
    act_hbm,
    up_hbm,
    out_ref,
    point_ref,
    cot_ref,
    depth_ref,
    pair_ref,
    across_ref,
    back_ref,
    act_ref,
    up_ref,
    lines_ref,
    rows_ref,
    spec_ref,
    point_sems,
    cot_sems,
    act_sems,
    up_sems,
    table_sems,
):
    tables_in = start_tables(
        [
            (back_hbm, back_ref),
            (depth_hbm, depth_ref),
            (pair_hbm, pair_ref),
            (across_hbm, across_ref),
        ],
        table_sems,
    )
    start_parts(point_hbm, point_ref, point_sems, STEP, 0, 1)
    start_parts(cot_hbm, cot_ref, cot_sems, STEP, 0, 1)
    rows_gather(block_ref, rows_ref, spec_ref)
    start_parts(point_hbm, point_ref, point_sems, STEP, 1, 2)
    start_parts(cot_hbm, cot_ref, cot_sems, STEP, 1, 2)
    for copy in tables_in:
        copy.wait()
    steps = point_ref.shape[0] // STEP
    groups = point_ref.shape[0] // GROUP
    per_step = STEP // GROUP

    def activate(index, spectral):
        hidden = spectral + flat(point_ref[index]).astype(F32) + bias_ref[index]
        square = hidden * hidden
        gate = 0.5 + 0.5 * jnp.tanh(hidden * (SQRT_TWO_PI + (SQRT_TWO_PI * CUBIC_COEF) * square))
        slope = hidden * (2.0 * SQRT_TWO_PI + (6.0 * SQRT_TWO_PI * CUBIC_COEF) * square)
        derivative = gate + (gate - gate * gate) * slope
        upstream = (flat(cot_ref[index]).astype(F32) * derivative).astype(BF16)
        act_ref[index] = (hidden * gate).astype(BF16).reshape(act_ref.shape[1:])
        up_ref[index] = upstream.reshape(up_ref.shape[1:])
        return upstream

    def quarter(wide, at):
        return dot_nn(wide, depth_ref[:, at * 256 : (at + 1) * 256])

    wides = lines_synthesis(0, spec_ref, back_ref[...], inverse_scale)
    spectral = [quarter(wides[0], at) for at in range(4)]
    last = None
    for group in range(groups):
        step = group // per_step
        if group % per_step == 0:
            part_copy(point_hbm, point_ref, point_sems, step, STEP).wait()
            part_copy(cot_hbm, cot_ref, cot_sems, step, STEP).wait()
            start_parts(point_hbm, point_ref, point_sems, STEP, step + 2, step + 3)
            start_parts(cot_hbm, cot_ref, cot_sems, STEP, step + 2, step + 3)
            if step + 1 < steps:
                wides += lines_synthesis(step + 1, spec_ref, back_ref[...], inverse_scale)
        following, slabs = [], []
        for at in range(4):
            if group + 1 < groups:
                following.append(quarter(wides[group + 1], at))
            for k in range(2):
                oi = 2 * at + k
                slabs.append(
                    activate(group * GROUP + oi, spectral[at][:, k * 128 : (k + 1) * 128])
                )
            if last is not None and at % 2 == 0:
                depth_quad(last, at // 2, pair_ref[...], inverse_scale, group - 1, lines_ref)
        if group % per_step == per_step - 1:
            part_copy(act_ref, act_hbm, act_sems, step, STEP).start()
            part_copy(up_ref, up_hbm, up_sems, step, STEP).start()
        spectral, last = following, slabs
    depth_analysis(last, pair_ref[...], inverse_scale, groups - 1, lines_ref)
    rows_analysis(lines_ref, across_ref, rows_ref, out_ref)
    for step in range(steps):
        part_copy(act_ref, act_hbm, act_sems, step, STEP).wait()
        part_copy(up_ref, up_hbm, up_sems, step, STEP).wait()


def final_kernel(
    block_ref,
    point_hbm,
    depth_hbm,
    back_hbm,
    out_hbm,
    point_ref,
    depth_ref,
    back_ref,
    out_ref,
    rows_ref,
    spec_ref,
    point_sems,
    out_sems,
    table_sems,
):
    tables_in = start_tables([(back_hbm, back_ref), (depth_hbm, depth_ref)], table_sems)
    start_parts(point_hbm, point_ref, point_sems, STEP, 0, 1)
    rows_gather(block_ref, rows_ref, spec_ref)
    start_parts(point_hbm, point_ref, point_sems, STEP, 1, 4)
    for copy in tables_in:
        copy.wait()
    steps = point_ref.shape[0] // STEP
    groups = point_ref.shape[0] // GROUP
    per_step = STEP // GROUP

    def quarter(wide, at):
        return dot_nn(wide, depth_ref[:, at * 256 : (at + 1) * 256])

    wides = lines_synthesis(0, spec_ref, back_ref[...], None)
    spectral = [quarter(wides[0], at) for at in range(4)]
    for group in range(groups):
        step = group // per_step
        if group % per_step == 0:
            part_copy(point_hbm, point_ref, point_sems, step, STEP).wait()
            if step + 1 < steps:
                wides += lines_synthesis(step + 1, spec_ref, back_ref[...], None)
        following = []
        for at in range(4):
            if group + 1 < groups:
                following.append(quarter(wides[group + 1], at))
            for k in range(2):
                index = group * GROUP + 2 * at + k
                total = spectral[at][:, k * 128 : (k + 1) * 128] + flat(point_ref[index]).astype(F32)
                out_ref[index] = total.astype(BF16).reshape(out_ref.shape[1:])
        if group % per_step == per_step - 1:
            part_copy(out_ref, out_hbm, out_sems, step, STEP).start()
        spectral = following

    for step in range(steps):
        part_copy(out_ref, out_hbm, out_sems, step, STEP).wait()


def point_kernel(
    transposed,
    weight_ref,
    field_hbm,
    modes_hbm,
    out_hbm,
    head_ref,
    field_ref,
    out_ref,
    wide_ref,
    in_sems,
    out_sems,
    head_sems,
):
    size = wide_ref.shape[0]
    planes = field_ref.shape[1]
    copies = []
    for plane in range(planes):
        part = (slice(None), pl.ds(plane, 1))
        copy = pltpu.make_async_copy(field_hbm.at[part], field_ref.at[part], in_sems.at[plane])
        copy.start()
        copies.append(copy)
    heads = weight_copies(modes_hbm, head_ref, head_sems, 0)
    for copy in heads:
        copy.start()
    tall = (sublanes((size, 64)) // 16 == lanes((size, 64))).astype(BF16)
    weight = weight_ref[...]
    left = dot_nt(tall, weight) if transposed else dot_nn(tall, weight)
    left = left.astype(BF16)
    rows = size // 4
    same = sublanes((rows, size)) % 16 == lanes((rows, size)) % 16
    for quarter in range(4):
        spread = dot_nt(left[quarter * rows : (quarter + 1) * rows], tall)
        wide_ref[quarter * rows : (quarter + 1) * rows, :] = jnp.where(same, spread, 0.0).astype(
            BF16
        )
    sends = []
    for plane in range(planes):
        copies[plane].wait()
        for pair in range(2):
            right = jnp.concatenate(
                [
                    field_ref[:, plane, yc * 16 : (yc + 1) * 16, :].reshape(size, 128)
                    for yc in (2 * pair, 2 * pair + 1)
                ],
                axis=1,
            )
            result = dot_nn(wide_ref[...], right).astype(BF16)
            for k in range(2):
                yc = 2 * pair + k
                out_ref[:, plane, yc * 16 : (yc + 1) * 16, :] = result[
                    :, k * 128 : (k + 1) * 128
                ].reshape(size // 16, 16, 128)
        part = (slice(None), pl.ds(plane, 1))
        copy = pltpu.make_async_copy(out_ref.at[part], out_hbm.at[part], out_sems.at[plane])
        copy.start()
        sends.append(copy)
    for copy in sends + heads:
        copy.wait()


def weight_copies(weight_hbm, weight_ref, sems, first):
    rows = weight_hbm.shape[0] // 16
    copies = []
    for index in range(weight_ref.shape[0] // rows):
        copy = pltpu.make_async_copy(
            weight_hbm.at[pl.ds((first + index) * rows, rows)],
            weight_ref.at[pl.ds(index * rows, rows)],
            sems.at[index],
        )
        copies.append(copy)
    return copies


def next_weights(copies, j):
    if j < HEAD or (j - HEAD) % 2:
        return
    for index in range(j - HEAD, min(j - HEAD + 2, len(copies))):
        copies[index].wait()
        if index + FLIGHT < len(copies):
            copies[index + FLIGHT].start()


def mode_pair(head_ref, weight_ref, j, h, u):
    source = head_ref if j < HEAD else weight_ref
    start = (((j if j < HEAD else j - HEAD) * 2 + h) * MX + 8 * u) * 64
    return jnp.concatenate(
        [source[start : start + 256, :], source[start + 256 : start + 512, :]], axis=1
    )


def plane_sums(back_ref, mixed_ref, res_ref, quarter):
    count = res_ref.shape[0] // 16
    wide = jnp.concatenate([mixed_ref[quarter * 4 + k] for k in range(4)], axis=1)
    rows = dot_nn(back_ref[...], wide)
    for k in range(4):
        res_ref[pl.ds(quarter * 4 + k, count, stride=16), :] = rows[:, k * 128 : (k + 1) * 128]


def mode_kernel(
    scale,
    block_ref,
    head_ref,
    weight_hbm,
    both_ref,
    plain_ref,
    back_ref,
    coeff_hbm,
    out_ref,
    coeff_ref,
    weight_ref,
    rows_ref,
    res_ref,
    left_ref,
    mixed_ref,
    sems,
    coeff_sems,
):
    copies = weight_copies(weight_hbm, weight_ref, sems, HEAD)
    for copy in copies[:FLIGHT]:
        copy.start()
    count = rows_ref.shape[0] // 16
    rows_ref[...] = block_ref[...].astype(F32)
    low = lanes((128, 128)) < 64
    kxl = sublanes((128, 128)) % 4
    half = lanes((128, 128)) // 64
    first = (kxl == half).astype(BF16)
    second = (kxl == 2 + half).astype(BF16)
    low8 = lanes((8, 128)) < 64
    sign = jnp.where(sublanes((8, 128)) < 4, -1.0, 1.0)
    for quarter in range(4):
        wide = jnp.concatenate(
            [rows_ref[pl.ds(quarter * 4 + k, count, stride=16), :] for k in range(4)], axis=1
        ).astype(BF16)
        plain = (dot_nn(plain_ref[...], wide) * scale).astype(BF16)
        both = dot_nn(both_ref[...], wide) * scale
        for k in range(4):
            j = quarter * 4 + k
            coeff_ref[j] = plain[:, k * 128 : (k + 1) * 128]
            coeffs = both[:, k * 128 : (k + 1) * 128]
            swapped = swap_halves(coeffs)
            for h in range(2):
                twice = jnp.where(low if h == 0 else ~low, coeffs, swapped).astype(BF16)
                left_ref[j, h] = jnp.concatenate([twice * first, twice * second], axis=1)
    send = pltpu.make_async_copy(coeff_ref, coeff_hbm, coeff_sems.at[0])
    send.start()
    for j in range(16):
        next_weights(copies, j)
        mixed = []
        for u in range(MX // 8):
            halves = [
                dot_nn(left_ref[j, h, u * 32 : (u + 1) * 32, :], mode_pair(head_ref, weight_ref, j, h, u))
                for h in range(2)
            ]
            for t in range(2):
                low_h, high_h = [
                    part[t * 16 : (t + 1) * 16, t * 128 : (t + 1) * 128] for part in halves
                ]
                keep = jnp.where(low8, low_h[:8], sign * high_h[8:])
                move = jnp.where(low8, high_h[:8], sign * low_h[8:])
                mixed.append(keep + swap_halves(move))
        mixed_ref[j] = jnp.concatenate(mixed, axis=0).astype(BF16)
        if j > 4 and j % 4 == 1:
            plane_sums(back_ref, mixed_ref, res_ref, j // 4 - 1)
    plane_sums(back_ref, mixed_ref, res_ref, 3)
    out_ref[...] = res_ref[...].astype(BF16)
    send.wait()


def mode_grad_kernel(
    scale,
    block_ref,
    head_ref,
    weight_hbm,
    straight_ref,
    back_ref,
    coeff_hbm,
    pair_ref,
    coeff_ref,
    out_ref,
    weight_ref,
    rows_ref,
    res_ref,
    mixed_ref,
    sems,
    coeff_sems,
):
    send = pltpu.make_async_copy(coeff_hbm, coeff_ref, coeff_sems.at[0])
    send.start()
    copies = weight_copies(weight_hbm, weight_ref, sems, HEAD)
    for copy in copies[:FLIGHT]:
        copy.start()
    count = rows_ref.shape[0] // 16
    rows_ref[...] = block_ref[...].astype(F32)
    low = lanes((64, 128)) < 64
    low16 = lanes((16, 128)) < 64
    row = sublanes((16, 128)) % 4
    upper = row < 2
    valid = lanes((16, 128)) // 64 == row % 2
    even = (sublanes((16, 128)) < 8).astype(BF16)
    odd = (sublanes((16, 128)) >= 8).astype(BF16)
    for j in range(16):
        section = rows_ref[pl.ds(j, count, stride=16), :]
        swapped = swap_halves(section)
        twice = jnp.concatenate(
            [jnp.where(low, section, swapped), jnp.where(low, swapped, section)], axis=1
        ).astype(BF16)
        turned = dot_nn(straight_ref[...], twice)
        for h in range(2):
            part = turned[:, h * 128 : (h + 1) * 128]
            pair_ref[2 * j + h] = jnp.where(low, part[:64], part[64:]).astype(BF16)
    for j in range(16):
        next_weights(copies, j)
        mixed = []
        for u in range(MX // 8):
            found = []
            for h in range(2):
                pair = pair_ref[2 * j + h, u * 16 : (u + 1) * 16, :]
                rows = dot_nt(
                    jnp.concatenate([pair * even, pair * odd], axis=1),
                    mode_pair(head_ref, weight_ref, j, h, u),
                )
                found.append(jnp.where(valid, jnp.where(upper, rows[:, :128], rows[:, 128:]), 0.0))
            keep = jnp.where(low16, found[0], found[1])
            move = jnp.where(low16, found[1], found[0])
            mixed.append(keep + swap_halves(move))
        mixed_ref[j] = (jnp.concatenate(mixed, axis=0) * scale).astype(BF16)
        if j > 4 and j % 4 == 1:
            plane_sums(back_ref, mixed_ref, res_ref, j // 4 - 1)
    plane_sums(back_ref, mixed_ref, res_ref, 3)
    out_ref[...] = res_ref[...].astype(BF16)
    send.wait()


def weight_grad_kernel(
    scale, coeff_ref, pair_ref, out_hbm, out_ref, mask_ref, turned_ref, pairs_ref, sems
):
    lane = lanes((128, 64))
    part = sublanes((128, 64)) // 64
    for t in range(MX // 4 - VECTOR):
        mask_ref[t] = ((lane // 8 == t) & (lane % 4 // 2 == part)).astype(BF16)
    eye = (sublanes((128, 128)) == lanes((128, 128))).astype(BF16)
    for j in range(16):
        turned_ref[j] = (dot_nt(eye, coeff_ref[j]) * scale).astype(BF16)
        for h in range(2):
            pairs_ref[2 * j + h] = pair_ref[2 * j + h].astype(F32)
    even = (sublanes((64, 128)) % 2 == 0).astype(BF16)
    odd = (sublanes((64, 128)) % 2 == 1).astype(BF16)

    def one_pair(j):
        for h in range(2):
            one = turned_ref[j, h * 64 : (h + 1) * 64, :]
            left = jnp.concatenate([one, one], axis=0)
            pair = pair_ref[j * 2 + h]
            right = jnp.concatenate([pair * even, pair * odd], axis=1)
            for t in range(MX // 4):
                mode = (j * 2 + h) * MX + 4 * t
                if t < MX // 4 - VECTOR:
                    four = dot_nn(left * mask_ref[t], right)
                    for k in range(4):
                        out_ref[mode + k] = four[
                            k // 2 * 64 : (k // 2 + 1) * 64, k % 2 * 128 : (k % 2 + 1) * 128
                        ].astype(BF16)
                    continue
                for k in range(4):
                    total = None
                    for b in range(2):
                        at = t * 8 + b * 4 + k
                        column = jnp.broadcast_to(one[:, at : at + 1], (64, 128))
                        row = jnp.broadcast_to(
                            pairs_ref[j * 2 + h, at : at + 1, :], (64, 128)
                        ).astype(BF16)
                        total = column * row if total is None else total + column * row
                    out_ref[mode + k] = total
        part_copy(out_ref, out_hbm, sems, j, 2 * MX).start()

    @pl.loop(0, 4)
    def _(trip):
        for k in range(4):
            one_pair(trip * 4 + k)

    for j in range(16):
        part_copy(out_ref, out_hbm, sems, j, 2 * MX).wait()


def params(mib):
    return pltpu.CompilerParams(vmem_limit_bytes=mib * 1024 * 1024)


def cost(flops, moved):
    return pl.CostEstimate(flops=int(flops), bytes_accessed=int(moved), transcendentals=0)


def fast_body(features, cotangent, spectral_weight, channel_weight, channel_bias):
    channels, planes, lines, depth_len = features.shape
    devices = lax.axis_size("gx")
    owned_modes = spectral_weight.shape[0]
    wave_pairs = MY * MZ
    volume = planes * devices * lines * depth_len
    forward_scale = 1.0 / math.sqrt(volume)
    inverse_scale = 1.0 / math.sqrt(MX * wave_pairs)
    weight_scale = math.sqrt(MX * wave_pairs / volume)
    table = {name: jnp.asarray(value) for name, value in tables(devices, lines, depth_len).items()}
    for name in ("depth", "depth_pair", "across_y", "back_y"):
        table[name] = pltpu.with_memory_space_constraint(table[name], pltpu.HBM)
    block_rows = devices * 64
    block_shape = jax.ShapeDtypeStruct((block_rows, 128), BF16)
    vmem = pl.BlockSpec(memory_space=pltpu.VMEM)
    hbm = pl.BlockSpec(memory_space=pltpu.HBM)
    smem = pl.BlockSpec(memory_space=pltpu.SMEM)
    field_scratch = pltpu.VMEM(features.shape, BF16)
    field_shape = jax.ShapeDtypeStruct(features.shape, BF16)

    def sems(count):
        return pltpu.SemaphoreType.DMA((count,))

    def scratch(name):
        return pltpu.VMEM(table[name].shape, BF16)

    def in_hbm(array):
        return pltpu.with_memory_space_constraint(array, pltpu.HBM)

    def in_vmem(array):
        return pltpu.with_memory_space_constraint(array, pltpu.VMEM)

    steps = channels // STEP
    lines_scratch = pltpu.VMEM((channels * 2 * MZ, planes * lines), F32)
    rows_scratch = pltpu.VMEM((block_rows, 128), F32)
    spec_scratch = pltpu.VMEM((channels // GROUP, MZ * GROUP, 128), F32)
    weight_rows = pltpu.with_memory_space_constraint(
        spectral_weight.reshape(owned_modes * channels, 2 * channels), pltpu.HBM
    )
    field_bytes = features.size * 2

    def exchange(block):
        return lax.all_to_all(
            block.reshape(devices, 64, 128), "gx", 0, 0, tiled=True
        ).reshape(block_rows, 128)

    def point(field, transposed):
        return pl.pallas_call(
            functools.partial(point_kernel, transposed),
            out_shape=[
                pltpu.HBM(features.shape, BF16),
                pltpu.VMEM((weight_rows.shape[0] * HEAD // 16, weight_rows.shape[1]), BF16),
            ],
            in_specs=[vmem, hbm, hbm],
            out_specs=[hbm, vmem],
            scratch_shapes=[
                field_scratch,
                field_scratch,
                pltpu.VMEM((channels * 16, channels * 16), BF16),
                sems(planes),
                sems(planes),
                sems(HEAD),
            ],
            compiler_params=params(VMEM_MIB),
            cost_estimate=cost(2 * 1024**3, 2 * field_bytes),
            name="channel_map_back" if transposed else "channel_map",
        )(channel_weight, in_hbm(field), weight_rows)

    block = pl.pallas_call(
        analysis_kernel,
        out_shape=block_shape,
        in_specs=[hbm, hbm, hbm],
        out_specs=vmem,
        scratch_shapes=[
            field_scratch,
            scratch("depth_pair"),
            scratch("across_y"),
            lines_scratch,
            rows_scratch,
            sems(steps),
            sems(2),
        ],
        compiler_params=params(VMEM_MIB),
        cost_estimate=cost(2 * 256 * 1024 * 1024, field_bytes),
        name="field_analysis",
    )(in_hbm(features), table["depth_pair"], table["across_y"])
    pointwise, head = point(features, False)
    block, pointwise, head = lax.optimization_barrier((exchange(block), pointwise, head))

    weight_scratch = pltpu.VMEM(
        (weight_rows.shape[0] * (16 - HEAD) // 16, weight_rows.shape[1]), BF16
    )
    mixed_scratch = pltpu.VMEM((16, 64, 128), BF16)
    weight_sems = sems(16 - HEAD)
    coeffs, block = pl.pallas_call(
        functools.partial(mode_kernel, forward_scale),
        out_shape=[pltpu.HBM((16, 64, 128), BF16), block_shape],
        in_specs=[vmem, vmem, hbm, vmem, vmem, vmem],
        out_specs=[hbm, vmem],
        scratch_shapes=[
            pltpu.VMEM((16, 64, 128), BF16),
            weight_scratch,
            rows_scratch,
            rows_scratch,
            pltpu.VMEM((16, 2, 128, 256), BF16),
            mixed_scratch,
            weight_sems,
            sems(1),
        ],
        compiler_params=params(VMEM_MIB),
        cost_estimate=cost(256 * 2 * 16 * 256 * 128, 17 * 2**20),
        name="mode_product",
    )(block, in_vmem(head), weight_rows, table["both_x"], table["plain_x"], table["back_x"])
    block = exchange(block)

    activated, upstream, block = pl.pallas_call(
        functools.partial(middle_kernel, inverse_scale),
        out_shape=[field_shape, pltpu.HBM(features.shape, BF16), block_shape],
        in_specs=[vmem, smem, hbm, hbm, hbm, hbm, hbm, hbm],
        out_specs=[hbm, hbm, vmem],
        scratch_shapes=[
            field_scratch,
            field_scratch,
            scratch("depth"),
            scratch("depth_pair"),
            scratch("across_y"),
            scratch("back_y"),
            field_scratch,
            field_scratch,
            lines_scratch,
            rows_scratch,
            spec_scratch,
            sems(steps),
            sems(steps),
            sems(steps),
            sems(steps),
            sems(4),
        ],
        compiler_params=params(VMEM_MIB),
        cost_estimate=cost(2**30, 4 * field_bytes),
        name="gelu_and_gradient",
    )(
        block,
        channel_bias,
        in_hbm(pointwise),
        in_hbm(cotangent),
        table["depth"],
        table["depth_pair"],
        table["across_y"],
        table["back_y"],
    )
    channel_back, head = point(upstream, True)
    block, channel_back, head = lax.optimization_barrier((exchange(block), channel_back, head))

    pairs, coeffs, block = pl.pallas_call(
        functools.partial(mode_grad_kernel, forward_scale),
        out_shape=[
            pltpu.VMEM((32, 64, 128), BF16),
            pltpu.VMEM((16, 64, 128), BF16),
            block_shape,
        ],
        in_specs=[vmem, vmem, hbm, vmem, vmem, hbm],
        out_specs=[vmem, vmem, vmem],
        scratch_shapes=[
            weight_scratch,
            rows_scratch,
            rows_scratch,
            mixed_scratch,
            weight_sems,
            sems(1),
        ],
        compiler_params=params(VMEM_MIB),
        cost_estimate=cost(256 * 2 * 16 * 256 * 128, 17 * 2**20),
        name="mode_gradient",
    )(block, in_vmem(head), weight_rows, table["straight_x"], table["back_x"], in_hbm(coeffs))
    block = exchange(block)

    spectral_grad = pl.pallas_call(
        functools.partial(weight_grad_kernel, weight_scale),
        out_shape=jax.ShapeDtypeStruct(spectral_weight.shape, BF16),
        in_specs=[vmem, vmem],
        out_specs=hbm,
        scratch_shapes=[
            pltpu.VMEM(spectral_weight.shape, BF16),
            pltpu.VMEM((MX // 4, 128, 64), BF16),
            pltpu.VMEM((16, 128, 64), BF16),
            pltpu.VMEM((32, 64, 128), F32),
            sems(16),
        ],
        compiler_params=params(VMEM_MIB),
        cost_estimate=cost(512 * 2 * 64 * 64 * 256, 17 * 2**20),
        name="weight_gradient",
    )(
        in_vmem(coeffs),
        in_vmem(pairs),
    )

    feature_grad = pl.pallas_call(
        final_kernel,
        out_shape=field_shape,
        in_specs=[vmem, hbm, hbm, hbm],
        out_specs=hbm,
        scratch_shapes=[
            field_scratch,
            scratch("depth"),
            scratch("back_y"),
            field_scratch,
            rows_scratch,
            spec_scratch,
            sems(steps),
            sems(steps),
            sems(2),
        ],
        compiler_params=params(VMEM_MIB),
        cost_estimate=cost(2**29, 2 * field_bytes),
        name="field_gradient",
    )(block, in_hbm(channel_back), table["depth"], table["back_y"])
    return (activated, feature_grad, spectral_grad)


def body(features, cotangent, spectral_weight, channel_weight, channel_bias):
    channels, planes, lines, depth_len = features.shape
    devices = lax.axis_size("gx")
    fits = (
        (channels, planes, lines, depth_len) == (64, PLANES, 64, 128)
        and spectral_weight.shape[0] == 2 * MZ * MX
        and devices * 2 == MY
        and devices * 2 == MX
    )
    run = fast_body if fits else general_body
    return run(features, cotangent, spectral_weight, channel_weight, channel_bias)


def solution(mesh):
    in_specs = (
        P("grp", "gx", None, None),
        P("grp", "gx", None, None),
        P("gx", None, None),
        P(),
        P(),
    )
    out_specs = (
        P("grp", "gx", None, None),
        P("grp", "gx", None, None),
        P(("grp", "gx"), None, None),
    )
    return jax.shard_map(body, mesh=mesh, in_specs=in_specs, out_specs=out_specs, check_vma=False)
```

```python
import functools
import math

import jax
import jax.numpy as jnp
import ml_dtypes
import numpy as np
from jax import lax
from jax.experimental import pallas as pl
from jax.experimental.pallas import tpu as pltpu
from jax.sharding import PartitionSpec as P

MX = 32
MY = 32
MZ = 16


SQRT_TWO_PI = math.sqrt(2.0 / math.pi)
CUBIC_COEF = 0.044715


def freq_index(retained, length):
    ladder = jnp.arange(retained, dtype=jnp.int32)
    return jnp.where(ladder < retained // 2, ladder, length - retained + ladder)


def cos_sin(wavenum, length):
    points = jnp.arange(length, dtype=jnp.int32)
    angles = (wavenum[:, None] * points[None, :] % length).astype(jnp.float32) * (
        2.0 * math.pi / length
    )
    return (jnp.cos(angles), jnp.sin(angles))


def analysis_pair(wavenum, length):
    cosine, sine_wave = cos_sin(wavenum, length)
    cosine, sine_wave = (cosine.T, sine_wave.T)
    return jnp.stack(
        [jnp.stack([cosine, -sine_wave], 1), jnp.stack([sine_wave, cosine], 1)], 1
    ).astype(jnp.bfloat16)


def synthesis_pair(wavenum, length):
    cosine, sine_wave = cos_sin(wavenum, length)
    return jnp.stack(
        [jnp.stack([cosine, sine_wave], 1), jnp.stack([-sine_wave, cosine], 1)], 1
    ).astype(jnp.bfloat16)


def depth_table(retained, length):
    cosine, sine_wave = cos_sin(jnp.arange(retained, dtype=jnp.int32), length)
    return jnp.concatenate([cosine, -sine_wave], 0).astype(jnp.bfloat16)


def gelu_parts(inputs):
    cubed_in = inputs * inputs * inputs
    tangent = jnp.tanh(SQRT_TWO_PI * (inputs + CUBIC_COEF * cubed_in))
    output = 0.5 * inputs * (1.0 + tangent)
    derivative = 0.5 * (1.0 + tangent) + 0.5 * inputs * (1.0 - tangent * tangent) * SQRT_TWO_PI * (
        1.0 + 3.0 * CUBIC_COEF * inputs * inputs
    )
    return (output, derivative)


def mode_product(coeffs, weights, channels):
    stacked = coeffs.reshape(coeffs.shape[0], 2, channels)
    halves = jnp.einsum("mac,mcj->amj", stacked, weights, preferred_element_type=jnp.float32)
    real_out = halves[0, :, :channels] - halves[1, :, channels:]
    imag_out = halves[0, :, channels:] + halves[1, :, :channels]
    return jnp.concatenate([real_out, imag_out], 1).astype(jnp.bfloat16)


def mode_grads(coeffs, weights, grad_modes, channels, weight_scale, input_scale):
    number = coeffs.shape[0]
    stacked = coeffs.reshape(number, 2, channels)
    grad_pairs = grad_modes.reshape(number, 2, channels)
    real_w = jnp.einsum("mac,mao->mco", stacked, grad_pairs, preferred_element_type=jnp.float32)
    imag_w = jnp.einsum(
        "mc,mo->mco", stacked[:, 0], grad_pairs[:, 1], preferred_element_type=jnp.float32
    ) - jnp.einsum(
        "mc,mo->mco", stacked[:, 1], grad_pairs[:, 0], preferred_element_type=jnp.float32
    )
    weight_grad = (jnp.concatenate([real_w, imag_w], 2) * weight_scale).astype(jnp.bfloat16)
    straight = jnp.concatenate([grad_pairs[:, 0], grad_pairs[:, 1]], 1)
    rotated = jnp.concatenate([grad_pairs[:, 1], -grad_pairs[:, 0]], 1)
    real_x = jnp.einsum("mcj,mj->mc", weights, straight, preferred_element_type=jnp.float32)
    imag_x = jnp.einsum("mcj,mj->mc", weights, rotated, preferred_element_type=jnp.float32)
    input_grad = (jnp.concatenate([real_x, imag_x], 1) * input_scale).astype(jnp.bfloat16)
    return (weight_grad, input_grad)


def general_body(features, cotangent, spectral_weight, channel_weight, channel_bias):
    channels, planes, lines, depth_len = features.shape
    devices = lax.axis_size("gx")
    all_planes = planes * devices
    owned_modes = spectral_weight.shape[0]
    wave_pairs = MY * MZ
    forward_scale = 1.0 / math.sqrt(all_planes * lines * depth_len)
    inverse_scale = 1.0 / math.sqrt(MX * wave_pairs)
    weight_scale = math.sqrt(MX * wave_pairs / (all_planes * lines * depth_len))
    depth_basis = depth_table(MZ, depth_len)
    across_y = analysis_pair(freq_index(MY, lines), lines)
    back_y = synthesis_pair(freq_index(MY, lines), lines)
    across_full = analysis_pair(freq_index(MX, all_planes), all_planes)
    back_full = synthesis_pair(freq_index(MX, all_planes), all_planes)
    depth_part = jnp.dot(features, depth_basis.T, preferred_element_type=jnp.float32).astype(
        jnp.bfloat16
    )
    plane_part = (
        jnp.einsum(
            "cxyaz,yabk->cxbkz",
            depth_part.reshape(channels, planes, lines, 2, MZ),
            across_y,
            preferred_element_type=jnp.float32,
        )
        .astype(jnp.bfloat16)
        .reshape(channels, planes, 2, wave_pairs)
    )
    all_rows = lax.all_to_all(plane_part, "gx", split_axis=3, concat_axis=1, tiled=True)
    mode_sums = jnp.einsum(
        "cxaq,xabk->qkbc", all_rows, across_full, preferred_element_type=jnp.float32
    ).reshape(owned_modes, 2 * channels)
    coeffs = (mode_sums * forward_scale).astype(jnp.bfloat16)
    spectral = mode_product(coeffs, spectral_weight, channels)
    planes_all = jnp.einsum(
        "qkao,kabx->oxbq",
        spectral.reshape(owned_modes // MX, MX, 2, channels),
        back_full,
        preferred_element_type=jnp.float32,
    ).astype(jnp.bfloat16)
    planes_back = lax.all_to_all(planes_all, "gx", split_axis=1, concat_axis=3, tiled=True)
    lines_back = (
        jnp.einsum(
            "oxakz,kaby->oxybz",
            planes_back.reshape(channels, planes, 2, MY, MZ),
            back_y,
            preferred_element_type=jnp.float32,
        )
        .astype(jnp.bfloat16)
        .reshape(channels, planes, lines, 2 * MZ)
    )
    spectral_term = (
        jnp.dot(lines_back, depth_basis, preferred_element_type=jnp.float32) * inverse_scale
    )
    pointwise = jnp.einsum(
        "oc,cxyz->oxyz", channel_weight, features, preferred_element_type=jnp.float32
    )
    hidden = spectral_term + pointwise + channel_bias[:, None, None, None]
    activated, derivative = gelu_parts(hidden)
    upstream = (cotangent.astype(jnp.float32) * derivative).astype(jnp.bfloat16)
    lines_grad = (
        jnp.dot(upstream, depth_basis.T, preferred_element_type=jnp.float32) * inverse_scale
    ).astype(jnp.bfloat16)
    rows_grad = (
        jnp.einsum(
            "oxybz,kaby->oxakz",
            lines_grad.reshape(channels, planes, lines, 2, MZ),
            back_y,
            preferred_element_type=jnp.float32,
        )
        .astype(jnp.bfloat16)
        .reshape(channels, planes, 2, wave_pairs)
    )
    all_grads = lax.all_to_all(rows_grad, "gx", split_axis=3, concat_axis=1, tiled=True)
    grad_sums = jnp.einsum(
        "oxbq,kabx->qkao", all_grads, back_full, preferred_element_type=jnp.float32
    ).reshape(owned_modes, 2 * channels)
    grad_modes = grad_sums.astype(jnp.bfloat16)
    spectral_grad, coeff_grad = mode_grads(
        coeffs, spectral_weight, grad_modes, channels, weight_scale, forward_scale
    )
    plane_all = jnp.einsum(
        "qkbc,xabk->cxaq",
        coeff_grad.reshape(owned_modes // MX, MX, 2, channels),
        across_full,
        preferred_element_type=jnp.float32,
    ).astype(jnp.bfloat16)
    plane_grad = lax.all_to_all(plane_all, "gx", split_axis=1, concat_axis=3, tiled=True)
    depth_grad = (
        jnp.einsum(
            "cxbkz,yabk->cxyaz",
            plane_grad.reshape(channels, planes, 2, MY, MZ),
            across_y,
            preferred_element_type=jnp.float32,
        )
        .astype(jnp.bfloat16)
        .reshape(channels, planes, lines, 2 * MZ)
    )
    channel_back = jnp.einsum(
        "oc,oxyz->cxyz", channel_weight, upstream, preferred_element_type=jnp.float32
    )
    feature_grad = (
        jnp.dot(depth_grad, depth_basis, preferred_element_type=jnp.float32) + channel_back
    ).astype(jnp.bfloat16)
    return (activated.astype(jnp.bfloat16), feature_grad, spectral_grad)


PLANES = 2
GROUP = 8
STEP = 16
VMEM_MIB = 32
VECTOR = 1
HEAD = 2
FLIGHT = 6
NT = (((1,), (1,)), ((), ()))
F32 = jnp.float32
BF16 = jnp.bfloat16


def np_freq(retained, length):
    ladder = np.arange(retained)
    return np.where(ladder < retained // 2, ladder, length - retained + ladder)


def np_angles(wavenum, length):
    points = np.arange(length)
    return (wavenum[:, None] * points[None, :] % length) * (2.0 * math.pi / length)


def as_bf16(table):
    return np.asarray(table, np.float32).astype(ml_dtypes.bfloat16)


def rotation(angle, sign):
    cosine, sine_wave = np.cos(angle), sign * np.sin(angle)
    return np.stack([np.stack([cosine, -sine_wave]), np.stack([sine_wave, cosine])])


@functools.lru_cache(maxsize=None)
def tables(devices, lines, depth_len):
    planes_all = devices * PLANES
    angle = np_angles(np.arange(MZ), depth_len)
    depth = np.stack([np.cos(angle), -np.sin(angle)])
    eye = np.eye(GROUP)
    depth_block = np.einsum("akz,ij->akijz", depth, eye).reshape(2 * MZ * GROUP, GROUP * depth_len)
    depth_pair = np.einsum("akz,ij->iakjz", depth, np.eye(2)).reshape(4 * MZ, 2 * depth_len)
    plane_eye = np.eye(PLANES)
    angle = np_angles(np_freq(MY, lines), lines).reshape(devices, MY // devices, lines)
    across = np.einsum("badly,xw->ldbxawy", rotation(angle, -1.0), plane_eye)
    across = across.reshape(MY * 2 * PLANES, 2 * PLANES * lines)
    back = np.einsum("pbdly,xw->pxyldbw", rotation(angle, 1.0), plane_eye)
    back = back.reshape(2 * PLANES * lines, MY * 2 * PLANES)
    angle = np_angles(np_freq(MX, planes_all), planes_all).reshape(MX // 4, 4, devices, PLANES)
    forward = rotation(angle, -1.0)
    rows = np.einsum("batksx->tbksax", forward).reshape(MX // 4, 2, 4, devices * 2 * PLANES)
    plain = rows.reshape(2 * MX, -1)
    both = np.stack([rows, rows[:, ::-1]], 1).reshape(4 * MX, -1)
    turned = np.concatenate([rows[:, 1:], -rows[:, :1]], 1).reshape(2 * MX, -1)
    straight_rotated = np.concatenate([plain, turned], 0)
    inverse = np.einsum("batksx->sbxtak", rotation(angle, 1.0)).reshape(-1, 2 * MX)
    return {
        "depth": as_bf16(depth_block),
        "depth_pair": as_bf16(depth_pair),
        "across_y": as_bf16(across),
        "back_y": as_bf16(back),
        "plain_x": as_bf16(plain),
        "both_x": as_bf16(both),
        "straight_x": as_bf16(straight_rotated),
        "back_x": as_bf16(inverse),
    }


def dot_nn(left, right):
    return jnp.dot(left, right, preferred_element_type=F32)


def dot_nt(left, right):
    return lax.dot_general(left, right, NT, preferred_element_type=F32)


def lanes(shape):
    return lax.broadcasted_iota(jnp.int32, shape, len(shape) - 1)


def sublanes(shape):
    return lax.broadcasted_iota(jnp.int32, shape, len(shape) - 2)


def swap_halves(block):
    return pltpu.roll(block, 64, 1)


def part_copy(source, target, sems, index, size):
    start = index * size if isinstance(index, int) else pl.multiple_of(index * size, size)
    part = pl.ds(start, size)
    return pltpu.make_async_copy(source.at[part], target.at[part], sems.at[index])


def start_parts(source, target, sems, size, first, last):
    for index in range(first, min(last, source.shape[0] // size)):
        part_copy(source, target, sems, index, size).start()


def start_tables(pairs, sems):
    copies = []
    for index, (source, target) in enumerate(pairs):
        copy = pltpu.make_async_copy(source, target, sems.at[index])
        copy.start()
        copies.append(copy)
    return copies


def depth_quad(slabs, quad, depth_pair, scale, group, lines_ref):
    four = slabs[quad * 4 : quad * 4 + 4]
    wide = jnp.concatenate(
        [jnp.concatenate(four[2 * pair : 2 * pair + 2], axis=1) for pair in range(2)], axis=0
    )
    parts = dot_nt(depth_pair, wide)
    if scale is not None:
        parts = parts * scale
    half = wide.shape[0] // 2
    for pair in range(2):
        start = (group * GROUP + quad * 4 + pair * 2) * 2 * MZ
        if not isinstance(start, int):
            start = pl.multiple_of(start, 4 * MZ)
        lines_ref[pl.ds(start, 4 * MZ), :] = parts[:, pair * half : (pair + 1) * half]


def depth_analysis(slabs, depth_pair, scale, group, lines_ref):
    for quad in range(2):
        depth_quad(slabs, quad, depth_pair, scale, group, lines_ref)


def rows_analysis(lines_ref, across_ref, rows_ref, out_ref):
    channels = lines_ref.shape[0] // (2 * MZ)
    across = across_ref[...]
    half = across.shape[0] // 2
    for first in range(0, MZ // 2, 2):
        pair = jnp.concatenate(
            [
                jnp.concatenate(
                    [
                        lines_ref[pl.ds(a * MZ + kz, channels, stride=2 * MZ), :]
                        for a in range(2)
                    ],
                    axis=1,
                )
                for kz in range(2 * first, 2 * first + 4)
            ],
            axis=0,
        ).astype(BF16)
        rows = dot_nt(across, pair)
        for k in range(2):
            for kyl in range(2):
                rows_ref[pl.ds(kyl * 8 + first + k, half, stride=16), :] = rows[
                    kyl * half : (kyl + 1) * half, k * 128 : (k + 1) * 128
                ]
    out_ref[...] = rows_ref[...].astype(BF16)


def rows_gather(block_ref, rows_ref, spec_ref):
    rows_ref[...] = block_ref[...].astype(F32)
    count = rows_ref.shape[0] // 16
    eye = (sublanes((128, 128)) == lanes((128, 128))).astype(BF16)
    for first in range(0, MZ // 2, 2):
        both = jnp.concatenate(
            [
                rows_ref[pl.ds(kyl * 8 + first + k, count, stride=16), :]
                for k in range(2)
                for kyl in range(2)
            ],
            axis=0,
        ).astype(BF16)
        turned = dot_nt(eye, both)
        half = turned.shape[1] // 2
        for k in range(2):
            for h in range(2):
                at = (2 * (first + k) + h) * GROUP
                spec_ref[:, at : at + GROUP, :] = turned[
                    h * 64 : (h + 1) * 64, k * half : (k + 1) * half
                ].reshape(8, GROUP, half)


def lines_synthesis(step, spec_ref, back, scale):
    count = STEP // GROUP
    both = jnp.concatenate([spec_ref[step * count + g] for g in range(count)], axis=0)
    lines = dot_nt(back, both.astype(BF16))
    if scale is not None:
        lines = lines * scale
    lines = lines.astype(BF16)
    half = lines.shape[0] // 2
    return [
        jnp.concatenate(
            [lines[p * half : (p + 1) * half, g * 128 : (g + 1) * 128] for p in range(2)], axis=1
        )
        for g in range(count)
    ]


def flat(slab):
    return slab.reshape(slab.shape[0] * slab.shape[1], slab.shape[2])


def analysis_kernel(
    field_hbm,
    pair_hbm,
    across_hbm,
    out_ref,
    field_ref,
    pair_ref,
    across_ref,
    lines_ref,
    rows_ref,
    field_sems,
    table_sems,
):
    first, second = start_tables([(pair_hbm, pair_ref), (across_hbm, across_ref)], table_sems)
    start_parts(field_hbm, field_ref, field_sems, STEP, 0, field_ref.shape[0] // STEP)
    first.wait()

    for step in range(field_ref.shape[0] // STEP):
        part_copy(field_hbm, field_ref, field_sems, step, STEP).wait()
        for g in range(STEP // GROUP):
            group = step * (STEP // GROUP) + g
            slabs = [flat(field_ref[group * GROUP + ci]) for ci in range(GROUP)]
            depth_analysis(slabs, pair_ref[...], None, group, lines_ref)

    second.wait()
    rows_analysis(lines_ref, across_ref, rows_ref, out_ref)


def middle_kernel(
    inverse_scale,
    block_ref,
    bias_ref,
    point_hbm,
    cot_hbm,
    depth_hbm,
    pair_hbm,
    across_hbm,
    back_hbm,
    act_hbm,
    up_hbm,
    out_ref,
    point_ref,
    cot_ref,
    depth_ref,
    pair_ref,
    across_ref,
    back_ref,
    act_ref,
    up_ref,
    lines_ref,
    rows_ref,
    spec_ref,
    point_sems,
    cot_sems,
    act_sems,
    up_sems,
    table_sems,
):
    tables_in = start_tables(
        [
            (back_hbm, back_ref),
            (depth_hbm, depth_ref),
            (pair_hbm, pair_ref),
            (across_hbm, across_ref),
        ],
        table_sems,
    )
    start_parts(point_hbm, point_ref, point_sems, STEP, 0, 1)
    start_parts(cot_hbm, cot_ref, cot_sems, STEP, 0, 1)
    rows_gather(block_ref, rows_ref, spec_ref)
    start_parts(point_hbm, point_ref, point_sems, STEP, 1, 2)
    start_parts(cot_hbm, cot_ref, cot_sems, STEP, 1, 2)
    for copy in tables_in:
        copy.wait()
    steps = point_ref.shape[0] // STEP
    groups = point_ref.shape[0] // GROUP
    per_step = STEP // GROUP

    def activate(index, spectral):
        hidden = spectral + flat(point_ref[index]).astype(F32) + bias_ref[index]
        square = hidden * hidden
        gate = 0.5 + 0.5 * jnp.tanh(hidden * (SQRT_TWO_PI + (SQRT_TWO_PI * CUBIC_COEF) * square))
        slope = hidden * (2.0 * SQRT_TWO_PI + (6.0 * SQRT_TWO_PI * CUBIC_COEF) * square)
        derivative = gate + (gate - gate * gate) * slope
        upstream = (flat(cot_ref[index]).astype(F32) * derivative).astype(BF16)
        act_ref[index] = (hidden * gate).astype(BF16).reshape(act_ref.shape[1:])
        up_ref[index] = upstream.reshape(up_ref.shape[1:])
        return upstream

    def quarter(wide, at):
        return dot_nn(wide, depth_ref[:, at * 256 : (at + 1) * 256])

    wides = lines_synthesis(0, spec_ref, back_ref[...], inverse_scale)
    spectral = [quarter(wides[0], at) for at in range(4)]
    last = None
    for group in range(groups):
        step = group // per_step
        if group % per_step == 0:
            part_copy(point_hbm, point_ref, point_sems, step, STEP).wait()
            part_copy(cot_hbm, cot_ref, cot_sems, step, STEP).wait()
            start_parts(point_hbm, point_ref, point_sems, STEP, step + 2, step + 3)
            start_parts(cot_hbm, cot_ref, cot_sems, STEP, step + 2, step + 3)
            if step + 1 < steps:
                wides += lines_synthesis(step + 1, spec_ref, back_ref[...], inverse_scale)
        following, slabs = [], []
        for at in range(4):
            if group + 1 < groups:
                following.append(quarter(wides[group + 1], at))
            for k in range(2):
                oi = 2 * at + k
                slabs.append(
                    activate(group * GROUP + oi, spectral[at][:, k * 128 : (k + 1) * 128])
                )
            if last is not None and at % 2 == 0:
                depth_quad(last, at // 2, pair_ref[...], inverse_scale, group - 1, lines_ref)
        if group % per_step == per_step - 1:
            part_copy(act_ref, act_hbm, act_sems, step, STEP).start()
            part_copy(up_ref, up_hbm, up_sems, step, STEP).start()
        spectral, last = following, slabs
    depth_analysis(last, pair_ref[...], inverse_scale, groups - 1, lines_ref)
    rows_analysis(lines_ref, across_ref, rows_ref, out_ref)
    for step in range(steps):
        part_copy(act_ref, act_hbm, act_sems, step, STEP).wait()
        part_copy(up_ref, up_hbm, up_sems, step, STEP).wait()


def final_kernel(
    block_ref,
    point_hbm,
    depth_hbm,
    back_hbm,
    out_hbm,
    point_ref,
    depth_ref,
    back_ref,
    out_ref,
    rows_ref,
    spec_ref,
    point_sems,
    out_sems,
    table_sems,
):
    tables_in = start_tables([(back_hbm, back_ref), (depth_hbm, depth_ref)], table_sems)
    start_parts(point_hbm, point_ref, point_sems, STEP, 0, 1)
    rows_gather(block_ref, rows_ref, spec_ref)
    start_parts(point_hbm, point_ref, point_sems, STEP, 1, 4)
    for copy in tables_in:
        copy.wait()
    steps = point_ref.shape[0] // STEP
    groups = point_ref.shape[0] // GROUP
    per_step = STEP // GROUP

    def quarter(wide, at):
        return dot_nn(wide, depth_ref[:, at * 256 : (at + 1) * 256])

    wides = lines_synthesis(0, spec_ref, back_ref[...], None)
    spectral = [quarter(wides[0], at) for at in range(4)]
    for group in range(groups):
        step = group // per_step
        if group % per_step == 0:
            part_copy(point_hbm, point_ref, point_sems, step, STEP).wait()
            if step + 1 < steps:
                wides += lines_synthesis(step + 1, spec_ref, back_ref[...], None)
        following = []
        for at in range(4):
            if group + 1 < groups:
                following.append(quarter(wides[group + 1], at))
            for k in range(2):
                index = group * GROUP + 2 * at + k
                total = spectral[at][:, k * 128 : (k + 1) * 128] + flat(point_ref[index]).astype(F32)
                out_ref[index] = total.astype(BF16).reshape(out_ref.shape[1:])
        if group % per_step == per_step - 1:
            part_copy(out_ref, out_hbm, out_sems, step, STEP).start()
        spectral = following

    for step in range(steps):
        part_copy(out_ref, out_hbm, out_sems, step, STEP).wait()


def point_kernel(
    transposed,
    weight_ref,
    field_hbm,
    modes_hbm,
    out_hbm,
    head_ref,
    field_ref,
    out_ref,
    wide_ref,
    in_sems,
    out_sems,
    head_sems,
):
    size = wide_ref.shape[0]
    planes = field_ref.shape[1]
    copies = []
    for plane in range(planes):
        part = (slice(None), pl.ds(plane, 1))
        copy = pltpu.make_async_copy(field_hbm.at[part], field_ref.at[part], in_sems.at[plane])
        copy.start()
        copies.append(copy)
    heads = weight_copies(modes_hbm, head_ref, head_sems, 0)
    for copy in heads:
        copy.start()
    tall = (sublanes((size, 64)) // 16 == lanes((size, 64))).astype(BF16)
    weight = weight_ref[...]
    left = dot_nt(tall, weight) if transposed else dot_nn(tall, weight)
    left = left.astype(BF16)
    rows = size // 4
    same = sublanes((rows, size)) % 16 == lanes((rows, size)) % 16
    for quarter in range(4):
        spread = dot_nt(left[quarter * rows : (quarter + 1) * rows], tall)
        wide_ref[quarter * rows : (quarter + 1) * rows, :] = jnp.where(same, spread, 0.0).astype(
            BF16
        )
    sends = []
    for plane in range(planes):
        copies[plane].wait()
        for pair in range(2):
            right = jnp.concatenate(
                [
                    field_ref[:, plane, yc * 16 : (yc + 1) * 16, :].reshape(size, 128)
                    for yc in (2 * pair, 2 * pair + 1)
                ],
                axis=1,
            )
            result = dot_nn(wide_ref[...], right).astype(BF16)
            for k in range(2):
                yc = 2 * pair + k
                out_ref[:, plane, yc * 16 : (yc + 1) * 16, :] = result[
                    :, k * 128 : (k + 1) * 128
                ].reshape(size // 16, 16, 128)
        part = (slice(None), pl.ds(plane, 1))
        copy = pltpu.make_async_copy(out_ref.at[part], out_hbm.at[part], out_sems.at[plane])
        copy.start()
        sends.append(copy)
    for copy in sends + heads:
        copy.wait()


def weight_copies(weight_hbm, weight_ref, sems, first):
    rows = weight_hbm.shape[0] // 16
    copies = []
    for index in range(weight_ref.shape[0] // rows):
        copy = pltpu.make_async_copy(
            weight_hbm.at[pl.ds((first + index) * rows, rows)],
            weight_ref.at[pl.ds(index * rows, rows)],
            sems.at[index],
        )
        copies.append(copy)
    return copies


def next_weights(copies, j):
    if j < HEAD or (j - HEAD) % 2:
        return
    for index in range(j - HEAD, min(j - HEAD + 2, len(copies))):
        copies[index].wait()
        if index + FLIGHT < len(copies):
            copies[index + FLIGHT].start()


def mode_pair(head_ref, weight_ref, j, h, u):
    source = head_ref if j < HEAD else weight_ref
    start = (((j if j < HEAD else j - HEAD) * 2 + h) * MX + 8 * u) * 64
    return jnp.concatenate(
        [source[start : start + 256, :], source[start + 256 : start + 512, :]], axis=1
    )


def plane_sums(back_ref, mixed_ref, res_ref, quarter):
    count = res_ref.shape[0] // 16
    wide = jnp.concatenate([mixed_ref[quarter * 4 + k] for k in range(4)], axis=1)
    rows = dot_nn(back_ref[...], wide)
    for k in range(4):
        res_ref[pl.ds(quarter * 4 + k, count, stride=16), :] = rows[:, k * 128 : (k + 1) * 128]


def mode_kernel(
    scale,
    block_ref,
    head_ref,
    weight_hbm,
    both_ref,
    plain_ref,
    back_ref,
    coeff_hbm,
    out_ref,
    coeff_ref,
    weight_ref,
    rows_ref,
    res_ref,
    left_ref,
    mixed_ref,
    sems,
    coeff_sems,
):
    copies = weight_copies(weight_hbm, weight_ref, sems, HEAD)
    for copy in copies[:FLIGHT]:
        copy.start()
    count = rows_ref.shape[0] // 16
    rows_ref[...] = block_ref[...].astype(F32)
    low = lanes((128, 128)) < 64
    kxl = sublanes((128, 128)) % 4
    half = lanes((128, 128)) // 64
    first = (kxl == half).astype(BF16)
    second = (kxl == 2 + half).astype(BF16)
    low8 = lanes((8, 128)) < 64
    sign = jnp.where(sublanes((8, 128)) < 4, -1.0, 1.0)
    for quarter in range(4):
        wide = jnp.concatenate(
            [rows_ref[pl.ds(quarter * 4 + k, count, stride=16), :] for k in range(4)], axis=1
        ).astype(BF16)
        plain = (dot_nn(plain_ref[...], wide) * scale).astype(BF16)
        both = dot_nn(both_ref[...], wide) * scale
        for k in range(4):
            j = quarter * 4 + k
            coeff_ref[j] = plain[:, k * 128 : (k + 1) * 128]
            coeffs = both[:, k * 128 : (k + 1) * 128]
            swapped = swap_halves(coeffs)
            for h in range(2):
                twice = jnp.where(low if h == 0 else ~low, coeffs, swapped).astype(BF16)
                left_ref[j, h] = jnp.concatenate([twice * first, twice * second], axis=1)
    send = pltpu.make_async_copy(coeff_ref, coeff_hbm, coeff_sems.at[0])
    send.start()
    for j in range(16):
        next_weights(copies, j)
        mixed = []
        for u in range(MX // 8):
            halves = [
                dot_nn(left_ref[j, h, u * 32 : (u + 1) * 32, :], mode_pair(head_ref, weight_ref, j, h, u))
                for h in range(2)
            ]
            for t in range(2):
                low_h, high_h = [
                    part[t * 16 : (t + 1) * 16, t * 128 : (t + 1) * 128] for part in halves
                ]
                keep = jnp.where(low8, low_h[:8], sign * high_h[8:])
                move = jnp.where(low8, high_h[:8], sign * low_h[8:])
                mixed.append(keep + swap_halves(move))
        mixed_ref[j] = jnp.concatenate(mixed, axis=0).astype(BF16)
        if j > 4 and j % 4 == 1:
            plane_sums(back_ref, mixed_ref, res_ref, j // 4 - 1)
    plane_sums(back_ref, mixed_ref, res_ref, 3)
    out_ref[...] = res_ref[...].astype(BF16)
    send.wait()


def mode_grad_kernel(
    scale,
    block_ref,
    head_ref,
    weight_hbm,
    straight_ref,
    back_ref,
    coeff_hbm,
    pair_ref,
    coeff_ref,
    out_ref,
    weight_ref,
    rows_ref,
    res_ref,
    mixed_ref,
    sems,
    coeff_sems,
):
    send = pltpu.make_async_copy(coeff_hbm, coeff_ref, coeff_sems.at[0])
    send.start()
    copies = weight_copies(weight_hbm, weight_ref, sems, HEAD)
    for copy in copies[:FLIGHT]:
        copy.start()
    count = rows_ref.shape[0] // 16
    rows_ref[...] = block_ref[...].astype(F32)
    low = lanes((64, 128)) < 64
    low16 = lanes((16, 128)) < 64
    row = sublanes((16, 128)) % 4
    upper = row < 2
    valid = lanes((16, 128)) // 64 == row % 2
    even = (sublanes((16, 128)) < 8).astype(BF16)
    odd = (sublanes((16, 128)) >= 8).astype(BF16)
    for j in range(16):
        section = rows_ref[pl.ds(j, count, stride=16), :]
        swapped = swap_halves(section)
        twice = jnp.concatenate(
            [jnp.where(low, section, swapped), jnp.where(low, swapped, section)], axis=1
        ).astype(BF16)
        turned = dot_nn(straight_ref[...], twice)
        for h in range(2):
            part = turned[:, h * 128 : (h + 1) * 128]
            pair_ref[2 * j + h] = jnp.where(low, part[:64], part[64:]).astype(BF16)
    for j in range(16):
        next_weights(copies, j)
        mixed = []
        for u in range(MX // 8):
            found = []
            for h in range(2):
                pair = pair_ref[2 * j + h, u * 16 : (u + 1) * 16, :]
                rows = dot_nt(
                    jnp.concatenate([pair * even, pair * odd], axis=1),
                    mode_pair(head_ref, weight_ref, j, h, u),
                )
                found.append(jnp.where(valid, jnp.where(upper, rows[:, :128], rows[:, 128:]), 0.0))
            keep = jnp.where(low16, found[0], found[1])
            move = jnp.where(low16, found[1], found[0])
            mixed.append(keep + swap_halves(move))
        mixed_ref[j] = (jnp.concatenate(mixed, axis=0) * scale).astype(BF16)
        if j > 4 and j % 4 == 1:
            plane_sums(back_ref, mixed_ref, res_ref, j // 4 - 1)
    plane_sums(back_ref, mixed_ref, res_ref, 3)
    out_ref[...] = res_ref[...].astype(BF16)
    send.wait()


def weight_grad_kernel(
    scale, coeff_ref, pair_ref, out_hbm, out_ref, mask_ref, turned_ref, pairs_ref, sems
):
    lane = lanes((128, 64))
    part = sublanes((128, 64)) // 64
    for t in range(MX // 4 - VECTOR):
        mask_ref[t] = ((lane // 8 == t) & (lane % 4 // 2 == part)).astype(BF16)
    eye = (sublanes((128, 128)) == lanes((128, 128))).astype(BF16)
    for j in range(16):
        turned_ref[j] = (dot_nt(eye, coeff_ref[j]) * scale).astype(BF16)
        for h in range(2):
            pairs_ref[2 * j + h] = pair_ref[2 * j + h].astype(F32)
    even = (sublanes((64, 128)) % 2 == 0).astype(BF16)
    odd = (sublanes((64, 128)) % 2 == 1).astype(BF16)

    def one_pair(j):
        for h in range(2):
            one = turned_ref[j, h * 64 : (h + 1) * 64, :]
            left = jnp.concatenate([one, one], axis=0)
            pair = pair_ref[j * 2 + h]
            right = jnp.concatenate([pair * even, pair * odd], axis=1)
            for t in range(MX // 4):
                mode = (j * 2 + h) * MX + 4 * t
                if t < MX // 4 - VECTOR:
                    four = dot_nn(left * mask_ref[t], right)
                    for k in range(4):
                        out_ref[mode + k] = four[
                            k // 2 * 64 : (k // 2 + 1) * 64, k % 2 * 128 : (k % 2 + 1) * 128
                        ].astype(BF16)
                    continue
                for k in range(4):
                    total = None
                    for b in range(2):
                        at = t * 8 + b * 4 + k
                        column = jnp.broadcast_to(one[:, at : at + 1], (64, 128))
                        row = jnp.broadcast_to(
                            pairs_ref[j * 2 + h, at : at + 1, :], (64, 128)
                        ).astype(BF16)
                        total = column * row if total is None else total + column * row
                    out_ref[mode + k] = total
        part_copy(out_ref, out_hbm, sems, j, 2 * MX).start()

    @pl.loop(0, 4)
    def _(trip):
        for k in range(4):
            one_pair(trip * 4 + k)

    for j in range(16):
        part_copy(out_ref, out_hbm, sems, j, 2 * MX).wait()


def params(mib):
    return pltpu.CompilerParams(vmem_limit_bytes=mib * 1024 * 1024)


def cost(flops, moved):
    return pl.CostEstimate(flops=int(flops), bytes_accessed=int(moved), transcendentals=0)


def fast_body(features, cotangent, spectral_weight, channel_weight, channel_bias):
    channels, planes, lines, depth_len = features.shape
    devices = lax.axis_size("gx")
    owned_modes = spectral_weight.shape[0]
    wave_pairs = MY * MZ
    volume = planes * devices * lines * depth_len
    forward_scale = 1.0 / math.sqrt(volume)
    inverse_scale = 1.0 / math.sqrt(MX * wave_pairs)
    weight_scale = math.sqrt(MX * wave_pairs / volume)
    table = {name: jnp.asarray(value) for name, value in tables(devices, lines, depth_len).items()}
    for name in ("depth", "depth_pair", "across_y", "back_y"):
        table[name] = pltpu.with_memory_space_constraint(table[name], pltpu.HBM)
    block_rows = devices * 64
    block_shape = jax.ShapeDtypeStruct((block_rows, 128), BF16)
    vmem = pl.BlockSpec(memory_space=pltpu.VMEM)
    hbm = pl.BlockSpec(memory_space=pltpu.HBM)
    smem = pl.BlockSpec(memory_space=pltpu.SMEM)
    field_scratch = pltpu.VMEM(features.shape, BF16)
    field_shape = jax.ShapeDtypeStruct(features.shape, BF16)

    def sems(count):
        return pltpu.SemaphoreType.DMA((count,))

    def scratch(name):
        return pltpu.VMEM(table[name].shape, BF16)

    def in_hbm(array):
        return pltpu.with_memory_space_constraint(array, pltpu.HBM)

    def in_vmem(array):
        return pltpu.with_memory_space_constraint(array, pltpu.VMEM)

    steps = channels // STEP
    lines_scratch = pltpu.VMEM((channels * 2 * MZ, planes * lines), F32)
    rows_scratch = pltpu.VMEM((block_rows, 128), F32)
    spec_scratch = pltpu.VMEM((channels // GROUP, MZ * GROUP, 128), F32)
    weight_rows = pltpu.with_memory_space_constraint(
        spectral_weight.reshape(owned_modes * channels, 2 * channels), pltpu.HBM
    )
    field_bytes = features.size * 2

    def exchange(block):
        return lax.all_to_all(
            block.reshape(devices, 64, 128), "gx", 0, 0, tiled=True
        ).reshape(block_rows, 128)

    def point(field, transposed):
        return pl.pallas_call(
            functools.partial(point_kernel, transposed),
            out_shape=[
                pltpu.HBM(features.shape, BF16),
                pltpu.VMEM((weight_rows.shape[0] * HEAD // 16, weight_rows.shape[1]), BF16),
            ],
            in_specs=[vmem, hbm, hbm],
            out_specs=[hbm, vmem],
            scratch_shapes=[
                field_scratch,
                field_scratch,
                pltpu.VMEM((channels * 16, channels * 16), BF16),
                sems(planes),
                sems(planes),
                sems(HEAD),
            ],
            compiler_params=params(VMEM_MIB),
            cost_estimate=cost(2 * 1024**3, 2 * field_bytes),
            name="channel_map_back" if transposed else "channel_map",
        )(channel_weight, in_hbm(field), weight_rows)

    block = pl.pallas_call(
        analysis_kernel,
        out_shape=block_shape,
        in_specs=[hbm, hbm, hbm],
        out_specs=vmem,
        scratch_shapes=[
            field_scratch,
            scratch("depth_pair"),
            scratch("across_y"),
            lines_scratch,
            rows_scratch,
            sems(steps),
            sems(2),
        ],
        compiler_params=params(VMEM_MIB),
        cost_estimate=cost(2 * 256 * 1024 * 1024, field_bytes),
        name="field_analysis",
    )(in_hbm(features), table["depth_pair"], table["across_y"])
    pointwise, head = point(features, False)
    block, pointwise, head = lax.optimization_barrier((exchange(block), pointwise, head))

    weight_scratch = pltpu.VMEM(
        (weight_rows.shape[0] * (16 - HEAD) // 16, weight_rows.shape[1]), BF16
    )
    mixed_scratch = pltpu.VMEM((16, 64, 128), BF16)
    weight_sems = sems(16 - HEAD)
    coeffs, block = pl.pallas_call(
        functools.partial(mode_kernel, forward_scale),
        out_shape=[pltpu.HBM((16, 64, 128), BF16), block_shape],
        in_specs=[vmem, vmem, hbm, vmem, vmem, vmem],
        out_specs=[hbm, vmem],
        scratch_shapes=[
            pltpu.VMEM((16, 64, 128), BF16),
            weight_scratch,
            rows_scratch,
            rows_scratch,
            pltpu.VMEM((16, 2, 128, 256), BF16),
            mixed_scratch,
            weight_sems,
            sems(1),
        ],
        compiler_params=params(VMEM_MIB),
        cost_estimate=cost(256 * 2 * 16 * 256 * 128, 17 * 2**20),
        name="mode_product",
    )(block, in_vmem(head), weight_rows, table["both_x"], table["plain_x"], table["back_x"])
    block = exchange(block)

    activated, upstream, block = pl.pallas_call(
        functools.partial(middle_kernel, inverse_scale),
        out_shape=[field_shape, pltpu.HBM(features.shape, BF16), block_shape],
        in_specs=[vmem, smem, hbm, hbm, hbm, hbm, hbm, hbm],
        out_specs=[hbm, hbm, vmem],
        scratch_shapes=[
            field_scratch,
            field_scratch,
            scratch("depth"),
            scratch("depth_pair"),
            scratch("across_y"),
            scratch("back_y"),
            field_scratch,
            field_scratch,
            lines_scratch,
            rows_scratch,
            spec_scratch,
            sems(steps),
            sems(steps),
            sems(steps),
            sems(steps),
            sems(4),
        ],
        compiler_params=params(VMEM_MIB),
        cost_estimate=cost(2**30, 4 * field_bytes),
        name="gelu_and_gradient",
    )(
        block,
        channel_bias,
        in_hbm(pointwise),
        in_hbm(cotangent),
        table["depth"],
        table["depth_pair"],
        table["across_y"],
        table["back_y"],
    )
    channel_back, head = point(upstream, True)
    block, channel_back, head = lax.optimization_barrier((exchange(block), channel_back, head))

    pairs, coeffs, block = pl.pallas_call(
        functools.partial(mode_grad_kernel, forward_scale),
        out_shape=[
            pltpu.VMEM((32, 64, 128), BF16),
            pltpu.VMEM((16, 64, 128), BF16),
            block_shape,
        ],
        in_specs=[vmem, vmem, hbm, vmem, vmem, hbm],
        out_specs=[vmem, vmem, vmem],
        scratch_shapes=[
            weight_scratch,
            rows_scratch,
            rows_scratch,
            mixed_scratch,
            weight_sems,
            sems(1),
        ],
        compiler_params=params(VMEM_MIB),
        cost_estimate=cost(256 * 2 * 16 * 256 * 128, 17 * 2**20),
        name="mode_gradient",
    )(block, in_vmem(head), weight_rows, table["straight_x"], table["back_x"], in_hbm(coeffs))
    block = exchange(block)

    spectral_grad = pl.pallas_call(
        functools.partial(weight_grad_kernel, weight_scale),
        out_shape=jax.ShapeDtypeStruct(spectral_weight.shape, BF16),
        in_specs=[vmem, vmem],
        out_specs=hbm,
        scratch_shapes=[
            pltpu.VMEM(spectral_weight.shape, BF16),
            pltpu.VMEM((MX // 4, 128, 64), BF16),
            pltpu.VMEM((16, 128, 64), BF16),
            pltpu.VMEM((32, 64, 128), F32),
            sems(16),
        ],
        compiler_params=params(VMEM_MIB),
        cost_estimate=cost(512 * 2 * 64 * 64 * 256, 17 * 2**20),
        name="weight_gradient",
    )(
        in_vmem(coeffs),
        in_vmem(pairs),
    )

    feature_grad = pl.pallas_call(
        final_kernel,
        out_shape=field_shape,
        in_specs=[vmem, hbm, hbm, hbm],
        out_specs=hbm,
        scratch_shapes=[
            field_scratch,
            scratch("depth"),
            scratch("back_y"),
            field_scratch,
            rows_scratch,
            spec_scratch,
            sems(steps),
            sems(steps),
            sems(2),
        ],
        compiler_params=params(VMEM_MIB),
        cost_estimate=cost(2**29, 2 * field_bytes),
        name="field_gradient",
    )(block, in_hbm(channel_back), table["depth"], table["back_y"])
    return (activated, feature_grad, spectral_grad)


def body(features, cotangent, spectral_weight, channel_weight, channel_bias):
    channels, planes, lines, depth_len = features.shape
    devices = lax.axis_size("gx")
    fits = (
        (channels, planes, lines, depth_len) == (64, PLANES, 64, 128)
        and spectral_weight.shape[0] == 2 * MZ * MX
        and devices * 2 == MY
        and devices * 2 == MX
    )
    run = fast_body if fits else general_body
    return run(features, cotangent, spectral_weight, channel_weight, channel_bias)


def solution(mesh):
    in_specs = (
        P("grp", "gx", None, None),
        P("grp", "gx", None, None),
        P("gx", None, None),
        P(),
        P(),
    )
    out_specs = (
        P("grp", "gx", None, None),
        P("grp", "gx", None, None),
        P(("grp", "gx"), None, None),
    )
    return jax.shard_map(body, mesh=mesh, in_specs=in_specs, out_specs=out_specs, check_vma=False)
```
